32 devices in a mesh: dp: 8 (over z, y), ctx: 4 (over x, core).
Axes of the slice: x: 2, y: 2, z: 4, core: 2. Of those that a mesh axis runs over, the one named last changes fastest.
Arguments:
- tokens: bfloat16 [16, 256, 1152], P('dp', 'ctx'), may hold values from -6 to 6
- lengths: int32 [16], P('dp'), may hold values from 64 to 256, as said below
- gain_one: bfloat16 [1152], P('dp'), may hold values from 0.099609375 to 1.8984375
- w_qkv: bfloat16 [1152, 1920], P('dp', 'ctx'), may hold values from -0.25 to 0.25
- w_out: bfloat16 [1152, 1152], P('dp', 'ctx'), may hold values from -0.75 to 0.75
- gain_two: bfloat16 [1152], P('dp'), may hold values from 0.099609375 to 1.8984375
- w_gate_up: bfloat16 [1152, 6144], P('dp', 'ctx'), may hold values from -0.1875 to 0.1875
- w_down: bfloat16 [3072, 1152], P('dp', 'ctx'), may hold values from -0.109375 to 0.109375
- cotangent: bfloat16 [16, 256, 1152], P('dp', 'ctx'), may hold values from -6 to 6
Outputs:
- output: bfloat16 [16, 256, 1152], P('dp', 'ctx')
- grad_tokens: bfloat16 [16, 256, 1152], P('dp', 'ctx')
- grad_norm_one: float32 [1152], P('dp')
- grad_qkv: float32 [1152, 1920], P('dp', 'ctx')
- grad_out_proj: float32 [1152, 1152], P('dp', 'ctx')
- grad_norm_two: float32 [1152], P('dp')
- grad_gate_up: float32 [1152, 6144], P('dp', 'ctx')
- grad_down: float32 [3072, 1152], P('dp', 'ctx')
The draws below stay inside these ranges and needn't reach their ends.
Inputs may be any that keep to these rules, and one draw needn't show every extreme that they name: `lengths`: in each run of 4 consecutive sequences (those of one dp index) one, which is drawn, fills all 256 slots; the others hold 64 slots or more.
All inputs are finite; a program needn't handle non-finite values.
Results may differ from the reference program's by a relative error of at most 0.02.
Values may be sent and summed in bfloat16 or wider, within the bound.
A program may use at most 128 MiB of HBM per device.

```python
import math
import jax
import jax.numpy as jnp
from jax import lax

D = 1152
QH = 18
KVH = 6
HD = 64
FF = 3072
SEQS = 2
SLOTS = 256
BATCH = 16
QKV = 1920


def draw_lengths(key, part):
    key = jax.random.fold_in(key, 7)
    length_key, pick_key = jax.random.split(key)
    short_lengths = jax.random.randint(length_key, (BATCH,), SLOTS // 4, SLOTS + 1)
    chosen = jax.random.randint(pick_key, (BATCH // SEQS,), 0, SEQS)
    member = jnp.arange(BATCH) % SEQS
    is_full = jnp.repeat(chosen, SEQS) == member
    return jnp.where(is_full, SLOTS, short_lengths).astype(jnp.int32)


def level_of(own_key, dims, pieces, smallest, largest):
    factor_of = 1.0
    for axis_at, blocks in pieces:
        steps = jax.random.uniform(jax.random.fold_in(jax.random.fold_in(own_key, 6), axis_at), (blocks,), jnp.float32, smallest / len(pieces), largest / len(pieces))
        factor_of = factor_of * jnp.repeat(jnp.exp(steps), dims[axis_at] // blocks).reshape((-1,) + (1,) * (len(dims) - 1 - axis_at))
    return factor_of


def scatter_about(rng, extent, scale, most, shards=(), held_as=jnp.bfloat16):
    loudness = level_of(rng, extent, shards, -0.22, 0.18) if shards else 1.0
    values = jax.random.normal(rng, extent, jnp.float32) * scale * loudness
    return jnp.minimum(jnp.maximum(values, -most), most).astype(held_as)


def setup_inputs(seed: int = 0) -> dict:
    seeds = jax.random.split(jax.random.key(seed), 10)
    return {
        "tokens": scatter_about(seeds[0], (BATCH, SLOTS, D), 1.0, 6.0, ((0, 8), (1, 4))),
        "lengths": draw_lengths(jax.random.fold_in(seeds[9], 71), 0),
        "gain_one": jnp.clip(1.0 + 0.18 * jax.random.normal(seeds[2], (D,), jnp.float32), 0.099609375, 1.8984375).astype(jnp.bfloat16),
        "w_qkv": scatter_about(seeds[3], (D, QKV), (D // 2) ** -0.5, 0.25, ((0, 8), (1, 4))),
        "w_out": scatter_about(seeds[4], (QH * HD, D), (QH * HD // 16) ** -0.5, 0.75, ((0, 8), (1, 4))),
        "gain_two": jnp.clip(1.0 + 0.18 * jax.random.normal(seeds[5], (D,), jnp.float32), 0.099609375, 1.8984375).astype(jnp.bfloat16),
        "w_gate_up": scatter_about(seeds[6], (D, 2 * FF), D ** -0.5, 0.1875, ((0, 8), (1, 4))),
        "w_down": scatter_about(seeds[7], (FF, D), FF ** -0.5, 0.109375, ((0, 8), (1, 4))),
        "cotangent": scatter_about(seeds[8], (BATCH, SLOTS, D), 1.0, 6.0, ((0, 8), (1, 4))),
    }


@jax.custom_vjp
def low(v):
    return lax.optimization_barrier(v.astype(jnp.bfloat16)).astype(jnp.float32)

@jax.custom_vjp
def low_back(v):
    return v

def low_keep(v):
    return (low(v), None)

def low_pass(kept, grad):
    return (grad,)

def back_keep(v):
    return (v, None)

def back_low(kept, grad):
    return (low(grad),)
low.defvjp(low_keep, low_pass)
low_back.defvjp(back_keep, back_low)
EPS = 1e-05
PRECISE = lax.Precision.HIGHEST

def tables(item_count, head_width):
    position = jnp.arange(item_count, dtype=jnp.float32)
    frequency = 10000.0 ** (-jnp.arange(head_width // 2, dtype=jnp.float32) * 2.0 / head_width)
    angle_table = position[:, None] * frequency[None, :]
    return (jnp.cos(angle_table), jnp.sin(angle_table))

def rotate(values_in, cosine, sine_table):
    half_width = values_in.shape[-1] // 2
    first_half = values_in[..., :half_width]
    second = values_in[..., half_width:]
    return jnp.concatenate([first_half * cosine - second * sine_table, second * cosine + first_half * sine_table], axis=-1)

def apply_norm(values_in, gain):
    return values_in * lax.rsqrt(lax.optimization_barrier(jnp.mean(values_in * values_in, axis=-1, keepdims=True)) + EPS) * gain

def attend(block_in):
    queries, key_heads, values, length = block_in
    slot_count = queries.shape[0]
    grouped = queries.reshape(slot_count, KVH, QH // KVH, HD)
    scores = jnp.einsum('skgd,tkd->kgst', grouped, key_heads, precision=PRECISE) * (1.0 / math.sqrt(HD))
    scores = low_back(scores)
    rowidx = jnp.arange(slot_count, dtype=jnp.int32)
    allowed = (rowidx[None, :] <= rowidx[:, None]) & (rowidx[None, :] < length)
    scores = jnp.where(allowed, scores, -1e+30)
    prob_rows = low(jax.nn.softmax(scores, axis=-1))
    attended = jnp.einsum('kgst,tkd->skgd', prob_rows, values, precision=PRECISE)
    return attended.reshape(slot_count, QH * HD)

def forward(tokens, gain_one, w_qkv, w_out, gain_two, w_gate_up, w_down, lengths):
    batch_count, slot_count, model_width = tokens.shape
    query_cols = QH * HD
    key_cols = KVH * HD
    valid_rows = (jnp.arange(slot_count, dtype=jnp.int32)[None, :] < lengths[:, None]).astype(tokens.dtype)[..., None]
    normed_one = low(apply_norm(tokens, gain_one))
    projected = low_back(jnp.einsum('bsd,de->bse', normed_one, w_qkv, precision=PRECISE))
    cosine, sine_table = tables(slot_count, HD)
    cosine = cosine[:, None, :]
    sine_table = sine_table[:, None, :]
    queries = low(rotate(projected[..., :query_cols].reshape(batch_count, slot_count, QH, HD), cosine, sine_table))
    key_heads = low(rotate(projected[..., query_cols:query_cols + key_cols].reshape(batch_count, slot_count, KVH, HD), cosine, sine_table))
    values = low(projected[..., query_cols + key_cols:].reshape(batch_count, slot_count, KVH, HD))
    context = lax.map(jax.checkpoint(attend), (queries, key_heads, values, lengths))
    context = low_back(low(context))
    hidden = tokens + low_back(jnp.einsum('bse,ed->bsd', context, w_out, precision=PRECISE))
    normed_two = low(apply_norm(hidden, gain_two))
    gate_up = low_back(jnp.einsum('bsd,df->bsf', normed_two, w_gate_up, precision=PRECISE))
    activation = low(jax.nn.silu(gate_up[..., :FF]) * gate_up[..., FF:])
    return valid_rows * (hidden + jnp.einsum('bsf,fd->bsd', activation, w_down, precision=PRECISE))

def reference(tokens, lengths, gain_one, w_qkv, w_out, gain_two, w_gate_up, w_down, cotangent):

    def wrapped(tok_in, gain_a, qkv_in, out_in, gain_b, gate_in, down_in):
        return forward(tok_in, gain_a, qkv_in, out_in, gain_b, gate_in, down_in, lengths)
    result, pullback = jax.vjp(wrapped, tokens.astype(jnp.float32), gain_one.astype(jnp.float32), w_qkv.astype(jnp.float32), w_out.astype(jnp.float32), gain_two.astype(jnp.float32), w_gate_up.astype(jnp.float32), w_down.astype(jnp.float32))
    grads = pullback(cotangent.astype(jnp.float32))
    return (result.astype(jnp.bfloat16), grads[0].astype(jnp.bfloat16), grads[1], grads[2], grads[3], grads[4], grads[5], grads[6])
```

```python
import functools
import math

import jax
import jax.numpy as jnp
from jax import lax
from jax.experimental import pallas as pl
from jax.experimental.pallas import tpu as pltpu
from jax.sharding import PartitionSpec as P

QH = 18
KVH = 6
HD = 64
FF = 3072


EPS = 1e-05
NEGATIVE = -1e30


def angles(position, head_width):
    frequency = 10000.0 ** (-jnp.arange(head_width // 2, dtype=jnp.float32) * 2.0 / head_width)
    angle_table = position.astype(jnp.float32)[:, None] * frequency[None, :]
    return (jnp.cos(angle_table), jnp.sin(angle_table))


def rotate(values_in, cosine, sine_table):
    half_width = values_in.shape[-1] // 2
    first_half = values_in[..., :half_width]
    second = values_in[..., half_width:]
    return jnp.concatenate(
        [first_half * cosine - second * sine_table, second * cosine + first_half * sine_table],
        axis=-1,
    )


def split_heads(values_in, head_count):
    seq_count, row_count, col_count = values_in.shape
    head_width = col_count // head_count
    moved = values_in.reshape(seq_count, row_count, head_count, head_width).transpose(0, 2, 1, 3)
    return moved.reshape(seq_count * head_count, row_count, head_width)


def join_heads(values_in, seq_count):
    item_count, row_count, head_width = values_in.shape
    head_count = item_count // seq_count
    moved = values_in.reshape(seq_count, head_count, row_count, head_width).transpose(0, 2, 1, 3)
    return moved.reshape(seq_count, row_count, head_count * head_width)


def norm_back(source, inverse, gain, grad_in):
    scaled = grad_in * gain
    mean_term = jnp.mean(scaled * source, axis=-1, keepdims=True)
    back_rows = inverse * scaled - source * (inverse * inverse * inverse) * mean_term
    return (back_rows, jnp.sum(grad_in * source * inverse, axis=(0, 1)))


def block_scores(query_rows, key_rows, position, length, group_count, score_scale):
    raw_scores = (
        jnp.einsum("nd,td->nt", query_rows, key_rows, preferred_element_type=jnp.float32)
        * score_scale
    )
    raw_scores = raw_scores.reshape(group_count, position.shape[0], key_rows.shape[0])
    keyidx = jnp.arange(key_rows.shape[0], dtype=jnp.int32)
    allowed = (keyidx[None, :] <= position[:, None]) & (keyidx[None, :] < length)
    return jnp.where(allowed[None], raw_scores, NEGATIVE)


def on_device(tokens, lengths, gain_one, w_qkv, w_out, gain_two, w_gate_up, w_down, cotangent):
    forward_wide = (
        lax.all_gather(w_qkv, "ctx", axis=1, tiled=True),
        lax.all_gather(w_out, "ctx", axis=1, tiled=True),
        lax.all_gather(w_gate_up, "ctx", axis=1, tiled=True),
        lax.all_gather(w_down, "ctx", axis=1, tiled=True),
    )
    qkv_full, out_full, gate_up_full, down_full, gain_fa, gain_fb = (
        lax.all_gather(forward_wide[0], "dp", axis=0, tiled=True),
        lax.all_gather(forward_wide[1], "dp", axis=0, tiled=True),
        lax.all_gather(forward_wide[2], "dp", axis=0, tiled=True),
        lax.all_gather(forward_wide[3], "dp", axis=0, tiled=True),
        lax.all_gather(gain_one, "dp", axis=0, tiled=True),
        lax.all_gather(gain_two, "dp", axis=0, tiled=True),
    )
    seq_count, row_count, model_width = tokens.shape
    query_cols = QH * HD
    key_cols = KVH * HD
    group_count = QH // KVH
    score_scale = 1.0 / math.sqrt(HD)
    position = lax.axis_index("ctx") * row_count + jnp.arange(row_count, dtype=jnp.int32)
    valid_rows = position[None, :] < lengths[:, None]
    cosine, sine_table = angles(position, HD)
    cosine = cosine[:, None, :]
    sine_table = sine_table[:, None, :]
    source = tokens.astype(jnp.float32)
    inverse_one = lax.rsqrt(jnp.mean(source * source, axis=-1, keepdims=True) + EPS)
    normed_one = (source * inverse_one * gain_fa.astype(jnp.float32)).astype(jnp.bfloat16)
    projected = jnp.einsum("bsd,de->bse", normed_one, qkv_full, preferred_element_type=jnp.float32)
    queries = rotate(
        projected[..., :query_cols].reshape(seq_count, row_count, QH, HD), cosine, sine_table
    )
    queries = queries.astype(jnp.bfloat16).reshape(seq_count, row_count, query_cols)
    key_heads = rotate(
        projected[..., query_cols : query_cols + key_cols].reshape(seq_count, row_count, KVH, HD),
        cosine,
        sine_table,
    )
    key_heads = key_heads.astype(jnp.bfloat16).reshape(seq_count, row_count, key_cols)
    value_heads = projected[..., query_cols + key_cols :].astype(jnp.bfloat16)
    keys_all, values_all = (
        lax.all_gather(key_heads, "ctx", axis=1, tiled=True),
        lax.all_gather(value_heads, "ctx", axis=1, tiled=True),
    )
    query_blocks = split_heads(queries, QH).reshape(seq_count * KVH, group_count * row_count, HD)
    key_blocks = split_heads(keys_all, KVH)
    value_blocks = split_heads(values_all, KVH)
    pair_lengths = jnp.repeat(lengths, KVH)

    def forward_block(block_in):
        query_rows, key_rows, value_rows, length = block_in
        scores = block_scores(query_rows, key_rows, position, length, group_count, score_scale)
        row_max = jnp.max(scores, axis=-1, keepdims=True)
        exp_terms = jnp.exp(scores - row_max)
        row_total = jnp.sum(exp_terms, axis=-1, keepdims=True)
        prob_rows = (exp_terms / row_total).astype(jnp.bfloat16)
        result = jnp.einsum(
            "gst,td->gsd", prob_rows, value_rows, preferred_element_type=jnp.float32
        )
        return (result.reshape(-1, HD), (row_max + jnp.log(row_total))[..., 0])

    context_blocks, log_totals = lax.map(
        forward_block, (query_blocks, key_blocks, value_blocks, pair_lengths)
    )
    context = join_heads(context_blocks.reshape(seq_count * QH, row_count, HD), seq_count).astype(
        jnp.bfloat16
    )
    hidden = source + jnp.einsum(
        "bse,ed->bsd", context, out_full, preferred_element_type=jnp.float32
    )
    inverse_two = lax.rsqrt(jnp.mean(hidden * hidden, axis=-1, keepdims=True) + EPS)
    normed_two = (hidden * inverse_two * gain_fb.astype(jnp.float32)).astype(jnp.bfloat16)
    gate_up = jnp.einsum(
        "bsd,df->bsf", normed_two, gate_up_full, preferred_element_type=jnp.float32
    )
    gate_part = gate_up[..., :FF]
    up_part = gate_up[..., FF:]
    gate_sig = jax.nn.sigmoid(gate_part)
    swish_part = gate_part * gate_sig
    activation = (swish_part * up_part).astype(jnp.bfloat16)
    result_rows = hidden + jnp.einsum(
        "bsf,fd->bsd", activation, down_full, preferred_element_type=jnp.float32
    )
    output = jnp.where(valid_rows[..., None], result_rows, 0.0).astype(jnp.bfloat16)
    back_wide = (
        lax.all_gather(w_qkv, "ctx", axis=1, tiled=True),
        lax.all_gather(w_out, "ctx", axis=1, tiled=True),
        lax.all_gather(w_gate_up, "ctx", axis=1, tiled=True),
        lax.all_gather(w_down, "ctx", axis=1, tiled=True),
    )
    qkv_back, out_back, gate_up_back, down_back, gain_ba, gain_bb = (
        lax.all_gather(back_wide[0], "dp", axis=0, tiled=True),
        lax.all_gather(back_wide[1], "dp", axis=0, tiled=True),
        lax.all_gather(back_wide[2], "dp", axis=0, tiled=True),
        lax.all_gather(back_wide[3], "dp", axis=0, tiled=True),
        lax.all_gather(gain_one, "dp", axis=0, tiled=True),
        lax.all_gather(gain_two, "dp", axis=0, tiled=True),
    )
    grad_rows = jnp.where(valid_rows[..., None], cotangent, jnp.zeros_like(cotangent))
    grad_activation = jnp.einsum(
        "bsd,fd->bsf", grad_rows, down_back, preferred_element_type=jnp.float32
    )
    grad_gate = grad_activation * up_part * gate_sig * (1.0 + gate_part * (1.0 - gate_sig))
    grad_up = grad_activation * swish_part
    grad_mix = jnp.concatenate([grad_gate, grad_up], axis=-1).astype(jnp.bfloat16)
    grad_normed_two = jnp.einsum(
        "bsf,df->bsd", grad_mix, gate_up_back, preferred_element_type=jnp.float32
    )
    back_two, grad_gain_two = norm_back(
        hidden, inverse_two, gain_bb.astype(jnp.float32), grad_normed_two
    )
    grad_hidden = grad_rows.astype(jnp.float32) + back_two
    grad_branch = grad_hidden.astype(jnp.bfloat16)
    grad_context = jnp.einsum(
        "bsd,ed->bse", grad_branch, out_back, preferred_element_type=jnp.float32
    ).astype(jnp.bfloat16)
    grad_blocks = split_heads(grad_context, QH).reshape(
        seq_count * KVH, group_count * row_count, HD
    )

    def backward_block(block_in):
        query_rows, key_rows, value_rows, length, log_total, grad_in = block_in
        scores = block_scores(query_rows, key_rows, position, length, group_count, score_scale)
        prob_rows = jnp.exp(scores - log_total[..., None])
        grad_grouped = grad_in.reshape(group_count, -1, HD)
        grad_probs = jnp.einsum(
            "gsd,td->gst", grad_grouped, value_rows, preferred_element_type=jnp.float32
        )
        grad_value = jnp.einsum(
            "gst,gsd->td",
            prob_rows.astype(jnp.bfloat16),
            grad_grouped,
            preferred_element_type=jnp.float32,
        )
        row_delta = jnp.sum(prob_rows * grad_probs, axis=-1, keepdims=True)
        grad_scores = (prob_rows * (grad_probs - row_delta)).astype(jnp.bfloat16)
        grad_query = (
            jnp.einsum("gst,td->gsd", grad_scores, key_rows, preferred_element_type=jnp.float32)
            * score_scale
        )
        grad_key = (
            jnp.einsum(
                "gst,gsd->td",
                grad_scores,
                query_rows.reshape(group_count, -1, HD),
                preferred_element_type=jnp.float32,
            )
            * score_scale
        )
        return (grad_query.reshape(-1, HD), grad_key, grad_value)

    query_grads, key_grads, value_grads = lax.map(
        backward_block,
        (query_blocks, key_blocks, value_blocks, pair_lengths, log_totals, grad_blocks),
    )
    key_sums, value_sums = (
        lax.psum_scatter(
            join_heads(key_grads, seq_count).astype(jnp.bfloat16),
            "ctx",
            scatter_dimension=1,
            tiled=True,
        ).astype(jnp.float32),
        lax.psum_scatter(
            join_heads(value_grads, seq_count).astype(jnp.bfloat16),
            "ctx",
            scatter_dimension=1,
            tiled=True,
        ).astype(jnp.float32),
    )
    grad_queries = join_heads(query_grads.reshape(seq_count * QH, row_count, HD), seq_count)
    turned_queries = rotate(grad_queries.reshape(seq_count, row_count, QH, HD), cosine, -sine_table)
    turned_keys = rotate(key_sums.reshape(seq_count, row_count, KVH, HD), cosine, -sine_table)
    grad_mixed = jnp.concatenate(
        [
            turned_queries.reshape(seq_count, row_count, query_cols),
            turned_keys.reshape(seq_count, row_count, key_cols),
            value_sums,
        ],
        axis=-1,
    ).astype(jnp.bfloat16)
    grad_normed_one = jnp.einsum(
        "bse,de->bsd", grad_mixed, qkv_back, preferred_element_type=jnp.float32
    )
    back_one, grad_gain_one = norm_back(
        source, inverse_one, gain_ba.astype(jnp.float32), grad_normed_one
    )
    grad_tokens = (grad_hidden + back_one).astype(jnp.bfloat16)
    exchanged = (
        lax.all_to_all(grad_mixed, "ctx", split_axis=2, concat_axis=1, tiled=True),
        lax.all_to_all(grad_branch, "ctx", split_axis=2, concat_axis=1, tiled=True),
        lax.all_to_all(grad_mix, "ctx", split_axis=2, concat_axis=1, tiled=True),
        lax.all_to_all(grad_rows, "ctx", split_axis=2, concat_axis=1, tiled=True),
    )
    initial = (
        jnp.zeros((model_width, exchanged[0].shape[2]), jnp.float32),
        jnp.zeros((context.shape[2], exchanged[1].shape[2]), jnp.float32),
        jnp.zeros((model_width, exchanged[2].shape[2]), jnp.float32),
        jnp.zeros((activation.shape[2], exchanged[3].shape[2]), jnp.float32),
    )
    pieces = (
        lax.all_gather(normed_one, "ctx", axis=1, tiled=True),
        lax.all_gather(context, "ctx", axis=1, tiled=True),
        lax.all_gather(normed_two, "ctx", axis=1, tiled=True),
        lax.all_gather(activation, "ctx", axis=1, tiled=True),
    )
    updated = []
    for total, piece, right in zip(initial, pieces, exchanged):
        updated.append(jnp.einsum("bsr,bsc->rc", piece, right, preferred_element_type=jnp.float32))
    column_grads = tuple(updated)
    gain_whole = lax.psum((grad_gain_one, grad_gain_two), "ctx")
    final_qkv, final_out, final_gate_up, final_down, final_gain_one, final_gain_two = (
        lax.psum_scatter(
            column_grads[0].astype(jnp.bfloat16), "dp", scatter_dimension=0, tiled=True
        ).astype(jnp.float32),
        lax.psum_scatter(
            column_grads[1].astype(jnp.bfloat16), "dp", scatter_dimension=0, tiled=True
        ).astype(jnp.float32),
        lax.psum_scatter(
            column_grads[2].astype(jnp.bfloat16), "dp", scatter_dimension=0, tiled=True
        ).astype(jnp.float32),
        lax.psum_scatter(
            column_grads[3].astype(jnp.bfloat16), "dp", scatter_dimension=0, tiled=True
        ).astype(jnp.float32),
        lax.psum_scatter(
            gain_whole[0].astype(jnp.bfloat16), "dp", scatter_dimension=0, tiled=True
        ).astype(jnp.float32),
        lax.psum_scatter(
            gain_whole[1].astype(jnp.bfloat16), "dp", scatter_dimension=0, tiled=True
        ).astype(jnp.float32),
    )
    return (
        output,
        grad_tokens,
        final_gain_one,
        final_qkv,
        final_out,
        final_gain_two,
        final_gate_up,
        final_down,
    )


MESH = pl.DeviceIdType.MESH


class Place:
    def __init__(self):
        self.dp = lax.axis_index("dp")
        self.ctx = lax.axis_index("ctx")
        self.z = lax.div(self.dp, 2)
        self.y = lax.rem(self.dp, 2)
        self.x = lax.div(self.ctx, 2)
        self.c = lax.rem(self.ctx, 2)
        self.up = (self.dp + 2, self.ctx)
        self.down = (self.dp - 2, self.ctx)
        self.across = (self.dp + 1 - 2 * self.y, self.ctx)
        self.chip = (self.dp, (1 - self.x) * 2 + self.c)
        self.core = (self.dp, self.x * 2 + 1 - self.c)
        self.has_up = self.z < 3
        self.has_down = self.z > 0


def greet(place):
    barrier = pltpu.get_barrier_semaphore()

    def tell(device):
        pl.semaphore_signal(barrier, inc=1, device_id=device, device_id_type=MESH)

    pl.when(place.has_up)(lambda: tell(place.up))
    pl.when(place.has_down)(lambda: tell(place.down))
    tell(place.across)
    for step in (1, 2, 3):
        tell((place.dp, lax.rem(place.ctx + step, 4)))
    ends = place.has_up.astype(jnp.int32) + place.has_down.astype(jnp.int32)
    pl.semaphore_wait(barrier, 4 + ends)


class Wires:
    def __init__(self, send_sems, recv_sems, names):
        self.send_sems = send_sems
        self.recv_sems = recv_sems
        self.index = names
        self.count = 0
        self.pending = []

    def slot(self, name):
        if name not in self.index:
            self.index[name] = len(self.index)
        return self.index[name]

    def send(self, src, dst, name, device, cond=None, extra=None):
        number = self.count
        self.count += 1
        at = self.slot(name)
        if extra is not None:
            at = at + extra
        copy = pltpu.make_async_remote_copy(
            src_ref=src,
            dst_ref=dst,
            send_sem=self.send_sems.at[number],
            recv_sem=self.recv_sems.at[at],
            device_id=device,
            device_id_type=MESH,
        )
        if cond is None:
            copy.start()
        else:
            pl.when(cond)(copy.start)
        self.pending.append((copy, cond))

    def take(self, dst, name, device, extra=None):
        at = self.slot(name)
        if extra is not None:
            at = at + extra
        pltpu.make_async_remote_copy(
            src_ref=dst,
            dst_ref=dst,
            send_sem=self.send_sems.at[0],
            recv_sem=self.recv_sems.at[at],
            device_id=device,
            device_id_type=MESH,
        ).wait_recv()

    def drain(self):
        for copy, cond in self.pending:
            if cond is None:
                copy.wait_send()
            else:
                pl.when(cond)(copy.wait_send)
        self.pending = []


BELOW, ABOVE = 0, 1


def both(first, second):
    return second if first is None else jnp.logical_and(first, second)


def source_valid(place, way, dist):
    return place.z >= dist if way == BELOW else place.z + dist <= 3


def source_pos(place, way, dist):
    return place.dp - 2 * dist if way == BELOW else place.dp + 2 * dist


def flood_start(wires, place, name, own, block, spread):
    wires.send(own, block(place.dp), (name, BELOW, 1), place.up, place.has_up)
    wires.send(own, block(place.dp), (name, ABOVE, 1), place.down, place.has_down)
    wires.send(own, block(place.dp), (name, "y", 0, 0), place.across)
    spread(own, place.dp, (0, 0, 0), None)


def flood_step(wires, place, name, block, spread, way, dist):
    here = source_valid(place, way, dist)
    pos = source_pos(place, way, dist)
    view = block(pos)
    came_from = place.down if way == BELOW else place.up
    pl.when(here)(lambda: wires.take(view, (name, way, dist), came_from))
    if dist < 3:
        onward = place.up if way == BELOW else place.down
        more = place.has_up if way == BELOW else place.has_down
        wires.send(view, view, (name, way, dist + 1), onward, jnp.logical_and(here, more))
    wires.send(view, view, (name, "y", way, dist), place.across, here)
    spread(view, pos, (0, way, dist), here)


def flood_side(wires, place, name, block, spread, way, dist):
    if dist == 0:
        here, pos = None, place.dp
    else:
        here, pos = source_valid(place, way, dist), source_pos(place, way, dist)
    pos = pos + 1 - 2 * place.y
    view = block(pos)
    if here is None:
        wires.take(view, (name, "y", 0, 0), place.across)
    else:
        pl.when(here)(lambda: wires.take(view, (name, "y", way, dist), place.across))
    spread(view, pos, (1, way, dist), here)


HOPS = [(way, dist) for dist in (1, 2, 3) for way in (BELOW, ABOVE)]


def no_spread(view, pos, key, cond):
    return None


def gather_kernel(
    names,
    qkv_ref, out_ref, gu_ref, downt_ref, gain_ref,
    qkv_all, out_all, gu_all, downt_all, gain_all,
    send_sems, recv_sems, local_sems,
):
    place = Place()
    wires = Wires(send_sems, recv_sems, names)
    rows = qkv_ref.shape[0]
    units = gu_all.shape[2]
    half = downt_ref.shape[1]
    strip = downt_ref.shape[0]
    dp, ctx = place.dp, place.ctx
    greet(place)

    def row_view(ref, lead, pos):
        return ref.at[lead, pl.ds(pl.multiple_of(pos * rows, 16), rows)]

    locals_ = []

    def local(src, dst, cond=None):
        copy = pltpu.make_async_copy(src, dst, local_sems.at[len(locals_)])
        locals_.append((copy, cond))
        if cond is None:
            copy.start()
        else:
            pl.when(cond)(copy.start)

    for part in range(2):
        target = 2 * place.c + part
        src = gu_ref.at[:, pl.ds(part * units, units)]
        dst = row_view(gu_all, place.x, dp)
        away = target != ctx
        wires.send(src, dst, ("gu_mix", 0), (dp, target), away, extra=place.x)
        local(src, dst, target == ctx)
    wires.slot(("gu_mix", 1))

    def attention_spread(name, ref):
        def spread(view, pos, key, cond):
            dst = row_view(ref, ctx, pos)
            wires.send(view, dst, (name, "x") + key, place.chip, cond)
            wires.send(view, dst, (name, "c") + key, place.core, cond)
        return spread

    attention = [("qkv", qkv_ref, qkv_all), ("out", out_ref, out_all)]
    for name, own, ref in attention:
        block = functools.partial(row_view, ref, ctx)
        local(own, block(dp))
        flood_start(wires, place, name, own, block, attention_spread(name, ref))
    gain_block = lambda pos: gain_all.at[pos]
    local(gain_ref, gain_block(dp))
    flood_start(wires, place, "gain", gain_ref, gain_block, no_spread)

    lanes = pl.ds(pl.multiple_of(place.y * half, 128), half)
    other_lanes = pl.ds(pl.multiple_of((1 - place.y) * half, 128), half)
    dst = downt_all.at[pl.ds(pl.multiple_of(ctx * strip, 16), strip), lanes]
    wires.send(downt_ref, dst, ("down_mix", 0), (dp, place.z), ctx != place.z, extra=ctx)
    for j in range(1, 4):
        wires.slot(("down_mix", j))
    local(downt_ref, dst, ctx == place.z)

    def gu_view(part):
        return functools.partial(row_view, gu_all, part)

    for part in range(2):
        remote = (part * 2 + place.x) != ctx
        came_from = (dp, part * 2 + place.x)
        view = gu_view(part)(dp)
        pl.when(remote)(lambda: wires.take(view, ("gu_mix", part), came_from))
    for copy, cond in locals_:
        if cond is None:
            copy.wait()
        else:
            pl.when(cond)(copy.wait)
    for part in range(2):
        flood_start(wires, place, ("gu", part), gu_view(part)(dp), gu_view(part), no_spread)

    at_home = ctx == place.z
    strips = [downt_all.at[pl.ds(j * strip, strip), lanes] for j in range(4)]
    other_strips = [downt_all.at[pl.ds(j * strip, strip), other_lanes] for j in range(4)]

    def take_strips():
        for j in range(4):
            pl.when(ctx != j)(
                functools.partial(wires.take, strips[j], ("down_mix", j), (dp, j))
            )

    pl.when(at_home)(take_strips)
    for j in range(4):
        wires.send(strips[j], strips[j], ("down", j, BELOW, 1), place.up, jnp.logical_and(at_home, place.has_up))
        wires.send(strips[j], strips[j], ("down", j, ABOVE, 1), place.down, jnp.logical_and(at_home, place.has_down))
        wires.send(strips[j], strips[j], ("down_y", j), place.across, at_home)

    def down_step(way, dist):
        offset = place.z - ctx if way == BELOW else ctx - place.z
        here = offset == dist
        came_from = place.down if way == BELOW else place.up
        onward = place.up if way == BELOW else place.down
        more = place.has_up if way == BELOW else place.has_down
        for j in range(4):
            pl.when(here)(functools.partial(wires.take, strips[j], ("down", j, way, dist), came_from))
            if dist < 3:
                wires.send(strips[j], strips[j], ("down", j, way, dist + 1), onward, jnp.logical_and(here, more))
            wires.send(strips[j], strips[j], ("down_y", j), place.across, here)

    for way, dist in HOPS:
        for name, own, ref in attention:
            flood_step(wires, place, name, functools.partial(row_view, ref, ctx), attention_spread(name, ref), way, dist)
        flood_step(wires, place, "gain", gain_block, no_spread, way, dist)
        for part in range(2):
            flood_step(wires, place, ("gu", part), gu_view(part), no_spread, way, dist)
        down_step(way, dist)
    for way, dist in [(0, 0)] + HOPS:
        for name, own, ref in attention:
            flood_side(wires, place, name, functools.partial(row_view, ref, ctx), attention_spread(name, ref), way, dist)
        flood_side(wires, place, "gain", gain_block, no_spread, way, dist)

    def positions():
        for side in range(2):
            for way, dist in [(0, 0)] + HOPS:
                if dist == 0:
                    here, pos = None, place.dp
                else:
                    here, pos = source_valid(place, way, dist), source_pos(place, way, dist)
                if side == 1:
                    pos = pos + 1 - 2 * place.y
                yield (side, way, dist), here, pos

    far = place.chip[1]
    for name, own, ref in attention:
        for key, here, pos in positions():
            view = row_view(ref, far, pos)
            def arrive():
                wires.take(view, (name, "x") + key, place.chip)
            if here is None:
                arrive()
            else:
                pl.when(here)(arrive)
            wires.send(view, view, (name, "d") + key, place.core, here)
    for name, own, ref in attention:
        for key, here, pos in positions():
            for mark, lead in (("c", place.core[1]), ("d", 3 - ctx)):
                view = row_view(ref, lead, pos)
                def arrive():
                    wires.take(view, (name, mark) + key, place.core)
                if here is None:
                    arrive()
                else:
                    pl.when(here)(arrive)
    for part in range(2):
        for way, dist in [(0, 0)] + HOPS:
            flood_side(wires, place, ("gu", part), gu_view(part), no_spread, way, dist)
    for j in range(4):
        wires.take(other_strips[j], ("down_y", j), place.across)
    wires.drain()


def gather_weights(w_qkv, w_out, w_gate_up, down_t, gains):
    dtype = w_qkv.dtype
    rows = w_qkv.shape[0]
    units = w_gate_up.shape[1] // 2
    shapes = (
        jax.ShapeDtypeStruct((4, 8 * rows, w_qkv.shape[1]), dtype),
        jax.ShapeDtypeStruct((4, 8 * rows, w_out.shape[1]), dtype),
        jax.ShapeDtypeStruct((2, 8 * rows, units), dtype),
        jax.ShapeDtypeStruct((4 * down_t.shape[0], 2 * down_t.shape[1]), dtype),
        jax.ShapeDtypeStruct((8,) + gains.shape, gains.dtype),
    )
    anywhere = pl.BlockSpec(memory_space=pltpu.MemorySpace.HBM)
    return pl.pallas_call(
        functools.partial(gather_kernel, {}),
        out_shape=shapes,
        in_specs=[anywhere] * 5,
        out_specs=[anywhere] * 5,
        scratch_shapes=[
            pltpu.SemaphoreType.DMA((260,)),
            pltpu.SemaphoreType.DMA((260,)),
            pltpu.SemaphoreType.DMA((8,)),
        ],
        compiler_params=pltpu.CompilerParams(collective_id=0, has_side_effects=True),
        name="gather_weights",
    )(w_qkv, w_out, w_gate_up, down_t, gains)


def add_rows(dst, srcs, out=None, cast=None, chunk=48):
    out = dst if out is None else out
    total_rows = dst.shape[0]
    assert total_rows % chunk == 0

    def body(i, carry):
        at = pl.ds(pl.multiple_of(i * chunk, 16), chunk)
        total = dst[at, :].astype(jnp.float32)
        for src in srcs:
            total = total + src[at, :].astype(jnp.float32)
        out[at, :] = total.astype(out.dtype)
        return carry

    lax.fori_loop(0, total_rows // chunk, body, 0)


def when(cond, action):
    if cond is None:
        action()
    else:
        pl.when(cond)(action)


DRAIN = [(way, dist) for dist in (3, 2, 1, 0) for way in (BELOW, ABOVE)]


def sink_step(wires, place, name, block, inbox, way, dist):
    here = source_valid(place, way, dist)
    pos = source_pos(place, way, dist)
    view = block(pos)
    fed = place.has_up if way == BELOW else place.has_down
    feeder = place.up if way == BELOW else place.down
    onward = place.down if way == BELOW else place.up
    if dist < 3:

        def arrive():
            wires.take(inbox.at[way, dist], (name, way, dist), feeder)
            add_rows(view, [inbox.at[way, dist]])

        pl.when(jnp.logical_and(here, fed))(arrive)
    if dist > 0:
        wires.send(view, inbox.at[way, dist - 1], (name, way, dist - 1), onward, here)


def scatter_kernel(
    names,
    qkv_in, out_in, gu_in, downt_in, gain_in,
    qkv_out, out_out, gu_out, downt_out, gain_out,
    qkv, out, gu, downt,
    qkv_core, out_core, qkv_chip, out_chip, qkv_side, out_side, gu_side, down_side,
    qkv_inbox, out_inbox, gu_inbox, down_inbox, gu_mix, down_mix, gain_box,
    send_sems, recv_sems, local_sems,
):
    place = Place()
    wires = Wires(send_sems, recv_sems, names)
    dp, ctx, z, y = place.dp, place.ctx, place.z, place.y
    rows = qkv_out.shape[0]
    units = gu.shape[2]
    strip, half = downt_out.shape
    loads = []
    for src, dst in ((gu_in, gu), (downt_in, downt), (out_in, out), (qkv_in, qkv)):
        copy = pltpu.make_async_copy(src, dst, local_sems.at[len(loads)])
        copy.start()
        loads.append(copy)
    greet(place)

    def row_view(ref, lead, pos):
        return ref.at[lead, pl.ds(pl.multiple_of(pos * rows, 16), rows)]

    lanes = pl.ds(pl.multiple_of(y * half, 128), half)
    other_lanes = pl.ds(pl.multiple_of((1 - y) * half, 128), half)
    strips = [downt.at[pl.ds(j * strip, strip), lanes] for j in range(4)]
    other_strips = [downt.at[pl.ds(j * strip, strip), other_lanes] for j in range(4)]
    loads[0].wait()
    for zs in range(4):
        for part in range(2):
            wires.send(row_view(gu, part, 2 * zs + 1 - y), gu_side.at[part, zs], ("gu_y", part, zs), place.across)
    loads[1].wait()
    for j in range(4):
        wires.send(other_strips[j], down_side.at[j], ("down_y", j), place.across)
    attention = [
        ("out", out, out_core, out_chip, out_side, out_inbox, out_out),
        ("qkv", qkv, qkv_core, qkv_chip, qkv_side, qkv_inbox, qkv_out),
    ]
    pair = 2 * rows

    def pair_view(ref, lead, zs):
        return ref.at[lead, pl.ds(zs * pair, pair)]

    for number, (name, ref, core, chip, side, inbox, final) in enumerate(attention):
        loads[2 + number].wait()
        for zs in range(4):
            for xx in range(2):
                wires.send(
                    pair_view(ref, 2 * xx + 1 - place.c, zs), pair_view(core, xx, zs),
                    (name, "c", xx, zs), place.core,
                )
    for name, ref, core, chip, side, inbox, final in attention:
        far = place.chip[1]
        for zs in range(4):
            for xx in range(2):
                wires.take(pair_view(core, xx, zs), (name, "c", xx, zs), place.core)
                add_rows(pair_view(ref, 2 * xx + place.c, zs), [pair_view(core, xx, zs)])
            wires.send(pair_view(ref, far, zs), chip.at[pl.ds(zs * pair, pair)], (name, "x", zs), place.chip)
    for zs in range(4):
        for part in range(2):
            wires.take(gu_side.at[part, zs], ("gu_y", part, zs), place.across)
            add_rows(row_view(gu, part, 2 * zs + y), [gu_side.at[part, zs]])
    for j in range(4):
        wires.take(down_side.at[j], ("down_y", j), place.across)
        add_rows(strips[j], [down_side.at[j]])
    for name, ref, core, chip, side, inbox, final in attention:
        for zs in range(4):
            span = chip.at[pl.ds(zs * pair, pair)]
            wires.take(span, (name, "x", zs), place.chip)
            add_rows(pair_view(ref, ctx, zs), [span])
            wires.send(row_view(ref, ctx, 2 * zs + 1 - y), side.at[zs], (name, "y", zs), place.across)

    def down_step(dist):
        for way in (BELOW, ABOVE):
            offset = z - ctx if way == BELOW else ctx - z
            here = offset == dist
            fed = place.has_up if way == BELOW else place.has_down
            feeder = place.up if way == BELOW else place.down
            onward = place.down if way == BELOW else place.up
            for j in range(4):
                def arrive():
                    wires.take(down_inbox.at[way, j], ("down", j, way), feeder)
                    add_rows(strips[j], [down_inbox.at[way, j]])
                pl.when(jnp.logical_and(here, fed))(arrive)
                if dist > 0:
                    wires.send(strips[j], down_inbox.at[way, j], ("down", j, way), onward, here)

    for way, dist in DRAIN:
        for part in range(2):
            sink_step(wires, place, ("gu", part), functools.partial(row_view, gu, part), gu_inbox.at[part], way, dist)
        if way == BELOW:
            down_step(dist)
    for part in range(2):
        target = part * 2 + place.x
        block = row_view(gu, part, dp)
        wires.send(block, gu_mix.at[place.c], ("gu_mix", 0), (dp, target), target != ctx, extra=place.c)

        def keep():
            add_rows(block, [], out=gu_mix.at[place.c])

        pl.when(target == ctx)(keep)
    wires.slot(("gu_mix", 1))
    for j in range(4):
        here = ctx == z
        wires.send(strips[j], down_mix, ("down_mix",), (dp, j), jnp.logical_and(here, ctx != j))
        pl.when(jnp.logical_and(here, ctx == j))(functools.partial(add_rows, strips[j], [], down_mix))
    for name, ref, core, chip, side, inbox, final in attention:
        for zs in range(4):
            wires.take(side.at[zs], (name, "y", zs), place.across)
            add_rows(row_view(ref, ctx, 2 * zs + y), [side.at[zs]])
        for way, dist in DRAIN:
            sink_step(wires, place, name, functools.partial(row_view, ref, ctx), inbox, way, dist)
        add_rows(row_view(ref, ctx, dp), [], out=final)

    gain_out[...] = gain_in[...]

    def swap(slot, device, cond=None):
        wires.send(gain_out, gain_box.at[slot], ("gain", slot), device, cond)

    def add_gain(slot, device):
        wires.take(gain_box.at[slot], ("gain", slot), device)
        gain_out[...] = gain_out[...] + gain_box[slot]

    def settle():
        copy, cond = wires.pending.pop()
        when(cond, copy.wait_send)

    for slot, device in enumerate((place.core, place.chip, place.across)):
        swap(slot, device)
        settle()
        add_gain(slot, device)
    low_end, high_end = z == 0, z == 3
    mid_low, mid_high = z == 1, z == 2
    swap(3, place.up, low_end)
    settle()
    swap(3, place.down, high_end)
    settle()
    pl.when(mid_low)(lambda: add_gain(3, place.down))
    pl.when(mid_high)(lambda: add_gain(3, place.up))
    swap(4, place.up, mid_low)
    settle()
    swap(4, place.down, mid_high)
    settle()
    pl.when(mid_low)(lambda: add_gain(4, place.up))
    pl.when(mid_high)(lambda: add_gain(4, place.down))
    swap(5, place.down, mid_low)
    swap(5, place.up, mid_high)

    def last(device):
        wires.take(gain_box.at[5], ("gain", 5), device)
        gain_out[...] = gain_box[5]

    pl.when(low_end)(lambda: last(place.up))
    pl.when(high_end)(lambda: last(place.down))

    for part in range(2):
        source = 2 * place.c + part
        pl.when(source != ctx)(
            lambda: wires.take(gu_mix.at[part], ("gu_mix", part), (dp, source))
        )
        add_rows(gu_mix.at[part], [], out=gu_out.at[:, pl.ds(part * units, units)])
    pl.when(ctx != z)(lambda: wires.take(down_mix, ("down_mix",), (dp, z)))
    add_rows(down_mix, [], out=downt_out)
    wires.drain()


def scatter_grads(qkv, out, gu, downt, gains):
    rows = qkv.shape[1] // 8
    qkv_cols, out_cols, units = qkv.shape[2], out.shape[2], gu.shape[2]
    strip, half = downt.shape[0] // 4, downt.shape[1] // 2
    f32, low = jnp.float32, qkv.dtype
    shapes = (
        jax.ShapeDtypeStruct((rows, qkv_cols), f32),
        jax.ShapeDtypeStruct((rows, out_cols), f32),
        jax.ShapeDtypeStruct((rows, 2 * units), f32),
        jax.ShapeDtypeStruct((strip, half), f32),
        jax.ShapeDtypeStruct(gains.shape, f32),
    )
    anywhere = pl.BlockSpec(memory_space=pltpu.MemorySpace.HBM)
    vmem = pl.BlockSpec(memory_space=pltpu.MemorySpace.VMEM)

    def box(*shape, dtype=low):
        return pltpu.VMEM(shape, dtype)

    scratch = [
        box(*qkv.shape), box(*out.shape), box(*gu.shape), box(*downt.shape),
        box(2, 8 * rows, qkv_cols), box(2, 8 * rows, out_cols),
        box(8 * rows, qkv_cols), box(8 * rows, out_cols),
        box(4, rows, qkv_cols), box(4, rows, out_cols),
        box(2, 4, rows, units), box(4, strip, half),
        box(2, 3, rows, qkv_cols), box(2, 3, rows, out_cols),
        box(2, 2, 3, rows, units), box(2, 4, strip, half),
        box(2, rows, units), box(strip, half),
        box(6, *gains.shape, dtype=f32),
        pltpu.SemaphoreType.DMA((200,)),
        pltpu.SemaphoreType.DMA((200,)),
        pltpu.SemaphoreType.DMA((4,)),
    ]
    return pl.pallas_call(
        functools.partial(scatter_kernel, {}),
        out_shape=shapes,
        in_specs=[anywhere] * 4 + [vmem],
        out_specs=[vmem] * 5,
        scratch_shapes=scratch,
        compiler_params=pltpu.CompilerParams(
            collective_id=1, has_side_effects=True, vmem_limit_bytes=60 * 2**20
        ),
        name="scatter_grads",
    )(qkv, out, gu, downt, gains)


def split_columns(values_in, parts):
    return jnp.concatenate([values_in[j] for j in range(parts)], axis=-1)


def on_device_fast(tokens, lengths, gain_one, w_qkv, w_out, gain_two, w_gate_up, w_down, cotangent):
    seq_count, row_count, width = tokens.shape
    rows = seq_count * row_count
    f32, low = jnp.float32, jnp.bfloat16
    block = gain_one.shape[0]
    gains = jnp.zeros((8, 256), f32)
    gains = gains.at[0, :block].set(gain_one.astype(f32)).at[1, :block].set(gain_two.astype(f32))
    qkv_all, out_all, gu_all, down_t, gain_all = gather_weights(
        w_qkv, w_out, w_gate_up, w_down.T, gains
    )
    gain_a = gain_all[:, 0, :block].reshape(-1)
    gain_b = gain_all[:, 1, :block].reshape(-1)
    query_cols, key_cols = QH * HD, KVH * HD
    group = QH // KVH
    scale = 1.0 / math.sqrt(HD)
    position = lax.axis_index("ctx") * row_count + jnp.arange(row_count, dtype=jnp.int32)
    valid_rows = position[None, :] < lengths[:, None]
    cosine, sine_table = angles(position, HD)
    cosine, sine_table = cosine[:, None, :], sine_table[:, None, :]
    grad_rows = jnp.where(valid_rows[..., None], cotangent, jnp.zeros_like(cotangent))
    grad_all = lax.all_gather(grad_rows, "ctx").reshape(-1, width)
    source = tokens.astype(f32).reshape(rows, width)
    inverse_one = lax.rsqrt(jnp.mean(source * source, axis=-1, keepdims=True) + EPS)
    normed_one = (source * inverse_one * gain_a).astype(low)
    projected = split_columns(
        jnp.einsum("rd,jde->jre", normed_one, qkv_all, preferred_element_type=f32), 4
    ).reshape(seq_count, row_count, -1)
    queries = rotate(
        projected[..., :query_cols].reshape(seq_count, row_count, QH, HD), cosine, sine_table
    ).astype(low)
    keys = rotate(
        projected[..., query_cols : query_cols + key_cols].reshape(seq_count, row_count, KVH, HD),
        cosine, sine_table,
    ).astype(low)
    values = projected[..., query_cols + key_cols :].astype(low).reshape(seq_count, row_count, KVH, HD)
    both_all = lax.all_gather(jnp.stack([keys, values]), "ctx", axis=2, tiled=True)
    keys_all = both_all[0].transpose(0, 2, 1, 3)
    values_all = both_all[1].transpose(0, 2, 1, 3)
    slots = keys_all.shape[2]
    query_blocks = (
        queries.reshape(seq_count, row_count, KVH, group, HD)
        .transpose(0, 2, 3, 1, 4)
        .reshape(seq_count, KVH, group * row_count, HD)
    )
    keyidx = jnp.arange(slots, dtype=jnp.int32)
    allowed = (keyidx[None, None, :] <= position[None, :, None]) & (
        keyidx[None, None, :] < lengths[:, None, None]
    )
    allowed = jnp.broadcast_to(
        allowed[:, None, None], (seq_count, 1, group, row_count, slots)
    ).reshape(seq_count, 1, group * row_count, slots)
    scores = jnp.einsum("bksd,bktd->bkst", query_blocks, keys_all, preferred_element_type=f32) * scale
    scores = jnp.where(allowed, scores, NEGATIVE)
    row_max = jnp.max(scores, axis=-1, keepdims=True)
    terms = jnp.exp(scores - row_max)
    probs = terms / jnp.sum(terms, axis=-1, keepdims=True)
    probs_low = probs.astype(low)
    attended = jnp.einsum("bkst,bktd->bksd", probs_low, values_all, preferred_element_type=f32)

    def join(blocks):
        return (
            blocks.reshape(seq_count, KVH, group, row_count, HD)
            .transpose(0, 3, 1, 2, 4)
            .reshape(rows, query_cols)
        )

    context = join(attended.astype(low))
    hidden = source + split_columns(
        jnp.einsum("re,jed->jrd", context, out_all, preferred_element_type=f32), 4
    )
    inverse_two = lax.rsqrt(jnp.mean(hidden * hidden, axis=-1, keepdims=True) + EPS)
    normed_two = (hidden * inverse_two * gain_b).astype(low)
    normed_all = lax.all_gather(normed_two, "ctx").reshape(-1, width)
    gate = jnp.dot(normed_all, gu_all[0], preferred_element_type=f32)
    up = jnp.dot(normed_all, gu_all[1], preferred_element_type=f32)
    gate_sig = jax.nn.sigmoid(gate)
    swish = gate * gate_sig
    activation = (swish * up).astype(low)
    partial = jnp.einsum("rf,df->rd", activation, down_t, preferred_element_type=f32)
    branch = lax.psum_scatter(
        partial.astype(low).reshape(4, rows, width), "ctx", scatter_dimension=0, tiled=False
    )
    result = hidden + branch.astype(f32)
    output = jnp.where(
        valid_rows[..., None], result.reshape(seq_count, row_count, width), 0.0
    ).astype(low)
    grad_act = jnp.dot(grad_all, down_t, preferred_element_type=f32)
    grad_gate = (grad_act * up * gate_sig * (1.0 + gate * (1.0 - gate_sig))).astype(low)
    grad_up = (grad_act * swish).astype(low)
    grad_normed = jnp.einsum("rf,df->rd", grad_gate, gu_all[0], preferred_element_type=f32)
    grad_normed = grad_normed + jnp.einsum("rf,df->rd", grad_up, gu_all[1], preferred_element_type=f32)
    grad_down_t = jnp.einsum("rd,rf->df", grad_all, activation, preferred_element_type=f32).astype(low)
    grad_gu = jnp.stack(
        [
            jnp.einsum("rd,rf->df", normed_all, grad_gate, preferred_element_type=f32),
            jnp.einsum("rd,rf->df", normed_all, grad_up, preferred_element_type=f32),
        ]
    ).astype(low)
    grad_normed_two = lax.psum_scatter(
        grad_normed.astype(low).reshape(4, rows, width), "ctx", scatter_dimension=0, tiled=False
    ).astype(f32)
    flat_grad = grad_rows.astype(f32).reshape(rows, width)

    def norm_rows(source_in, inverse, gain, grad_in):
        scaled = grad_in * gain
        mean_term = jnp.mean(scaled * source_in, axis=-1, keepdims=True)
        back = inverse * scaled - source_in * (inverse * inverse * inverse) * mean_term
        return back, jnp.sum(grad_in * source_in * inverse, axis=0)

    back_two, grad_gain_two = norm_rows(hidden, inverse_two, gain_b, grad_normed_two)
    grad_hidden = flat_grad + back_two
    grad_branch = grad_hidden.astype(low)
    wide = grad_branch.reshape(rows, 4, -1)
    grad_out = jnp.einsum("re,rjd->jed", context, wide, preferred_element_type=f32).astype(low)
    grad_context = jnp.einsum("rjd,jed->re", wide, out_all, preferred_element_type=f32).astype(low)
    grad_blocks = (
        grad_context.reshape(seq_count, row_count, KVH, group, HD)
        .transpose(0, 2, 3, 1, 4)
        .reshape(seq_count, KVH, group * row_count, HD)
    )
    grad_probs = jnp.einsum("bksd,bktd->bkst", grad_blocks, values_all, preferred_element_type=f32)
    delta = jnp.sum(probs * grad_probs, axis=-1, keepdims=True)
    grad_scores = (probs * (grad_probs - delta)).astype(low)
    grad_values = jnp.einsum("bkst,bksd->bktd", probs_low, grad_blocks, preferred_element_type=f32)
    grad_keys = jnp.einsum("bkst,bksd->bktd", grad_scores, query_blocks, preferred_element_type=f32) * scale
    grad_queries = jnp.einsum("bkst,bktd->bksd", grad_scores, keys_all, preferred_element_type=f32) * scale
    sums = lax.psum_scatter(
        jnp.stack([grad_keys, grad_values]).astype(low).transpose(3, 0, 1, 2, 4),
        "ctx", scatter_dimension=0, tiled=True,
    ).astype(f32)
    sums = sums.transpose(1, 2, 0, 3, 4)
    turned_queries = rotate(
        join(grad_queries).reshape(seq_count, row_count, QH, HD), cosine, -sine_table
    )
    turned_keys = rotate(sums[0], cosine, -sine_table)
    grad_mixed = jnp.concatenate(
        [
            turned_queries.reshape(rows, query_cols),
            turned_keys.reshape(rows, key_cols),
            sums[1].reshape(rows, key_cols),
        ],
        axis=-1,
    ).astype(low).reshape(rows, 4, -1)
    grad_qkv = jnp.einsum("rd,rje->jde", normed_one, grad_mixed, preferred_element_type=f32).astype(low)
    grad_normed_one = jnp.einsum("rje,jde->rd", grad_mixed, qkv_all, preferred_element_type=f32)
    back_one, grad_gain_one = norm_rows(source, inverse_one, gain_a, grad_normed_one)
    grad_tokens = (grad_hidden + back_one).astype(low).reshape(tokens.shape)
    gain_rows = jnp.zeros((8, width), f32).at[0].set(grad_gain_one).at[1].set(grad_gain_two)
    final_qkv, final_out, final_gu, final_down, gain_sums = scatter_grads(
        grad_qkv, grad_out, grad_gu, grad_down_t, gain_rows
    )
    mine = lax.dynamic_slice(gain_sums, (0, lax.axis_index("dp") * block), (8, block))
    return (output, grad_tokens, mine[0], final_qkv, final_out, mine[1], final_gu, final_down.T)


def solution(mesh):
    fits = mesh.shape["dp"] == 8 and mesh.shape["ctx"] == 4
    return jax.shard_map(
        on_device_fast if fits else on_device,
        mesh=mesh,
        in_specs=(
            P("dp", "ctx", None),
            P("dp"),
            P("dp"),
            P("dp", "ctx"),
            P("dp", "ctx"),
            P("dp"),
            P("dp", "ctx"),
            P("dp", "ctx"),
            P("dp", "ctx", None),
        ),
        out_specs=(
            P("dp", "ctx", None),
            P("dp", "ctx", None),
            P("dp"),
            P("dp", "ctx"),
            P("dp", "ctx"),
            P("dp"),
            P("dp", "ctx"),
            P("dp", "ctx"),
        ),
        check_vma=False,
    )
```

```python
import functools
import math

import jax
import jax.numpy as jnp
from jax import lax
from jax.experimental import pallas as pl
from jax.experimental.pallas import tpu as pltpu
from jax.sharding import PartitionSpec as P

QH = 18
KVH = 6
HD = 64
FF = 3072


EPS = 1e-05
NEGATIVE = -1e30


def angles(position, head_width):
    frequency = 10000.0 ** (-jnp.arange(head_width // 2, dtype=jnp.float32) * 2.0 / head_width)
    angle_table = position.astype(jnp.float32)[:, None] * frequency[None, :]
    return (jnp.cos(angle_table), jnp.sin(angle_table))


def rotate(values_in, cosine, sine_table):
    half_width = values_in.shape[-1] // 2
    first_half = values_in[..., :half_width]
    second = values_in[..., half_width:]
    return jnp.concatenate(
        [first_half * cosine - second * sine_table, second * cosine + first_half * sine_table],
        axis=-1,
    )


def split_heads(values_in, head_count):
    seq_count, row_count, col_count = values_in.shape
    head_width = col_count // head_count
    moved = values_in.reshape(seq_count, row_count, head_count, head_width).transpose(0, 2, 1, 3)
    return moved.reshape(seq_count * head_count, row_count, head_width)


def join_heads(values_in, seq_count):
    item_count, row_count, head_width = values_in.shape
    head_count = item_count // seq_count
    moved = values_in.reshape(seq_count, head_count, row_count, head_width).transpose(0, 2, 1, 3)
    return moved.reshape(seq_count, row_count, head_count * head_width)


def norm_back(source, inverse, gain, grad_in):
    scaled = grad_in * gain
    mean_term = jnp.mean(scaled * source, axis=-1, keepdims=True)
    back_rows = inverse * scaled - source * (inverse * inverse * inverse) * mean_term
    return (back_rows, jnp.sum(grad_in * source * inverse, axis=(0, 1)))


def block_scores(query_rows, key_rows, position, length, group_count, score_scale):
    raw_scores = (
        jnp.einsum("nd,td->nt", query_rows, key_rows, preferred_element_type=jnp.float32)
        * score_scale
    )
    raw_scores = raw_scores.reshape(group_count, position.shape[0], key_rows.shape[0])
    keyidx = jnp.arange(key_rows.shape[0], dtype=jnp.int32)
    allowed = (keyidx[None, :] <= position[:, None]) & (keyidx[None, :] < length)
    return jnp.where(allowed[None], raw_scores, NEGATIVE)


def on_device(tokens, lengths, gain_one, w_qkv, w_out, gain_two, w_gate_up, w_down, cotangent):
    forward_wide = (
        lax.all_gather(w_qkv, "ctx", axis=1, tiled=True),
        lax.all_gather(w_out, "ctx", axis=1, tiled=True),
        lax.all_gather(w_gate_up, "ctx", axis=1, tiled=True),
        lax.all_gather(w_down, "ctx", axis=1, tiled=True),
    )
    qkv_full, out_full, gate_up_full, down_full, gain_fa, gain_fb = (
        lax.all_gather(forward_wide[0], "dp", axis=0, tiled=True),
        lax.all_gather(forward_wide[1], "dp", axis=0, tiled=True),
        lax.all_gather(forward_wide[2], "dp", axis=0, tiled=True),
        lax.all_gather(forward_wide[3], "dp", axis=0, tiled=True),
        lax.all_gather(gain_one, "dp", axis=0, tiled=True),
        lax.all_gather(gain_two, "dp", axis=0, tiled=True),
    )
    seq_count, row_count, model_width = tokens.shape
    query_cols = QH * HD
    key_cols = KVH * HD
    group_count = QH // KVH
    score_scale = 1.0 / math.sqrt(HD)
    position = lax.axis_index("ctx") * row_count + jnp.arange(row_count, dtype=jnp.int32)
    valid_rows = position[None, :] < lengths[:, None]
    cosine, sine_table = angles(position, HD)
    cosine = cosine[:, None, :]
    sine_table = sine_table[:, None, :]
    source = tokens.astype(jnp.float32)
    inverse_one = lax.rsqrt(jnp.mean(source * source, axis=-1, keepdims=True) + EPS)
    normed_one = (source * inverse_one * gain_fa.astype(jnp.float32)).astype(jnp.bfloat16)
    projected = jnp.einsum("bsd,de->bse", normed_one, qkv_full, preferred_element_type=jnp.float32)
    queries = rotate(
        projected[..., :query_cols].reshape(seq_count, row_count, QH, HD), cosine, sine_table
    )
    queries = queries.astype(jnp.bfloat16).reshape(seq_count, row_count, query_cols)
    key_heads = rotate(
        projected[..., query_cols : query_cols + key_cols].reshape(seq_count, row_count, KVH, HD),
        cosine,
        sine_table,
    )
    key_heads = key_heads.astype(jnp.bfloat16).reshape(seq_count, row_count, key_cols)
    value_heads = projected[..., query_cols + key_cols :].astype(jnp.bfloat16)
    keys_all, values_all = (
        lax.all_gather(key_heads, "ctx", axis=1, tiled=True),
        lax.all_gather(value_heads, "ctx", axis=1, tiled=True),
    )
    query_blocks = split_heads(queries, QH).reshape(seq_count * KVH, group_count * row_count, HD)
    key_blocks = split_heads(keys_all, KVH)
    value_blocks = split_heads(values_all, KVH)
    pair_lengths = jnp.repeat(lengths, KVH)

    def forward_block(block_in):
        query_rows, key_rows, value_rows, length = block_in
        scores = block_scores(query_rows, key_rows, position, length, group_count, score_scale)
        row_max = jnp.max(scores, axis=-1, keepdims=True)
        exp_terms = jnp.exp(scores - row_max)
        row_total = jnp.sum(exp_terms, axis=-1, keepdims=True)
        prob_rows = (exp_terms / row_total).astype(jnp.bfloat16)
        result = jnp.einsum(
            "gst,td->gsd", prob_rows, value_rows, preferred_element_type=jnp.float32
        )
        return (result.reshape(-1, HD), (row_max + jnp.log(row_total))[..., 0])

    context_blocks, log_totals = lax.map(
        forward_block, (query_blocks, key_blocks, value_blocks, pair_lengths)
    )
    context = join_heads(context_blocks.reshape(seq_count * QH, row_count, HD), seq_count).astype(
        jnp.bfloat16
    )
    hidden = source + jnp.einsum(
        "bse,ed->bsd", context, out_full, preferred_element_type=jnp.float32
    )
    inverse_two = lax.rsqrt(jnp.mean(hidden * hidden, axis=-1, keepdims=True) + EPS)
    normed_two = (hidden * inverse_two * gain_fb.astype(jnp.float32)).astype(jnp.bfloat16)
    gate_up = jnp.einsum(
        "bsd,df->bsf", normed_two, gate_up_full, preferred_element_type=jnp.float32
    )
    gate_part = gate_up[..., :FF]
    up_part = gate_up[..., FF:]
    gate_sig = jax.nn.sigmoid(gate_part)
    swish_part = gate_part * gate_sig
    activation = (swish_part * up_part).astype(jnp.bfloat16)
    result_rows = hidden + jnp.einsum(
        "bsf,fd->bsd", activation, down_full, preferred_element_type=jnp.float32
    )
    output = jnp.where(valid_rows[..., None], result_rows, 0.0).astype(jnp.bfloat16)
    back_wide = (
        lax.all_gather(w_qkv, "ctx", axis=1, tiled=True),
        lax.all_gather(w_out, "ctx", axis=1, tiled=True),
        lax.all_gather(w_gate_up, "ctx", axis=1, tiled=True),
        lax.all_gather(w_down, "ctx", axis=1, tiled=True),
    )
    qkv_back, out_back, gate_up_back, down_back, gain_ba, gain_bb = (
        lax.all_gather(back_wide[0], "dp", axis=0, tiled=True),
        lax.all_gather(back_wide[1], "dp", axis=0, tiled=True),
        lax.all_gather(back_wide[2], "dp", axis=0, tiled=True),
        lax.all_gather(back_wide[3], "dp", axis=0, tiled=True),
        lax.all_gather(gain_one, "dp", axis=0, tiled=True),
        lax.all_gather(gain_two, "dp", axis=0, tiled=True),
    )
    grad_rows = jnp.where(valid_rows[..., None], cotangent, jnp.zeros_like(cotangent))
    grad_activation = jnp.einsum(
        "bsd,fd->bsf", grad_rows, down_back, preferred_element_type=jnp.float32
    )
    grad_gate = grad_activation * up_part * gate_sig * (1.0 + gate_part * (1.0 - gate_sig))
    grad_up = grad_activation * swish_part
    grad_mix = jnp.concatenate([grad_gate, grad_up], axis=-1).astype(jnp.bfloat16)
    grad_normed_two = jnp.einsum(
        "bsf,df->bsd", grad_mix, gate_up_back, preferred_element_type=jnp.float32
    )
    back_two, grad_gain_two = norm_back(
        hidden, inverse_two, gain_bb.astype(jnp.float32), grad_normed_two
    )
    grad_hidden = grad_rows.astype(jnp.float32) + back_two
    grad_branch = grad_hidden.astype(jnp.bfloat16)
    grad_context = jnp.einsum(
        "bsd,ed->bse", grad_branch, out_back, preferred_element_type=jnp.float32
    ).astype(jnp.bfloat16)
    grad_blocks = split_heads(grad_context, QH).reshape(
        seq_count * KVH, group_count * row_count, HD
    )

    def backward_block(block_in):
        query_rows, key_rows, value_rows, length, log_total, grad_in = block_in
        scores = block_scores(query_rows, key_rows, position, length, group_count, score_scale)
        prob_rows = jnp.exp(scores - log_total[..., None])
        grad_grouped = grad_in.reshape(group_count, -1, HD)
        grad_probs = jnp.einsum(
            "gsd,td->gst", grad_grouped, value_rows, preferred_element_type=jnp.float32
        )
        grad_value = jnp.einsum(
            "gst,gsd->td",
            prob_rows.astype(jnp.bfloat16),
            grad_grouped,
            preferred_element_type=jnp.float32,
        )
        row_delta = jnp.sum(prob_rows * grad_probs, axis=-1, keepdims=True)
        grad_scores = (prob_rows * (grad_probs - row_delta)).astype(jnp.bfloat16)
        grad_query = (
            jnp.einsum("gst,td->gsd", grad_scores, key_rows, preferred_element_type=jnp.float32)
            * score_scale
        )
        grad_key = (
            jnp.einsum(
                "gst,gsd->td",
                grad_scores,
                query_rows.reshape(group_count, -1, HD),
                preferred_element_type=jnp.float32,
            )
            * score_scale
        )
        return (grad_query.reshape(-1, HD), grad_key, grad_value)

    query_grads, key_grads, value_grads = lax.map(
        backward_block,
        (query_blocks, key_blocks, value_blocks, pair_lengths, log_totals, grad_blocks),
    )
    key_sums, value_sums = (
        lax.psum_scatter(
            join_heads(key_grads, seq_count).astype(jnp.bfloat16),
            "ctx",
            scatter_dimension=1,
            tiled=True,
        ).astype(jnp.float32),
        lax.psum_scatter(
            join_heads(value_grads, seq_count).astype(jnp.bfloat16),
            "ctx",
            scatter_dimension=1,
            tiled=True,
        ).astype(jnp.float32),
    )
    grad_queries = join_heads(query_grads.reshape(seq_count * QH, row_count, HD), seq_count)
    turned_queries = rotate(grad_queries.reshape(seq_count, row_count, QH, HD), cosine, -sine_table)
    turned_keys = rotate(key_sums.reshape(seq_count, row_count, KVH, HD), cosine, -sine_table)
    grad_mixed = jnp.concatenate(
        [
            turned_queries.reshape(seq_count, row_count, query_cols),
            turned_keys.reshape(seq_count, row_count, key_cols),
            value_sums,
        ],
        axis=-1,
    ).astype(jnp.bfloat16)
    grad_normed_one = jnp.einsum(
        "bse,de->bsd", grad_mixed, qkv_back, preferred_element_type=jnp.float32
    )
    back_one, grad_gain_one = norm_back(
        source, inverse_one, gain_ba.astype(jnp.float32), grad_normed_one
    )
    grad_tokens = (grad_hidden + back_one).astype(jnp.bfloat16)
    exchanged = (
        lax.all_to_all(grad_mixed, "ctx", split_axis=2, concat_axis=1, tiled=True),
        lax.all_to_all(grad_branch, "ctx", split_axis=2, concat_axis=1, tiled=True),
        lax.all_to_all(grad_mix, "ctx", split_axis=2, concat_axis=1, tiled=True),
        lax.all_to_all(grad_rows, "ctx", split_axis=2, concat_axis=1, tiled=True),
    )
    initial = (
        jnp.zeros((model_width, exchanged[0].shape[2]), jnp.float32),
        jnp.zeros((context.shape[2], exchanged[1].shape[2]), jnp.float32),
        jnp.zeros((model_width, exchanged[2].shape[2]), jnp.float32),
        jnp.zeros((activation.shape[2], exchanged[3].shape[2]), jnp.float32),
    )
    pieces = (
        lax.all_gather(normed_one, "ctx", axis=1, tiled=True),
        lax.all_gather(context, "ctx", axis=1, tiled=True),
        lax.all_gather(normed_two, "ctx", axis=1, tiled=True),
        lax.all_gather(activation, "ctx", axis=1, tiled=True),
    )
    updated = []
    for total, piece, right in zip(initial, pieces, exchanged):
        updated.append(jnp.einsum("bsr,bsc->rc", piece, right, preferred_element_type=jnp.float32))
    column_grads = tuple(updated)
    gain_whole = lax.psum((grad_gain_one, grad_gain_two), "ctx")
    final_qkv, final_out, final_gate_up, final_down, final_gain_one, final_gain_two = (
        lax.psum_scatter(
            column_grads[0].astype(jnp.bfloat16), "dp", scatter_dimension=0, tiled=True
        ).astype(jnp.float32),
        lax.psum_scatter(
            column_grads[1].astype(jnp.bfloat16), "dp", scatter_dimension=0, tiled=True
        ).astype(jnp.float32),
        lax.psum_scatter(
            column_grads[2].astype(jnp.bfloat16), "dp", scatter_dimension=0, tiled=True
        ).astype(jnp.float32),
        lax.psum_scatter(
            column_grads[3].astype(jnp.bfloat16), "dp", scatter_dimension=0, tiled=True
        ).astype(jnp.float32),
        lax.psum_scatter(
            gain_whole[0].astype(jnp.bfloat16), "dp", scatter_dimension=0, tiled=True
        ).astype(jnp.float32),
        lax.psum_scatter(
            gain_whole[1].astype(jnp.bfloat16), "dp", scatter_dimension=0, tiled=True
        ).astype(jnp.float32),
    )
    return (
        output,
        grad_tokens,
        final_gain_one,
        final_qkv,
        final_out,
        final_gain_two,
        final_gate_up,
        final_down,
    )


MESH = pl.DeviceIdType.MESH


class Place:
    def __init__(self):
        self.dp = lax.axis_index("dp")
        self.ctx = lax.axis_index("ctx")
        self.z = lax.div(self.dp, 2)
        self.y = lax.rem(self.dp, 2)
        self.x = lax.div(self.ctx, 2)
        self.c = lax.rem(self.ctx, 2)
        self.up = (self.dp + 2, self.ctx)
        self.down = (self.dp - 2, self.ctx)
        self.across = (self.dp + 1 - 2 * self.y, self.ctx)
        self.chip = (self.dp, (1 - self.x) * 2 + self.c)
        self.core = (self.dp, self.x * 2 + 1 - self.c)
        self.has_up = self.z < 3
        self.has_down = self.z > 0


def greet(place):
    barrier = pltpu.get_barrier_semaphore()

    def tell(device):
        pl.semaphore_signal(barrier, inc=1, device_id=device, device_id_type=MESH)

    pl.when(place.has_up)(lambda: tell(place.up))
    pl.when(place.has_down)(lambda: tell(place.down))
    tell(place.across)
    for step in (1, 2, 3):
        tell((place.dp, lax.rem(place.ctx + step, 4)))
    ends = place.has_up.astype(jnp.int32) + place.has_down.astype(jnp.int32)
    pl.semaphore_wait(barrier, 4 + ends)


class Wires:
    def __init__(self, send_sems, recv_sems, names):
        self.send_sems = send_sems
        self.recv_sems = recv_sems
        self.index = names
        self.count = 0
        self.pending = []

    def slot(self, name):
        if name not in self.index:
            self.index[name] = len(self.index)
        return self.index[name]

    def send(self, src, dst, name, device, cond=None, extra=None):
        number = self.count
        self.count += 1
        at = self.slot(name)
        if extra is not None:
            at = at + extra
        copy = pltpu.make_async_remote_copy(
            src_ref=src,
            dst_ref=dst,
            send_sem=self.send_sems.at[number],
            recv_sem=self.recv_sems.at[at],
            device_id=device,
            device_id_type=MESH,
        )
        if cond is None:
            copy.start()
        else:
            pl.when(cond)(copy.start)
        self.pending.append((copy, cond))

    def take(self, dst, name, device, extra=None):
        at = self.slot(name)
        if extra is not None:
            at = at + extra
        pltpu.make_async_remote_copy(
            src_ref=dst,
            dst_ref=dst,
            send_sem=self.send_sems.at[0],
            recv_sem=self.recv_sems.at[at],
            device_id=device,
            device_id_type=MESH,
        ).wait_recv()

    def drain(self, first=None):
        first = len(self.pending) if first is None else first
        for copy, cond in self.pending[:first]:
            when(cond, copy.wait_send)
        self.pending = self.pending[first:]


BELOW, ABOVE = 0, 1


def both(first, second):
    return second if first is None else jnp.logical_and(first, second)


def source_valid(place, way, dist):
    return place.z >= dist if way == BELOW else place.z + dist <= 3


def source_pos(place, way, dist):
    return place.dp - 2 * dist if way == BELOW else place.dp + 2 * dist


def flood_start(wires, place, name, own, block, spread):
    wires.send(own, block(place.dp), (name, BELOW, 1), place.up, place.has_up)
    wires.send(own, block(place.dp), (name, ABOVE, 1), place.down, place.has_down)
    wires.send(own, block(place.dp), (name, "y", 0, 0), place.across)
    spread(own, place.dp, (0, 0, 0), None)


def flood_step(wires, place, name, block, spread, way, dist):
    here = source_valid(place, way, dist)
    pos = source_pos(place, way, dist)
    view = block(pos)
    came_from = place.down if way == BELOW else place.up
    pl.when(here)(lambda: wires.take(view, (name, way, dist), came_from))
    if dist < 3:
        onward = place.up if way == BELOW else place.down
        more = place.has_up if way == BELOW else place.has_down
        wires.send(view, view, (name, way, dist + 1), onward, jnp.logical_and(here, more))
    wires.send(view, view, (name, "y", way, dist), place.across, here)
    spread(view, pos, (0, way, dist), here)


def flood_side(wires, place, name, block, spread, way, dist):
    if dist == 0:
        here, pos = None, place.dp
    else:
        here, pos = source_valid(place, way, dist), source_pos(place, way, dist)
    pos = pos + 1 - 2 * place.y
    view = block(pos)
    if here is None:
        wires.take(view, (name, "y", 0, 0), place.across)
    else:
        pl.when(here)(lambda: wires.take(view, (name, "y", way, dist), place.across))
    spread(view, pos, (1, way, dist), here)


HOPS = [(way, dist) for dist in (1, 2, 3) for way in (BELOW, ABOVE)]


def no_spread(view, pos, key, cond):
    return None


def add_rows(dst, srcs, out=None, cast=None, chunk=48):
    out = dst if out is None else out
    total_rows = dst.shape[0]
    assert total_rows % chunk == 0

    def body(i, carry):
        at = pl.ds(pl.multiple_of(i * chunk, 16), chunk)
        total = dst[at, :].astype(jnp.float32)
        for src in srcs:
            total = total + src[at, :].astype(jnp.float32)
        out[at, :] = total.astype(out.dtype)
        return carry

    lax.fori_loop(0, total_rows // chunk, body, 0)


def when(cond, action):
    if cond is None:
        action()
    else:
        pl.when(cond)(action)


DRAIN = [(way, dist) for dist in (3, 2, 1, 0) for way in (BELOW, ABOVE)]


def sink_step(wires, place, name, block, inbox, way, dist):
    here = source_valid(place, way, dist)
    pos = source_pos(place, way, dist)
    view = block(pos)
    fed = place.has_up if way == BELOW else place.has_down
    feeder = place.up if way == BELOW else place.down
    onward = place.down if way == BELOW else place.up
    if dist < 3:

        def arrive():
            wires.take(inbox.at[way, dist], (name, way, dist), feeder)
            add_rows(view, [inbox.at[way, dist]])

        pl.when(jnp.logical_and(here, fed))(arrive)
    if dist > 0:
        wires.send(view, inbox.at[way, dist - 1], (name, way, dist - 1), onward, here)


def nn(a, b):
    return jnp.dot(a, b, preferred_element_type=jnp.float32)


def nt(a, b):
    return lax.dot_general(a, b, (((1,), (1,)), ((), ())), preferred_element_type=jnp.float32)


def tn(a, b):
    return lax.dot_general(a, b, (((0,), (0,)), ((), ())), preferred_element_type=jnp.float32)


def layer_kernel(
    names,
    tokens, cot, lengths, qkv_in, out_in, gu_in, dt_in, gain_in, cos, sin,
    output, grad_tokens, gain_out, qkv_out, out_out, gu_out, dt_out,
    w_qkv, w_out, w_ff, gain_all, gain_row,
    n1, n2_all, g_all, context, hidden, grad_hidden, proj, q_st, kv_all, p_st, att, go_st, wide, gm,
    act, d_gate, d_up, gp, gp_box, op, op_box, dkv, dkv_box,
    d_gu, d_dt,
    qkv_core, out_core, qkv_chip, out_chip, qkv_side, out_side, gu_side, down_side,
    qkv_inbox, out_inbox, gu_inbox, down_inbox, gu_mix, down_mix, gain_box,
    send_sems, recv_sems, local_sems,
):
    f32, low = jnp.float32, jnp.bfloat16
    place = Place()
    wires = Wires(send_sems, recv_sems, names)
    dp, ctx, z, y, x, c = place.dp, place.ctx, place.z, place.y, place.x, place.c
    rows = qkv_in.shape[0]
    strip, half = dt_in.shape
    units = act.shape[1]
    width = tokens.shape[1]
    own_rows = tokens.shape[0]
    slots_here = own_rows // 2
    qkv_cols, out_cols = qkv_in.shape[1], out_in.shape[1]
    qkv_wide, out_wide = w_qkv.shape[2], w_out.shape[2]
    group = QH // KVH
    slabs = KVH // 2
    gate_at, up_at, down_at = 0, units, 2 * units

    greet(place)

    def row_view(ref, lead, pos):
        return ref.at[lead, pl.ds(pl.multiple_of(pos * rows, 16), rows)]

    def ff_view(at, pos):
        return w_ff.at[pl.ds(pl.multiple_of(pos * rows, 16), rows), pl.ds(at, units)]

    locals_ = []

    def local(src, dst, cond=None):
        copy = pltpu.make_async_copy(src, dst, local_sems.at[len(locals_)])
        locals_.append((copy, cond))
        when(cond, copy.start)

    my_rows = pl.ds(pl.multiple_of(dp * rows, 16), rows)
    gu_places = ((gate_at, 0), (up_at, 1))
    for part in range(2):
        target = 2 * c + part
        src = gu_in.at[:, pl.ds(part * units, units)]
        for at, half_x in gu_places:
            here = x == half_x
            wires.send(src, ff_view(at, dp), ("gu_mix", half_x), (dp, target), jnp.logical_and(here, target != ctx))
            local(src, ff_view(at, dp), jnp.logical_and(here, target == ctx))

    def attention_spread(name, ref):
        def spread(view, pos, key, cond):
            dst = row_view(ref, ctx, pos)
            wires.send(view, dst, (name, "x") + key, place.chip, cond)
            wires.send(view, dst, (name, "c") + key, place.core, cond)
        return spread

    attention = [("qkv", qkv_in, w_qkv, qkv_cols), ("out", out_in, w_out, out_cols)]

    def attention_start(name, own, ref, cols):
        ref[ctx, my_rows, :] = jnp.zeros((rows, ref.shape[2]), low)
        ref[ctx, my_rows, :cols] = own[...]
        block = functools.partial(row_view, ref, ctx)
        flood_start(wires, place, name, block(dp), block, attention_spread(name, ref))

    attention_start(*attention[0])
    gain_block = lambda pos: gain_all.at[pos]
    gain_all[dp] = gain_in[...]
    flood_start(wires, place, "gain", gain_block(dp), gain_block, no_spread)
    attention_start(*attention[1])

    lanes = pl.ds(pl.multiple_of(down_at + y * half, 128), half)
    other_lanes = pl.ds(pl.multiple_of(down_at + (1 - y) * half, 128), half)
    dst = w_ff.at[pl.ds(pl.multiple_of(ctx * strip, 16), strip), lanes]
    wires.send(dt_in, dst, ("down_mix", 0), (dp, z), ctx != z, extra=ctx)
    for j in range(1, 4):
        wires.slot(("down_mix", j))
    local(dt_in, dst, ctx == z)

    row_at = lax.broadcasted_iota(jnp.int32, (own_rows, 1), 0)
    first_seq = row_at < slots_here
    position = ctx * slots_here + jnp.where(first_seq, row_at, row_at - slots_here)
    row_length = jnp.where(first_seq, lengths[0], lengths[1])
    valid = position < row_length

    def share(name, ref):
        mine = ref.at[pl.ds(pl.multiple_of(ctx * own_rows, 16), own_rows)]
        wires.send(mine, mine, (name, "x"), place.chip)
        wires.send(mine, mine, (name, "c"), place.core)

    def share_on(name, ref):
        far = ref.at[pl.ds(pl.multiple_of(place.chip[1] * own_rows, 16), own_rows)]
        wires.take(far, (name, "x"), place.chip)
        wires.send(far, far, (name, "d"), place.core)

    def share_end(name, ref):
        for mark, lead in (("c", place.core[1]), ("d", 3 - ctx)):
            view = ref.at[pl.ds(pl.multiple_of(lead * own_rows, 16), own_rows)]
            wires.take(view, (name, mark), place.core)

    here_rows = pl.ds(pl.multiple_of(ctx * own_rows, 16), own_rows)
    g_all[here_rows, :] = jnp.where(valid, cot[...].astype(f32), 0.0).astype(low)

    for part in range(2):
        remote = (part * 2 + x) != ctx
        view = ff_view(gu_places[part][0], dp)
        pl.when(remote)(lambda: wires.take(view, ("gu_mix", part), (dp, part * 2 + x)))
    for copy, cond in locals_:
        when(cond, copy.wait)
    gu_blocks = [functools.partial(ff_view, at) for at, _ in gu_places]
    for part in range(2):
        flood_start(wires, place, ("gu", part), gu_blocks[part](dp), gu_blocks[part], no_spread)
    share("cot", g_all)

    at_home = ctx == z
    strips = [w_ff.at[pl.ds(j * strip, strip), lanes] for j in range(4)]
    other_strips = [w_ff.at[pl.ds(j * strip, strip), other_lanes] for j in range(4)]

    def take_strips():
        for j in range(4):
            pl.when(ctx != j)(functools.partial(wires.take, strips[j], ("down_mix", j), (dp, j)))

    def down_start():
        pl.when(at_home)(take_strips)
        for j in range(4):
            wires.send(strips[j], strips[j], ("down", j, BELOW, 1), place.up, jnp.logical_and(at_home, place.has_up))
            wires.send(strips[j], strips[j], ("down", j, ABOVE, 1), place.down, jnp.logical_and(at_home, place.has_down))
            wires.send(strips[j], strips[j], ("down_y", j), place.across, at_home)

    def down_step(way, dist):
        offset = z - ctx if way == BELOW else ctx - z
        here = offset == dist
        came_from = place.down if way == BELOW else place.up
        onward = place.up if way == BELOW else place.down
        more = place.has_up if way == BELOW else place.has_down
        for j in range(4):
            pl.when(here)(functools.partial(wires.take, strips[j], ("down", j, way, dist), came_from))
            if dist < 3:
                wires.send(strips[j], strips[j], ("down", j, way, dist + 1), onward, jnp.logical_and(here, more))
            wires.send(strips[j], strips[j], ("down_y", j), place.across, here)

    def attention_step(way, dist):
        for name, own, ref, cols in attention:
            flood_step(wires, place, name, functools.partial(row_view, ref, ctx), attention_spread(name, ref), way, dist)

    def gain_step(way, dist):
        flood_step(wires, place, "gain", gain_block, no_spread, way, dist)

    def gu_step(way, dist):
        for part in range(2):
            flood_step(wires, place, ("gu", part), gu_blocks[part], no_spread, way, dist)

    SIDES = [(0, 0)] + HOPS

    def positions():
        for side in range(2):
            for way, dist in SIDES:
                if dist == 0:
                    here, pos = None, dp
                else:
                    here, pos = source_valid(place, way, dist), source_pos(place, way, dist)
                if side == 1:
                    pos = pos + 1 - 2 * y
                yield (side, way, dist), here, pos

    def attention_sides(which):
        name, own, ref, cols = which
        for way, dist in SIDES:
            flood_side(wires, place, name, functools.partial(row_view, ref, ctx), attention_spread(name, ref), way, dist)

    def attention_chip(which):
        name, own, ref, cols = which
        for key, here, pos in positions():
            view = row_view(ref, place.chip[1], pos)
            when(here, lambda: wires.take(view, (name, "x") + key, place.chip))
            wires.send(view, view, (name, "d") + key, place.core, here)

    def attention_core(which):
        name, own, ref, cols = which
        for key, here, pos in positions():
            for mark, lead in (("c", place.core[1]), ("d", 3 - ctx)):
                view = row_view(ref, lead, pos)
                when(here, lambda: wires.take(view, (name, mark) + key, place.core))

    down_start()
    for dist in (1, 2, 3):
        for way in (BELOW, ABOVE):
            attention_step(way, dist)
            gain_step(way, dist)
        for way in (BELOW, ABOVE):
            gu_step(way, dist)
            down_step(way, dist)
    for way, dist in SIDES:
        flood_side(wires, place, "gain", gain_block, no_spread, way, dist)
    attention_sides(attention[0])
    share_on("cot", g_all)
    attention_chip(attention[0])
    attention_core(attention[0])
    attention_sides(attention[1])
    attention_chip(attention[1])

    gain_row[...] = jnp.zeros(gain_row.shape, f32)
    for pos in range(8):
        piece = gain_all[pos]
        shift = (pos * rows) % 128
        if shift:
            piece = pltpu.roll(piece, shift, 1)
        at = (pos * rows) // 128 * 128
        gain_row[:, at : at + 256] += piece
    gain_a = lambda: gain_row[0:1, :width]
    gain_b = lambda: gain_row[1:2, :width]

    def norm(values):
        return lax.rsqrt(jnp.mean(values * values, axis=-1, keepdims=True) + EPS)

    source = tokens[...].astype(f32)
    n1[...] = (source * norm(source) * gain_a()).astype(low)
    proj[...] = jnp.zeros(proj.shape, f32)
    for j in range(4):
        part = nn(n1[...], w_qkv[j])
        part = jnp.concatenate([part, jnp.zeros((own_rows, 128), f32)], axis=1)
        at = qkv_cols * j
        if at % 128:
            part = pltpu.roll(part, at % 128, 1)
        proj[:, at // 128 * 128 : at // 128 * 128 + qkv_wide + 128] += part

    lane = lax.broadcasted_iota(jnp.int32, (own_rows, 128), 1)
    low_half = lax.rem(lane, HD) < HD // 2
    side_of = lax.div(lane, HD)

    def turn(values, sign):
        swapped = jnp.where(low_half, pltpu.roll(values, 128 - HD // 2, 1), pltpu.roll(values, HD // 2, 1))
        return values * cos[...] + swapped * (sin[...] * sign)

    def head_spots():
        for head in range(QH):
            kv = head // group
            yield head // 2, head % 2, kv // 2, kv % 2, (kv % 2 * group + head % group) * slots_here

    def stack_heads(slab_of, dest, scale):
        for slab, side, key_slab, key_side, at in head_spots():
            values = slab_of(slab)
            if side != key_side:
                values = pltpu.roll(values, HD, 1)
            values = (jnp.where(side_of == key_side, values, 0.0) * scale).astype(low)
            for seq in range(2):
                dest[seq * slabs + key_slab, at : at + slots_here, :] = values[
                    seq * slots_here : (seq + 1) * slots_here
                ]

    def unstack_heads(src, slab):
        total = jnp.zeros((own_rows, 128), f32)
        for at_slab, side, key_slab, key_side, at in head_spots():
            if at_slab != slab:
                continue
            values = jnp.concatenate(
                [src[seq * slabs + key_slab, at : at + slots_here, :] for seq in range(2)], axis=0
            )
            values = jnp.where(side_of == key_side, values, 0.0)
            if side != key_side:
                values = pltpu.roll(values, HD, 1)
            total = total + values
        return total

    turned = {}

    def query_slab(slab):
        if slab not in turned:
            turned[slab] = turn(proj[:, slab * 128 : slab * 128 + 128], 1.0)
        return turned[slab]

    score_scale = 1.0 / math.sqrt(HD)
    stack_heads(query_slab, q_st, score_scale)
    q_slabs = QH // 2
    my_slots = pl.ds(pl.multiple_of(ctx * slots_here, 16), slots_here)
    for slab in range(2 * slabs):
        at = (q_slabs + slab) * 128
        values = proj[:, at : at + 128]
        if slab < slabs:
            values = turn(values, 1.0)
        values = values.astype(low)
        for seq in range(2):
            kv_all[seq, slab, my_slots, :] = values[seq * slots_here : (seq + 1) * slots_here]

    def slot_view(lead):
        return kv_all.at[:, :, pl.ds(pl.multiple_of(lead * slots_here, 16), slots_here)]

    for step in (1, 2, 3):
        wires.send(slot_view(ctx), slot_view(ctx), ("kv", step), (dp, lax.rem(ctx + step, 4)))
    attention_core(attention[1])
    for step in (1, 2, 3):
        peer = lax.rem(ctx + 4 - step, 4)
        wires.take(slot_view(peer), ("kv", step), (dp, peer))

    stack = q_st.shape[1]
    slots = kv_all.shape[2]

    def attend(i, carry):
        seq, slab = lax.div(i, slabs), lax.rem(i, slabs)
        scores = nt(q_st[i], kv_all[seq, slab])
        at = ctx * slots_here + lax.rem(lax.broadcasted_iota(jnp.int32, (stack, slots), 0), slots_here)
        key_at = lax.broadcasted_iota(jnp.int32, (stack, slots), 1)
        length = jnp.where(seq == 0, lengths[0], lengths[1])
        allowed = jnp.logical_and(key_at <= at, key_at < length)
        scores = jnp.where(allowed, scores, NEGATIVE)
        terms = jnp.exp(scores - jnp.max(scores, axis=-1, keepdims=True))
        probs = (terms / jnp.sum(terms, axis=-1, keepdims=True)).astype(low)
        p_st[i] = probs
        att[i] = nn(probs, kv_all[seq, slabs + slab])
        return carry

    lax.fori_loop(0, 2 * slabs, attend, 0)
    for slab in range(q_slabs):
        context[:, slab * 128 : slab * 128 + 128] = unstack_heads(att, slab).astype(low)
    hidden[...] = source
    for j in range(4):
        part = nn(context[...], w_out[j])
        at = out_cols * j
        if at % 128:
            part = pltpu.roll(part, at % 128, 1)
        hidden[:, at // 128 * 128 : at // 128 * 128 + out_wide] += part
    n2_all[here_rows, :] = (hidden[...] * norm(hidden[...]) * gain_b()).astype(low)
    share("n2", n2_all)
    share_end("cot", g_all)

    gathered = len(wires.pending)

    for part in range(2):
        for way, dist in SIDES:
            flood_side(wires, place, ("gu", part), gu_blocks[part], no_spread, way, dist)
    for j in range(4):
        wires.take(other_strips[j], ("down_y", j), place.across)
    share_on("n2", n2_all)
    share_end("n2", n2_all)

    tall, tile = 256, 256

    def feed(i, carry):
        at = pl.ds(pl.multiple_of(lax.div(i, units // tile) * tall, tall), tall)
        unit = lax.rem(i, units // tile) * tile

        def cols(base):
            return pl.ds(pl.multiple_of(base + unit, tile), tile)

        gate = nn(n2_all[at, :], w_ff[:, cols(gate_at)])
        up = nn(n2_all[at, :], w_ff[:, cols(up_at)])
        back = nn(g_all[at, :], w_ff[:, cols(down_at)])
        sig = jax.nn.sigmoid(gate)
        swish = gate * sig
        act[at, cols(0)] = (swish * up).astype(low)
        d_gate[at, cols(0)] = (back * up * sig * (1.0 + gate * (1.0 - sig))).astype(low)
        d_up[at, cols(0)] = (back * swish).astype(low)
        return carry

    lax.fori_loop(0, (4 * own_rows // tall) * (units // tile), feed, 0)

    across_core = (1 - x) * 2 + 1 - c
    across_own = (1 - x) * 2 + c
    beside = x * 2 + 1 - c
    wide_tile = 384

    def group_blocks(compute, name, ref, box):
        for mark, lead in (("cx", across_core), ("", across_own), ("cc", beside), ("", ctx)):
            compute(lead)
            if mark:
                wires.send(ref.at[lead], box.at[0 if mark == "cx" else 1], (name, mark), place.core)

    def group_on(name, ref, box):
        wires.take(box.at[0], (name, "cx"), place.core)
        add_any(ref.at[across_own], box.at[0])
        wires.send(ref.at[across_own], box.at[2], (name, "x"), place.chip)

    def group_end(name, ref, box):
        wires.take(box.at[1], (name, "cc"), place.core)
        wires.take(box.at[2], (name, "x"), place.chip)
        return ref[ctx].astype(f32) + box[1].astype(f32) + box[2].astype(f32)

    def add_any(dst, src):
        dst[...] = (dst[...].astype(f32) + src[...].astype(f32)).astype(low)

    def lead_rows(lead):
        return pl.ds(pl.multiple_of(lead * own_rows, 16), own_rows)

    def back_block(lead):
        def body(n, carry):
            at = pl.ds(pl.multiple_of(n * wide_tile, 128), wide_tile)
            total = nt(d_gate[lead_rows(lead), :], w_ff[at, pl.ds(gate_at, units)])
            total = total + nt(d_up[lead_rows(lead), :], w_ff[at, pl.ds(up_at, units)])
            gp[lead, :, at] = total.astype(low)
            return carry

        lax.fori_loop(0, width // wide_tile, body, 0)

    def forward_block(lead):
        def body(n, carry):
            at = pl.ds(pl.multiple_of(n * wide_tile, 128), wide_tile)
            op[lead, :, at] = nt(act[lead_rows(lead), :], w_ff[at, pl.ds(down_at, units)]).astype(low)
            return carry

        lax.fori_loop(0, width // wide_tile, body, 0)

    group_blocks(back_block, "gp", gp, gp_box)

    def grad_ff(m, carry):
        at = pl.ds(pl.multiple_of(m * 128, 128), 128)
        left = n2_all[:, at]
        d_gu[0, at, :] = tn(left, d_gate[...]).astype(low)
        d_gu[1, at, :] = tn(left, d_up[...]).astype(low)
        d_dt[at, :] = tn(g_all[:, at], act[...]).astype(low)
        return carry

    lax.fori_loop(0, width // 128, grad_ff, 0)
    group_on("gp", gp, gp_box)

    d_lanes = pl.ds(pl.multiple_of(y * half, 128), half)
    d_other = pl.ds(pl.multiple_of((1 - y) * half, 128), half)
    d_strips = [d_dt.at[pl.ds(j * strip, strip), d_lanes] for j in range(4)]
    d_other_strips = [d_dt.at[pl.ds(j * strip, strip), d_other] for j in range(4)]
    for zs in range(4):
        for part in range(2):
            wires.send(row_view(d_gu, part, 2 * zs + 1 - y), gu_side.at[part, zs], ("dgu_y", part, zs), place.across)
    for j in range(4):
        wires.send(d_other_strips[j], down_side.at[j], ("ddown_y", j), place.across)

    group_blocks(forward_block, "op", op, op_box)
    group_on("op", op, op_box)

    def norm_back(values, inverse, gain, grad_in):
        scaled = grad_in * gain
        mean_term = jnp.mean(scaled * values, axis=-1, keepdims=True)
        back = inverse * scaled - values * (inverse * inverse * inverse) * mean_term
        return back, jnp.sum(grad_in * values * inverse, axis=0, keepdims=True)

    gain_out[...] = jnp.zeros(gain_out.shape, f32)
    back_two, gain_two_grad = norm_back(hidden[...], norm(hidden[...]), gain_b(), group_end("gp", gp, gp_box))
    gain_out[1:2, :] = gain_two_grad
    grad_hidden[...] = g_all[here_rows, :].astype(f32) + back_two
    out_lane = lax.broadcasted_iota(jnp.int32, (own_rows, out_wide), 1)
    for j in range(4):
        at = out_cols * j
        part = grad_hidden[:, at // 128 * 128 : at // 128 * 128 + out_wide]
        if at % 128:
            part = pltpu.roll(part, out_wide - at % 128, 1)
        wide[j] = jnp.where(out_lane < out_cols, part, 0.0).astype(low)

    def context_back(n, carry):
        at = pl.ds(pl.multiple_of(n * wide_tile, 128), wide_tile)
        total = nt(wide[0], w_out[0, at, :])
        for j in range(1, 4):
            total = total + nt(wide[j], w_out[j, at, :])
        proj[:, at] = total
        return carry

    lax.fori_loop(0, width // wide_tile, context_back, 0)
    stack_heads(lambda slab: proj[:, slab * 128 : slab * 128 + 128], go_st, 1.0)

    wires.drain(gathered)
    pair = 2 * rows

    def out_view(lead, at, size):
        return w_out.at[lead, pl.ds(at, size)]

    def qkv_view(lead, at, size):
        return w_ff.at[pl.ds(at, size), pl.ds(pl.multiple_of(lead * qkv_wide, 128), qkv_wide)]

    def grad_out(m, carry):
        at = pl.ds(pl.multiple_of(m * 128, 128), 128)
        for j in range(4):
            w_out[j, at, :] = tn(context[:, at], wide[j]).astype(low)
        return carry

    lax.fori_loop(0, width // 128, grad_out, 0)

    def core_send(name, view, core):
        for zs in range(4):
            for xx in range(2):
                wires.send(
                    view(2 * xx + 1 - c, zs * pair, pair), core.at[xx, pl.ds(zs * pair, pair)],
                    (name, "gc", xx, zs), place.core,
                )

    def core_add(name, view, core, chip):
        for zs in range(4):
            for xx in range(2):
                box = core.at[xx, pl.ds(zs * pair, pair)]
                wires.take(box, (name, "gc", xx, zs), place.core)
                add_rows(view(2 * xx + c, zs * pair, pair), [box])
            wires.send(view(place.chip[1], zs * pair, pair), chip.at[pl.ds(zs * pair, pair)], (name, "gx", zs), place.chip)

    def own_view(view, pos):
        return view(ctx, pl.multiple_of(pos * rows, 16), rows)

    def chip_add(name, view, chip, side):
        for zs in range(4):
            span = chip.at[pl.ds(zs * pair, pair)]
            wires.take(span, (name, "gx", zs), place.chip)
            add_rows(view(ctx, zs * pair, pair), [span])
            wires.send(own_view(view, 2 * zs + 1 - y), side.at[zs], (name, "gy", zs), place.across)

    def side_add(name, view, side):
        for zs in range(4):
            wires.take(side.at[zs], (name, "gy", zs), place.across)
            add_rows(own_view(view, 2 * zs + y), [side.at[zs]])

    def drain_z(name, view, inbox):
        for way, dist in DRAIN:
            sink_step(wires, place, (name, "g"), functools.partial(own_view, view), inbox, way, dist)

    core_send("out", out_view, out_core)

    def attend_back(i, carry):
        seq, slab = lax.div(i, slabs), lax.rem(i, slabs)
        grad_probs = nt(go_st[i], kv_all[seq, slabs + slab])
        probs = p_st[i].astype(f32)
        delta = jnp.sum(probs * grad_probs, axis=-1, keepdims=True)
        grad_scores = (probs * (grad_probs - delta)).astype(low)
        att[i] = nn(grad_scores, kv_all[seq, slab]) * score_scale
        grad_key = tn(grad_scores, q_st[i])
        grad_value = tn(p_st[i], go_st[i])
        for j in range(4):
            part = slice(j * slots_here, (j + 1) * slots_here)
            dkv[j, seq, slab] = grad_key[part].astype(low)
            dkv[j, seq, slabs + slab] = grad_value[part].astype(low)
        return carry

    lax.fori_loop(0, 2 * slabs, attend_back, 0)
    group_blocks(lambda lead: None, "dkv", dkv, dkv_box)
    core_add("out", out_view, out_core, out_chip)
    group_on("dkv", dkv, dkv_box)

    for zs in range(4):
        for part in range(2):
            wires.take(gu_side.at[part, zs], ("dgu_y", part, zs), place.across)
            add_rows(row_view(d_gu, part, 2 * zs + y), [gu_side.at[part, zs]])
    for j in range(4):
        wires.take(down_side.at[j], ("ddown_y", j), place.across)
        add_rows(d_strips[j], [down_side.at[j]])

    sums = group_end("dkv", dkv, dkv_box)
    proj[...] = jnp.zeros(proj.shape, f32)
    for slab in range(q_slabs):
        proj[:, slab * 128 : slab * 128 + 128] = turn(unstack_heads(att, slab), -1.0)
    for slab in range(2 * slabs):
        values = jnp.concatenate([sums[0, slab], sums[1, slab]], axis=0)
        if slab < slabs:
            values = turn(values, -1.0)
        at = (q_slabs + slab) * 128
        proj[:, at : at + 128] = values
    qkv_lane = lax.broadcasted_iota(jnp.int32, (own_rows, qkv_wide), 1)
    for j in range(4):
        at = qkv_cols * j
        part = proj[:, at // 128 * 128 : at // 128 * 128 + qkv_wide + 128]
        if at % 128:
            part = pltpu.roll(part, qkv_wide + 128 - at % 128, 1)
        gm[j] = jnp.where(qkv_lane < qkv_cols, part[:, :qkv_wide], 0.0).astype(low)

    def grad_qkv(m, carry):
        at = pl.ds(pl.multiple_of(m * 128, 128), 128)
        for j in range(4):
            w_ff[at, pl.ds(j * qkv_wide, qkv_wide)] = tn(n1[:, at], gm[j]).astype(low)
        return carry

    lax.fori_loop(0, width // 128, grad_qkv, 0)
    core_send("qkv", qkv_view, qkv_core)
    chip_add("out", out_view, out_chip, out_side)

    def tokens_back(n, carry):
        at = pl.ds(pl.multiple_of(n * wide_tile, 128), wide_tile)
        total = nt(gm[0], w_qkv[0, at, :])
        for j in range(1, 4):
            total = total + nt(gm[j], w_qkv[j, at, :])
        proj[:, at] = total
        return carry

    lax.fori_loop(0, width // wide_tile, tokens_back, 0)
    core_add("qkv", qkv_view, qkv_core, qkv_chip)
    source = tokens[...].astype(f32)
    back_one, gain_one_grad = norm_back(source, norm(source), gain_a(), proj[:, :width])
    gain_out[0:1, :] = gain_one_grad
    grad_tokens[...] = (grad_hidden[...] + back_one).astype(low)
    result = hidden[...] + group_end("op", op, op_box)
    output[...] = jnp.where(valid, result, 0.0).astype(low)

    def down_sink(dist):
        for way in (BELOW, ABOVE):
            offset = z - ctx if way == BELOW else ctx - z
            here = offset == dist
            fed = place.has_up if way == BELOW else place.has_down
            feeder = place.up if way == BELOW else place.down
            onward = place.down if way == BELOW else place.up
            for j in range(4):

                def arrive():
                    wires.take(down_inbox.at[way, j], ("ddown", j, way), feeder)
                    add_rows(d_strips[j], [down_inbox.at[way, j]])

                pl.when(jnp.logical_and(here, fed))(arrive)
                if dist > 0:
                    wires.send(d_strips[j], down_inbox.at[way, j], ("ddown", j, way), onward, here)

    for way, dist in DRAIN:
        for part in range(2):
            sink_step(wires, place, ("dgu", part), functools.partial(row_view, d_gu, part), gu_inbox.at[part], way, dist)
        if way == BELOW:
            down_sink(dist)
    for part in range(2):
        target = part * 2 + x
        block = row_view(d_gu, part, dp)
        wires.send(block, gu_mix.at[c], ("dgu_mix", 0), (dp, target), target != ctx, extra=c)
        pl.when(target == ctx)(lambda: add_rows(block, [], out=gu_mix.at[c]))
    wires.slot(("dgu_mix", 1))
    for j in range(4):
        wires.send(d_strips[j], down_mix, ("ddown_mix",), (dp, j), jnp.logical_and(at_home, ctx != j))
        pl.when(jnp.logical_and(at_home, ctx == j))(functools.partial(add_rows, d_strips[j], [], down_mix))
    chip_add("qkv", qkv_view, qkv_chip, qkv_side)
    side_add("out", out_view, out_side)
    drain_z("out", out_view, out_inbox)
    side_add("qkv", qkv_view, qkv_side)
    drain_z("qkv", qkv_view, qkv_inbox)
    out_out[...] = own_view(out_view, dp)[...].astype(f32)[:, :out_cols]
    qkv_out[...] = own_view(qkv_view, dp)[...].astype(f32)[:, :qkv_cols]

    def swap(slot, device, cond=None):
        wires.send(gain_out, gain_box.at[slot], ("gain_sum", slot), device, cond)

    def add_gain(slot, device):
        wires.take(gain_box.at[slot], ("gain_sum", slot), device)
        gain_out[...] = gain_out[...] + gain_box[slot]

    def settle():
        copy, cond = wires.pending.pop()
        when(cond, copy.wait_send)

    for slot, device in enumerate((place.core, place.chip, place.across)):
        swap(slot, device)
        settle()
        add_gain(slot, device)
    low_end, high_end = z == 0, z == 3
    mid_low, mid_high = z == 1, z == 2
    swap(3, place.up, low_end)
    settle()
    swap(3, place.down, high_end)
    settle()
    pl.when(mid_low)(lambda: add_gain(3, place.down))
    pl.when(mid_high)(lambda: add_gain(3, place.up))
    swap(4, place.up, mid_low)
    settle()
    swap(4, place.down, mid_high)
    settle()
    pl.when(mid_low)(lambda: add_gain(4, place.up))
    pl.when(mid_high)(lambda: add_gain(4, place.down))
    swap(5, place.down, mid_low)
    swap(5, place.up, mid_high)

    def last(device):
        wires.take(gain_box.at[5], ("gain_sum", 5), device)
        gain_out[...] = gain_box[5]

    pl.when(low_end)(lambda: last(place.up))
    pl.when(high_end)(lambda: last(place.down))

    for part in range(2):
        origin = 2 * c + part
        pl.when(origin != ctx)(lambda: wires.take(gu_mix.at[part], ("dgu_mix", part), (dp, origin)))
        add_rows(gu_mix.at[part], [], out=gu_out.at[:, pl.ds(part * units, units)])
    pl.when(ctx != z)(lambda: wires.take(down_mix, ("ddown_mix",), (dp, z)))
    add_rows(down_mix, [], out=dt_out)
    wires.drain()


def on_device_fast(tokens, lengths, gain_one, w_qkv, w_out, gain_two, w_gate_up, w_down, cotangent):
    seq_count, row_count, width = tokens.shape
    own_rows = seq_count * row_count
    f32, low = jnp.float32, jnp.bfloat16
    block = gain_one.shape[0]
    gains = jnp.stack([gain_one, gain_two]).astype(f32)
    gains = jnp.pad(gains, ((0, 6), (0, 256 - block)))
    position = lax.axis_index("ctx") * row_count + jnp.arange(row_count, dtype=jnp.int32)
    cosine, sine = angles(position, HD)
    cosine = jnp.tile(cosine, (seq_count, 4))
    sine = jnp.tile(jnp.concatenate([-sine, sine], axis=1), (seq_count, 2))
    rows, qkv_cols = w_qkv.shape
    out_cols = w_out.shape[1]
    units = w_gate_up.shape[1] // 2
    half, strip = w_down.shape
    qkv_wide = -(-qkv_cols // 128) * 128
    out_wide = -(-out_cols // 128) * 128
    deep = 8 * rows
    slots = 4 * row_count
    slabs = KVH // 2
    stack = 2 * QH // KVH * row_count

    def box(*shape, dtype=low):
        return pltpu.VMEM(shape, dtype)

    scratch = [
        box(4, deep, qkv_wide), box(4, deep, out_wide), box(deep, 3 * units),
        box(8, 8, 256, dtype=f32), box(8, deep + 128, dtype=f32),
        box(own_rows, width), box(4 * own_rows, width), box(4 * own_rows, width),
        box(own_rows, QH * HD), box(own_rows, width, dtype=f32), box(own_rows, width, dtype=f32),
        box(own_rows, 4 * qkv_wide, dtype=f32),
        box(seq_count * slabs, stack, 128), box(seq_count, 2 * slabs, slots, 128),
        box(seq_count * slabs, stack, slots), box(seq_count * slabs, stack, 128, dtype=f32),
        box(seq_count * slabs, stack, 128), box(4, own_rows, out_wide), box(4, own_rows, qkv_wide),
        box(4 * own_rows, units), box(4 * own_rows, units), box(4 * own_rows, units),
        box(4, own_rows, width), box(3, own_rows, width),
        box(4, own_rows, width), box(3, own_rows, width),
        box(4, seq_count, 2 * slabs, row_count, 128), box(3, seq_count, 2 * slabs, row_count, 128),
        box(2, deep, units), box(deep, units),
        box(2, deep, qkv_wide), box(2, deep, out_wide),
        box(deep, qkv_wide), box(deep, out_wide),
        box(4, rows, qkv_wide), box(4, rows, out_wide),
        box(2, 4, rows, units), box(4, strip, half),
        box(2, 3, rows, qkv_wide), box(2, 3, rows, out_wide),
        box(2, 2, 3, rows, units), box(2, 4, strip, half),
        box(2, rows, units), box(strip, half),
        box(6, 8, width, dtype=f32),
        pltpu.SemaphoreType.DMA((480,)),
        pltpu.SemaphoreType.DMA((480,)),
        pltpu.SemaphoreType.DMA((8,)),
    ]
    vmem = pl.BlockSpec(memory_space=pltpu.MemorySpace.VMEM)
    smem = pl.BlockSpec(memory_space=pltpu.MemorySpace.SMEM)
    shapes = (
        jax.ShapeDtypeStruct((own_rows, width), low),
        jax.ShapeDtypeStruct((own_rows, width), low),
        jax.ShapeDtypeStruct((8, width), f32),
        jax.ShapeDtypeStruct((rows, qkv_cols), f32),
        jax.ShapeDtypeStruct((rows, out_cols), f32),
        jax.ShapeDtypeStruct((rows, 2 * units), f32),
        jax.ShapeDtypeStruct((strip, half), f32),
    )
    output, grad_tokens, gain_sums, final_qkv, final_out, final_gu, final_dt = pl.pallas_call(
        functools.partial(layer_kernel, {}),
        out_shape=shapes,
        in_specs=[vmem, vmem, smem] + [vmem] * 7,
        out_specs=[vmem] * 7,
        scratch_shapes=scratch,
        compiler_params=pltpu.CompilerParams(
            collective_id=0, has_side_effects=True, vmem_limit_bytes=64 * 2**20
        ),
        name="layer",
    )(
        tokens.reshape(own_rows, width), cotangent.reshape(own_rows, width), lengths,
        w_qkv, w_out, w_gate_up, w_down.T, gains, cosine, sine,
    )
    mine = lax.dynamic_slice(gain_sums, (0, lax.axis_index("dp") * block), (8, block))
    return (
        output.reshape(tokens.shape), grad_tokens.reshape(tokens.shape),
        mine[0], final_qkv, final_out, mine[1], final_gu, final_dt.T,
    )


def solution(mesh):
    fits = mesh.shape["dp"] == 8 and mesh.shape["ctx"] == 4
    return jax.shard_map(
        on_device_fast if fits else on_device,
        mesh=mesh,
        in_specs=(
            P("dp", "ctx", None),
            P("dp"),
            P("dp"),
            P("dp", "ctx"),
            P("dp", "ctx"),
            P("dp"),
            P("dp", "ctx"),
            P("dp", "ctx"),
            P("dp", "ctx", None),
        ),
        out_specs=(
            P("dp", "ctx", None),
            P("dp", "ctx", None),
            P("dp"),
            P("dp", "ctx"),
            P("dp", "ctx"),
            P("dp"),
            P("dp", "ctx"),
            P("dp", "ctx"),
        ),
        check_vma=False,
    )
```

```python
import functools
import math

import jax
import jax.numpy as jnp
from jax import lax
from jax.experimental import pallas as pl
from jax.experimental.pallas import tpu as pltpu
from jax.sharding import PartitionSpec as P

QH = 18
KVH = 6
HD = 64
FF = 3072


EPS = 1e-05
NEGATIVE = -1e30


def angles(position, head_width):
    frequency = 10000.0 ** (-jnp.arange(head_width // 2, dtype=jnp.float32) * 2.0 / head_width)
    angle_table = position.astype(jnp.float32)[:, None] * frequency[None, :]
    return (jnp.cos(angle_table), jnp.sin(angle_table))


def rotate(values_in, cosine, sine_table):
    half_width = values_in.shape[-1] // 2
    first_half = values_in[..., :half_width]
    second = values_in[..., half_width:]
    return jnp.concatenate(
        [first_half * cosine - second * sine_table, second * cosine + first_half * sine_table],
        axis=-1,
    )


def split_heads(values_in, head_count):
    seq_count, row_count, col_count = values_in.shape
    head_width = col_count // head_count
    moved = values_in.reshape(seq_count, row_count, head_count, head_width).transpose(0, 2, 1, 3)
    return moved.reshape(seq_count * head_count, row_count, head_width)


def join_heads(values_in, seq_count):
    item_count, row_count, head_width = values_in.shape
    head_count = item_count // seq_count
    moved = values_in.reshape(seq_count, head_count, row_count, head_width).transpose(0, 2, 1, 3)
    return moved.reshape(seq_count, row_count, head_count * head_width)


def norm_back(source, inverse, gain, grad_in):
    scaled = grad_in * gain
    mean_term = jnp.mean(scaled * source, axis=-1, keepdims=True)
    back_rows = inverse * scaled - source * (inverse * inverse * inverse) * mean_term
    return (back_rows, jnp.sum(grad_in * source * inverse, axis=(0, 1)))


def block_scores(query_rows, key_rows, position, length, group_count, score_scale):
    raw_scores = (
        jnp.einsum("nd,td->nt", query_rows, key_rows, preferred_element_type=jnp.float32)
        * score_scale
    )
    raw_scores = raw_scores.reshape(group_count, position.shape[0], key_rows.shape[0])
    keyidx = jnp.arange(key_rows.shape[0], dtype=jnp.int32)
    allowed = (keyidx[None, :] <= position[:, None]) & (keyidx[None, :] < length)
    return jnp.where(allowed[None], raw_scores, NEGATIVE)


def on_device(tokens, lengths, gain_one, w_qkv, w_out, gain_two, w_gate_up, w_down, cotangent):
    forward_wide = (
        lax.all_gather(w_qkv, "ctx", axis=1, tiled=True),
        lax.all_gather(w_out, "ctx", axis=1, tiled=True),
        lax.all_gather(w_gate_up, "ctx", axis=1, tiled=True),
        lax.all_gather(w_down, "ctx", axis=1, tiled=True),
    )
    qkv_full, out_full, gate_up_full, down_full, gain_fa, gain_fb = (
        lax.all_gather(forward_wide[0], "dp", axis=0, tiled=True),
        lax.all_gather(forward_wide[1], "dp", axis=0, tiled=True),
        lax.all_gather(forward_wide[2], "dp", axis=0, tiled=True),
        lax.all_gather(forward_wide[3], "dp", axis=0, tiled=True),
        lax.all_gather(gain_one, "dp", axis=0, tiled=True),
        lax.all_gather(gain_two, "dp", axis=0, tiled=True),
    )
    seq_count, row_count, model_width = tokens.shape
    query_cols = QH * HD
    key_cols = KVH * HD
    group_count = QH // KVH
    score_scale = 1.0 / math.sqrt(HD)
    position = lax.axis_index("ctx") * row_count + jnp.arange(row_count, dtype=jnp.int32)
    valid_rows = position[None, :] < lengths[:, None]
    cosine, sine_table = angles(position, HD)
    cosine = cosine[:, None, :]
    sine_table = sine_table[:, None, :]
    source = tokens.astype(jnp.float32)
    inverse_one = lax.rsqrt(jnp.mean(source * source, axis=-1, keepdims=True) + EPS)
    normed_one = (source * inverse_one * gain_fa.astype(jnp.float32)).astype(jnp.bfloat16)
    projected = jnp.einsum("bsd,de->bse", normed_one, qkv_full, preferred_element_type=jnp.float32)
    queries = rotate(
        projected[..., :query_cols].reshape(seq_count, row_count, QH, HD), cosine, sine_table
    )
    queries = queries.astype(jnp.bfloat16).reshape(seq_count, row_count, query_cols)
    key_heads = rotate(
        projected[..., query_cols : query_cols + key_cols].reshape(seq_count, row_count, KVH, HD),
        cosine,
        sine_table,
    )
    key_heads = key_heads.astype(jnp.bfloat16).reshape(seq_count, row_count, key_cols)
    value_heads = projected[..., query_cols + key_cols :].astype(jnp.bfloat16)
    keys_all, values_all = (
        lax.all_gather(key_heads, "ctx", axis=1, tiled=True),
        lax.all_gather(value_heads, "ctx", axis=1, tiled=True),
    )
    query_blocks = split_heads(queries, QH).reshape(seq_count * KVH, group_count * row_count, HD)
    key_blocks = split_heads(keys_all, KVH)
    value_blocks = split_heads(values_all, KVH)
    pair_lengths = jnp.repeat(lengths, KVH)

    def forward_block(block_in):
        query_rows, key_rows, value_rows, length = block_in
        scores = block_scores(query_rows, key_rows, position, length, group_count, score_scale)
        row_max = jnp.max(scores, axis=-1, keepdims=True)
        exp_terms = jnp.exp(scores - row_max)
        row_total = jnp.sum(exp_terms, axis=-1, keepdims=True)
        prob_rows = (exp_terms / row_total).astype(jnp.bfloat16)
        result = jnp.einsum(
            "gst,td->gsd", prob_rows, value_rows, preferred_element_type=jnp.float32
        )
        return (result.reshape(-1, HD), (row_max + jnp.log(row_total))[..., 0])

    context_blocks, log_totals = lax.map(
        forward_block, (query_blocks, key_blocks, value_blocks, pair_lengths)
    )
    context = join_heads(context_blocks.reshape(seq_count * QH, row_count, HD), seq_count).astype(
        jnp.bfloat16
    )
    hidden = source + jnp.einsum(
        "bse,ed->bsd", context, out_full, preferred_element_type=jnp.float32
    )
    inverse_two = lax.rsqrt(jnp.mean(hidden * hidden, axis=-1, keepdims=True) + EPS)
    normed_two = (hidden * inverse_two * gain_fb.astype(jnp.float32)).astype(jnp.bfloat16)
    gate_up = jnp.einsum(
        "bsd,df->bsf", normed_two, gate_up_full, preferred_element_type=jnp.float32
    )
    gate_part = gate_up[..., :FF]
    up_part = gate_up[..., FF:]
    gate_sig = jax.nn.sigmoid(gate_part)
    swish_part = gate_part * gate_sig
    activation = (swish_part * up_part).astype(jnp.bfloat16)
    result_rows = hidden + jnp.einsum(
        "bsf,fd->bsd", activation, down_full, preferred_element_type=jnp.float32
    )
    output = jnp.where(valid_rows[..., None], result_rows, 0.0).astype(jnp.bfloat16)
    back_wide = (
        lax.all_gather(w_qkv, "ctx", axis=1, tiled=True),
        lax.all_gather(w_out, "ctx", axis=1, tiled=True),
        lax.all_gather(w_gate_up, "ctx", axis=1, tiled=True),
        lax.all_gather(w_down, "ctx", axis=1, tiled=True),
    )
    qkv_back, out_back, gate_up_back, down_back, gain_ba, gain_bb = (
        lax.all_gather(back_wide[0], "dp", axis=0, tiled=True),
        lax.all_gather(back_wide[1], "dp", axis=0, tiled=True),
        lax.all_gather(back_wide[2], "dp", axis=0, tiled=True),
        lax.all_gather(back_wide[3], "dp", axis=0, tiled=True),
        lax.all_gather(gain_one, "dp", axis=0, tiled=True),
        lax.all_gather(gain_two, "dp", axis=0, tiled=True),
    )
    grad_rows = jnp.where(valid_rows[..., None], cotangent, jnp.zeros_like(cotangent))
    grad_activation = jnp.einsum(
        "bsd,fd->bsf", grad_rows, down_back, preferred_element_type=jnp.float32
    )
    grad_gate = grad_activation * up_part * gate_sig * (1.0 + gate_part * (1.0 - gate_sig))
    grad_up = grad_activation * swish_part
    grad_mix = jnp.concatenate([grad_gate, grad_up], axis=-1).astype(jnp.bfloat16)
    grad_normed_two = jnp.einsum(
        "bsf,df->bsd", grad_mix, gate_up_back, preferred_element_type=jnp.float32
    )
    back_two, grad_gain_two = norm_back(
        hidden, inverse_two, gain_bb.astype(jnp.float32), grad_normed_two
    )
    grad_hidden = grad_rows.astype(jnp.float32) + back_two
    grad_branch = grad_hidden.astype(jnp.bfloat16)
    grad_context = jnp.einsum(
        "bsd,ed->bse", grad_branch, out_back, preferred_element_type=jnp.float32
    ).astype(jnp.bfloat16)
    grad_blocks = split_heads(grad_context, QH).reshape(
        seq_count * KVH, group_count * row_count, HD
    )

    def backward_block(block_in):
        query_rows, key_rows, value_rows, length, log_total, grad_in = block_in
        scores = block_scores(query_rows, key_rows, position, length, group_count, score_scale)
        prob_rows = jnp.exp(scores - log_total[..., None])
        grad_grouped = grad_in.reshape(group_count, -1, HD)
        grad_probs = jnp.einsum(
            "gsd,td->gst", grad_grouped, value_rows, preferred_element_type=jnp.float32
        )
        grad_value = jnp.einsum(
            "gst,gsd->td",
            prob_rows.astype(jnp.bfloat16),
            grad_grouped,
            preferred_element_type=jnp.float32,
        )
        row_delta = jnp.sum(prob_rows * grad_probs, axis=-1, keepdims=True)
        grad_scores = (prob_rows * (grad_probs - row_delta)).astype(jnp.bfloat16)
        grad_query = (
            jnp.einsum("gst,td->gsd", grad_scores, key_rows, preferred_element_type=jnp.float32)
            * score_scale
        )
        grad_key = (
            jnp.einsum(
                "gst,gsd->td",
                grad_scores,
                query_rows.reshape(group_count, -1, HD),
                preferred_element_type=jnp.float32,
            )
            * score_scale
        )
        return (grad_query.reshape(-1, HD), grad_key, grad_value)

    query_grads, key_grads, value_grads = lax.map(
        backward_block,
        (query_blocks, key_blocks, value_blocks, pair_lengths, log_totals, grad_blocks),
    )
    key_sums, value_sums = (
        lax.psum_scatter(
            join_heads(key_grads, seq_count).astype(jnp.bfloat16),
            "ctx",
            scatter_dimension=1,
            tiled=True,
        ).astype(jnp.float32),
        lax.psum_scatter(
            join_heads(value_grads, seq_count).astype(jnp.bfloat16),
            "ctx",
            scatter_dimension=1,
            tiled=True,
        ).astype(jnp.float32),
    )
    grad_queries = join_heads(query_grads.reshape(seq_count * QH, row_count, HD), seq_count)
    turned_queries = rotate(grad_queries.reshape(seq_count, row_count, QH, HD), cosine, -sine_table)
    turned_keys = rotate(key_sums.reshape(seq_count, row_count, KVH, HD), cosine, -sine_table)
    grad_mixed = jnp.concatenate(
        [
            turned_queries.reshape(seq_count, row_count, query_cols),
            turned_keys.reshape(seq_count, row_count, key_cols),
            value_sums,
        ],
        axis=-1,
    ).astype(jnp.bfloat16)
    grad_normed_one = jnp.einsum(
        "bse,de->bsd", grad_mixed, qkv_back, preferred_element_type=jnp.float32
    )
    back_one, grad_gain_one = norm_back(
        source, inverse_one, gain_ba.astype(jnp.float32), grad_normed_one
    )
    grad_tokens = (grad_hidden + back_one).astype(jnp.bfloat16)
    exchanged = (
        lax.all_to_all(grad_mixed, "ctx", split_axis=2, concat_axis=1, tiled=True),
        lax.all_to_all(grad_branch, "ctx", split_axis=2, concat_axis=1, tiled=True),
        lax.all_to_all(grad_mix, "ctx", split_axis=2, concat_axis=1, tiled=True),
        lax.all_to_all(grad_rows, "ctx", split_axis=2, concat_axis=1, tiled=True),
    )
    initial = (
        jnp.zeros((model_width, exchanged[0].shape[2]), jnp.float32),
        jnp.zeros((context.shape[2], exchanged[1].shape[2]), jnp.float32),
        jnp.zeros((model_width, exchanged[2].shape[2]), jnp.float32),
        jnp.zeros((activation.shape[2], exchanged[3].shape[2]), jnp.float32),
    )
    pieces = (
        lax.all_gather(normed_one, "ctx", axis=1, tiled=True),
        lax.all_gather(context, "ctx", axis=1, tiled=True),
        lax.all_gather(normed_two, "ctx", axis=1, tiled=True),
        lax.all_gather(activation, "ctx", axis=1, tiled=True),
    )
    updated = []
    for total, piece, right in zip(initial, pieces, exchanged):
        updated.append(jnp.einsum("bsr,bsc->rc", piece, right, preferred_element_type=jnp.float32))
    column_grads = tuple(updated)
    gain_whole = lax.psum((grad_gain_one, grad_gain_two), "ctx")
    final_qkv, final_out, final_gate_up, final_down, final_gain_one, final_gain_two = (
        lax.psum_scatter(
            column_grads[0].astype(jnp.bfloat16), "dp", scatter_dimension=0, tiled=True
        ).astype(jnp.float32),
        lax.psum_scatter(
            column_grads[1].astype(jnp.bfloat16), "dp", scatter_dimension=0, tiled=True
        ).astype(jnp.float32),
        lax.psum_scatter(
            column_grads[2].astype(jnp.bfloat16), "dp", scatter_dimension=0, tiled=True
        ).astype(jnp.float32),
        lax.psum_scatter(
            column_grads[3].astype(jnp.bfloat16), "dp", scatter_dimension=0, tiled=True
        ).astype(jnp.float32),
        lax.psum_scatter(
            gain_whole[0].astype(jnp.bfloat16), "dp", scatter_dimension=0, tiled=True
        ).astype(jnp.float32),
        lax.psum_scatter(
            gain_whole[1].astype(jnp.bfloat16), "dp", scatter_dimension=0, tiled=True
        ).astype(jnp.float32),
    )
    return (
        output,
        grad_tokens,
        final_gain_one,
        final_qkv,
        final_out,
        final_gain_two,
        final_gate_up,
        final_down,
    )


MESH = pl.DeviceIdType.MESH


class Place:
    def __init__(self):
        self.dp = lax.axis_index("dp")
        self.ctx = lax.axis_index("ctx")
        self.z = lax.div(self.dp, 2)
        self.y = lax.rem(self.dp, 2)
        self.x = lax.div(self.ctx, 2)
        self.c = lax.rem(self.ctx, 2)
        self.up = (self.dp + 2, self.ctx)
        self.down = (self.dp - 2, self.ctx)
        self.across = (self.dp + 1 - 2 * self.y, self.ctx)
        self.chip = (self.dp, (1 - self.x) * 2 + self.c)
        self.core = (self.dp, self.x * 2 + 1 - self.c)
        self.has_up = self.z < 3
        self.has_down = self.z > 0


def greet(place):
    barrier = pltpu.get_barrier_semaphore()

    def tell(device):
        pl.semaphore_signal(barrier, inc=1, device_id=device, device_id_type=MESH)

    pl.when(place.has_up)(lambda: tell(place.up))
    pl.when(place.has_down)(lambda: tell(place.down))
    tell(place.across)
    for step in (1, 2, 3):
        tell((place.dp, lax.rem(place.ctx + step, 4)))
    ends = place.has_up.astype(jnp.int32) + place.has_down.astype(jnp.int32)
    pl.semaphore_wait(barrier, 4 + ends)


class Wires:
    def __init__(self, send_sems, recv_sems, names):
        self.send_sems = send_sems
        self.recv_sems = recv_sems
        self.index = names
        self.count = 0
        self.pending = []

    def slot(self, name):
        if name not in self.index:
            self.index[name] = len(self.index)
        return self.index[name]

    def send(self, src, dst, name, device, cond=None, extra=None):
        number = self.count
        self.count += 1
        at = self.slot(name)
        if extra is not None:
            at = at + extra
        copy = pltpu.make_async_remote_copy(
            src_ref=src,
            dst_ref=dst,
            send_sem=self.send_sems.at[number],
            recv_sem=self.recv_sems.at[at],
            device_id=device,
            device_id_type=MESH,
        )
        if cond is None:
            copy.start()
        else:
            pl.when(cond)(copy.start)
        self.pending.append((copy, cond))

    def take(self, dst, name, device, extra=None):
        at = self.slot(name)
        if extra is not None:
            at = at + extra
        pltpu.make_async_remote_copy(
            src_ref=dst,
            dst_ref=dst,
            send_sem=self.send_sems.at[0],
            recv_sem=self.recv_sems.at[at],
            device_id=device,
            device_id_type=MESH,
        ).wait_recv()

    def drain(self, first=None):
        first = len(self.pending) if first is None else first
        for copy, cond in self.pending[:first]:
            when(cond, copy.wait_send)
        self.pending = self.pending[first:]


BELOW, ABOVE = 0, 1


def both(first, second):
    return second if first is None else jnp.logical_and(first, second)


def source_valid(place, way, dist):
    return place.z >= dist if way == BELOW else place.z + dist <= 3


def source_pos(place, way, dist):
    return place.dp - 2 * dist if way == BELOW else place.dp + 2 * dist


def flood_start(wires, place, name, own, block, spread):
    wires.send(own, block(place.dp), (name, BELOW, 1), place.up, place.has_up)
    wires.send(own, block(place.dp), (name, ABOVE, 1), place.down, place.has_down)
    wires.send(own, block(place.dp), (name, "y", 0, 0), place.across)
    spread(own, place.dp, (0, 0, 0), None)


def flood_step(wires, place, name, block, spread, way, dist):
    here = source_valid(place, way, dist)
    pos = source_pos(place, way, dist)
    view = block(pos)
    came_from = place.down if way == BELOW else place.up
    pl.when(here)(lambda: wires.take(view, (name, way, dist), came_from))
    if dist < 3:
        onward = place.up if way == BELOW else place.down
        more = place.has_up if way == BELOW else place.has_down
        wires.send(view, view, (name, way, dist + 1), onward, jnp.logical_and(here, more))
    wires.send(view, view, (name, "y", way, dist), place.across, here)
    spread(view, pos, (0, way, dist), here)


def flood_side(wires, place, name, block, spread, way, dist):
    if dist == 0:
        here, pos = None, place.dp
    else:
        here, pos = source_valid(place, way, dist), source_pos(place, way, dist)
    pos = pos + 1 - 2 * place.y
    view = block(pos)
    if here is None:
        wires.take(view, (name, "y", 0, 0), place.across)
    else:
        pl.when(here)(lambda: wires.take(view, (name, "y", way, dist), place.across))
    spread(view, pos, (1, way, dist), here)


HOPS = [(way, dist) for dist in (1, 2, 3) for way in (BELOW, ABOVE)]


def no_spread(view, pos, key, cond):
    return None


def add_rows(dst, srcs, out=None, cast=None, chunk=48):
    out = dst if out is None else out
    total_rows = dst.shape[0]
    assert total_rows % chunk == 0

    def body(i, carry):
        at = pl.ds(pl.multiple_of(i * chunk, 16), chunk)
        total = dst[at, :].astype(jnp.float32)
        for src in srcs:
            total = total + src[at, :].astype(jnp.float32)
        out[at, :] = total.astype(out.dtype)
        return carry

    lax.fori_loop(0, total_rows // chunk, body, 0)


def when(cond, action):
    if cond is None:
        action()
    else:
        pl.when(cond)(action)


DRAIN = [(way, dist) for dist in (3, 2, 1, 0) for way in (BELOW, ABOVE)]


def nn(a, b):
    return jnp.dot(a, b, preferred_element_type=jnp.float32)


def nt(a, b):
    return lax.dot_general(a, b, (((1,), (1,)), ((), ())), preferred_element_type=jnp.float32)


def tn(a, b):
    return lax.dot_general(a, b, (((0,), (0,)), ((), ())), preferred_element_type=jnp.float32)


def layer_kernel(
    names,
    tokens, cot, lengths, qkv_in, out_in, gu_in, dt_in, gain_in, cos, sin,
    output, grad_tokens, gain_out, qkv_out, out_out, gu_out, dt_out,
    w_qkv, w_out, w_ff, gain_all, gain_row,
    n1, n2_all, g_all, context, hidden, grad_hidden, proj, q_st, kv_all, p_st, att, go_st, wide, gm,
    act, d_gate, d_up, gp, gp_box, op, op_box, dkv, dkv_box,
    d_gu, d_dt,
    qkv_core, out_core, qkv_chip, out_chip, qkv_side, out_side, gu_side, down_side,
    qkv_inbox, out_inbox, gu_inbox, down_inbox, gu_mix, down_mix, gain_box,
    send_sems, recv_sems, local_sems,
):
    f32, low = jnp.float32, jnp.bfloat16
    place = Place()
    wires = Wires(send_sems, recv_sems, names)
    dp, ctx, z, y, x, c = place.dp, place.ctx, place.z, place.y, place.x, place.c
    rows = qkv_in.shape[0]
    strip, half = dt_in.shape
    units = act.shape[1]
    width = tokens.shape[1]
    own_rows = tokens.shape[0]
    slots_here = own_rows // 2
    qkv_cols, out_cols = qkv_in.shape[1], out_in.shape[1]
    qkv_wide, out_wide = w_qkv.shape[2], w_out.shape[2]
    group = QH // KVH
    slabs = KVH // 2
    gate_at, up_at, down_at = 0, units, 2 * units

    greet(place)

    def row_view(ref, lead, pos):
        return ref.at[lead, pl.ds(pl.multiple_of(pos * rows, 16), rows)]

    def ff_view(at, pos):
        return w_ff.at[pl.ds(pl.multiple_of(pos * rows, 16), rows), pl.ds(at, units)]

    locals_ = []

    def local(src, dst, cond=None):
        copy = pltpu.make_async_copy(src, dst, local_sems.at[len(locals_)])
        locals_.append((copy, cond))
        when(cond, copy.start)

    my_rows = pl.ds(pl.multiple_of(dp * rows, 16), rows)
    gu_places = ((gate_at, 0), (up_at, 1))
    for part in range(2):
        target = 2 * c + part
        src = gu_in.at[:, pl.ds(part * units, units)]
        for at, half_x in gu_places:
            here = x == half_x
            wires.send(src, ff_view(at, dp), ("gu_mix", half_x), (dp, target), jnp.logical_and(here, target != ctx))
            local(src, ff_view(at, dp), jnp.logical_and(here, target == ctx))

    def attention_spread(name, ref):
        def spread(view, pos, key, cond):
            dst = row_view(ref, ctx, pos)
            wires.send(view, dst, (name, "x") + key, place.chip, cond)
            wires.send(view, dst, (name, "c") + key, place.core, cond)
        return spread

    attention = [("qkv", qkv_in, w_qkv, qkv_cols), ("out", out_in, w_out, out_cols)]

    def attention_start(name, own, ref, cols):
        ref[ctx, my_rows, :] = jnp.zeros((rows, ref.shape[2]), low)
        ref[ctx, my_rows, :cols] = own[...]
        block = functools.partial(row_view, ref, ctx)
        flood_start(wires, place, name, block(dp), block, attention_spread(name, ref))

    attention_start(*attention[0])
    gain_block = lambda pos: gain_all.at[pos]
    gain_all[dp] = gain_in[...]
    flood_start(wires, place, "gain", gain_block(dp), gain_block, no_spread)

    lanes = pl.ds(pl.multiple_of(down_at + y * half, 128), half)
    other_lanes = pl.ds(pl.multiple_of(down_at + (1 - y) * half, 128), half)
    dst = w_ff.at[pl.ds(pl.multiple_of(ctx * strip, 16), strip), lanes]
    wires.send(dt_in, dst, ("down_mix", 0), (dp, z), ctx != z, extra=ctx)
    for j in range(1, 4):
        wires.slot(("down_mix", j))
    local(dt_in, dst, ctx == z)

    row_at = lax.broadcasted_iota(jnp.int32, (own_rows, 1), 0)
    first_seq = row_at < slots_here
    position = ctx * slots_here + jnp.where(first_seq, row_at, row_at - slots_here)
    row_length = jnp.where(first_seq, lengths[0], lengths[1])
    valid = position < row_length

    def share(name, ref):
        mine = ref.at[pl.ds(pl.multiple_of(ctx * own_rows, 16), own_rows)]
        wires.send(mine, mine, (name, "x"), place.chip)
        wires.send(mine, mine, (name, "c"), place.core)

    def share_on(name, ref):
        far = ref.at[pl.ds(pl.multiple_of(place.chip[1] * own_rows, 16), own_rows)]
        wires.take(far, (name, "x"), place.chip)
        wires.send(far, far, (name, "d"), place.core)

    def share_end(name, ref):
        for mark, lead in (("c", place.core[1]), ("d", 3 - ctx)):
            view = ref.at[pl.ds(pl.multiple_of(lead * own_rows, 16), own_rows)]
            wires.take(view, (name, mark), place.core)

    here_rows = pl.ds(pl.multiple_of(ctx * own_rows, 16), own_rows)
    g_all[here_rows, :] = jnp.where(valid, cot[...].astype(f32), 0.0).astype(low)

    for part in range(2):
        remote = (part * 2 + x) != ctx
        view = ff_view(gu_places[part][0], dp)
        pl.when(remote)(lambda: wires.take(view, ("gu_mix", part), (dp, part * 2 + x)))
    for copy, cond in locals_:
        when(cond, copy.wait)
    gu_blocks = [functools.partial(ff_view, at) for at, _ in gu_places]
    for part in range(2):
        flood_start(wires, place, ("gu", part), gu_blocks[part](dp), gu_blocks[part], no_spread)

    at_home = ctx == z
    strips = [w_ff.at[pl.ds(j * strip, strip), lanes] for j in range(4)]
    other_strips = [w_ff.at[pl.ds(j * strip, strip), other_lanes] for j in range(4)]

    def take_strips():
        for j in range(4):
            pl.when(ctx != j)(functools.partial(wires.take, strips[j], ("down_mix", j), (dp, j)))

    def down_start():
        pl.when(at_home)(take_strips)
        for j in range(4):
            wires.send(strips[j], strips[j], ("down", j, BELOW, 1), place.up, jnp.logical_and(at_home, place.has_up))
            wires.send(strips[j], strips[j], ("down", j, ABOVE, 1), place.down, jnp.logical_and(at_home, place.has_down))
            wires.send(strips[j], strips[j], ("down_y", j, 0, 0), place.across, at_home)

    def down_step(way, dist):
        offset = z - ctx if way == BELOW else ctx - z
        here = offset == dist
        came_from = place.down if way == BELOW else place.up
        onward = place.up if way == BELOW else place.down
        more = place.has_up if way == BELOW else place.has_down
        for j in range(4):
            pl.when(here)(functools.partial(wires.take, strips[j], ("down", j, way, dist), came_from))
            if dist < 3:
                wires.send(strips[j], strips[j], ("down", j, way, dist + 1), onward, jnp.logical_and(here, more))
            wires.send(strips[j], strips[j], ("down_y", j, way, dist), place.across, here)

    SIDES = [(0, 0)] + HOPS
    WAYS = {0: [(0, 0)], 1: HOPS[:2], 2: HOPS[2:4], 3: HOPS[4:]}
    att_w, out_w = attention

    def hop(which, dist):
        name, own, ref, cols = which
        for way, dist in WAYS[dist]:
            flood_step(wires, place, name, functools.partial(row_view, ref, ctx), attention_spread(name, ref), way, dist)

    def side(which, dist):
        name, own, ref, cols = which
        for way, dist in WAYS[dist]:
            flood_side(wires, place, name, functools.partial(row_view, ref, ctx), attention_spread(name, ref), way, dist)

    def gain_step(dist):
        for way, dist in WAYS[dist]:
            flood_step(wires, place, "gain", gain_block, no_spread, way, dist)

    def ff_step(dist):
        for way, dist in WAYS[dist]:
            for part in range(2):
                flood_step(wires, place, ("gu", part), gu_blocks[part], no_spread, way, dist)
            down_step(way, dist)

    def spots(column, dist):
        for way, dist in WAYS[dist]:
            if dist == 0:
                here, pos = None, dp
            else:
                here, pos = source_valid(place, way, dist), source_pos(place, way, dist)
            if column == 1:
                pos = pos + 1 - 2 * y
            yield (column, way, dist), here, pos

    def chip(which, column, dist):
        name, own, ref, cols = which
        for key, here, pos in spots(column, dist):
            view = row_view(ref, place.chip[1], pos)
            when(here, lambda: wires.take(view, (name, "x") + key, place.chip))
            wires.send(view, view, (name, "d") + key, place.core, here)

    def core(which):
        name, own, ref, cols = which
        for column in range(2):
            for dist in range(4):
                for key, here, pos in spots(column, dist):
                    for mark, lead in (("c", place.core[1]), ("d", 3 - ctx)):
                        view = row_view(ref, lead, pos)
                        when(here, lambda: wires.take(view, (name, mark) + key, place.core))

    down_start()
    hop(att_w, 1)
    gain_step(1)
    side(att_w, 0)
    attention_start(*out_w)
    ff_step(1)
    hop(att_w, 2)
    gain_step(2)
    side(att_w, 1)
    chip(att_w, 0, 0)
    chip(att_w, 0, 1)
    hop(out_w, 1)
    side(out_w, 0)
    ff_step(2)
    hop(att_w, 3)
    gain_step(3)
    side(att_w, 2)
    chip(att_w, 1, 0)
    chip(att_w, 0, 2)
    hop(out_w, 2)
    side(out_w, 1)
    chip(out_w, 0, 0)
    ff_step(3)
    side(att_w, 3)
    chip(att_w, 1, 1)
    chip(att_w, 0, 3)
    hop(out_w, 3)
    side(out_w, 2)
    chip(out_w, 0, 1)
    chip(out_w, 1, 0)
    for way, dist in SIDES:
        flood_side(wires, place, "gain", gain_block, no_spread, way, dist)
    chip(att_w, 1, 2)
    chip(att_w, 1, 3)
    side(out_w, 3)
    chip(out_w, 0, 2)
    chip(out_w, 1, 1)
    core(att_w)

    gain_row[...] = jnp.zeros(gain_row.shape, f32)
    for pos in range(8):
        piece = gain_all[pos]
        shift = (pos * rows) % 128
        if shift:
            piece = pltpu.roll(piece, shift, 1)
        at = (pos * rows) // 128 * 128
        gain_row[:, at : at + 256] += piece
    gain_a = lambda: gain_row[0:1, :width]
    gain_b = lambda: gain_row[1:2, :width]

    def norm(values):
        return lax.rsqrt(jnp.mean(values * values, axis=-1, keepdims=True) + EPS)

    source = tokens[...].astype(f32)
    n1[...] = (source * norm(source) * gain_a()).astype(low)
    proj[...] = jnp.zeros(proj.shape, f32)
    for j in range(4):
        part = nn(n1[...], w_qkv[j])
        part = jnp.concatenate([part, jnp.zeros((own_rows, 128), f32)], axis=1)
        at = qkv_cols * j
        if at % 128:
            part = pltpu.roll(part, at % 128, 1)
        proj[:, at // 128 * 128 : at // 128 * 128 + qkv_wide + 128] += part

    lane = lax.broadcasted_iota(jnp.int32, (own_rows, 128), 1)
    low_half = lax.rem(lane, HD) < HD // 2
    side_of = lax.div(lane, HD)

    def turn(values, sign):
        swapped = jnp.where(low_half, pltpu.roll(values, 128 - HD // 2, 1), pltpu.roll(values, HD // 2, 1))
        return values * cos[...] + swapped * (sin[...] * sign)

    def head_spots():
        for head in range(QH):
            kv = head // group
            yield head // 2, head % 2, kv // 2, kv % 2, (kv % 2 * group + head % group) * slots_here

    def stack_heads(slab_of, dest, scale):
        for slab, side, key_slab, key_side, at in head_spots():
            values = slab_of(slab)
            if side != key_side:
                values = pltpu.roll(values, HD, 1)
            values = (jnp.where(side_of == key_side, values, 0.0) * scale).astype(low)
            for seq in range(2):
                dest[seq * slabs + key_slab, at : at + slots_here, :] = values[
                    seq * slots_here : (seq + 1) * slots_here
                ]

    def unstack_heads(src, slab):
        total = jnp.zeros((own_rows, 128), f32)
        for at_slab, side, key_slab, key_side, at in head_spots():
            if at_slab != slab:
                continue
            values = jnp.concatenate(
                [src[seq * slabs + key_slab, at : at + slots_here, :] for seq in range(2)], axis=0
            )
            values = jnp.where(side_of == key_side, values, 0.0)
            if side != key_side:
                values = pltpu.roll(values, HD, 1)
            total = total + values
        return total

    turned = {}

    def query_slab(slab):
        if slab not in turned:
            turned[slab] = turn(proj[:, slab * 128 : slab * 128 + 128], 1.0)
        return turned[slab]

    score_scale = 1.0 / math.sqrt(HD)
    stack_heads(query_slab, q_st, score_scale)
    q_slabs = QH // 2
    my_slots = pl.ds(pl.multiple_of(ctx * slots_here, 16), slots_here)
    for slab in range(2 * slabs):
        at = (q_slabs + slab) * 128
        values = proj[:, at : at + 128]
        if slab < slabs:
            values = turn(values, 1.0)
        values = values.astype(low)
        for seq in range(2):
            kv_all[seq, slab, my_slots, :] = values[seq * slots_here : (seq + 1) * slots_here]

    def slot_view(lead):
        return kv_all.at[:, :, pl.ds(pl.multiple_of(lead * slots_here, 16), slots_here)]

    for step in (1, 2, 3):
        wires.send(slot_view(ctx), slot_view(ctx), ("kv", step), (dp, lax.rem(ctx + step, 4)))
    share("cot", g_all)
    chip(out_w, 0, 3)
    chip(out_w, 1, 2)
    chip(out_w, 1, 3)
    for step in (1, 2, 3):
        peer = lax.rem(ctx + 4 - step, 4)
        wires.take(slot_view(peer), ("kv", step), (dp, peer))

    stack = q_st.shape[1]
    slots = kv_all.shape[2]

    def attend(i, carry):
        seq, slab = lax.div(i, slabs), lax.rem(i, slabs)
        scores = nt(q_st[i], kv_all[seq, slab])
        at = ctx * slots_here + lax.rem(lax.broadcasted_iota(jnp.int32, (stack, slots), 0), slots_here)
        key_at = lax.broadcasted_iota(jnp.int32, (stack, slots), 1)
        length = jnp.where(seq == 0, lengths[0], lengths[1])
        allowed = jnp.logical_and(key_at <= at, key_at < length)
        scores = jnp.where(allowed, scores, NEGATIVE)
        terms = jnp.exp(scores - jnp.max(scores, axis=-1, keepdims=True))
        probs = (terms / jnp.sum(terms, axis=-1, keepdims=True)).astype(low)
        p_st[i] = probs
        att[i] = nn(probs, kv_all[seq, slabs + slab])
        return carry

    lax.fori_loop(0, 2 * slabs, attend, 0)
    core(out_w)
    for slab in range(q_slabs):
        context[:, slab * 128 : slab * 128 + 128] = unstack_heads(att, slab).astype(low)
    hidden[...] = source
    for j in range(4):
        part = nn(context[...], w_out[j])
        at = out_cols * j
        if at % 128:
            part = pltpu.roll(part, at % 128, 1)
        hidden[:, at // 128 * 128 : at // 128 * 128 + out_wide] += part
    n2_all[here_rows, :] = (hidden[...] * norm(hidden[...]) * gain_b()).astype(low)
    share("n2", n2_all)
    share_on("cot", g_all)

    gathered = len(wires.pending)

    for part in range(2):
        for way, dist in SIDES:
            flood_side(wires, place, ("gu", part), gu_blocks[part], no_spread, way, dist)
    for way, dist in SIDES:
        here = at_home if dist == 0 else (z - ctx if way == BELOW else ctx - z) == dist

        def side_strips():
            for j in range(4):
                wires.take(other_strips[j], ("down_y", j, way, dist), place.across)

        pl.when(here)(side_strips)
    share_on("n2", n2_all)
    share_end("cot", g_all)
    share_end("n2", n2_all)

    tall, tile = 256, 256

    def feed(i, carry):
        at = pl.ds(pl.multiple_of(lax.div(i, units // tile) * tall, tall), tall)
        unit = lax.rem(i, units // tile) * tile

        def cols(base):
            return pl.ds(pl.multiple_of(base + unit, tile), tile)

        gate = nn(n2_all[at, :], w_ff[:, cols(gate_at)])
        up = nn(n2_all[at, :], w_ff[:, cols(up_at)])
        back = nn(g_all[at, :], w_ff[:, cols(down_at)])
        sig = jax.nn.sigmoid(gate)
        swish = gate * sig
        act[at, cols(0)] = (swish * up).astype(low)
        d_gate[at, cols(0)] = (back * up * sig * (1.0 + gate * (1.0 - sig))).astype(low)
        d_up[at, cols(0)] = (back * swish).astype(low)
        return carry

    lax.fori_loop(0, (4 * own_rows // tall) * (units // tile), feed, 0)

    across_core = (1 - x) * 2 + 1 - c
    across_own = (1 - x) * 2 + c
    beside = x * 2 + 1 - c
    wide_tile = 384

    def group_blocks(compute, name, ref, box):
        compute(1 - x)
        wires.send(ref.at[across_core], box.at[0], (name, "cx"), place.core)
        compute(x)
        wires.send(ref.at[beside], box.at[1], (name, "cc"), place.core)

    def group_on(name, ref, box):
        wires.take(box.at[0], (name, "cx"), place.core)
        add_any(ref.at[across_own], box.at[0])
        wires.send(ref.at[across_own], box.at[2], (name, "x"), place.chip)

    def group_end(name, ref, box):
        wires.take(box.at[1], (name, "cc"), place.core)
        wires.take(box.at[2], (name, "x"), place.chip)
        return ref[ctx].astype(f32) + box[1].astype(f32) + box[2].astype(f32)

    def add_any(dst, src):
        dst[...] = (dst[...].astype(f32) + src[...].astype(f32)).astype(low)

    def pair_rows(half_x):
        return pl.ds(pl.multiple_of(half_x * 2 * own_rows, 16), 2 * own_rows)

    def back_block(half_x):
        def body(n, carry):
            at = pl.ds(pl.multiple_of(n * wide_tile, 128), wide_tile)
            total = nt(d_gate[pair_rows(half_x), :], w_ff[at, pl.ds(gate_at, units)])
            total = total + nt(d_up[pair_rows(half_x), :], w_ff[at, pl.ds(up_at, units)])
            gp[2 * half_x, :, at] = total[:own_rows].astype(low)
            gp[2 * half_x + 1, :, at] = total[own_rows:].astype(low)
            return carry

        lax.fori_loop(0, width // wide_tile, body, 0)

    def forward_block(half_x):
        def body(n, carry):
            at = pl.ds(pl.multiple_of(n * wide_tile, 128), wide_tile)
            total = nt(act[pair_rows(half_x), :], w_ff[at, pl.ds(down_at, units)])
            op[2 * half_x, :, at] = total[:own_rows].astype(low)
            op[2 * half_x + 1, :, at] = total[own_rows:].astype(low)
            return carry

        lax.fori_loop(0, width // wide_tile, body, 0)

    group_blocks(back_block, "gp", gp, gp_box)
    group_on("gp", gp, gp_box)

    def grad_ff(m, carry):
        at = pl.ds(pl.multiple_of(m * 128, 128), 128)
        left = n2_all[:, at]
        d_gu[0, at, :] = tn(left, d_gate[...]).astype(low)
        d_gu[1, at, :] = tn(left, d_up[...]).astype(low)
        d_dt[at, :] = tn(g_all[:, at], act[...]).astype(low)
        return carry

    lax.fori_loop(0, width // 128, grad_ff, 0)

    d_lanes = pl.ds(pl.multiple_of(y * half, 128), half)
    d_other = pl.ds(pl.multiple_of((1 - y) * half, 128), half)
    d_strips = [d_dt.at[pl.ds(j * strip, strip), d_lanes] for j in range(4)]
    d_other_strips = [d_dt.at[pl.ds(j * strip, strip), d_other] for j in range(4)]
    def key_pos(way, dist):
        if dist == 0:
            return None, dp
        return source_valid(place, way, dist), source_pos(place, way, dist)

    KEYS = {3: DRAIN[:2], 2: DRAIN[2:4], 1: DRAIN[4:6], 0: [(BELOW, 0)]}
    flip = 1 - 2 * y

    def gu_send(dist):
        for way, dist in KEYS[dist]:
            here, pos = key_pos(way, dist)
            for part in range(2):
                wires.send(
                    row_view(d_gu, part, pos + flip), gu_side.at[part, way, dist],
                    (("dgu", part), "y", way, dist), place.across, here,
                )

    def z_add(name, view, boxes, inbox, way, dist):
        here, pos = key_pos(way, dist)
        mine = view(pos)
        if dist == 0:
            wires.take(boxes.at[way, dist], (name, "y", way, dist), place.across)
            add_rows(mine, [boxes.at[way, dist]])
            for end, fed, feeder in ((BELOW, place.has_up, place.up), (ABOVE, place.has_down, place.down)):

                def own():
                    wires.take(inbox.at[end, 0], (name, "z", end, 0), feeder)
                    add_rows(mine, [inbox.at[end, 0]])

                pl.when(fed)(own)
            return
        fed = place.has_up if way == BELOW else place.has_down
        feeder = place.up if way == BELOW else place.down
        onward = place.down if way == BELOW else place.up
        side = boxes.at[way, dist]

        def first():
            wires.take(side, (name, "y", way, dist), place.across)
            add_rows(mine, [side])

        if dist == 3:
            pl.when(here)(first)
        else:

            def more():
                wires.take(side, (name, "y", way, dist), place.across)
                wires.take(inbox.at[way, dist], (name, "z", way, dist), feeder)
                add_rows(mine, [side, inbox.at[way, dist]])

            pl.when(jnp.logical_and(here, jnp.logical_not(fed)))(first)
            pl.when(jnp.logical_and(here, fed))(more)
        wires.send(mine, inbox.at[way, dist - 1], (name, "z", way, dist - 1), onward, here)

    def gu_add(dist):
        for way, dist in KEYS[dist]:
            for part in range(2):
                z_add(("dgu", part), functools.partial(row_view, d_gu, part), gu_side.at[part], gu_inbox.at[part], way, dist)

    def down_send():
        for j in range(4):
            wires.send(d_other_strips[j], down_side.at[j], ("ddown_y", j), place.across)

    def down_add(dist):
        away = jnp.abs(z - ctx) == dist
        if dist == 0:
            for j in range(4):

                def finish(j=j):
                    wires.take(down_side.at[j], ("ddown_y", j), place.across)
                    add_rows(d_strips[j], [down_side.at[j]])
                    for end, fed, feeder in ((BELOW, place.has_up, place.up), (ABOVE, place.has_down, place.down)):

                        def more():
                            wires.take(down_inbox.at[end, j], ("ddown", j, end, 0), feeder)
                            add_rows(d_strips[j], [down_inbox.at[end, j]])

                        pl.when(fed)(more)

                pl.when(away)(finish)
            return
        for way in (BELOW, ABOVE):
            here = (z - ctx if way == BELOW else ctx - z) == dist
            fed = place.has_up if way == BELOW else place.has_down
            feeder = place.up if way == BELOW else place.down
            onward = place.down if way == BELOW else place.up
            for j in range(4):

                def first():
                    wires.take(down_side.at[j], ("ddown_y", j), place.across)
                    add_rows(d_strips[j], [down_side.at[j]])

                def more():
                    wires.take(down_inbox.at[way, j], ("ddown", j, way, dist), feeder)
                    add_rows(d_strips[j], [down_inbox.at[way, j]])

                pl.when(here)(first)
                pl.when(jnp.logical_and(here, fed))(more)
                wires.send(d_strips[j], down_inbox.at[way, j], ("ddown", j, way, dist - 1), onward, here)

    def ff_add(dist):
        down_add(dist)
        gu_add(dist)

    def ff_finish():
        for part in range(2):
            target = part * 2 + x
            block = row_view(d_gu, part, dp)
            wires.send(block, gu_mix.at[c], ("dgu_mix", 0), (dp, target), target != ctx, extra=c)
            pl.when(target == ctx)(lambda: add_rows(block, [], out=gu_mix.at[c]))
        wires.slot(("dgu_mix", 1))
        for j in range(4):
            wires.send(d_strips[j], down_mix, ("ddown_mix",), (dp, j), jnp.logical_and(at_home, ctx != j))
            pl.when(jnp.logical_and(at_home, ctx == j))(functools.partial(add_rows, d_strips[j], [], down_mix))

    gu_send(3)
    down_send()
    for dist in (2, 1, 0):
        gu_send(dist)

    group_blocks(forward_block, "op", op, op_box)
    group_on("op", op, op_box)

    def norm_back(values, inverse, gain, grad_in):
        scaled = grad_in * gain
        mean_term = jnp.mean(scaled * values, axis=-1, keepdims=True)
        back = inverse * scaled - values * (inverse * inverse * inverse) * mean_term
        return back, jnp.sum(grad_in * values * inverse, axis=0, keepdims=True)

    gain_out[...] = jnp.zeros(gain_out.shape, f32)
    back_two, gain_two_grad = norm_back(hidden[...], norm(hidden[...]), gain_b(), group_end("gp", gp, gp_box))
    gain_out[1:2, :] = gain_two_grad
    grad_hidden[...] = g_all[here_rows, :].astype(f32) + back_two
    out_lane = lax.broadcasted_iota(jnp.int32, (own_rows, out_wide), 1)
    for j in range(4):
        at = out_cols * j
        part = grad_hidden[:, at // 128 * 128 : at // 128 * 128 + out_wide]
        if at % 128:
            part = pltpu.roll(part, out_wide - at % 128, 1)
        wide[j] = jnp.where(out_lane < out_cols, part, 0.0).astype(low)

    def context_back(n, carry):
        at = pl.ds(pl.multiple_of(n * wide_tile, 128), wide_tile)
        total = nt(wide[0], w_out[0, at, :])
        for j in range(1, 4):
            total = total + nt(wide[j], w_out[j, at, :])
        proj[:, at] = total
        return carry

    lax.fori_loop(0, width // wide_tile, context_back, 0)
    stack_heads(lambda slab: proj[:, slab * 128 : slab * 128 + 128], go_st, 1.0)

    wires.drain(gathered)
    pair = 2 * rows

    def out_view(lead, at, size):
        return w_out.at[lead, pl.ds(at, size)]

    def qkv_view(lead, at, size):
        return w_ff.at[pl.ds(at, size), pl.ds(pl.multiple_of(lead * qkv_wide, 128), qkv_wide)]

    def grad_out(m, carry):
        at = pl.ds(pl.multiple_of(m * 128, 128), 128)
        for j in range(4):
            w_out[j, at, :] = tn(context[:, at], wide[j]).astype(low)
        return carry

    lax.fori_loop(0, width // 128, grad_out, 0)

    def core_send(name, view, box):
        for dist in (3, 2, 1, 0):
            for way, dist in KEYS[dist]:
                here, pos = key_pos(way, dist)
                at = pl.multiple_of((pos - y) * rows, 16)
                for xx in range(2):
                    wires.send(
                        view(2 * xx + 1 - c, at, pair), box.at[xx, pl.ds(at, pair)],
                        (name, "gc", xx, way, dist), place.core, here,
                    )

    def core_add(name, view, box, chip_box, dist):
        for way, dist in KEYS[dist]:
            here, pos = key_pos(way, dist)
            at = pl.multiple_of((pos - y) * rows, 16)

            def add():
                for xx in range(2):
                    part = box.at[xx, pl.ds(at, pair)]
                    wires.take(part, (name, "gc", xx, way, dist), place.core)
                    add_rows(view(2 * xx + c, at, pair), [part])

            when(here, add)
            wires.send(view(place.chip[1], at, pair), chip_box.at[pl.ds(at, pair)], (name, "gx", way, dist), place.chip, here)

    def chip_add(name, view, chip_box, side_box, dist):
        for way, dist in KEYS[dist]:
            here, pos = key_pos(way, dist)
            at = pl.multiple_of((pos - y) * rows, 16)

            def add():
                span = chip_box.at[pl.ds(at, pair)]
                wires.take(span, (name, "gx", way, dist), place.chip)
                add_rows(view(ctx, at, pair), [span])

            when(here, add)
            wires.send(own_view(view, pos + flip), side_box.at[way, dist], ((name, "g"), "y", way, dist), place.across, here)

    def own_view(view, pos):
        return view(ctx, pl.multiple_of(pos * rows, 16), rows)

    def side_add(name, view, side_box, inbox, dist):
        for way, dist in KEYS[dist]:
            z_add((name, "g"), functools.partial(own_view, view), side_box, inbox, way, dist)

    core_send("out", out_view, out_core)

    def attend_back(i, carry):
        seq, slab = lax.div(i, slabs), lax.rem(i, slabs)
        grad_probs = nt(go_st[i], kv_all[seq, slabs + slab])
        probs = p_st[i].astype(f32)
        delta = jnp.sum(probs * grad_probs, axis=-1, keepdims=True)
        grad_scores = (probs * (grad_probs - delta)).astype(low)
        att[i] = nn(grad_scores, kv_all[seq, slab]) * score_scale
        grad_key = tn(grad_scores, q_st[i])
        grad_value = tn(p_st[i], go_st[i])
        for j in range(4):
            part = slice(j * slots_here, (j + 1) * slots_here)
            dkv[j, seq, slab] = grad_key[part].astype(low)
            dkv[j, seq, slabs + slab] = grad_value[part].astype(low)
        return carry

    lax.fori_loop(0, 2 * slabs, attend_back, 0)
    group_blocks(lambda lead: None, "dkv", dkv, dkv_box)
    for dist in (3, 2, 1, 0):
        core_add("out", out_view, out_core, out_chip, dist)
    group_on("dkv", dkv, dkv_box)
    ff_add(3)
    for dist in (3, 2):
        chip_add("out", out_view, out_chip, out_side, dist)
    sums = group_end("dkv", dkv, dkv_box)
    proj[...] = jnp.zeros(proj.shape, f32)
    for slab in range(q_slabs):
        proj[:, slab * 128 : slab * 128 + 128] = turn(unstack_heads(att, slab), -1.0)
    for slab in range(2 * slabs):
        values = jnp.concatenate([sums[0, slab], sums[1, slab]], axis=0)
        if slab < slabs:
            values = turn(values, -1.0)
        at = (q_slabs + slab) * 128
        proj[:, at : at + 128] = values
    qkv_lane = lax.broadcasted_iota(jnp.int32, (own_rows, qkv_wide), 1)
    for j in range(4):
        at = qkv_cols * j
        part = proj[:, at // 128 * 128 : at // 128 * 128 + qkv_wide + 128]
        if at % 128:
            part = pltpu.roll(part, qkv_wide + 128 - at % 128, 1)
        gm[j] = jnp.where(qkv_lane < qkv_cols, part[:, :qkv_wide], 0.0).astype(low)

    def grad_qkv(m, carry):
        at = pl.ds(pl.multiple_of(m * 128, 128), 128)
        for j in range(4):
            w_ff[at, pl.ds(j * qkv_wide, qkv_wide)] = tn(n1[:, at], gm[j]).astype(low)
        return carry

    lax.fori_loop(0, width // 128, grad_qkv, 0)
    core_send("qkv", qkv_view, qkv_core)
    ff_add(2)
    for dist in (1, 0):
        chip_add("out", out_view, out_chip, out_side, dist)
    for dist in (3, 2, 1, 0):
        core_add("qkv", qkv_view, qkv_core, qkv_chip, dist)

    def tokens_back(n, carry):
        at = pl.ds(pl.multiple_of(n * wide_tile, 128), wide_tile)
        total = nt(gm[0], w_qkv[0, at, :])
        for j in range(1, 4):
            total = total + nt(gm[j], w_qkv[j, at, :])
        proj[:, at] = total
        return carry

    lax.fori_loop(0, width // wide_tile, tokens_back, 0)
    source = tokens[...].astype(f32)
    back_one, gain_one_grad = norm_back(source, norm(source), gain_a(), proj[:, :width])
    gain_out[0:1, :] = gain_one_grad
    grad_tokens[...] = (grad_hidden[...] + back_one).astype(low)
    result = hidden[...] + group_end("op", op, op_box)
    output[...] = jnp.where(valid, result, 0.0).astype(low)

    def swap(slot, device, cond=None):
        wires.send(gain_out, gain_box.at[slot], ("gain_sum", slot), device, cond)

    def add_gain(slot, device):
        wires.take(gain_box.at[slot], ("gain_sum", slot), device)
        gain_out[...] = gain_out[...] + gain_box[slot]

    def settle():
        copy, cond = wires.pending.pop()
        when(cond, copy.wait_send)

    def gain_hop(slot):
        device = (place.core, place.chip, place.across)[slot]
        swap(slot, device)
        settle()
        add_gain(slot, device)

    low_end, high_end = z == 0, z == 3
    mid_low, mid_high = z == 1, z == 2

    def gain_hop_3():
        swap(3, place.up, low_end)
        settle()
        swap(3, place.down, high_end)
        settle()
        pl.when(mid_low)(lambda: add_gain(3, place.down))
        pl.when(mid_high)(lambda: add_gain(3, place.up))

    def gain_hop_4():
        swap(4, place.up, mid_low)
        settle()
        swap(4, place.down, mid_high)
        settle()
        pl.when(mid_low)(lambda: add_gain(4, place.up))
        pl.when(mid_high)(lambda: add_gain(4, place.down))
        swap(5, place.down, mid_low)
        swap(5, place.up, mid_high)

    def last(device):
        wires.take(gain_box.at[5], ("gain_sum", 5), device)
        gain_out[...] = gain_box[5]

    ff_add(1)
    gain_hop(0)
    chip_add("qkv", qkv_view, qkv_chip, qkv_side, 3)
    side_add("out", out_view, out_side, out_inbox, 3)
    gain_hop(1)
    ff_add(0)
    ff_finish()
    chip_add("qkv", qkv_view, qkv_chip, qkv_side, 2)
    side_add("out", out_view, out_side, out_inbox, 2)
    gain_hop(2)
    side_add("qkv", qkv_view, qkv_side, qkv_inbox, 3)
    chip_add("qkv", qkv_view, qkv_chip, qkv_side, 1)
    side_add("out", out_view, out_side, out_inbox, 1)
    gain_hop_3()
    side_add("qkv", qkv_view, qkv_side, qkv_inbox, 2)
    chip_add("qkv", qkv_view, qkv_chip, qkv_side, 0)
    side_add("out", out_view, out_side, out_inbox, 0)
    out_out[...] = own_view(out_view, dp)[...].astype(f32)[:, :out_cols]
    gain_hop_4()
    for part in range(2):
        origin = 2 * c + part
        pl.when(origin != ctx)(lambda: wires.take(gu_mix.at[part], ("dgu_mix", part), (dp, origin)))
        add_rows(gu_mix.at[part], [], out=gu_out.at[:, pl.ds(part * units, units)])
    pl.when(ctx != z)(lambda: wires.take(down_mix, ("ddown_mix",), (dp, z)))
    add_rows(down_mix, [], out=dt_out)
    pl.when(low_end)(lambda: last(place.up))
    pl.when(high_end)(lambda: last(place.down))
    side_add("qkv", qkv_view, qkv_side, qkv_inbox, 1)
    side_add("qkv", qkv_view, qkv_side, qkv_inbox, 0)
    qkv_out[...] = own_view(qkv_view, dp)[...].astype(f32)[:, :qkv_cols]
    wires.drain()


def on_device_fast(tokens, lengths, gain_one, w_qkv, w_out, gain_two, w_gate_up, w_down, cotangent):
    seq_count, row_count, width = tokens.shape
    own_rows = seq_count * row_count
    f32, low = jnp.float32, jnp.bfloat16
    block = gain_one.shape[0]
    gains = jnp.stack([gain_one, gain_two]).astype(f32)
    gains = jnp.pad(gains, ((0, 6), (0, 256 - block)))
    position = lax.axis_index("ctx") * row_count + jnp.arange(row_count, dtype=jnp.int32)
    cosine, sine = angles(position, HD)
    cosine = jnp.tile(cosine, (seq_count, 4))
    sine = jnp.tile(jnp.concatenate([-sine, sine], axis=1), (seq_count, 2))
    rows, qkv_cols = w_qkv.shape
    out_cols = w_out.shape[1]
    units = w_gate_up.shape[1] // 2
    half, strip = w_down.shape
    qkv_wide = -(-qkv_cols // 128) * 128
    out_wide = -(-out_cols // 128) * 128
    deep = 8 * rows
    slots = 4 * row_count
    slabs = KVH // 2
    stack = 2 * QH // KVH * row_count

    def box(*shape, dtype=low):
        return pltpu.VMEM(shape, dtype)

    scratch = [
        box(4, deep, qkv_wide), box(4, deep, out_wide), box(deep, 3 * units),
        box(8, 8, 256, dtype=f32), box(8, deep + 128, dtype=f32),
        box(own_rows, width), box(4 * own_rows, width), box(4 * own_rows, width),
        box(own_rows, QH * HD), box(own_rows, width, dtype=f32), box(own_rows, width, dtype=f32),
        box(own_rows, 4 * qkv_wide, dtype=f32),
        box(seq_count * slabs, stack, 128), box(seq_count, 2 * slabs, slots, 128),
        box(seq_count * slabs, stack, slots), box(seq_count * slabs, stack, 128, dtype=f32),
        box(seq_count * slabs, stack, 128), box(4, own_rows, out_wide), box(4, own_rows, qkv_wide),
        box(4 * own_rows, units), box(4 * own_rows, units), box(4 * own_rows, units),
        box(4, own_rows, width), box(3, own_rows, width),
        box(4, own_rows, width), box(3, own_rows, width),
        box(4, seq_count, 2 * slabs, row_count, 128), box(3, seq_count, 2 * slabs, row_count, 128),
        box(2, deep, units), box(deep, units),
        box(2, deep, qkv_wide), box(2, deep, out_wide),
        box(deep, qkv_wide), box(deep, out_wide),
        box(2, 4, rows, qkv_wide), box(2, 4, rows, out_wide),
        box(2, 2, 4, rows, units), box(4, strip, half),
        box(2, 3, rows, qkv_wide), box(2, 3, rows, out_wide),
        box(2, 2, 3, rows, units), box(2, 4, strip, half),
        box(2, rows, units), box(strip, half),
        box(6, 8, width, dtype=f32),
        pltpu.SemaphoreType.DMA((480,)),
        pltpu.SemaphoreType.DMA((480,)),
        pltpu.SemaphoreType.DMA((8,)),
    ]
    vmem = pl.BlockSpec(memory_space=pltpu.MemorySpace.VMEM)
    smem = pl.BlockSpec(memory_space=pltpu.MemorySpace.SMEM)
    shapes = (
        jax.ShapeDtypeStruct((own_rows, width), low),
        jax.ShapeDtypeStruct((own_rows, width), low),
        jax.ShapeDtypeStruct((8, width), f32),
        jax.ShapeDtypeStruct((rows, qkv_cols), f32),
        jax.ShapeDtypeStruct((rows, out_cols), f32),
        jax.ShapeDtypeStruct((rows, 2 * units), f32),
        jax.ShapeDtypeStruct((strip, half), f32),
    )
    output, grad_tokens, gain_sums, final_qkv, final_out, final_gu, final_dt = pl.pallas_call(
        functools.partial(layer_kernel, {}),
        out_shape=shapes,
        in_specs=[vmem, vmem, smem] + [vmem] * 7,
        out_specs=[vmem] * 7,
        scratch_shapes=scratch,
        compiler_params=pltpu.CompilerParams(
            collective_id=0, has_side_effects=True, vmem_limit_bytes=64 * 2**20
        ),
        name="layer",
    )(
        tokens.reshape(own_rows, width), cotangent.reshape(own_rows, width), lengths,
        w_qkv, w_out, w_gate_up, w_down.T, gains, cosine, sine,
    )
    mine = lax.dynamic_slice(gain_sums, (0, lax.axis_index("dp") * block), (8, block))
    return (
        output.reshape(tokens.shape), grad_tokens.reshape(tokens.shape),
        mine[0], final_qkv, final_out, mine[1], final_gu, final_dt.T,
    )


def solution(mesh):
    fits = mesh.shape["dp"] == 8 and mesh.shape["ctx"] == 4
    return jax.shard_map(
        on_device_fast if fits else on_device,
        mesh=mesh,
        in_specs=(
            P("dp", "ctx", None),
            P("dp"),
            P("dp"),
            P("dp", "ctx"),
            P("dp", "ctx"),
            P("dp"),
            P("dp", "ctx"),
            P("dp", "ctx"),
            P("dp", "ctx", None),
        ),
        out_specs=(
            P("dp", "ctx", None),
            P("dp", "ctx", None),
            P("dp"),
            P("dp", "ctx"),
            P("dp", "ctx"),
            P("dp"),
            P("dp", "ctx"),
            P("dp", "ctx"),
        ),
        check_vma=False,
    )
```

```python
import functools
import math

import jax
import jax.numpy as jnp
from jax import lax
from jax.experimental import pallas as pl
from jax.experimental.pallas import tpu as pltpu
from jax.sharding import PartitionSpec as P

QH = 18
KVH = 6
HD = 64
FF = 3072


EPS = 1e-05
NEGATIVE = -1e30


def angles(position, head_width):
    frequency = 10000.0 ** (-jnp.arange(head_width // 2, dtype=jnp.float32) * 2.0 / head_width)
    angle_table = position.astype(jnp.float32)[:, None] * frequency[None, :]
    return (jnp.cos(angle_table), jnp.sin(angle_table))


def rotate(values_in, cosine, sine_table):
    half_width = values_in.shape[-1] // 2
    first_half = values_in[..., :half_width]
    second = values_in[..., half_width:]
    return jnp.concatenate(
        [first_half * cosine - second * sine_table, second * cosine + first_half * sine_table],
        axis=-1,
    )


def split_heads(values_in, head_count):
    seq_count, row_count, col_count = values_in.shape
    head_width = col_count // head_count
    moved = values_in.reshape(seq_count, row_count, head_count, head_width).transpose(0, 2, 1, 3)
    return moved.reshape(seq_count * head_count, row_count, head_width)


def join_heads(values_in, seq_count):
    item_count, row_count, head_width = values_in.shape
    head_count = item_count // seq_count
    moved = values_in.reshape(seq_count, head_count, row_count, head_width).transpose(0, 2, 1, 3)
    return moved.reshape(seq_count, row_count, head_count * head_width)


def norm_back(source, inverse, gain, grad_in):
    scaled = grad_in * gain
    mean_term = jnp.mean(scaled * source, axis=-1, keepdims=True)
    back_rows = inverse * scaled - source * (inverse * inverse * inverse) * mean_term
    return (back_rows, jnp.sum(grad_in * source * inverse, axis=(0, 1)))


def block_scores(query_rows, key_rows, position, length, group_count, score_scale):
    raw_scores = (
        jnp.einsum("nd,td->nt", query_rows, key_rows, preferred_element_type=jnp.float32)
        * score_scale
    )
    raw_scores = raw_scores.reshape(group_count, position.shape[0], key_rows.shape[0])
    keyidx = jnp.arange(key_rows.shape[0], dtype=jnp.int32)
    allowed = (keyidx[None, :] <= position[:, None]) & (keyidx[None, :] < length)
    return jnp.where(allowed[None], raw_scores, NEGATIVE)


def on_device(tokens, lengths, gain_one, w_qkv, w_out, gain_two, w_gate_up, w_down, cotangent):
    forward_wide = (
        lax.all_gather(w_qkv, "ctx", axis=1, tiled=True),
        lax.all_gather(w_out, "ctx", axis=1, tiled=True),
        lax.all_gather(w_gate_up, "ctx", axis=1, tiled=True),
        lax.all_gather(w_down, "ctx", axis=1, tiled=True),
    )
    qkv_full, out_full, gate_up_full, down_full, gain_fa, gain_fb = (
        lax.all_gather(forward_wide[0], "dp", axis=0, tiled=True),
        lax.all_gather(forward_wide[1], "dp", axis=0, tiled=True),
        lax.all_gather(forward_wide[2], "dp", axis=0, tiled=True),
        lax.all_gather(forward_wide[3], "dp", axis=0, tiled=True),
        lax.all_gather(gain_one, "dp", axis=0, tiled=True),
        lax.all_gather(gain_two, "dp", axis=0, tiled=True),
    )
    seq_count, row_count, model_width = tokens.shape
    query_cols = QH * HD
    key_cols = KVH * HD
    group_count = QH // KVH
    score_scale = 1.0 / math.sqrt(HD)
    position = lax.axis_index("ctx") * row_count + jnp.arange(row_count, dtype=jnp.int32)
    valid_rows = position[None, :] < lengths[:, None]
    cosine, sine_table = angles(position, HD)
    cosine = cosine[:, None, :]
    sine_table = sine_table[:, None, :]
    source = tokens.astype(jnp.float32)
    inverse_one = lax.rsqrt(jnp.mean(source * source, axis=-1, keepdims=True) + EPS)
    normed_one = (source * inverse_one * gain_fa.astype(jnp.float32)).astype(jnp.bfloat16)
    projected = jnp.einsum("bsd,de->bse", normed_one, qkv_full, preferred_element_type=jnp.float32)
    queries = rotate(
        projected[..., :query_cols].reshape(seq_count, row_count, QH, HD), cosine, sine_table
    )
    queries = queries.astype(jnp.bfloat16).reshape(seq_count, row_count, query_cols)
    key_heads = rotate(
        projected[..., query_cols : query_cols + key_cols].reshape(seq_count, row_count, KVH, HD),
        cosine,
        sine_table,
    )
    key_heads = key_heads.astype(jnp.bfloat16).reshape(seq_count, row_count, key_cols)
    value_heads = projected[..., query_cols + key_cols :].astype(jnp.bfloat16)
    keys_all, values_all = (
        lax.all_gather(key_heads, "ctx", axis=1, tiled=True),
        lax.all_gather(value_heads, "ctx", axis=1, tiled=True),
    )
    query_blocks = split_heads(queries, QH).reshape(seq_count * KVH, group_count * row_count, HD)
    key_blocks = split_heads(keys_all, KVH)
    value_blocks = split_heads(values_all, KVH)
    pair_lengths = jnp.repeat(lengths, KVH)

    def forward_block(block_in):
        query_rows, key_rows, value_rows, length = block_in
        scores = block_scores(query_rows, key_rows, position, length, group_count, score_scale)
        row_max = jnp.max(scores, axis=-1, keepdims=True)
        exp_terms = jnp.exp(scores - row_max)
        row_total = jnp.sum(exp_terms, axis=-1, keepdims=True)
        prob_rows = (exp_terms / row_total).astype(jnp.bfloat16)
        result = jnp.einsum(
            "gst,td->gsd", prob_rows, value_rows, preferred_element_type=jnp.float32
        )
        return (result.reshape(-1, HD), (row_max + jnp.log(row_total))[..., 0])

    context_blocks, log_totals = lax.map(
        forward_block, (query_blocks, key_blocks, value_blocks, pair_lengths)
    )
    context = join_heads(context_blocks.reshape(seq_count * QH, row_count, HD), seq_count).astype(
        jnp.bfloat16
    )
    hidden = source + jnp.einsum(
        "bse,ed->bsd", context, out_full, preferred_element_type=jnp.float32
    )
    inverse_two = lax.rsqrt(jnp.mean(hidden * hidden, axis=-1, keepdims=True) + EPS)
    normed_two = (hidden * inverse_two * gain_fb.astype(jnp.float32)).astype(jnp.bfloat16)
    gate_up = jnp.einsum(
        "bsd,df->bsf", normed_two, gate_up_full, preferred_element_type=jnp.float32
    )
    gate_part = gate_up[..., :FF]
    up_part = gate_up[..., FF:]
    gate_sig = jax.nn.sigmoid(gate_part)
    swish_part = gate_part * gate_sig
    activation = (swish_part * up_part).astype(jnp.bfloat16)
    result_rows = hidden + jnp.einsum(
        "bsf,fd->bsd", activation, down_full, preferred_element_type=jnp.float32
    )
    output = jnp.where(valid_rows[..., None], result_rows, 0.0).astype(jnp.bfloat16)
    back_wide = (
        lax.all_gather(w_qkv, "ctx", axis=1, tiled=True),
        lax.all_gather(w_out, "ctx", axis=1, tiled=True),
        lax.all_gather(w_gate_up, "ctx", axis=1, tiled=True),
        lax.all_gather(w_down, "ctx", axis=1, tiled=True),
    )
    qkv_back, out_back, gate_up_back, down_back, gain_ba, gain_bb = (
        lax.all_gather(back_wide[0], "dp", axis=0, tiled=True),
        lax.all_gather(back_wide[1], "dp", axis=0, tiled=True),
        lax.all_gather(back_wide[2], "dp", axis=0, tiled=True),
        lax.all_gather(back_wide[3], "dp", axis=0, tiled=True),
        lax.all_gather(gain_one, "dp", axis=0, tiled=True),
        lax.all_gather(gain_two, "dp", axis=0, tiled=True),
    )
    grad_rows = jnp.where(valid_rows[..., None], cotangent, jnp.zeros_like(cotangent))
    grad_activation = jnp.einsum(
        "bsd,fd->bsf", grad_rows, down_back, preferred_element_type=jnp.float32
    )
    grad_gate = grad_activation * up_part * gate_sig * (1.0 + gate_part * (1.0 - gate_sig))
    grad_up = grad_activation * swish_part
    grad_mix = jnp.concatenate([grad_gate, grad_up], axis=-1).astype(jnp.bfloat16)
    grad_normed_two = jnp.einsum(
        "bsf,df->bsd", grad_mix, gate_up_back, preferred_element_type=jnp.float32
    )
    back_two, grad_gain_two = norm_back(
        hidden, inverse_two, gain_bb.astype(jnp.float32), grad_normed_two
    )
    grad_hidden = grad_rows.astype(jnp.float32) + back_two
    grad_branch = grad_hidden.astype(jnp.bfloat16)
    grad_context = jnp.einsum(
        "bsd,ed->bse", grad_branch, out_back, preferred_element_type=jnp.float32
    ).astype(jnp.bfloat16)
    grad_blocks = split_heads(grad_context, QH).reshape(
        seq_count * KVH, group_count * row_count, HD
    )

    def backward_block(block_in):
        query_rows, key_rows, value_rows, length, log_total, grad_in = block_in
        scores = block_scores(query_rows, key_rows, position, length, group_count, score_scale)
        prob_rows = jnp.exp(scores - log_total[..., None])
        grad_grouped = grad_in.reshape(group_count, -1, HD)
        grad_probs = jnp.einsum(
            "gsd,td->gst", grad_grouped, value_rows, preferred_element_type=jnp.float32
        )
        grad_value = jnp.einsum(
            "gst,gsd->td",
            prob_rows.astype(jnp.bfloat16),
            grad_grouped,
            preferred_element_type=jnp.float32,
        )
        row_delta = jnp.sum(prob_rows * grad_probs, axis=-1, keepdims=True)
        grad_scores = (prob_rows * (grad_probs - row_delta)).astype(jnp.bfloat16)
        grad_query = (
            jnp.einsum("gst,td->gsd", grad_scores, key_rows, preferred_element_type=jnp.float32)
            * score_scale
        )
        grad_key = (
            jnp.einsum(
                "gst,gsd->td",
                grad_scores,
                query_rows.reshape(group_count, -1, HD),
                preferred_element_type=jnp.float32,
            )
            * score_scale
        )
        return (grad_query.reshape(-1, HD), grad_key, grad_value)

    query_grads, key_grads, value_grads = lax.map(
        backward_block,
        (query_blocks, key_blocks, value_blocks, pair_lengths, log_totals, grad_blocks),
    )
    key_sums, value_sums = (
        lax.psum_scatter(
            join_heads(key_grads, seq_count).astype(jnp.bfloat16),
            "ctx",
            scatter_dimension=1,
            tiled=True,
        ).astype(jnp.float32),
        lax.psum_scatter(
            join_heads(value_grads, seq_count).astype(jnp.bfloat16),
            "ctx",
            scatter_dimension=1,
            tiled=True,
        ).astype(jnp.float32),
    )
    grad_queries = join_heads(query_grads.reshape(seq_count * QH, row_count, HD), seq_count)
    turned_queries = rotate(grad_queries.reshape(seq_count, row_count, QH, HD), cosine, -sine_table)
    turned_keys = rotate(key_sums.reshape(seq_count, row_count, KVH, HD), cosine, -sine_table)
    grad_mixed = jnp.concatenate(
        [
            turned_queries.reshape(seq_count, row_count, query_cols),
            turned_keys.reshape(seq_count, row_count, key_cols),
            value_sums,
        ],
        axis=-1,
    ).astype(jnp.bfloat16)
    grad_normed_one = jnp.einsum(
        "bse,de->bsd", grad_mixed, qkv_back, preferred_element_type=jnp.float32
    )
    back_one, grad_gain_one = norm_back(
        source, inverse_one, gain_ba.astype(jnp.float32), grad_normed_one
    )
    grad_tokens = (grad_hidden + back_one).astype(jnp.bfloat16)
    exchanged = (
        lax.all_to_all(grad_mixed, "ctx", split_axis=2, concat_axis=1, tiled=True),
        lax.all_to_all(grad_branch, "ctx", split_axis=2, concat_axis=1, tiled=True),
        lax.all_to_all(grad_mix, "ctx", split_axis=2, concat_axis=1, tiled=True),
        lax.all_to_all(grad_rows, "ctx", split_axis=2, concat_axis=1, tiled=True),
    )
    initial = (
        jnp.zeros((model_width, exchanged[0].shape[2]), jnp.float32),
        jnp.zeros((context.shape[2], exchanged[1].shape[2]), jnp.float32),
        jnp.zeros((model_width, exchanged[2].shape[2]), jnp.float32),
        jnp.zeros((activation.shape[2], exchanged[3].shape[2]), jnp.float32),
    )
    pieces = (
        lax.all_gather(normed_one, "ctx", axis=1, tiled=True),
        lax.all_gather(context, "ctx", axis=1, tiled=True),
        lax.all_gather(normed_two, "ctx", axis=1, tiled=True),
        lax.all_gather(activation, "ctx", axis=1, tiled=True),
    )
    updated = []
    for total, piece, right in zip(initial, pieces, exchanged):
        updated.append(jnp.einsum("bsr,bsc->rc", piece, right, preferred_element_type=jnp.float32))
    column_grads = tuple(updated)
    gain_whole = lax.psum((grad_gain_one, grad_gain_two), "ctx")
    final_qkv, final_out, final_gate_up, final_down, final_gain_one, final_gain_two = (
        lax.psum_scatter(
            column_grads[0].astype(jnp.bfloat16), "dp", scatter_dimension=0, tiled=True
        ).astype(jnp.float32),
        lax.psum_scatter(
            column_grads[1].astype(jnp.bfloat16), "dp", scatter_dimension=0, tiled=True
        ).astype(jnp.float32),
        lax.psum_scatter(
            column_grads[2].astype(jnp.bfloat16), "dp", scatter_dimension=0, tiled=True
        ).astype(jnp.float32),
        lax.psum_scatter(
            column_grads[3].astype(jnp.bfloat16), "dp", scatter_dimension=0, tiled=True
        ).astype(jnp.float32),
        lax.psum_scatter(
            gain_whole[0].astype(jnp.bfloat16), "dp", scatter_dimension=0, tiled=True
        ).astype(jnp.float32),
        lax.psum_scatter(
            gain_whole[1].astype(jnp.bfloat16), "dp", scatter_dimension=0, tiled=True
        ).astype(jnp.float32),
    )
    return (
        output,
        grad_tokens,
        final_gain_one,
        final_qkv,
        final_out,
        final_gain_two,
        final_gate_up,
        final_down,
    )


MESH = pl.DeviceIdType.MESH


class Place:
    def __init__(self):
        self.dp = lax.axis_index("dp")
        self.ctx = lax.axis_index("ctx")
        self.z = lax.div(self.dp, 2)
        self.y = lax.rem(self.dp, 2)
        self.x = lax.div(self.ctx, 2)
        self.c = lax.rem(self.ctx, 2)
        self.up = (self.dp + 2, self.ctx)
        self.down = (self.dp - 2, self.ctx)
        self.across = (self.dp + 1 - 2 * self.y, self.ctx)
        self.chip = (self.dp, (1 - self.x) * 2 + self.c)
        self.core = (self.dp, self.x * 2 + 1 - self.c)
        self.has_up = self.z < 3
        self.has_down = self.z > 0


def greet(place):
    barrier = pltpu.get_barrier_semaphore()

    def tell(device):
        pl.semaphore_signal(barrier, inc=1, device_id=device, device_id_type=MESH)

    pl.when(place.has_up)(lambda: tell(place.up))
    pl.when(place.has_down)(lambda: tell(place.down))
    tell(place.across)
    for step in (1, 2, 3):
        tell((place.dp, lax.rem(place.ctx + step, 4)))
    ends = place.has_up.astype(jnp.int32) + place.has_down.astype(jnp.int32)
    pl.semaphore_wait(barrier, 4 + ends)


class Wires:
    def __init__(self, send_sems, recv_sems, names):
        self.send_sems = send_sems
        self.recv_sems = recv_sems
        self.index = names
        self.count = 0
        self.pending = []

    def slot(self, name):
        if name not in self.index:
            self.index[name] = len(self.index)
        return self.index[name]

    def send(self, src, dst, name, device, cond=None, extra=None):
        number = self.count
        self.count += 1
        at = self.slot(name)
        if extra is not None:
            at = at + extra
        copy = pltpu.make_async_remote_copy(
            src_ref=src,
            dst_ref=dst,
            send_sem=self.send_sems.at[number],
            recv_sem=self.recv_sems.at[at],
            device_id=device,
            device_id_type=MESH,
        )
        if cond is None:
            copy.start()
        else:
            pl.when(cond)(copy.start)
        self.pending.append((copy, cond, name))

    def take(self, dst, name, device, extra=None):
        at = self.slot(name)
        if extra is not None:
            at = at + extra
        pltpu.make_async_remote_copy(
            src_ref=dst,
            dst_ref=dst,
            send_sem=self.send_sems.at[0],
            recv_sem=self.recv_sems.at[at],
            device_id=device,
            device_id_type=MESH,
        ).wait_recv()

    def drain(self):
        for copy, cond, name in self.pending:
            when(cond, copy.wait_send)
        self.pending = []

    def drain_named(self, first):
        for copy, cond, name in self.pending:
            if name[0] == first:
                when(cond, copy.wait_send)
        self.pending = [entry for entry in self.pending if entry[2][0] != first]


BELOW, ABOVE = 0, 1


def both(first, second):
    return second if first is None else jnp.logical_and(first, second)


def source_valid(place, way, dist):
    return place.z >= dist if way == BELOW else place.z + dist <= 3


def source_pos(place, way, dist):
    return place.dp - 2 * dist if way == BELOW else place.dp + 2 * dist


def flood_start(wires, place, name, own, block, spread):
    wires.send(own, block(place.dp), (name, BELOW, 1), place.up, place.has_up)
    wires.send(own, block(place.dp), (name, ABOVE, 1), place.down, place.has_down)
    wires.send(own, block(place.dp), (name, "y", 0, 0), place.across)
    spread(own, place.dp, (0, 0, 0), None)


def flood_step(wires, place, name, block, spread, way, dist):
    here = source_valid(place, way, dist)
    pos = source_pos(place, way, dist)
    view = block(pos)
    came_from = place.down if way == BELOW else place.up
    pl.when(here)(lambda: wires.take(view, (name, way, dist), came_from))
    if dist < 3:
        onward = place.up if way == BELOW else place.down
        more = place.has_up if way == BELOW else place.has_down
        wires.send(view, view, (name, way, dist + 1), onward, jnp.logical_and(here, more))
    wires.send(view, view, (name, "y", way, dist), place.across, here)
    spread(view, pos, (0, way, dist), here)


def flood_side(wires, place, name, block, spread, way, dist):
    if dist == 0:
        here, pos = None, place.dp
    else:
        here, pos = source_valid(place, way, dist), source_pos(place, way, dist)
    pos = pos + 1 - 2 * place.y
    view = block(pos)
    if here is None:
        wires.take(view, (name, "y", 0, 0), place.across)
    else:
        pl.when(here)(lambda: wires.take(view, (name, "y", way, dist), place.across))
    spread(view, pos, (1, way, dist), here)


HOPS = [(way, dist) for dist in (1, 2, 3) for way in (BELOW, ABOVE)]


def no_spread(view, pos, key, cond):
    return None


def add_rows(dst, srcs, out=None, cast=None, chunk=48):
    out = dst if out is None else out
    total_rows = dst.shape[0]
    assert total_rows % chunk == 0

    def body(i, carry):
        at = pl.ds(pl.multiple_of(i * chunk, 16), chunk)
        total = dst[at, :].astype(jnp.float32)
        for src in srcs:
            total = total + src[at, :].astype(jnp.float32)
        out[at, :] = total.astype(out.dtype)
        return carry

    lax.fori_loop(0, total_rows // chunk, body, 0)


def when(cond, action):
    if cond is None:
        action()
    else:
        pl.when(cond)(action)


DRAIN = [(way, dist) for dist in (3, 2, 1, 0) for way in (BELOW, ABOVE)]


def nn(a, b):
    return jnp.dot(a, b, preferred_element_type=jnp.float32)


def nt(a, b):
    return lax.dot_general(a, b, (((1,), (1,)), ((), ())), preferred_element_type=jnp.float32)


def tn(a, b):
    return lax.dot_general(a, b, (((0,), (0,)), ((), ())), preferred_element_type=jnp.float32)


def layer_kernel(
    names,
    tokens, cot, lengths, qkv_in, out_in, gu_in, dt_in, gain_in, cos, sin,
    output, grad_tokens, gain_out, qkv_out, out_out, gu_out, dt_out,
    w_qkv, w_out, w_ff, d_qkv, d_out, d_ff, gain_all, gain_row,
    tok_all, n1_all, n2_all, g_all, ctx_all, hidden, grad_hidden, proj, q_st, kv_all, p_st, att, go_st,
    wide, gm, pq, pq_in, gb_all, gm_all, act, d_gu, gp, gp_box, op, op_box, dkv, dkv_box,
    qkv_side, out_side, gu_side_a, gu_side_b, down_side, qkv_inbox, out_inbox, gu_inbox_a, gu_inbox_b, down_inbox,
    up_inbox, up_side, gu_mix, down_mix, gain_box, gain_acc,
    send_sems, recv_sems, local_sems,
):
    f32, low = jnp.float32, jnp.bfloat16
    place = Place()
    wires = Wires(send_sems, recv_sems, names)
    dp, ctx, z, y, x, c = place.dp, place.ctx, place.z, place.y, place.x, place.c
    rows = qkv_in.shape[0]
    strip, half = dt_in.shape
    width = tokens.shape[1]
    own_rows = tokens.shape[0]
    slots_here = own_rows // 2
    qkv_cols, out_cols = qkv_in.shape[1], out_in.shape[1]
    qkv_wide, out_wide = w_qkv.shape[1], w_out.shape[2]
    group = QH // KVH
    slabs = KVH // 2
    q_slabs = QH // 2
    span = 3 * half
    deep = w_ff.shape[0]
    score_scale = 1.0 / math.sqrt(HD)
    TILES = range(2)

    greet(place)

    def block_rows(pos):
        return pl.ds(pl.multiple_of(pos * rows, 16), rows)

    def lead_rows(lead):
        return pl.ds(pl.multiple_of(lead * own_rows, 16), own_rows)

    here_rows = lead_rows(ctx)
    my_rows = block_rows(dp)

    def share(name, ref):
        mine = ref.at[here_rows]
        wires.send(mine, mine, (name, "x"), place.chip)
        wires.send(mine, mine, (name, "c"), place.core)

    def share_on(name, ref):
        far = ref.at[lead_rows(place.chip[1])]
        wires.take(far, (name, "x"), place.chip)
        wires.send(far, far, (name, "d"), place.core)

    def share_end(name, ref):
        for mark, lead in (("c", place.core[1]), ("d", 3 - ctx)):
            wires.take(ref.at[lead_rows(lead)], (name, mark), place.core)

    def swap_start(name, src, dst):
        for step in (1, 2, 3):
            peer = lax.rem(ctx + step, 4)
            wires.send(src(peer), dst(ctx), (name, step), (dp, peer))

    def swap_end(name, dst):
        for step in (1, 2, 3):
            peer = lax.rem(ctx + 4 - step, 4)
            wires.take(dst(peer), (name, step), (dp, peer))

    locals_ = []

    def local(src, dst, cond=None):
        copy = pltpu.make_async_copy(src, dst, local_sems.at[len(locals_)])
        locals_.append((copy, cond))
        when(cond, copy.start)

    SIDES = [(0, 0)] + HOPS
    WAYS = {0: [(0, 0)], 1: HOPS[:2], 2: HOPS[2:4], 3: HOPS[4:]}

    class Flood:
        def __init__(self, name, block, spread=no_spread):
            self.name, self.block, self.spread = name, block, spread

        def start(self):
            flood_start(wires, place, self.name, self.block(dp), self.block, self.spread)

        def hop(self, dist):
            for way, dist in WAYS[dist]:
                flood_step(wires, place, self.name, self.block, self.spread, way, dist)

        def side(self, dist):
            for way, dist in WAYS[dist]:
                flood_side(wires, place, self.name, self.block, self.spread, way, dist)

    class PairFlood:
        def __init__(self, name, ref, cols):
            self.name, self.ref, self.cols = name, ref, cols

        def pair(self, plane):
            return self.ref.at[pl.ds(pl.multiple_of(2 * rows * plane, 16), 2 * rows), self.cols]

        def one(self, pos):
            return self.ref.at[block_rows(pos), self.cols]

        def start(self):
            wires.send(self.one(dp), self.one(dp), (self.name, "y"), place.across)

        def side(self):
            wires.take(self.one(place.across[0]), (self.name, "y"), place.across)
            view = self.pair(z)
            wires.send(view, view, (self.name, BELOW, 1), place.up, place.has_up)
            wires.send(view, view, (self.name, ABOVE, 1), place.down, place.has_down)

        def hop(self, dist):
            for way, dist in WAYS[dist]:
                here = source_valid(place, way, dist)
                view = self.pair(z - dist if way == BELOW else z + dist)
                came_from = place.down if way == BELOW else place.up
                pl.when(here)(lambda: wires.take(view, (self.name, way, dist), came_from))
                if dist < 3:
                    onward = place.up if way == BELOW else place.down
                    more = place.has_up if way == BELOW else place.has_down
                    wires.send(view, view, (self.name, way, dist + 1), onward, jnp.logical_and(here, more))

    def out_block(lead, pos):
        return w_out.at[lead, block_rows(pos)]

    def out_spread(view, pos, key, cond):
        wires.send(view, out_block(ctx, pos), ("out", "x") + key, place.chip, cond)
        wires.send(view, out_block(ctx, pos), ("out", "c") + key, place.core, cond)

    qkv_flood = Flood("qkv", lambda pos: w_qkv.at[block_rows(pos)])
    gain_flood = Flood("gain", lambda pos: gain_all.at[pos])
    out_flood = Flood("out", functools.partial(out_block, ctx), out_spread)

    GU_WIDTH = (2 * half, half)
    up_cols = pl.ds(span + half, half)

    def gu_view(ref, tile, pos):
        return ref.at[block_rows(pos), pl.ds(tile * span, GU_WIDTH[tile])]

    gu_floods = [Flood(("gu", tile), functools.partial(gu_view, w_ff, tile)) for tile in TILES]
    up_flood = PairFlood("up", w_ff, up_cols)

    def spots(column, dist):
        for way, dist in WAYS[dist]:
            if dist == 0:
                here, pos = None, dp
            else:
                here, pos = source_valid(place, way, dist), source_pos(place, way, dist)
            if column == 1:
                pos = pos + 1 - 2 * y
            yield (column, way, dist), here, pos

    def out_chip(column, dist):
        for key, here, pos in spots(column, dist):
            view = out_block(place.chip[1], pos)
            when(here, lambda: wires.take(view, ("out", "x") + key, place.chip))
            wires.send(view, view, ("out", "d") + key, place.core, here)

    def out_core():
        for column in range(2):
            for dist in range(4):
                for key, here, pos in spots(column, dist):
                    for mark, lead in (("c", place.core[1]), ("d", 3 - ctx)):
                        view = out_block(lead, pos)
                        when(here, lambda: wires.take(view, ("out", mark) + key, place.core))

    def mix_start(tile):
        for part in range(2):
            target = 2 * c + part
            src = gu_in.at[:, pl.ds((2 * part + tile) * half, half)]
            dst = w_ff.at[my_rows, pl.ds(pl.multiple_of(tile * span + x * half, 128), half)]
            wires.send(src, dst, ("gu_mix", tile, 0), (dp, target), target != ctx, extra=x)
            local(src, dst, target == ctx)
        wires.slot(("gu_mix", tile, 1))

    def mix_end(tile):
        for part in range(2):
            origin = part * 2 + x
            view = w_ff.at[my_rows, pl.ds(tile * span + part * half, half)]
            pl.when(origin != ctx)(lambda: wires.take(view, ("gu_mix", tile, part), (dp, origin)))

    lanes = pl.ds(pl.multiple_of(y * span + 2 * half, 128), half)
    other_lanes = pl.ds(pl.multiple_of((1 - y) * span + 2 * half, 128), half)
    at_home = ctx == z

    def strips_of(ref, at):
        return [ref.at[pl.ds(j * strip, strip), at] for j in range(4)]

    strips, other_strips = strips_of(w_ff, lanes), strips_of(w_ff, other_lanes)

    def down_mix_start():
        dst = w_ff.at[pl.ds(pl.multiple_of(ctx * strip, 16), strip), lanes]
        wires.send(dt_in, dst, ("down_mix", 0), (dp, z), ctx != z, extra=ctx)
        for j in range(1, 4):
            wires.slot(("down_mix", j))
        local(dt_in, dst, ctx == z)

    def down_start():
        def take_strips():
            for j in range(4):
                pl.when(ctx != j)(functools.partial(wires.take, strips[j], ("down_mix", j), (dp, j)))

        pl.when(at_home)(take_strips)
        for j in range(4):
            wires.send(strips[j], strips[j], ("down", j, BELOW, 1), place.up, jnp.logical_and(at_home, place.has_up))
            wires.send(strips[j], strips[j], ("down", j, ABOVE, 1), place.down, jnp.logical_and(at_home, place.has_down))
            wires.send(strips[j], strips[j], ("down_y", j, 0, 0), place.across, at_home)

    def down_hop(dist):
        for way in (BELOW, ABOVE):
            here = (z - ctx if way == BELOW else ctx - z) == dist
            came_from = place.down if way == BELOW else place.up
            onward = place.up if way == BELOW else place.down
            more = place.has_up if way == BELOW else place.has_down
            for j in range(4):
                pl.when(here)(functools.partial(wires.take, strips[j], ("down", j, way, dist), came_from))
                if dist < 3:
                    wires.send(strips[j], strips[j], ("down", j, way, dist + 1), onward, jnp.logical_and(here, more))
                wires.send(strips[j], strips[j], ("down_y", j, way, dist), place.across, here)

    def down_side_end():
        for way, dist in SIDES:
            here = at_home if dist == 0 else (z - ctx if way == BELOW else ctx - z) == dist

            def take():
                for j in range(4):
                    wires.take(other_strips[j], ("down_y", j, way, dist), place.across)

            pl.when(here)(take)

    row_at = lax.broadcasted_iota(jnp.int32, (own_rows, 1), 0)
    first_seq = row_at < slots_here
    position = ctx * slots_here + jnp.where(first_seq, row_at, row_at - slots_here)
    valid = position < jnp.where(first_seq, lengths[0], lengths[1])
    def tokens_start():
        tok_all[here_rows, :] = tokens[...]
        share("tok", tok_all)

    def qkv_start():
        w_qkv[my_rows, :] = jnp.zeros((rows, qkv_wide), low)
        w_qkv[my_rows, :qkv_cols] = qkv_in[...]
        qkv_flood.start()

    def gain_start():
        gain_all[dp] = gain_in[...]
        gain_flood.start()

    def out_start():
        w_out[ctx, my_rows, :] = jnp.zeros((rows, out_wide), low)
        w_out[ctx, my_rows, :out_cols] = out_in[...]
        out_flood.start()

    def cot_start():
        g_all[here_rows, :] = jnp.where(valid, cot[...].astype(f32), 0.0).astype(low)
        share("cot", g_all)

    def gain_sides():
        for dist in range(4):
            gain_flood.side(dist)

    gain_a = lambda: gain_row[0:1, :width]
    gain_b = lambda: gain_row[1:2, :width]

    def norm(values):
        return lax.rsqrt(jnp.mean(values * values, axis=-1, keepdims=True) + EPS)

    lane = lax.broadcasted_iota(jnp.int32, (own_rows, 128), 1)
    low_half = lax.rem(lane, HD) < HD // 2
    side_of = lax.div(lane, HD)

    def turn(values, sign):
        swapped = jnp.where(low_half, pltpu.roll(values, 128 - HD // 2, 1), pltpu.roll(values, HD // 2, 1))
        return values * cos[...] + swapped * (sin[...] * sign)

    def head_spots():
        for head in range(QH):
            kv = head // group
            yield head // 2, head % 2, kv // 2, kv % 2, (kv % 2 * group + head % group) * slots_here

    def stack_heads(slab_of, dest, scale):
        for slab, side, key_slab, key_side, at in head_spots():
            values = slab_of(slab)
            if side != key_side:
                values = pltpu.roll(values, HD, 1)
            values = (jnp.where(side_of == key_side, values, 0.0) * scale).astype(low)
            for seq in range(2):
                dest[seq * slabs + key_slab, at : at + slots_here, :] = values[
                    seq * slots_here : (seq + 1) * slots_here
                ]

    def unstack_heads(src, slab):
        total = jnp.zeros((own_rows, 128), f32)
        for at_slab, side, key_slab, key_side, at in head_spots():
            if at_slab != slab:
                continue
            values = jnp.concatenate(
                [src[seq * slabs + key_slab, at : at + slots_here, :] for seq in range(2)], axis=0
            )
            values = jnp.where(side_of == key_side, values, 0.0)
            if side != key_side:
                values = pltpu.roll(values, HD, 1)
            total = total + values
        return total

    def project():
        gain_row[...] = jnp.zeros(gain_row.shape, f32)
        for pos in range(8):
            piece = gain_all[pos]
            shift = (pos * rows) % 128
            if shift:
                piece = pltpu.roll(piece, shift, 1)
            at = (pos * rows) // 128 * 128
            gain_row[:, at : at + 256] += piece

        def body(i, carry):
            at = lead_rows(i)
            source = tok_all[at, :].astype(f32)
            n1_all[at, :] = (source * norm(source) * gain_a()).astype(low)
            pq[i] = nn(n1_all[at, :], w_qkv[...])
            return carry

        lax.fori_loop(0, 4, body, 0)
        pq_in[ctx] = pq[ctx]
        swap_start("pq", lambda peer: pq.at[peer], lambda sender: pq_in.at[sender])

    def pq_end():
        swap_end("pq", lambda sender: pq_in.at[sender])
        proj[...] = jnp.zeros(proj.shape, f32)
        for j in range(4):
            part = jnp.concatenate([pq_in[j], jnp.zeros((own_rows, 128), f32)], axis=1)
            at = qkv_cols * j
            if at % 128:
                part = pltpu.roll(part, at % 128, 1)
            proj[:, at // 128 * 128 : at // 128 * 128 + qkv_wide + 128] += part

    turned = {}

    def query_slab(slab):
        if slab not in turned:
            turned[slab] = turn(proj[:, slab * 128 : slab * 128 + 128], 1.0)
        return turned[slab]

    def slot_view(lead):
        return kv_all.at[:, :, pl.ds(pl.multiple_of(lead * slots_here, 16), slots_here)]

    def kv_start():
        my_slots = pl.ds(pl.multiple_of(ctx * slots_here, 16), slots_here)
        for slab in range(2 * slabs):
            at = (q_slabs + slab) * 128
            values = proj[:, at : at + 128]
            if slab < slabs:
                values = turn(values, 1.0)
            values = values.astype(low)
            for seq in range(2):
                kv_all[seq, slab, my_slots, :] = values[seq * slots_here : (seq + 1) * slots_here]

        swap_start("kv", lambda peer: slot_view(ctx), slot_view)

    def queries():
        stack_heads(query_slab, q_st, score_scale)

    def kv_end():
        swap_end("kv", slot_view)

    stack = q_st.shape[1]
    slots = kv_all.shape[2]

    def attend(i, carry):
        seq, slab = lax.div(i, slabs), lax.rem(i, slabs)
        scores = nt(q_st[i], kv_all[seq, slab])
        at = ctx * slots_here + lax.rem(lax.broadcasted_iota(jnp.int32, (stack, slots), 0), slots_here)
        key_at = lax.broadcasted_iota(jnp.int32, (stack, slots), 1)
        length = jnp.where(seq == 0, lengths[0], lengths[1])
        allowed = jnp.logical_and(key_at <= at, key_at < length)
        scores = jnp.where(allowed, scores, NEGATIVE)
        terms = jnp.exp(scores - jnp.max(scores, axis=-1, keepdims=True))
        probs = (terms / jnp.sum(terms, axis=-1, keepdims=True)).astype(low)
        p_st[i] = probs
        att[i] = nn(probs, kv_all[seq, slabs + slab])
        return carry

    def attention():
        lax.fori_loop(0, 2 * slabs, attend, 0)
        for slab in range(q_slabs):
            ctx_all[here_rows, slab * 128 : slab * 128 + 128] = unstack_heads(att, slab).astype(low)
        share("ctx", ctx_all)

    def out_project():
        hidden[...] = tokens[...].astype(f32)
        for j in range(4):
            part = nn(ctx_all[here_rows, :], w_out[j])
            at = out_cols * j
            if at % 128:
                part = pltpu.roll(part, at % 128, 1)
            hidden[:, at // 128 * 128 : at // 128 * 128 + out_wide] += part
        n2_all[here_rows, :] = (hidden[...] * norm(hidden[...]) * gain_b()).astype(low)
        share("n2", n2_all)

    tall = 2 * own_rows

    def feed(tile):
        def body(i, carry):
            at = pl.ds(pl.multiple_of(i * tall, tall), tall)
            gate = nn(n2_all[at, :], w_ff[:, tile * span : tile * span + half])
            up = nn(n2_all[at, :], w_ff[:, tile * span + half : tile * span + 2 * half])
            back = nn(g_all[at, :], w_ff[:, tile * span + 2 * half : (tile + 1) * span])
            sig = jax.nn.sigmoid(gate)
            swish = gate * sig
            act[tile, at, :] = (swish * up).astype(low)
            d_gu[tile, at, :half] = (back * up * sig * (1.0 + gate * (1.0 - sig))).astype(low)
            d_gu[tile, at, half:] = (back * swish).astype(low)
            return carry

        lax.fori_loop(0, 4 * own_rows // tall, body, 0)

    def grad_ff(tile):
        def body(m, carry):
            at = pl.ds(pl.multiple_of(m * 128, 128), 128)
            d_ff[at, tile * span : tile * span + 2 * half] = tn(n2_all[:, at], d_gu[tile]).astype(low)
            d_ff[at, tile * span + 2 * half : (tile + 1) * span] = tn(g_all[:, at], act[tile]).astype(low)
            return carry

        lax.fori_loop(0, width // 128, body, 0)

    across_core = (1 - x) * 2 + 1 - c
    across_own = (1 - x) * 2 + c
    beside = x * 2 + 1 - c
    wide_tile = 384

    def group_send(name, ref, box, which):
        lead, mark = ((across_core, "cx"), (beside, "cc"))[which]
        wires.send(ref.at[lead], box.at[which], (name, mark), place.core)

    def group_on(name, ref, box):
        wires.take(box.at[0], (name, "cx"), place.core)
        mine = ref.at[across_own]
        mine[...] = (mine[...].astype(f32) + box[0].astype(f32)).astype(low)
        wires.send(mine, box.at[2], (name, "x"), place.chip)

    def group_end(name, ref, box):
        wires.take(box.at[1], (name, "cc"), place.core)
        wires.take(box.at[2], (name, "x"), place.chip)
        return ref[ctx].astype(f32) + box[1].astype(f32) + box[2].astype(f32)

    def pair_rows(half_x):
        return pl.ds(pl.multiple_of(half_x * tall, 16), tall)

    def group_product(ref, terms):
        def compute(half_x):
            def body(n, carry):
                at = pl.ds(pl.multiple_of(n * wide_tile, 128), wide_tile)
                total = None
                for left, right in terms:
                    term = nt(left(pair_rows(half_x)), right(at))
                    total = term if total is None else total + term
                ref[2 * half_x, :, at] = total[:own_rows].astype(low)
                ref[2 * half_x + 1, :, at] = total[own_rows:].astype(low)
                return carry

            lax.fori_loop(0, width // wide_tile, body, 0)

        return compute

    back_terms = [
        (lambda at, tile=tile: d_gu[tile, at, :], lambda at, tile=tile: w_ff[at, tile * span : tile * span + 2 * half])
        for tile in TILES
    ]
    forward_terms = [
        (lambda at, tile=tile: act[tile, at, :], lambda at, tile=tile: w_ff[at, tile * span + 2 * half : (tile + 1) * span])
        for tile in TILES
    ]

    def key_pos(way, dist):
        if dist == 0:
            return None, dp
        return source_valid(place, way, dist), source_pos(place, way, dist)

    KEYS = {3: DRAIN[:2], 2: DRAIN[2:4], 1: DRAIN[4:6], 0: [(BELOW, 0)]}
    flip = 1 - 2 * y

    def z_add(name, view, boxes, inbox, way, dist):
        here, pos = key_pos(way, dist)
        mine = view(pos)
        if dist == 0:
            wires.take(boxes.at[way, dist], (name, "y", way, dist), place.across)
            add_rows(mine, [boxes.at[way, dist]])
            for end, fed, feeder in ((BELOW, place.has_up, place.up), (ABOVE, place.has_down, place.down)):

                def own():
                    wires.take(inbox.at[end, 0], (name, "z", end, 0), feeder)
                    add_rows(mine, [inbox.at[end, 0]])

                pl.when(fed)(own)
            return
        fed = place.has_up if way == BELOW else place.has_down
        feeder = place.up if way == BELOW else place.down
        onward = place.down if way == BELOW else place.up
        side = boxes.at[way, dist]

        def first():
            wires.take(side, (name, "y", way, dist), place.across)
            add_rows(mine, [side])

        if dist == 3:
            pl.when(here)(first)
        else:

            def more():
                wires.take(side, (name, "y", way, dist), place.across)
                wires.take(inbox.at[way, dist], (name, "z", way, dist), feeder)
                add_rows(mine, [side, inbox.at[way, dist]])

            pl.when(jnp.logical_and(here, jnp.logical_not(fed)))(first)
            pl.when(jnp.logical_and(here, fed))(more)
        wires.send(mine, inbox.at[way, dist - 1], (name, "z", way, dist - 1), onward, here)

    class Sink:
        def __init__(self, name, view, side, inbox):
            self.name, self.view, self.side, self.inbox = name, view, side, inbox

        def send(self, dist):
            for way, dist in KEYS[dist]:
                here, pos = key_pos(way, dist)
                wires.send(
                    self.view(pos + flip), self.side.at[way, dist],
                    (self.name, "y", way, dist), place.across, here,
                )

        def send_all(self):
            for dist in (3, 2, 1, 0):
                self.send(dist)

        def add(self, dist):
            for way, dist in KEYS[dist]:
                z_add(self.name, self.view, self.side, self.inbox, way, dist)

    gu_sides, gu_inboxes = (gu_side_a, gu_side_b), (gu_inbox_a, gu_inbox_b)
    gu_sinks = [
        Sink(("dgu", tile), functools.partial(gu_view, d_ff, tile), gu_sides[tile], gu_inboxes[tile])
        for tile in TILES
    ]
    out_sink = Sink("dout", lambda pos: d_out.at[block_rows(pos)], out_side, out_inbox)
    qkv_sink = Sink("dqkv", lambda pos: d_qkv.at[block_rows(pos)], qkv_side, qkv_inbox)
    d_strips, d_other_strips = strips_of(d_ff, lanes), strips_of(d_ff, other_lanes)

    def down_send(tile):
        for j in range(4):
            wires.send(d_other_strips[j], down_side.at[j], ("ddown_y", j), place.across, (1 - y) == tile)

    def down_add(dist):
        if dist == 0:
            for j in range(4):

                def finish():
                    wires.take(down_side.at[j], ("ddown_y", j), place.across)
                    add_rows(d_strips[j], [down_side.at[j]])
                    for end, fed, feeder in ((BELOW, place.has_up, place.up), (ABOVE, place.has_down, place.down)):

                        def more():
                            wires.take(down_inbox.at[end, j], ("ddown", j, end, 0), feeder)
                            add_rows(d_strips[j], [down_inbox.at[end, j]])

                        pl.when(fed)(more)

                pl.when(at_home)(finish)
            return
        for way in (BELOW, ABOVE):
            here = (z - ctx if way == BELOW else ctx - z) == dist
            fed = place.has_up if way == BELOW else place.has_down
            feeder = place.up if way == BELOW else place.down
            onward = place.down if way == BELOW else place.up
            for j in range(4):

                def first():
                    wires.take(down_side.at[j], ("ddown_y", j), place.across)
                    add_rows(d_strips[j], [down_side.at[j]])

                def more():
                    wires.take(down_side.at[j], ("ddown_y", j), place.across)
                    wires.take(down_inbox.at[way, j], ("ddown", j, way, dist), feeder)
                    add_rows(d_strips[j], [down_side.at[j], down_inbox.at[way, j]])

                pl.when(jnp.logical_and(here, jnp.logical_not(fed)))(first)
                pl.when(jnp.logical_and(here, fed))(more)
                wires.send(d_strips[j], down_inbox.at[way, j], ("ddown", j, way, dist - 1), onward, here)

    class PairSink:
        def __init__(self, name, ref, cols, inbox, side):
            self.name, self.ref, self.cols, self.inbox, self.side = name, ref, cols, inbox, side

        def pair(self, plane):
            return self.ref.at[pl.ds(pl.multiple_of(2 * rows * plane, 16), 2 * rows), self.cols]

        def one(self, pos):
            return self.ref.at[block_rows(pos), self.cols]

        def add(self, dist):
            if dist == 0:
                mine = self.pair(z)
                for end, fed, feeder in ((BELOW, place.has_up, place.up), (ABOVE, place.has_down, place.down)):

                    def more():
                        wires.take(self.inbox.at[end, 0], (self.name, "z", end, 0), feeder)
                        add_rows(mine, [self.inbox.at[end, 0]])

                    pl.when(fed)(more)
                wires.send(self.one(place.across[0]), self.side, (self.name, "y"), place.across)
                return
            for way, dist in KEYS[dist]:
                here = source_valid(place, way, dist)
                mine = self.pair(z - dist if way == BELOW else z + dist)
                fed = place.has_up if way == BELOW else place.has_down
                feeder = place.up if way == BELOW else place.down
                onward = place.down if way == BELOW else place.up
                if dist < 3:

                    def more():
                        wires.take(self.inbox.at[way, dist], (self.name, "z", way, dist), feeder)
                        add_rows(mine, [self.inbox.at[way, dist]])

                    pl.when(jnp.logical_and(here, fed))(more)
                wires.send(mine, self.inbox.at[way, dist - 1], (self.name, "z", way, dist - 1), onward, here)

        def end(self):
            wires.take(self.side, (self.name, "y"), place.across)
            add_rows(self.one(dp), [self.side])

    up_sink = PairSink("dup", d_ff, up_cols, up_inbox, up_side)

    def gu_finish(tile):
        for part in range(2):
            target = part * 2 + x
            block = d_ff.at[my_rows, pl.ds(tile * span + part * half, half)]
            wires.send(block, gu_mix.at[c, tile], ("dgu_mix", tile, 0), (dp, target), target != ctx, extra=c)
            pl.when(target == ctx)(lambda: add_rows(block, [], out=gu_mix.at[c, tile]))
        wires.slot(("dgu_mix", tile, 1))

    def gu_end(tile):
        for part in range(2):
            origin = 2 * c + part
            box = gu_mix.at[part, tile]
            pl.when(origin != ctx)(lambda: wires.take(box, ("dgu_mix", tile, part), (dp, origin)))
            add_rows(box, [], out=gu_out.at[:, pl.ds((2 * part + tile) * half, half)])

    def down_finish():
        for j in range(4):
            wires.send(d_strips[j], down_mix, ("ddown_mix",), (dp, j), jnp.logical_and(at_home, ctx != j))
            pl.when(jnp.logical_and(at_home, ctx == j))(functools.partial(add_rows, d_strips[j], [], down_mix))

    def down_end():
        pl.when(ctx != z)(lambda: wires.take(down_mix, ("ddown_mix",), (dp, z)))
        add_rows(down_mix, [], out=dt_out)

    def norm_back(values, inverse, gain, grad_in):
        scaled = grad_in * gain
        mean_term = jnp.mean(scaled * values, axis=-1, keepdims=True)
        back = inverse * scaled - values * (inverse * inverse * inverse) * mean_term
        return back, jnp.sum(grad_in * values * inverse, axis=0, keepdims=True)

    def gp_block(which):
        half_x = 1 - x if which == 0 else x
        group_product(gp, back_terms)(half_x)
        group_send("gp", gp, gp_box, which)

    def op_block(which):
        half_x = 1 - x if which == 0 else x
        group_product(op, forward_terms)(half_x)
        group_send("op", op, op_box, which)

    def hidden_back():
        gain_acc[0] = jnp.zeros(gain_out.shape, f32)
        back_two, gain_two_grad = norm_back(hidden[...], norm(hidden[...]), gain_b(), group_end("gp", gp, gp_box))
        gain_acc[0, 1:2, :] = gain_two_grad
        grad_hidden[...] = g_all[here_rows, :].astype(f32) + back_two
        out_lane = lax.broadcasted_iota(jnp.int32, (own_rows, out_wide), 1)
        for j in range(4):
            at = out_cols * j
            part = grad_hidden[:, at // 128 * 128 : at // 128 * 128 + out_wide]
            if at % 128:
                part = pltpu.roll(part, out_wide - at % 128, 1)
            wide[j] = jnp.where(out_lane < out_cols, part, 0.0).astype(low)
        gb_all[here_rows, :] = wide[ctx]
        swap_start("gb", lambda peer: wide.at[peer], lambda sender: gb_all.at[lead_rows(sender)])

    def context_back(n, carry):
        at = pl.ds(pl.multiple_of(n * wide_tile, 128), wide_tile)
        total = nt(wide[0], w_out[0, at, :])
        for j in range(1, 4):
            total = total + nt(wide[j], w_out[j, at, :])
        proj[:, at] = total
        return carry

    def grad_context():
        lax.fori_loop(0, width // wide_tile, context_back, 0)
        stack_heads(lambda slab: proj[:, slab * 128 : slab * 128 + 128], go_st, 1.0)

    def attend_back(i, carry):
        seq, slab = lax.div(i, slabs), lax.rem(i, slabs)
        grad_probs = nt(go_st[i], kv_all[seq, slabs + slab])
        probs = p_st[i].astype(f32)
        delta = jnp.sum(probs * grad_probs, axis=-1, keepdims=True)
        grad_scores = (probs * (grad_probs - delta)).astype(low)
        att[i] = nn(grad_scores, kv_all[seq, slab]) * score_scale
        grad_key = tn(grad_scores, q_st[i])
        grad_value = tn(p_st[i], go_st[i])
        for j in range(4):
            part = slice(j * slots_here, (j + 1) * slots_here)
            dkv[j, seq, slab] = grad_key[part].astype(low)
            dkv[j, seq, slabs + slab] = grad_value[part].astype(low)
        return carry

    def attention_back():
        lax.fori_loop(0, 2 * slabs, attend_back, 0)
        group_send("dkv", dkv, dkv_box, 0)
        group_send("dkv", dkv, dkv_box, 1)

    def gb_end():
        swap_end("gb", lambda sender: gb_all.at[lead_rows(sender)])

    def grad_out(m, carry):
        at = pl.ds(pl.multiple_of(m * 128, 128), 128)
        d_out[at, :] = tn(ctx_all[:, at], gb_all[...]).astype(low)
        return carry

    def grad_out_all():
        lax.fori_loop(0, width // 128, grad_out, 0)

    def grad_mixed():
        sums = group_end("dkv", dkv, dkv_box)
        proj[...] = jnp.zeros(proj.shape, f32)
        for slab in range(q_slabs):
            proj[:, slab * 128 : slab * 128 + 128] = turn(unstack_heads(att, slab), -1.0)
        for slab in range(2 * slabs):
            values = jnp.concatenate([sums[0, slab], sums[1, slab]], axis=0)
            if slab < slabs:
                values = turn(values, -1.0)
            at = (q_slabs + slab) * 128
            proj[:, at : at + 128] = values
        qkv_lane = lax.broadcasted_iota(jnp.int32, (own_rows, qkv_wide), 1)
        for j in range(4):
            at = qkv_cols * j
            part = proj[:, at // 128 * 128 : at // 128 * 128 + qkv_wide + 128]
            if at % 128:
                part = pltpu.roll(part, qkv_wide + 128 - at % 128, 1)
            gm[j] = jnp.where(qkv_lane < qkv_cols, part[:, :qkv_wide], 0.0).astype(low)
        gm_all[here_rows, :] = gm[ctx]
        swap_start("gm", lambda peer: gm.at[peer], lambda sender: gm_all.at[lead_rows(sender)])

    def gm_end():
        swap_end("gm", lambda sender: gm_all.at[lead_rows(sender)])

    def grad_qkv(m, carry):
        at = pl.ds(pl.multiple_of(m * 128, 128), 128)
        d_qkv[at, :] = tn(n1_all[:, at], gm_all[...]).astype(low)
        return carry

    def grad_qkv_all():
        lax.fori_loop(0, width // 128, grad_qkv, 0)

    tokens_terms = [(lambda at: gm_all[at, :], lambda at: w_qkv[at, :])]

    def gt_block(which):
        if which == 0:
            wires.drain_named("gp")
        half_x = 1 - x if which == 0 else x
        group_product(gp, tokens_terms)(half_x)
        group_send("gt", gp, gp_box, which)

    def output_end():
        result = hidden[...] + group_end("op", op, op_box)
        output[...] = jnp.where(valid, result, 0.0).astype(low)

    def tokens_end():
        source = tokens[...].astype(f32)
        back_one, gain_one_grad = norm_back(source, norm(source), gain_a(), group_end("gt", gp, gp_box))
        gain_acc[0, 0:1, :] = gain_one_grad
        grad_tokens[...] = (grad_hidden[...] + back_one).astype(low)

    low_end, high_end = z == 0, z == 3
    mid_low, mid_high = z == 1, z == 2

    def gain_send(hop):
        def go(device, cond=None):
            wires.send(gain_acc.at[hop], gain_box.at[hop], ("gain_sum", hop), device, cond)

        if hop < 3:
            go((place.core, place.chip, place.across)[hop])
        elif hop == 3:
            go(place.up, low_end)
            go(place.down, high_end)
        elif hop == 4:
            go(place.up, mid_low)
            go(place.down, mid_high)
        else:
            go(place.down, mid_low)
            go(place.up, mid_high)

    def gain_take(hop):
        def add(device):
            wires.take(gain_box.at[hop], ("gain_sum", hop), device)
            gain_acc[hop + 1] = gain_acc[hop] + gain_box[hop]

        def last(device):
            wires.take(gain_box.at[hop], ("gain_sum", hop), device)
            gain_out[...] = gain_box[hop]

        def done():
            gain_out[...] = gain_acc[hop]

        if hop < 3:
            add((place.core, place.chip, place.across)[hop])
        elif hop == 3:
            pl.when(mid_low)(lambda: add(place.down))
            pl.when(mid_high)(lambda: add(place.up))
        elif hop == 4:
            pl.when(mid_low)(lambda: add(place.up))
            pl.when(mid_high)(lambda: add(place.down))
        else:
            pl.when(low_end)(lambda: last(place.up))
            pl.when(high_end)(lambda: last(place.down))
            pl.when(mid_low)(done)
            pl.when(mid_high)(done)

    def out_end():
        out_out[...] = d_out[my_rows, :].astype(f32)[:, :out_cols]

    def qkv_end():
        qkv_out[...] = d_qkv[my_rows, :].astype(f32)[:, :qkv_cols]

    def locals_end():
        for copy, cond in locals_:
            when(cond, copy.wait)

    mix_start(0)
    qkv_start()
    mix_start(1)
    gain_start()
    down_mix_start()
    locals_end()
    tokens_start()
    qkv_flood.hop(1)
    qkv_flood.hop(2)
    qkv_flood.hop(3)
    mix_end(1)
    qkv_flood.side(0)
    out_start()
    gain_flood.hop(1)
    cot_start()
    gain_flood.hop(2)
    mix_end(0)
    gu_floods[0].start()
    qkv_flood.side(3)
    gain_flood.hop(3)
    out_flood.hop(1)
    qkv_flood.side(2)
    share_on("tok", tok_all)
    share_end("tok", tok_all)
    down_start()
    gain_sides()
    gu_floods[1].start()
    qkv_flood.side(1)
    project()
    up_flood.start()
    share_on("cot", g_all)
    out_flood.hop(2)
    out_flood.hop(3)
    out_flood.side(0)
    down_hop(1)
    up_flood.side()
    gu_floods[1].side(0)
    gu_floods[1].hop(1)
    out_chip(0, 0)
    down_hop(2)
    gu_floods[0].hop(1)
    pq_end()
    kv_start()
    out_chip(1, 0)
    queries()
    share_end("cot", g_all)
    out_flood.side(2)
    out_flood.side(3)
    gu_floods[1].hop(2)
    out_flood.side(1)
    down_hop(3)
    out_chip(0, 2)
    gu_floods[0].hop(2)
    kv_end()
    attention()
    out_chip(1, 3)
    out_chip(0, 3)
    out_chip(0, 1)
    out_chip(1, 2)
    out_chip(1, 1)
    out_core()
    out_project()
    gu_floods[0].hop(3)
    down_side_end()
    gu_floods[0].side(1)
    gu_floods[0].side(0)
    up_flood.hop(1)
    up_flood.hop(2)
    gu_floods[1].hop(3)
    share_on("n2", n2_all)
    share_end("n2", n2_all)
    gu_floods[1].side(2)
    gu_floods[0].side(3)
    gu_floods[0].side(2)
    feed(0)
    grad_ff(0)
    gu_floods[1].side(3)
    gu_sinks[0].send(3)
    gu_sinks[0].send(2)
    up_flood.hop(3)
    gu_floods[1].side(1)
    feed(1)
    grad_ff(1)
    up_sink.add(3)
    down_send(0)
    down_send(1)
    share_on("ctx", ctx_all)
    gp_block(0)
    group_on("gp", gp, gp_box)
    gu_sinks[0].add(3)
    share_end("ctx", ctx_all)
    op_block(0)
    gp_block(1)
    up_sink.add(2)
    gu_sinks[1].send(3)
    down_add(3)
    hidden_back()
    grad_context()
    gu_sinks[0].send(1)
    gu_sinks[0].add(2)
    attention_back()
    group_on("dkv", dkv, dkv_box)
    up_sink.add(1)
    gu_sinks[1].send(2)
    gb_end()
    grad_out_all()
    out_sink.send(2)
    out_sink.send(3)
    grad_mixed()
    gu_sinks[1].add(3)
    down_add(2)
    gu_sinks[1].send(1)
    gu_sinks[0].add(1)
    group_on("op", op, op_box)
    out_sink.send(1)
    gm_end()
    grad_qkv_all()
    gu_sinks[1].add(2)
    gt_block(0)
    gu_sinks[1].send(0)
    group_on("gt", gp, gp_box)
    out_sink.add(3)
    gt_block(1)
    down_add(1)
    out_sink.send(0)
    gu_sinks[0].send(0)
    tokens_end()
    gain_send(0)
    gain_take(0)
    gain_send(1)
    gain_take(1)
    gain_send(2)
    qkv_sink.send(3)
    op_block(1)
    qkv_sink.send(2)
    out_sink.add(2)
    up_sink.add(0)
    gu_sinks[0].add(0)
    gu_finish(0)
    gain_take(2)
    gain_send(3)
    gu_sinks[1].add(1)
    gain_take(3)
    gain_send(4)
    down_add(0)
    down_finish()
    qkv_sink.send(1)
    qkv_sink.add(3)
    qkv_sink.add(2)
    up_sink.end()
    out_sink.add(1)
    gu_sinks[1].add(0)
    gu_finish(1)
    output_end()
    qkv_sink.send(0)
    gain_take(4)
    gain_send(5)
    down_end()
    qkv_sink.add(1)
    out_sink.add(0)
    out_end()
    gain_take(5)
    gu_end(0)
    gu_end(1)
    qkv_sink.add(0)
    qkv_end()
    wires.drain()


def on_device_fast(tokens, lengths, gain_one, w_qkv, w_out, gain_two, w_gate_up, w_down, cotangent):
    seq_count, row_count, width = tokens.shape
    own_rows = seq_count * row_count
    f32, low = jnp.float32, jnp.bfloat16
    block = gain_one.shape[0]
    gains = jnp.stack([gain_one, gain_two]).astype(f32)
    gains = jnp.pad(gains, ((0, 6), (0, 256 - block)))
    position = lax.axis_index("ctx") * row_count + jnp.arange(row_count, dtype=jnp.int32)
    cosine, sine = angles(position, HD)
    cosine = jnp.tile(cosine, (seq_count, 4))
    sine = jnp.tile(jnp.concatenate([-sine, sine], axis=1), (seq_count, 2))
    rows, qkv_cols = w_qkv.shape
    out_cols = w_out.shape[1]
    units = w_gate_up.shape[1] // 2
    half, strip = w_down.shape
    qkv_wide = -(-qkv_cols // 128) * 128
    out_wide = -(-out_cols // 128) * 128
    deep = 8 * rows
    slots = 4 * row_count
    slabs = KVH // 2
    stack = 2 * QH // KVH * row_count

    def box(*shape, dtype=low):
        return pltpu.VMEM(shape, dtype)

    scratch = [
        box(deep, qkv_wide), box(4, deep, out_wide), box(deep, 3 * units),
        box(deep, qkv_wide), box(deep, out_wide), box(deep, 3 * units),
        box(8, 8, 256, dtype=f32), box(8, deep + 128, dtype=f32),
        box(4 * own_rows, width), box(4 * own_rows, width), box(4 * own_rows, width),
        box(4 * own_rows, width), box(4 * own_rows, QH * HD),
        box(own_rows, width, dtype=f32), box(own_rows, width, dtype=f32),
        box(own_rows, 4 * qkv_wide, dtype=f32),
        box(seq_count * slabs, stack, 128), box(seq_count, 2 * slabs, slots, 128),
        box(seq_count * slabs, stack, slots), box(seq_count * slabs, stack, 128, dtype=f32),
        box(seq_count * slabs, stack, 128),
        box(4, own_rows, out_wide), box(4, own_rows, qkv_wide),
        box(4, own_rows, qkv_wide, dtype=f32), box(4, own_rows, qkv_wide, dtype=f32),
        box(4 * own_rows, out_wide), box(4 * own_rows, qkv_wide),
        box(2, 4 * own_rows, half), box(2, 4 * own_rows, 2 * half),
        box(4, own_rows, width), box(3, own_rows, width),
        box(4, own_rows, width), box(3, own_rows, width),
        box(4, seq_count, 2 * slabs, row_count, 128), box(3, seq_count, 2 * slabs, row_count, 128),
        box(2, 4, rows, qkv_wide), box(2, 4, rows, out_wide),
        box(2, 4, rows, 2 * half), box(2, 4, rows, half), box(4, strip, half),
        box(2, 3, rows, qkv_wide), box(2, 3, rows, out_wide),
        box(2, 3, rows, 2 * half), box(2, 3, rows, half), box(2, 4, strip, half),
        box(2, 3, 2 * rows, half), box(rows, half),
        box(2, 2, rows, half), box(strip, half),
        box(6, 8, width, dtype=f32), box(6, 8, width, dtype=f32),
        pltpu.SemaphoreType.DMA((400,)),
        pltpu.SemaphoreType.DMA((400,)),
        pltpu.SemaphoreType.DMA((8,)),
    ]
    vmem = pl.BlockSpec(memory_space=pltpu.MemorySpace.VMEM)
    smem = pl.BlockSpec(memory_space=pltpu.MemorySpace.SMEM)
    shapes = (
        jax.ShapeDtypeStruct((own_rows, width), low),
        jax.ShapeDtypeStruct((own_rows, width), low),
        jax.ShapeDtypeStruct((8, width), f32),
        jax.ShapeDtypeStruct((rows, qkv_cols), f32),
        jax.ShapeDtypeStruct((rows, out_cols), f32),
        jax.ShapeDtypeStruct((rows, 2 * units), f32),
        jax.ShapeDtypeStruct((strip, half), f32),
    )
    output, grad_tokens, gain_sums, final_qkv, final_out, final_gu, final_dt = pl.pallas_call(
        functools.partial(layer_kernel, {}),
        out_shape=shapes,
        in_specs=[vmem, vmem, smem] + [vmem] * 7,
        out_specs=[vmem] * 7,
        scratch_shapes=scratch,
        compiler_params=pltpu.CompilerParams(
            collective_id=0, has_side_effects=True, vmem_limit_bytes=64 * 2**20
        ),
        name="layer",
    )(
        tokens.reshape(own_rows, width), cotangent.reshape(own_rows, width), lengths,
        w_qkv, w_out, w_gate_up, w_down.T, gains, cosine, sine,
    )
    mine = lax.dynamic_slice(gain_sums, (0, lax.axis_index("dp") * block), (8, block))
    return (
        output.reshape(tokens.shape), grad_tokens.reshape(tokens.shape),
        mine[0], final_qkv, final_out, mine[1], final_gu, final_dt.T,
    )


def solution(mesh):
    fits = mesh.shape["dp"] == 8 and mesh.shape["ctx"] == 4
    return jax.shard_map(
        on_device_fast if fits else on_device,
        mesh=mesh,
        in_specs=(
            P("dp", "ctx", None),
            P("dp"),
            P("dp"),
            P("dp", "ctx"),
            P("dp", "ctx"),
            P("dp"),
            P("dp", "ctx"),
            P("dp", "ctx"),
            P("dp", "ctx", None),
        ),
        out_specs=(
            P("dp", "ctx", None),
            P("dp", "ctx", None),
            P("dp"),
            P("dp", "ctx"),
            P("dp", "ctx"),
            P("dp"),
            P("dp", "ctx"),
            P("dp", "ctx"),
        ),
        check_vma=False,
    )
```

```python
import functools
import math

import jax
import jax.numpy as jnp
import numpy as np
from jax import lax
from jax.experimental import pallas as pl
from jax.experimental.pallas import tpu as pltpu
from jax.sharding import PartitionSpec as P

QH = 18
KVH = 6
HD = 64
FF = 3072


EPS = 1e-05
NEGATIVE = -1e30


def angles(position, head_width):
    frequency = 10000.0 ** (-jnp.arange(head_width // 2, dtype=jnp.float32) * 2.0 / head_width)
    angle_table = position.astype(jnp.float32)[:, None] * frequency[None, :]
    return (jnp.cos(angle_table), jnp.sin(angle_table))


def rotate(values_in, cosine, sine_table):
    half_width = values_in.shape[-1] // 2
    first_half = values_in[..., :half_width]
    second = values_in[..., half_width:]
    return jnp.concatenate(
        [first_half * cosine - second * sine_table, second * cosine + first_half * sine_table],
        axis=-1,
    )


def split_heads(values_in, head_count):
    seq_count, row_count, col_count = values_in.shape
    head_width = col_count // head_count
    moved = values_in.reshape(seq_count, row_count, head_count, head_width).transpose(0, 2, 1, 3)
    return moved.reshape(seq_count * head_count, row_count, head_width)


def join_heads(values_in, seq_count):
    item_count, row_count, head_width = values_in.shape
    head_count = item_count // seq_count
    moved = values_in.reshape(seq_count, head_count, row_count, head_width).transpose(0, 2, 1, 3)
    return moved.reshape(seq_count, row_count, head_count * head_width)


def norm_back(source, inverse, gain, grad_in):
    scaled = grad_in * gain
    mean_term = jnp.mean(scaled * source, axis=-1, keepdims=True)
    back_rows = inverse * scaled - source * (inverse * inverse * inverse) * mean_term
    return (back_rows, jnp.sum(grad_in * source * inverse, axis=(0, 1)))


def block_scores(query_rows, key_rows, position, length, group_count, score_scale):
    raw_scores = (
        jnp.einsum("nd,td->nt", query_rows, key_rows, preferred_element_type=jnp.float32)
        * score_scale
    )
    raw_scores = raw_scores.reshape(group_count, position.shape[0], key_rows.shape[0])
    keyidx = jnp.arange(key_rows.shape[0], dtype=jnp.int32)
    allowed = (keyidx[None, :] <= position[:, None]) & (keyidx[None, :] < length)
    return jnp.where(allowed[None], raw_scores, NEGATIVE)


def on_device(tokens, lengths, gain_one, w_qkv, w_out, gain_two, w_gate_up, w_down, cotangent):
    forward_wide = (
        lax.all_gather(w_qkv, "ctx", axis=1, tiled=True),
        lax.all_gather(w_out, "ctx", axis=1, tiled=True),
        lax.all_gather(w_gate_up, "ctx", axis=1, tiled=True),
        lax.all_gather(w_down, "ctx", axis=1, tiled=True),
    )
    qkv_full, out_full, gate_up_full, down_full, gain_fa, gain_fb = (
        lax.all_gather(forward_wide[0], "dp", axis=0, tiled=True),
        lax.all_gather(forward_wide[1], "dp", axis=0, tiled=True),
        lax.all_gather(forward_wide[2], "dp", axis=0, tiled=True),
        lax.all_gather(forward_wide[3], "dp", axis=0, tiled=True),
        lax.all_gather(gain_one, "dp", axis=0, tiled=True),
        lax.all_gather(gain_two, "dp", axis=0, tiled=True),
    )
    seq_count, row_count, model_width = tokens.shape
    query_cols = QH * HD
    key_cols = KVH * HD
    group_count = QH // KVH
    score_scale = 1.0 / math.sqrt(HD)
    position = lax.axis_index("ctx") * row_count + jnp.arange(row_count, dtype=jnp.int32)
    valid_rows = position[None, :] < lengths[:, None]
    cosine, sine_table = angles(position, HD)
    cosine = cosine[:, None, :]
    sine_table = sine_table[:, None, :]
    source = tokens.astype(jnp.float32)
    inverse_one = lax.rsqrt(jnp.mean(source * source, axis=-1, keepdims=True) + EPS)
    normed_one = (source * inverse_one * gain_fa.astype(jnp.float32)).astype(jnp.bfloat16)
    projected = jnp.einsum("bsd,de->bse", normed_one, qkv_full, preferred_element_type=jnp.float32)
    queries = rotate(
        projected[..., :query_cols].reshape(seq_count, row_count, QH, HD), cosine, sine_table
    )
    queries = queries.astype(jnp.bfloat16).reshape(seq_count, row_count, query_cols)
    key_heads = rotate(
        projected[..., query_cols : query_cols + key_cols].reshape(seq_count, row_count, KVH, HD),
        cosine,
        sine_table,
    )
    key_heads = key_heads.astype(jnp.bfloat16).reshape(seq_count, row_count, key_cols)
    value_heads = projected[..., query_cols + key_cols :].astype(jnp.bfloat16)
    keys_all, values_all = (
        lax.all_gather(key_heads, "ctx", axis=1, tiled=True),
        lax.all_gather(value_heads, "ctx", axis=1, tiled=True),
    )
    query_blocks = split_heads(queries, QH).reshape(seq_count * KVH, group_count * row_count, HD)
    key_blocks = split_heads(keys_all, KVH)
    value_blocks = split_heads(values_all, KVH)
    pair_lengths = jnp.repeat(lengths, KVH)

    def forward_block(block_in):
        query_rows, key_rows, value_rows, length = block_in
        scores = block_scores(query_rows, key_rows, position, length, group_count, score_scale)
        row_max = jnp.max(scores, axis=-1, keepdims=True)
        exp_terms = jnp.exp(scores - row_max)
        row_total = jnp.sum(exp_terms, axis=-1, keepdims=True)
        prob_rows = (exp_terms / row_total).astype(jnp.bfloat16)
        result = jnp.einsum(
            "gst,td->gsd", prob_rows, value_rows, preferred_element_type=jnp.float32
        )
        return (result.reshape(-1, HD), (row_max + jnp.log(row_total))[..., 0])

    context_blocks, log_totals = lax.map(
        forward_block, (query_blocks, key_blocks, value_blocks, pair_lengths)
    )
    context = join_heads(context_blocks.reshape(seq_count * QH, row_count, HD), seq_count).astype(
        jnp.bfloat16
    )
    hidden = source + jnp.einsum(
        "bse,ed->bsd", context, out_full, preferred_element_type=jnp.float32
    )
    inverse_two = lax.rsqrt(jnp.mean(hidden * hidden, axis=-1, keepdims=True) + EPS)
    normed_two = (hidden * inverse_two * gain_fb.astype(jnp.float32)).astype(jnp.bfloat16)
    gate_up = jnp.einsum(
        "bsd,df->bsf", normed_two, gate_up_full, preferred_element_type=jnp.float32
    )
    gate_part = gate_up[..., :FF]
    up_part = gate_up[..., FF:]
    gate_sig = jax.nn.sigmoid(gate_part)
    swish_part = gate_part * gate_sig
    activation = (swish_part * up_part).astype(jnp.bfloat16)
    result_rows = hidden + jnp.einsum(
        "bsf,fd->bsd", activation, down_full, preferred_element_type=jnp.float32
    )
    output = jnp.where(valid_rows[..., None], result_rows, 0.0).astype(jnp.bfloat16)
    back_wide = (
        lax.all_gather(w_qkv, "ctx", axis=1, tiled=True),
        lax.all_gather(w_out, "ctx", axis=1, tiled=True),
        lax.all_gather(w_gate_up, "ctx", axis=1, tiled=True),
        lax.all_gather(w_down, "ctx", axis=1, tiled=True),
    )
    qkv_back, out_back, gate_up_back, down_back, gain_ba, gain_bb = (
        lax.all_gather(back_wide[0], "dp", axis=0, tiled=True),
        lax.all_gather(back_wide[1], "dp", axis=0, tiled=True),
        lax.all_gather(back_wide[2], "dp", axis=0, tiled=True),
        lax.all_gather(back_wide[3], "dp", axis=0, tiled=True),
        lax.all_gather(gain_one, "dp", axis=0, tiled=True),
        lax.all_gather(gain_two, "dp", axis=0, tiled=True),
    )
    grad_rows = jnp.where(valid_rows[..., None], cotangent, jnp.zeros_like(cotangent))
    grad_activation = jnp.einsum(
        "bsd,fd->bsf", grad_rows, down_back, preferred_element_type=jnp.float32
    )
    grad_gate = grad_activation * up_part * gate_sig * (1.0 + gate_part * (1.0 - gate_sig))
    grad_up = grad_activation * swish_part
    grad_mix = jnp.concatenate([grad_gate, grad_up], axis=-1).astype(jnp.bfloat16)
    grad_normed_two = jnp.einsum(
        "bsf,df->bsd", grad_mix, gate_up_back, preferred_element_type=jnp.float32
    )
    back_two, grad_gain_two = norm_back(
        hidden, inverse_two, gain_bb.astype(jnp.float32), grad_normed_two
    )
    grad_hidden = grad_rows.astype(jnp.float32) + back_two
    grad_branch = grad_hidden.astype(jnp.bfloat16)
    grad_context = jnp.einsum(
        "bsd,ed->bse", grad_branch, out_back, preferred_element_type=jnp.float32
    ).astype(jnp.bfloat16)
    grad_blocks = split_heads(grad_context, QH).reshape(
        seq_count * KVH, group_count * row_count, HD
    )

    def backward_block(block_in):
        query_rows, key_rows, value_rows, length, log_total, grad_in = block_in
        scores = block_scores(query_rows, key_rows, position, length, group_count, score_scale)
        prob_rows = jnp.exp(scores - log_total[..., None])
        grad_grouped = grad_in.reshape(group_count, -1, HD)
        grad_probs = jnp.einsum(
            "gsd,td->gst", grad_grouped, value_rows, preferred_element_type=jnp.float32
        )
        grad_value = jnp.einsum(
            "gst,gsd->td",
            prob_rows.astype(jnp.bfloat16),
            grad_grouped,
            preferred_element_type=jnp.float32,
        )
        row_delta = jnp.sum(prob_rows * grad_probs, axis=-1, keepdims=True)
        grad_scores = (prob_rows * (grad_probs - row_delta)).astype(jnp.bfloat16)
        grad_query = (
            jnp.einsum("gst,td->gsd", grad_scores, key_rows, preferred_element_type=jnp.float32)
            * score_scale
        )
        grad_key = (
            jnp.einsum(
                "gst,gsd->td",
                grad_scores,
                query_rows.reshape(group_count, -1, HD),
                preferred_element_type=jnp.float32,
            )
            * score_scale
        )
        return (grad_query.reshape(-1, HD), grad_key, grad_value)

    query_grads, key_grads, value_grads = lax.map(
        backward_block,
        (query_blocks, key_blocks, value_blocks, pair_lengths, log_totals, grad_blocks),
    )
    key_sums, value_sums = (
        lax.psum_scatter(
            join_heads(key_grads, seq_count).astype(jnp.bfloat16),
            "ctx",
            scatter_dimension=1,
            tiled=True,
        ).astype(jnp.float32),
        lax.psum_scatter(
            join_heads(value_grads, seq_count).astype(jnp.bfloat16),
            "ctx",
            scatter_dimension=1,
            tiled=True,
        ).astype(jnp.float32),
    )
    grad_queries = join_heads(query_grads.reshape(seq_count * QH, row_count, HD), seq_count)
    turned_queries = rotate(grad_queries.reshape(seq_count, row_count, QH, HD), cosine, -sine_table)
    turned_keys = rotate(key_sums.reshape(seq_count, row_count, KVH, HD), cosine, -sine_table)
    grad_mixed = jnp.concatenate(
        [
            turned_queries.reshape(seq_count, row_count, query_cols),
            turned_keys.reshape(seq_count, row_count, key_cols),
            value_sums,
        ],
        axis=-1,
    ).astype(jnp.bfloat16)
    grad_normed_one = jnp.einsum(
        "bse,de->bsd", grad_mixed, qkv_back, preferred_element_type=jnp.float32
    )
    back_one, grad_gain_one = norm_back(
        source, inverse_one, gain_ba.astype(jnp.float32), grad_normed_one
    )
    grad_tokens = (grad_hidden + back_one).astype(jnp.bfloat16)
    exchanged = (
        lax.all_to_all(grad_mixed, "ctx", split_axis=2, concat_axis=1, tiled=True),
        lax.all_to_all(grad_branch, "ctx", split_axis=2, concat_axis=1, tiled=True),
        lax.all_to_all(grad_mix, "ctx", split_axis=2, concat_axis=1, tiled=True),
        lax.all_to_all(grad_rows, "ctx", split_axis=2, concat_axis=1, tiled=True),
    )
    initial = (
        jnp.zeros((model_width, exchanged[0].shape[2]), jnp.float32),
        jnp.zeros((context.shape[2], exchanged[1].shape[2]), jnp.float32),
        jnp.zeros((model_width, exchanged[2].shape[2]), jnp.float32),
        jnp.zeros((activation.shape[2], exchanged[3].shape[2]), jnp.float32),
    )
    pieces = (
        lax.all_gather(normed_one, "ctx", axis=1, tiled=True),
        lax.all_gather(context, "ctx", axis=1, tiled=True),
        lax.all_gather(normed_two, "ctx", axis=1, tiled=True),
        lax.all_gather(activation, "ctx", axis=1, tiled=True),
    )
    updated = []
    for total, piece, right in zip(initial, pieces, exchanged):
        updated.append(jnp.einsum("bsr,bsc->rc", piece, right, preferred_element_type=jnp.float32))
    column_grads = tuple(updated)
    gain_whole = lax.psum((grad_gain_one, grad_gain_two), "ctx")
    final_qkv, final_out, final_gate_up, final_down, final_gain_one, final_gain_two = (
        lax.psum_scatter(
            column_grads[0].astype(jnp.bfloat16), "dp", scatter_dimension=0, tiled=True
        ).astype(jnp.float32),
        lax.psum_scatter(
            column_grads[1].astype(jnp.bfloat16), "dp", scatter_dimension=0, tiled=True
        ).astype(jnp.float32),
        lax.psum_scatter(
            column_grads[2].astype(jnp.bfloat16), "dp", scatter_dimension=0, tiled=True
        ).astype(jnp.float32),
        lax.psum_scatter(
            column_grads[3].astype(jnp.bfloat16), "dp", scatter_dimension=0, tiled=True
        ).astype(jnp.float32),
        lax.psum_scatter(
            gain_whole[0].astype(jnp.bfloat16), "dp", scatter_dimension=0, tiled=True
        ).astype(jnp.float32),
        lax.psum_scatter(
            gain_whole[1].astype(jnp.bfloat16), "dp", scatter_dimension=0, tiled=True
        ).astype(jnp.float32),
    )
    return (
        output,
        grad_tokens,
        final_gain_one,
        final_qkv,
        final_out,
        final_gain_two,
        final_gate_up,
        final_down,
    )


MESH = pl.DeviceIdType.MESH


class Place:
    def __init__(self):
        self.dp = lax.axis_index("dp")
        self.ctx = lax.axis_index("ctx")
        self.z = lax.div(self.dp, 2)
        self.y = lax.rem(self.dp, 2)
        self.x = lax.div(self.ctx, 2)
        self.c = lax.rem(self.ctx, 2)
        self.up = (self.dp + 2, self.ctx)
        self.down = (self.dp - 2, self.ctx)
        self.across = (self.dp + 1 - 2 * self.y, self.ctx)
        self.chip = (self.dp, (1 - self.x) * 2 + self.c)
        self.core = (self.dp, self.x * 2 + 1 - self.c)
        self.has_up = self.z < 3
        self.has_down = self.z > 0


def greet(place):
    barrier = pltpu.get_barrier_semaphore()

    def tell(device):
        pl.semaphore_signal(barrier, inc=1, device_id=device, device_id_type=MESH)

    pl.when(place.has_up)(lambda: tell(place.up))
    pl.when(place.has_down)(lambda: tell(place.down))
    tell(place.across)
    for step in (1, 2, 3):
        tell((place.dp, lax.rem(place.ctx + step, 4)))
    ends = place.has_up.astype(jnp.int32) + place.has_down.astype(jnp.int32)
    pl.semaphore_wait(barrier, 4 + ends)


class Wires:
    def __init__(self, send_sems, recv_sems, names):
        self.send_sems = send_sems
        self.recv_sems = recv_sems
        self.index = names
        self.count = 0
        self.pending = []

    def slot(self, name):
        if name not in self.index:
            self.index[name] = len(self.index)
        return self.index[name]

    def send(self, src, dst, name, device, cond=None, extra=None):
        number = self.count
        self.count += 1
        at = self.slot(name)
        if extra is not None:
            at = at + extra
        copy = pltpu.make_async_remote_copy(
            src_ref=src,
            dst_ref=dst,
            send_sem=self.send_sems.at[number],
            recv_sem=self.recv_sems.at[at],
            device_id=device,
            device_id_type=MESH,
        )
        if cond is None:
            copy.start()
        else:
            pl.when(cond)(copy.start)
        self.pending.append((copy, cond, name))

    def take(self, dst, name, device, extra=None):
        at = self.slot(name)
        if extra is not None:
            at = at + extra
        pltpu.make_async_remote_copy(
            src_ref=dst,
            dst_ref=dst,
            send_sem=self.send_sems.at[0],
            recv_sem=self.recv_sems.at[at],
            device_id=device,
            device_id_type=MESH,
        ).wait_recv()

    def drain(self):
        for copy, cond, name in self.pending:
            when(cond, copy.wait_send)
        self.pending = []

    def drain_named(self, first):
        for copy, cond, name in self.pending:
            if name[0] == first:
                when(cond, copy.wait_send)
        self.pending = [entry for entry in self.pending if entry[2][0] != first]


BELOW, ABOVE = 0, 1


def both(first, second):
    return second if first is None else jnp.logical_and(first, second)


def source_valid(place, way, dist):
    return place.z >= dist if way == BELOW else place.z + dist <= 3


def source_pos(place, way, dist):
    return place.dp - 2 * dist if way == BELOW else place.dp + 2 * dist


def flood_start(wires, place, name, own, block, spread):
    wires.send(own, block(place.dp), (name, BELOW, 1), place.up, place.has_up)
    wires.send(own, block(place.dp), (name, ABOVE, 1), place.down, place.has_down)
    wires.send(own, block(place.dp), (name, "y", 0, 0), place.across)
    spread(own, place.dp, (0, 0, 0), None)


def flood_step(wires, place, name, block, spread, way, dist):
    here = source_valid(place, way, dist)
    pos = source_pos(place, way, dist)
    view = block(pos)
    came_from = place.down if way == BELOW else place.up
    pl.when(here)(lambda: wires.take(view, (name, way, dist), came_from))
    if dist < 3:
        onward = place.up if way == BELOW else place.down
        more = place.has_up if way == BELOW else place.has_down
        wires.send(view, view, (name, way, dist + 1), onward, jnp.logical_and(here, more))
    wires.send(view, view, (name, "y", way, dist), place.across, here)
    spread(view, pos, (0, way, dist), here)


def flood_side(wires, place, name, block, spread, way, dist):
    if dist == 0:
        here, pos = None, place.dp
    else:
        here, pos = source_valid(place, way, dist), source_pos(place, way, dist)
    pos = pos + 1 - 2 * place.y
    view = block(pos)
    if here is None:
        wires.take(view, (name, "y", 0, 0), place.across)
    else:
        pl.when(here)(lambda: wires.take(view, (name, "y", way, dist), place.across))
    spread(view, pos, (1, way, dist), here)


HOPS = [(way, dist) for dist in (1, 2, 3) for way in (BELOW, ABOVE)]


def no_spread(view, pos, key, cond):
    return None


def add_rows(dst, srcs, out=None, cast=None, chunk=48):
    out = dst if out is None else out
    total_rows = dst.shape[0]
    assert total_rows % chunk == 0

    def body(i, carry):
        at = pl.ds(pl.multiple_of(i * chunk, 16), chunk)
        total = dst[at, :].astype(jnp.float32)
        for src in srcs:
            total = total + src[at, :].astype(jnp.float32)
        out[at, :] = total.astype(out.dtype)
        return carry

    lax.fori_loop(0, total_rows // chunk, body, 0)


def when(cond, action):
    if cond is None:
        action()
    else:
        pl.when(cond)(action)


DRAIN = [(way, dist) for dist in (3, 2, 1, 0) for way in (BELOW, ABOVE)]


def nn(a, b):
    return jnp.dot(a, b, preferred_element_type=jnp.float32)


def nt(a, b):
    return lax.dot_general(a, b, (((1,), (1,)), ((), ())), preferred_element_type=jnp.float32)


def tn(a, b):
    return lax.dot_general(a, b, (((0,), (0,)), ((), ())), preferred_element_type=jnp.float32)


def layer_kernel(
    names,
    tokens, cot, lengths, qkv_in, out_in, gu_in, dt_in, gain_one, gain_two, cos_table, sin_table,
    output, grad_tokens, gain_out, qkv_out, out_out, gu_out, dt_out,
    w_qkv, w_out, w_ff, d_qkv, d_out, d_ff, gain_all, gain_row, cos, sin,
    tok_all, n1_all, n2_all, g_all, ctx_all, hidden, grad_hidden, proj, q_st, kv_all, p_st, att, go_st,
    wide, gm, pq, pq_in, gb_all, gm_all, act, d_gu, gp, gp_box, op, op_box, dkv, dkv_box,
    qkv_side, out_side, gu_side_a, gu_side_b, down_side, qkv_inbox, out_inbox, gu_inbox_a, gu_inbox_b, down_inbox,
    up_inbox, up_side, gu_mix, down_mix, gain_box, gain_acc,
    send_sems, recv_sems, local_sems,
):
    f32, low = jnp.float32, jnp.bfloat16
    place = Place()
    wires = Wires(send_sems, recv_sems, names)
    dp, ctx, z, y, x, c = place.dp, place.ctx, place.z, place.y, place.x, place.c
    rows = qkv_in.shape[0]
    strip, half = dt_in.shape
    width = tokens.shape[1]
    own_rows = tokens.shape[0]
    slots_here = own_rows // 2
    qkv_cols, out_cols = qkv_in.shape[1], out_in.shape[1]
    qkv_wide, out_wide = w_qkv.shape[1], w_out.shape[2]
    group = QH // KVH
    slabs = KVH // 2
    q_slabs = QH // 2
    span = 3 * half
    deep = w_ff.shape[0]
    score_scale = 1.0 / math.sqrt(HD)
    TILES = range(2)

    greet(place)

    def block_rows(pos):
        return pl.ds(pl.multiple_of(pos * rows, 16), rows)

    def lead_rows(lead):
        return pl.ds(pl.multiple_of(lead * own_rows, 16), own_rows)

    here_rows = lead_rows(ctx)
    my_rows = block_rows(dp)

    def share(name, ref):
        mine = ref.at[here_rows]
        wires.send(mine, mine, (name, "x"), place.chip)
        wires.send(mine, mine, (name, "c"), place.core)

    def share_on(name, ref):
        far = ref.at[lead_rows(place.chip[1])]
        wires.take(far, (name, "x"), place.chip)
        wires.send(far, far, (name, "d"), place.core)

    def share_end(name, ref):
        for mark, lead in (("c", place.core[1]), ("d", 3 - ctx)):
            wires.take(ref.at[lead_rows(lead)], (name, mark), place.core)

    def swap_start(name, src, dst):
        for step in (1, 2, 3):
            peer = lax.rem(ctx + step, 4)
            wires.send(src(peer), dst(ctx), (name, step), (dp, peer))

    def swap_end(name, dst):
        for step in (1, 2, 3):
            peer = lax.rem(ctx + 4 - step, 4)
            wires.take(dst(peer), (name, step), (dp, peer))

    locals_ = []

    def local(src, dst, cond=None):
        copy = pltpu.make_async_copy(src, dst, local_sems.at[len(locals_)])
        locals_.append((copy, cond))
        when(cond, copy.start)

    SIDES = [(0, 0)] + HOPS
    WAYS = {0: [(0, 0)], 1: HOPS[:2], 2: HOPS[2:4], 3: HOPS[4:]}

    class Flood:
        def __init__(self, name, block, spread=no_spread):
            self.name, self.block, self.spread = name, block, spread

        def start(self):
            flood_start(wires, place, self.name, self.block(dp), self.block, self.spread)

        def hop(self, dist):
            for way, dist in WAYS[dist]:
                flood_step(wires, place, self.name, self.block, self.spread, way, dist)

        def side(self, dist):
            for way, dist in WAYS[dist]:
                flood_side(wires, place, self.name, self.block, self.spread, way, dist)

    class PairFlood:
        def __init__(self, name, ref, cols):
            self.name, self.ref, self.cols = name, ref, cols

        def pair(self, plane):
            return self.ref.at[pl.ds(pl.multiple_of(2 * rows * plane, 16), 2 * rows), self.cols]

        def one(self, pos):
            return self.ref.at[block_rows(pos), self.cols]

        def start(self):
            wires.send(self.one(dp), self.one(dp), (self.name, "y"), place.across)

        def side(self):
            wires.take(self.one(place.across[0]), (self.name, "y"), place.across)
            view = self.pair(z)
            wires.send(view, view, (self.name, BELOW, 1), place.up, place.has_up)
            wires.send(view, view, (self.name, ABOVE, 1), place.down, place.has_down)

        def hop(self, dist):
            for way, dist in WAYS[dist]:
                here = source_valid(place, way, dist)
                view = self.pair(z - dist if way == BELOW else z + dist)
                came_from = place.down if way == BELOW else place.up
                pl.when(here)(lambda: wires.take(view, (self.name, way, dist), came_from))
                if dist < 3:
                    onward = place.up if way == BELOW else place.down
                    more = place.has_up if way == BELOW else place.has_down
                    wires.send(view, view, (self.name, way, dist + 1), onward, jnp.logical_and(here, more))

    def out_block(lead, pos):
        return w_out.at[lead, block_rows(pos)]

    def out_spread(view, pos, key, cond):
        wires.send(view, out_block(ctx, pos), ("out", "x") + key, place.chip, cond)
        wires.send(view, out_block(ctx, pos), ("out", "c") + key, place.core, cond)

    qkv_flood = Flood("qkv", lambda pos: w_qkv.at[block_rows(pos)])
    gain_flood = Flood("gain", lambda pos: gain_all.at[pos])
    out_flood = Flood("out", functools.partial(out_block, ctx), out_spread)

    GU_WIDTH = (2 * half, half)
    up_cols = pl.ds(span + half, half)

    def gu_view(ref, tile, pos):
        return ref.at[block_rows(pos), pl.ds(tile * span, GU_WIDTH[tile])]

    gu_floods = [Flood(("gu", tile), functools.partial(gu_view, w_ff, tile)) for tile in TILES]
    up_flood = PairFlood("up", w_ff, up_cols)

    def spots(column, dist):
        for way, dist in WAYS[dist]:
            if dist == 0:
                here, pos = None, dp
            else:
                here, pos = source_valid(place, way, dist), source_pos(place, way, dist)
            if column == 1:
                pos = pos + 1 - 2 * y
            yield (column, way, dist), here, pos

    def out_chip(column, dist):
        for key, here, pos in spots(column, dist):
            view = out_block(place.chip[1], pos)
            when(here, lambda: wires.take(view, ("out", "x") + key, place.chip))
            wires.send(view, view, ("out", "d") + key, place.core, here)

    def out_core():
        for column in range(2):
            for dist in range(4):
                for key, here, pos in spots(column, dist):
                    for mark, lead in (("c", place.core[1]), ("d", 3 - ctx)):
                        view = out_block(lead, pos)
                        when(here, lambda: wires.take(view, ("out", mark) + key, place.core))

    def mix_start(tile):
        for part in range(2):
            target = 2 * c + part
            src = gu_in.at[:, pl.ds((2 * part + tile) * half, half)]
            dst = w_ff.at[my_rows, pl.ds(pl.multiple_of(tile * span + x * half, 128), half)]
            wires.send(src, dst, ("gu_mix", tile, 0), (dp, target), target != ctx, extra=x)
            local(src, dst, target == ctx)
        wires.slot(("gu_mix", tile, 1))

    def mix_end(tile):
        for part in range(2):
            origin = part * 2 + x
            view = w_ff.at[my_rows, pl.ds(tile * span + part * half, half)]
            pl.when(origin != ctx)(lambda: wires.take(view, ("gu_mix", tile, part), (dp, origin)))

    lanes = pl.ds(pl.multiple_of(y * span + 2 * half, 128), half)
    other_lanes = pl.ds(pl.multiple_of((1 - y) * span + 2 * half, 128), half)
    at_home = ctx == z

    def strips_of(ref, at):
        return [ref.at[pl.ds(j * strip, strip), at] for j in range(4)]

    strips, other_strips = strips_of(w_ff, lanes), strips_of(w_ff, other_lanes)

    def down_mix_start():
        dst = w_ff.at[pl.ds(pl.multiple_of(ctx * strip, 16), strip), lanes]
        wires.send(dt_in, dst, ("down_mix", 0), (dp, z), ctx != z, extra=ctx)
        for j in range(1, 4):
            wires.slot(("down_mix", j))
        local(dt_in, dst, ctx == z)

    def tables():
        for table, ref in ((cos_table, cos), (sin_table, sin)):
            mine = table[pl.ds(pl.multiple_of(ctx * slots_here, 16), slots_here), :]
            ref[:slots_here, :] = mine
            ref[slots_here:, :] = mine

    def down_start():
        def take_strips():
            for j in range(4):
                pl.when(ctx != j)(functools.partial(wires.take, strips[j], ("down_mix", j), (dp, j)))

        pl.when(at_home)(take_strips)
        for j in range(4):
            wires.send(strips[j], strips[j], ("down", j, BELOW, 1), place.up, jnp.logical_and(at_home, place.has_up))
            wires.send(strips[j], strips[j], ("down", j, ABOVE, 1), place.down, jnp.logical_and(at_home, place.has_down))
            wires.send(strips[j], strips[j], ("down_y", j, 0, 0), place.across, at_home)

    def down_hop(dist):
        for way in (BELOW, ABOVE):
            here = (z - ctx if way == BELOW else ctx - z) == dist
            came_from = place.down if way == BELOW else place.up
            onward = place.up if way == BELOW else place.down
            more = place.has_up if way == BELOW else place.has_down
            for j in range(4):
                pl.when(here)(functools.partial(wires.take, strips[j], ("down", j, way, dist), came_from))
                if dist < 3:
                    wires.send(strips[j], strips[j], ("down", j, way, dist + 1), onward, jnp.logical_and(here, more))
                wires.send(strips[j], strips[j], ("down_y", j, way, dist), place.across, here)

    def down_side_end():
        for way, dist in SIDES:
            here = at_home if dist == 0 else (z - ctx if way == BELOW else ctx - z) == dist

            def take():
                for j in range(4):
                    wires.take(other_strips[j], ("down_y", j, way, dist), place.across)

            pl.when(here)(take)

    row_at = lax.broadcasted_iota(jnp.int32, (own_rows, 1), 0)
    first_seq = row_at < slots_here
    position = ctx * slots_here + jnp.where(first_seq, row_at, row_at - slots_here)
    valid = position < jnp.where(first_seq, lengths[0], lengths[1])
    def tokens_start():
        tok_all[here_rows, :] = tokens[...]
        share("tok", tok_all)

    def qkv_start():
        w_qkv[my_rows, :] = jnp.zeros((rows, qkv_wide), low)
        w_qkv[my_rows, :qkv_cols] = qkv_in[...]
        qkv_flood.start()

    def gain_start():
        gain_all[dp] = jnp.zeros(gain_all.shape[1:], f32)
        gain_all[dp, 0:1, :rows] = gain_one[...].reshape(1, rows).astype(f32)
        gain_all[dp, 1:2, :rows] = gain_two[...].reshape(1, rows).astype(f32)
        gain_flood.start()

    def out_start():
        w_out[ctx, my_rows, :] = jnp.zeros((rows, out_wide), low)
        w_out[ctx, my_rows, :out_cols] = out_in[...]
        out_flood.start()

    def cot_start():
        g_all[here_rows, :] = jnp.where(valid, cot[...].astype(f32), 0.0).astype(low)
        share("cot", g_all)

    def gain_sides():
        for dist in range(4):
            gain_flood.side(dist)

    gain_a = lambda: gain_row[0:1, :width]
    gain_b = lambda: gain_row[1:2, :width]

    def norm(values):
        return lax.rsqrt(jnp.mean(values * values, axis=-1, keepdims=True) + EPS)

    lane = lax.broadcasted_iota(jnp.int32, (own_rows, 128), 1)
    low_half = lax.rem(lane, HD) < HD // 2
    side_of = lax.div(lane, HD)

    def turn(values, sign):
        swapped = jnp.where(low_half, pltpu.roll(values, 128 - HD // 2, 1), pltpu.roll(values, HD // 2, 1))
        return values * cos[...] + swapped * (sin[...] * sign)

    def head_spots():
        for head in range(QH):
            kv = head // group
            yield head // 2, head % 2, kv // 2, kv % 2, (kv % 2 * group + head % group) * slots_here

    def stack_heads(slab_of, dest, scale):
        for slab, side, key_slab, key_side, at in head_spots():
            values = slab_of(slab)
            if side != key_side:
                values = pltpu.roll(values, HD, 1)
            values = (jnp.where(side_of == key_side, values, 0.0) * scale).astype(low)
            for seq in range(2):
                dest[seq * slabs + key_slab, at : at + slots_here, :] = values[
                    seq * slots_here : (seq + 1) * slots_here
                ]

    def unstack_heads(src, slab):
        total = jnp.zeros((own_rows, 128), f32)
        for at_slab, side, key_slab, key_side, at in head_spots():
            if at_slab != slab:
                continue
            values = jnp.concatenate(
                [src[seq * slabs + key_slab, at : at + slots_here, :] for seq in range(2)], axis=0
            )
            values = jnp.where(side_of == key_side, values, 0.0)
            if side != key_side:
                values = pltpu.roll(values, HD, 1)
            total = total + values
        return total

    def project():
        gain_row[...] = jnp.zeros(gain_row.shape, f32)
        for pos in range(8):
            piece = gain_all[pos]
            shift = (pos * rows) % 128
            if shift:
                piece = pltpu.roll(piece, shift, 1)
            at = (pos * rows) // 128 * 128
            gain_row[:, at : at + 256] += piece

        def body(i, carry):
            at = lead_rows(i)
            source = tok_all[at, :].astype(f32)
            n1_all[at, :] = (source * norm(source) * gain_a()).astype(low)
            pq[i] = nn(n1_all[at, :], w_qkv[...])
            return carry

        lax.fori_loop(0, 4, body, 0)
        pq_in[ctx] = pq[ctx]
        swap_start("pq", lambda peer: pq.at[peer], lambda sender: pq_in.at[sender])

    def pq_end():
        swap_end("pq", lambda sender: pq_in.at[sender])
        proj[...] = jnp.zeros(proj.shape, f32)
        for j in range(4):
            part = jnp.concatenate([pq_in[j], jnp.zeros((own_rows, 128), f32)], axis=1)
            at = qkv_cols * j
            if at % 128:
                part = pltpu.roll(part, at % 128, 1)
            proj[:, at // 128 * 128 : at // 128 * 128 + qkv_wide + 128] += part

    turned = {}

    def query_slab(slab):
        if slab not in turned:
            turned[slab] = turn(proj[:, slab * 128 : slab * 128 + 128], 1.0)
        return turned[slab]

    def slot_view(lead):
        return kv_all.at[:, :, pl.ds(pl.multiple_of(lead * slots_here, 16), slots_here)]

    def kv_start():
        my_slots = pl.ds(pl.multiple_of(ctx * slots_here, 16), slots_here)
        for slab in range(2 * slabs):
            at = (q_slabs + slab) * 128
            values = proj[:, at : at + 128]
            if slab < slabs:
                values = turn(values, 1.0)
            values = values.astype(low)
            for seq in range(2):
                kv_all[seq, slab, my_slots, :] = values[seq * slots_here : (seq + 1) * slots_here]

        swap_start("kv", lambda peer: slot_view(ctx), slot_view)

    def queries():
        stack_heads(query_slab, q_st, score_scale)

    def kv_end():
        swap_end("kv", slot_view)

    stack = q_st.shape[1]
    slots = kv_all.shape[2]

    def attend(i, carry):
        seq, slab = lax.div(i, slabs), lax.rem(i, slabs)
        scores = nt(q_st[i], kv_all[seq, slab])
        at = ctx * slots_here + lax.rem(lax.broadcasted_iota(jnp.int32, (stack, slots), 0), slots_here)
        key_at = lax.broadcasted_iota(jnp.int32, (stack, slots), 1)
        length = jnp.where(seq == 0, lengths[0], lengths[1])
        allowed = jnp.logical_and(key_at <= at, key_at < length)
        scores = jnp.where(allowed, scores, NEGATIVE)
        terms = jnp.exp(scores - jnp.max(scores, axis=-1, keepdims=True))
        probs = (terms / jnp.sum(terms, axis=-1, keepdims=True)).astype(low)
        p_st[i] = probs
        att[i] = nn(probs, kv_all[seq, slabs + slab])
        return carry

    def attention():
        lax.fori_loop(0, 2 * slabs, attend, 0)
        for slab in range(q_slabs):
            ctx_all[here_rows, slab * 128 : slab * 128 + 128] = unstack_heads(att, slab).astype(low)
        share("ctx", ctx_all)

    def out_project():
        hidden[...] = tokens[...].astype(f32)
        for j in range(4):
            part = nn(ctx_all[here_rows, :], w_out[j])
            at = out_cols * j
            if at % 128:
                part = pltpu.roll(part, at % 128, 1)
            hidden[:, at // 128 * 128 : at // 128 * 128 + out_wide] += part
        n2_all[here_rows, :] = (hidden[...] * norm(hidden[...]) * gain_b()).astype(low)
        share("n2", n2_all)

    tall = 2 * own_rows

    def feed(tile):
        def body(i, carry):
            at = pl.ds(pl.multiple_of(i * tall, tall), tall)
            gate = nn(n2_all[at, :], w_ff[:, tile * span : tile * span + half])
            up = nn(n2_all[at, :], w_ff[:, tile * span + half : tile * span + 2 * half])
            back = nn(g_all[at, :], w_ff[:, tile * span + 2 * half : (tile + 1) * span])
            sig = jax.nn.sigmoid(gate)
            swish = gate * sig
            act[tile, at, :] = (swish * up).astype(low)
            d_gu[tile, at, :half] = (back * up * sig * (1.0 + gate * (1.0 - sig))).astype(low)
            d_gu[tile, at, half:] = (back * swish).astype(low)
            return carry

        lax.fori_loop(0, 4 * own_rows // tall, body, 0)

    def grad_ff(tile):
        def body(m, carry):
            at = pl.ds(pl.multiple_of(m * 128, 128), 128)
            d_ff[at, tile * span : tile * span + 2 * half] = tn(n2_all[:, at], d_gu[tile]).astype(low)
            d_ff[at, tile * span + 2 * half : (tile + 1) * span] = tn(g_all[:, at], act[tile]).astype(low)
            return carry

        lax.fori_loop(0, width // 128, body, 0)

    across_core = (1 - x) * 2 + 1 - c
    across_own = (1 - x) * 2 + c
    beside = x * 2 + 1 - c
    wide_tile = 384

    def group_send(name, ref, box, which):
        lead, mark = ((across_core, "cx"), (beside, "cc"))[which]
        wires.send(ref.at[lead], box.at[which], (name, mark), place.core)

    def group_on(name, ref, box):
        wires.take(box.at[0], (name, "cx"), place.core)
        mine = ref.at[across_own]
        mine[...] = (mine[...].astype(f32) + box[0].astype(f32)).astype(low)
        wires.send(mine, box.at[2], (name, "x"), place.chip)

    def group_end(name, ref, box):
        wires.take(box.at[1], (name, "cc"), place.core)
        wires.take(box.at[2], (name, "x"), place.chip)
        return ref[ctx].astype(f32) + box[1].astype(f32) + box[2].astype(f32)

    def pair_rows(half_x):
        return pl.ds(pl.multiple_of(half_x * tall, 16), tall)

    def group_product(ref, terms):
        def compute(half_x):
            def body(n, carry):
                at = pl.ds(pl.multiple_of(n * wide_tile, 128), wide_tile)
                total = None
                for left, right in terms:
                    term = nt(left(pair_rows(half_x)), right(at))
                    total = term if total is None else total + term
                ref[2 * half_x, :, at] = total[:own_rows].astype(low)
                ref[2 * half_x + 1, :, at] = total[own_rows:].astype(low)
                return carry

            lax.fori_loop(0, width // wide_tile, body, 0)

        return compute

    back_terms = [
        (lambda at, tile=tile: d_gu[tile, at, :], lambda at, tile=tile: w_ff[at, tile * span : tile * span + 2 * half])
        for tile in TILES
    ]
    forward_terms = [
        (lambda at, tile=tile: act[tile, at, :], lambda at, tile=tile: w_ff[at, tile * span + 2 * half : (tile + 1) * span])
        for tile in TILES
    ]

    def key_pos(way, dist):
        if dist == 0:
            return None, dp
        return source_valid(place, way, dist), source_pos(place, way, dist)

    KEYS = {3: DRAIN[:2], 2: DRAIN[2:4], 1: DRAIN[4:6], 0: [(BELOW, 0)]}
    flip = 1 - 2 * y

    def z_add(name, view, boxes, inbox, way, dist):
        here, pos = key_pos(way, dist)
        mine = view(pos)
        if dist == 0:
            wires.take(boxes.at[way, dist], (name, "y", way, dist), place.across)
            add_rows(mine, [boxes.at[way, dist]])
            for end, fed, feeder in ((BELOW, place.has_up, place.up), (ABOVE, place.has_down, place.down)):

                def own():
                    wires.take(inbox.at[end, 0], (name, "z", end, 0), feeder)
                    add_rows(mine, [inbox.at[end, 0]])

                pl.when(fed)(own)
            return
        fed = place.has_up if way == BELOW else place.has_down
        feeder = place.up if way == BELOW else place.down
        onward = place.down if way == BELOW else place.up
        side = boxes.at[way, dist]

        def first():
            wires.take(side, (name, "y", way, dist), place.across)
            add_rows(mine, [side])

        if dist == 3:
            pl.when(here)(first)
        else:

            def more():
                wires.take(side, (name, "y", way, dist), place.across)
                wires.take(inbox.at[way, dist], (name, "z", way, dist), feeder)
                add_rows(mine, [side, inbox.at[way, dist]])

            pl.when(jnp.logical_and(here, jnp.logical_not(fed)))(first)
            pl.when(jnp.logical_and(here, fed))(more)
        wires.send(mine, inbox.at[way, dist - 1], (name, "z", way, dist - 1), onward, here)

    class Sink:
        def __init__(self, name, view, side, inbox):
            self.name, self.view, self.side, self.inbox = name, view, side, inbox

        def send(self, dist):
            for way, dist in KEYS[dist]:
                here, pos = key_pos(way, dist)
                wires.send(
                    self.view(pos + flip), self.side.at[way, dist],
                    (self.name, "y", way, dist), place.across, here,
                )

        def send_all(self):
            for dist in (3, 2, 1, 0):
                self.send(dist)

        def add(self, dist):
            for way, dist in KEYS[dist]:
                z_add(self.name, self.view, self.side, self.inbox, way, dist)

    gu_sides, gu_inboxes = (gu_side_a, gu_side_b), (gu_inbox_a, gu_inbox_b)
    gu_sinks = [
        Sink(("dgu", tile), functools.partial(gu_view, d_ff, tile), gu_sides[tile], gu_inboxes[tile])
        for tile in TILES
    ]
    out_sink = Sink("dout", lambda pos: d_out.at[block_rows(pos)], out_side, out_inbox)
    qkv_sink = Sink("dqkv", lambda pos: d_qkv.at[block_rows(pos)], qkv_side, qkv_inbox)
    d_strips, d_other_strips = strips_of(d_ff, lanes), strips_of(d_ff, other_lanes)

    def down_send(tile):
        for j in range(4):
            wires.send(d_other_strips[j], down_side.at[j], ("ddown_y", j), place.across, (1 - y) == tile)

    def down_add(dist):
        if dist == 0:
            for j in range(4):

                def finish():
                    wires.take(down_side.at[j], ("ddown_y", j), place.across)
                    add_rows(d_strips[j], [down_side.at[j]])
                    for end, fed, feeder in ((BELOW, place.has_up, place.up), (ABOVE, place.has_down, place.down)):

                        def more():
                            wires.take(down_inbox.at[end, j], ("ddown", j, end, 0), feeder)
                            add_rows(d_strips[j], [down_inbox.at[end, j]])

                        pl.when(fed)(more)

                pl.when(at_home)(finish)
            return
        for way in (BELOW, ABOVE):
            here = (z - ctx if way == BELOW else ctx - z) == dist
            fed = place.has_up if way == BELOW else place.has_down
            feeder = place.up if way == BELOW else place.down
            onward = place.down if way == BELOW else place.up
            for j in range(4):

                def first():
                    wires.take(down_side.at[j], ("ddown_y", j), place.across)
                    add_rows(d_strips[j], [down_side.at[j]])

                def more():
                    wires.take(down_side.at[j], ("ddown_y", j), place.across)
                    wires.take(down_inbox.at[way, j], ("ddown", j, way, dist), feeder)
                    add_rows(d_strips[j], [down_side.at[j], down_inbox.at[way, j]])

                pl.when(jnp.logical_and(here, jnp.logical_not(fed)))(first)
                pl.when(jnp.logical_and(here, fed))(more)
                wires.send(d_strips[j], down_inbox.at[way, j], ("ddown", j, way, dist - 1), onward, here)

    class PairSink:
        def __init__(self, name, ref, cols, inbox, side):
            self.name, self.ref, self.cols, self.inbox, self.side = name, ref, cols, inbox, side

        def pair(self, plane):
            return self.ref.at[pl.ds(pl.multiple_of(2 * rows * plane, 16), 2 * rows), self.cols]

        def one(self, pos):
            return self.ref.at[block_rows(pos), self.cols]

        def add(self, dist):
            if dist == 0:
                mine = self.pair(z)
                for end, fed, feeder in ((BELOW, place.has_up, place.up), (ABOVE, place.has_down, place.down)):

                    def more():
                        wires.take(self.inbox.at[end, 0], (self.name, "z", end, 0), feeder)
                        add_rows(mine, [self.inbox.at[end, 0]])

                    pl.when(fed)(more)
                wires.send(self.one(place.across[0]), self.side, (self.name, "y"), place.across)
                return
            for way, dist in KEYS[dist]:
                here = source_valid(place, way, dist)
                mine = self.pair(z - dist if way == BELOW else z + dist)
                fed = place.has_up if way == BELOW else place.has_down
                feeder = place.up if way == BELOW else place.down
                onward = place.down if way == BELOW else place.up
                if dist < 3:

                    def more():
                        wires.take(self.inbox.at[way, dist], (self.name, "z", way, dist), feeder)
                        add_rows(mine, [self.inbox.at[way, dist]])

                    pl.when(jnp.logical_and(here, fed))(more)
                wires.send(mine, self.inbox.at[way, dist - 1], (self.name, "z", way, dist - 1), onward, here)

        def end(self):
            wires.take(self.side, (self.name, "y"), place.across)
            add_rows(self.one(dp), [self.side])

    up_sink = PairSink("dup", d_ff, up_cols, up_inbox, up_side)

    def gu_finish(tile):
        for part in range(2):
            target = part * 2 + x
            block = d_ff.at[my_rows, pl.ds(tile * span + part * half, half)]
            wires.send(block, gu_mix.at[c, tile], ("dgu_mix", tile, 0), (dp, target), target != ctx, extra=c)
            pl.when(target == ctx)(lambda: add_rows(block, [], out=gu_mix.at[c, tile]))
        wires.slot(("dgu_mix", tile, 1))

    def gu_end(tile):
        for part in range(2):
            origin = 2 * c + part
            box = gu_mix.at[part, tile]
            pl.when(origin != ctx)(lambda: wires.take(box, ("dgu_mix", tile, part), (dp, origin)))
            add_rows(box, [], out=gu_out.at[:, pl.ds((2 * part + tile) * half, half)])

    def down_finish():
        for j in range(4):
            wires.send(d_strips[j], down_mix, ("ddown_mix",), (dp, j), jnp.logical_and(at_home, ctx != j))
            pl.when(jnp.logical_and(at_home, ctx == j))(functools.partial(add_rows, d_strips[j], [], down_mix))

    def down_end():
        pl.when(ctx != z)(lambda: wires.take(down_mix, ("ddown_mix",), (dp, z)))
        add_rows(down_mix, [], out=dt_out)

    def norm_back(values, inverse, gain, grad_in):
        scaled = grad_in * gain
        mean_term = jnp.mean(scaled * values, axis=-1, keepdims=True)
        back = inverse * scaled - values * (inverse * inverse * inverse) * mean_term
        return back, jnp.sum(grad_in * values * inverse, axis=0, keepdims=True)

    def gp_block(which):
        half_x = 1 - x if which == 0 else x
        group_product(gp, back_terms)(half_x)
        group_send("gp", gp, gp_box, which)

    def op_block(which):
        half_x = 1 - x if which == 0 else x
        group_product(op, forward_terms)(half_x)
        group_send("op", op, op_box, which)

    def hidden_back():
        gain_acc[0] = jnp.zeros(gain_out.shape, f32)
        back_two, gain_two_grad = norm_back(hidden[...], norm(hidden[...]), gain_b(), group_end("gp", gp, gp_box))
        gain_acc[0, 1:2, :] = gain_two_grad
        grad_hidden[...] = g_all[here_rows, :].astype(f32) + back_two
        out_lane = lax.broadcasted_iota(jnp.int32, (own_rows, out_wide), 1)
        for j in range(4):
            at = out_cols * j
            part = grad_hidden[:, at // 128 * 128 : at // 128 * 128 + out_wide]
            if at % 128:
                part = pltpu.roll(part, out_wide - at % 128, 1)
            wide[j] = jnp.where(out_lane < out_cols, part, 0.0).astype(low)
        gb_all[here_rows, :] = wide[ctx]
        swap_start("gb", lambda peer: wide.at[peer], lambda sender: gb_all.at[lead_rows(sender)])

    def context_back(n, carry):
        at = pl.ds(pl.multiple_of(n * wide_tile, 128), wide_tile)
        total = nt(wide[0], w_out[0, at, :])
        for j in range(1, 4):
            total = total + nt(wide[j], w_out[j, at, :])
        proj[:, at] = total
        return carry

    def grad_context():
        lax.fori_loop(0, width // wide_tile, context_back, 0)
        stack_heads(lambda slab: proj[:, slab * 128 : slab * 128 + 128], go_st, 1.0)

    def attend_back(i, carry):
        seq, slab = lax.div(i, slabs), lax.rem(i, slabs)
        grad_probs = nt(go_st[i], kv_all[seq, slabs + slab])
        probs = p_st[i].astype(f32)
        delta = jnp.sum(probs * grad_probs, axis=-1, keepdims=True)
        grad_scores = (probs * (grad_probs - delta)).astype(low)
        att[i] = nn(grad_scores, kv_all[seq, slab]) * score_scale
        grad_key = tn(grad_scores, q_st[i])
        grad_value = tn(p_st[i], go_st[i])
        for j in range(4):
            part = slice(j * slots_here, (j + 1) * slots_here)
            dkv[j, seq, slab] = grad_key[part].astype(low)
            dkv[j, seq, slabs + slab] = grad_value[part].astype(low)
        return carry

    def attention_back():
        lax.fori_loop(0, 2 * slabs, attend_back, 0)
        group_send("dkv", dkv, dkv_box, 0)
        group_send("dkv", dkv, dkv_box, 1)

    def gb_end():
        swap_end("gb", lambda sender: gb_all.at[lead_rows(sender)])

    def grad_out(m, carry):
        at = pl.ds(pl.multiple_of(m * 128, 128), 128)
        d_out[at, :] = tn(ctx_all[:, at], gb_all[...]).astype(low)
        return carry

    def grad_out_all():
        lax.fori_loop(0, width // 128, grad_out, 0)

    def grad_mixed():
        sums = group_end("dkv", dkv, dkv_box)
        proj[...] = jnp.zeros(proj.shape, f32)
        for slab in range(q_slabs):
            proj[:, slab * 128 : slab * 128 + 128] = turn(unstack_heads(att, slab), -1.0)
        for slab in range(2 * slabs):
            values = jnp.concatenate([sums[0, slab], sums[1, slab]], axis=0)
            if slab < slabs:
                values = turn(values, -1.0)
            at = (q_slabs + slab) * 128
            proj[:, at : at + 128] = values
        qkv_lane = lax.broadcasted_iota(jnp.int32, (own_rows, qkv_wide), 1)
        for j in range(4):
            at = qkv_cols * j
            part = proj[:, at // 128 * 128 : at // 128 * 128 + qkv_wide + 128]
            if at % 128:
                part = pltpu.roll(part, qkv_wide + 128 - at % 128, 1)
            gm[j] = jnp.where(qkv_lane < qkv_cols, part[:, :qkv_wide], 0.0).astype(low)
        gm_all[here_rows, :] = gm[ctx]
        swap_start("gm", lambda peer: gm.at[peer], lambda sender: gm_all.at[lead_rows(sender)])

    def gm_end():
        swap_end("gm", lambda sender: gm_all.at[lead_rows(sender)])

    def grad_qkv(m, carry):
        at = pl.ds(pl.multiple_of(m * 128, 128), 128)
        d_qkv[at, :] = tn(n1_all[:, at], gm_all[...]).astype(low)
        return carry

    def grad_qkv_all():
        lax.fori_loop(0, width // 128, grad_qkv, 0)

    tokens_terms = [(lambda at: gm_all[at, :], lambda at: w_qkv[at, :])]

    def gt_block(which):
        if which == 0:
            wires.drain_named("gp")
        half_x = 1 - x if which == 0 else x
        group_product(gp, tokens_terms)(half_x)
        group_send("gt", gp, gp_box, which)

    def output_end():
        result = hidden[...] + group_end("op", op, op_box)
        output[...] = jnp.where(valid, result, 0.0).astype(low)

    def tokens_end():
        source = tokens[...].astype(f32)
        back_one, gain_one_grad = norm_back(source, norm(source), gain_a(), group_end("gt", gp, gp_box))
        gain_acc[0, 0:1, :] = gain_one_grad
        grad_tokens[...] = (grad_hidden[...] + back_one).astype(low)

    low_end, high_end = z == 0, z == 3
    mid_low, mid_high = z == 1, z == 2

    def gain_send(hop):
        def go(device, cond=None):
            wires.send(gain_acc.at[hop], gain_box.at[hop], ("gain_sum", hop), device, cond)

        if hop < 3:
            go((place.core, place.chip, place.across)[hop])
        elif hop == 3:
            go(place.up, low_end)
            go(place.down, high_end)
        elif hop == 4:
            go(place.up, mid_low)
            go(place.down, mid_high)
        else:
            go(place.down, mid_low)
            go(place.up, mid_high)

    def gain_take(hop):
        def add(device):
            wires.take(gain_box.at[hop], ("gain_sum", hop), device)
            gain_acc[hop + 1] = gain_acc[hop] + gain_box[hop]

        def last(device):
            wires.take(gain_box.at[hop], ("gain_sum", hop), device)
            gain_out[...] = gain_box[hop]

        def done():
            gain_out[...] = gain_acc[hop]

        if hop < 3:
            add((place.core, place.chip, place.across)[hop])
        elif hop == 3:
            pl.when(mid_low)(lambda: add(place.down))
            pl.when(mid_high)(lambda: add(place.up))
        elif hop == 4:
            pl.when(mid_low)(lambda: add(place.up))
            pl.when(mid_high)(lambda: add(place.down))
        else:
            pl.when(low_end)(lambda: last(place.up))
            pl.when(high_end)(lambda: last(place.down))
            pl.when(mid_low)(done)
            pl.when(mid_high)(done)

    def out_end():
        out_out[...] = d_out[my_rows, :]

    def qkv_end():
        qkv_out[...] = d_qkv[my_rows, :]

    def locals_end():
        for copy, cond in locals_:
            when(cond, copy.wait)

    mix_start(0)
    qkv_start()
    out_start()
    tokens_start()
    out_chip(0, 0)
    qkv_flood.hop(1)
    down_mix_start()
    mix_start(1)
    tables()
    locals_end()
    mix_end(0)
    gu_floods[0].start()
    cot_start()
    gain_start()
    gain_flood.hop(1)
    out_flood.hop(1)
    gain_flood.hop(2)
    gain_flood.hop(3)
    qkv_flood.hop(2)
    qkv_flood.side(1)
    qkv_flood.hop(3)
    share_on("tok", tok_all)
    out_flood.side(0)
    down_start()
    out_flood.hop(2)
    qkv_flood.side(3)
    gain_sides()
    mix_end(1)
    up_flood.start()
    gu_floods[1].start()
    qkv_flood.side(0)
    qkv_flood.side(2)
    share_end("tok", tok_all)
    project()
    gu_floods[0].side(0)
    out_flood.hop(3)
    down_hop(1)
    share_on("cot", g_all)
    gu_floods[1].hop(1)
    share_end("cot", g_all)
    gu_floods[0].hop(1)
    out_chip(0, 2)
    out_chip(0, 1)
    pq_end()
    kv_start()
    out_flood.side(1)
    down_hop(2)
    out_flood.side(3)
    queries()
    down_hop(3)
    out_flood.side(2)
    kv_end()
    up_flood.side()
    attention()
    gu_floods[1].side(1)
    out_chip(1, 2)
    gu_floods[0].hop(2)
    out_chip(1, 0)
    out_chip(0, 3)
    out_chip(1, 1)
    out_chip(1, 3)
    out_core()
    out_project()
    up_flood.hop(1)
    gu_floods[0].side(1)
    gu_floods[0].hop(3)
    down_side_end()
    gu_floods[1].hop(2)
    share_on("n2", n2_all)
    up_flood.hop(2)
    gu_floods[1].side(0)
    gu_floods[0].side(2)
    gu_floods[0].side(3)
    share_end("n2", n2_all)
    feed(0)
    gu_floods[1].hop(3)
    grad_ff(0)
    gu_sinks[0].send(3)
    gu_sinks[0].send(2)
    gu_floods[1].side(3)
    gu_floods[1].side(2)
    up_flood.hop(3)
    feed(1)
    grad_ff(1)
    up_sink.add(3)
    gu_sinks[1].send(3)
    down_send(1)
    down_send(0)
    gu_sinks[0].send(1)
    gu_sinks[1].send(2)
    gu_sinks[0].add(3)
    gu_sinks[1].send(0)
    gp_block(0)
    share_on("ctx", ctx_all)
    group_on("gp", gp, gp_box)
    gu_sinks[0].send(0)
    op_block(1)
    op_block(0)
    up_sink.add(2)
    gp_block(1)
    gu_sinks[1].add(3)
    gu_sinks[0].add(2)
    hidden_back()
    grad_context()
    attention_back()
    up_sink.add(1)
    group_on("dkv", dkv, dkv_box)
    gb_end()
    share_end("ctx", ctx_all)
    grad_out_all()
    gu_sinks[1].send(1)
    out_sink.send(3)
    down_add(3)
    grad_mixed()
    gu_sinks[0].add(1)
    down_add(2)
    out_sink.send(1)
    group_on("op", op, op_box)
    gu_sinks[1].add(2)
    gm_end()
    gt_block(0)
    gt_block(1)
    up_sink.add(0)
    grad_qkv_all()
    qkv_sink.send(3)
    out_sink.send(2)
    group_on("gt", gp, gp_box)
    qkv_sink.send(2)
    down_add(1)
    gu_sinks[0].add(0)
    gu_finish(0)
    tokens_end()
    gain_send(0)
    gain_take(0)
    gu_sinks[1].add(1)
    gain_send(1)
    gain_take(1)
    out_sink.add(3)
    gain_send(2)
    qkv_sink.send(1)
    qkv_sink.add(3)
    out_sink.add(2)
    qkv_sink.add(2)
    down_add(0)
    down_finish()
    gain_take(2)
    gu_sinks[1].add(0)
    out_sink.send(0)
    qkv_sink.send(0)
    output_end()
    up_sink.end()
    gain_send(3)
    out_sink.add(1)
    gain_take(3)
    gu_finish(1)
    gain_send(4)
    qkv_sink.add(1)
    out_sink.add(0)
    gain_take(4)
    gain_send(5)
    out_end()
    gu_end(0)
    down_end()
    gu_end(1)
    qkv_sink.add(0)
    qkv_end()
    gain_take(5)
    wires.drain()


def finish_kernel(
    output, grad_tokens, gains, qkv, out, gu, down_t,
    output_end, grad_tokens_end, qkv_end, out_end, gu_end, down_end, one_end, two_end,
):
    f32 = jnp.float32
    output_end[...] = output[...]
    grad_tokens_end[...] = grad_tokens[...]
    qkv_end[...] = qkv[:, : qkv_end.shape[1]].astype(f32)
    out_end[...] = out[:, : out_end.shape[1]].astype(f32)
    gu_end[...] = gu[...].astype(f32)
    down_end[...] = down_t[...].astype(f32)
    block = one_end.shape[0]
    width = gains.shape[1]
    start = lax.axis_index("dp") * block
    mine = pltpu.roll(gains[...], lax.rem(width - start, width), 1)
    one_end[...] = mine[0, :block]
    two_end[...] = mine[1, :block]


def on_device_fast(tokens, lengths, gain_one, w_qkv, w_out, gain_two, w_gate_up, w_down, cotangent):
    seq_count, row_count, width = tokens.shape
    own_rows = seq_count * row_count
    f32, low = jnp.float32, jnp.bfloat16
    block = gain_one.shape[0]
    slots = 4 * row_count
    place_of = np.arange(slots, dtype=np.float32)
    frequency = np.float32(10000.0) ** (-np.arange(HD // 2, dtype=np.float32) * np.float32(2.0 / HD))
    angle = place_of[:, None] * frequency[None, :]
    cosine = np.tile(np.cos(angle), (1, 4))
    sine = np.tile(np.concatenate([-np.sin(angle), np.sin(angle)], axis=1), (1, 2))
    rows, qkv_cols = w_qkv.shape
    out_cols = w_out.shape[1]
    units = w_gate_up.shape[1] // 2
    half, strip = w_down.shape
    qkv_wide = -(-qkv_cols // 128) * 128
    out_wide = -(-out_cols // 128) * 128
    deep = 8 * rows
    slabs = KVH // 2
    stack = 2 * QH // KVH * row_count

    def box(*shape, dtype=low):
        return pltpu.VMEM(shape, dtype)

    scratch = [
        box(deep, qkv_wide), box(4, deep, out_wide), box(deep, 3 * units),
        box(deep, qkv_wide), box(deep, out_wide), box(deep, 3 * units),
        box(8, 8, 256, dtype=f32), box(8, deep + 128, dtype=f32),
        box(own_rows, 128, dtype=f32), box(own_rows, 128, dtype=f32),
        box(4 * own_rows, width), box(4 * own_rows, width), box(4 * own_rows, width),
        box(4 * own_rows, width), box(4 * own_rows, QH * HD),
        box(own_rows, width, dtype=f32), box(own_rows, width, dtype=f32),
        box(own_rows, 4 * qkv_wide, dtype=f32),
        box(seq_count * slabs, stack, 128), box(seq_count, 2 * slabs, slots, 128),
        box(seq_count * slabs, stack, slots), box(seq_count * slabs, stack, 128, dtype=f32),
        box(seq_count * slabs, stack, 128),
        box(4, own_rows, out_wide), box(4, own_rows, qkv_wide),
        box(4, own_rows, qkv_wide, dtype=f32), box(4, own_rows, qkv_wide, dtype=f32),
        box(4 * own_rows, out_wide), box(4 * own_rows, qkv_wide),
        box(2, 4 * own_rows, half), box(2, 4 * own_rows, 2 * half),
        box(4, own_rows, width), box(3, own_rows, width),
        box(4, own_rows, width), box(3, own_rows, width),
        box(4, seq_count, 2 * slabs, row_count, 128), box(3, seq_count, 2 * slabs, row_count, 128),
        box(2, 4, rows, qkv_wide), box(2, 4, rows, out_wide),
        box(2, 4, rows, 2 * half), box(2, 4, rows, half), box(4, strip, half),
        box(2, 3, rows, qkv_wide), box(2, 3, rows, out_wide),
        box(2, 3, rows, 2 * half), box(2, 3, rows, half), box(2, 4, strip, half),
        box(2, 3, 2 * rows, half), box(rows, half),
        box(2, 2, rows, half), box(strip, half),
        box(6, 8, width, dtype=f32), box(6, 8, width, dtype=f32),
        pltpu.SemaphoreType.DMA((400,)),
        pltpu.SemaphoreType.DMA((400,)),
        pltpu.SemaphoreType.DMA((8,)),
    ]
    vmem = pl.BlockSpec(memory_space=pltpu.MemorySpace.VMEM)
    smem = pl.BlockSpec(memory_space=pltpu.MemorySpace.SMEM)
    shapes = (
        jax.ShapeDtypeStruct((own_rows, width), low),
        jax.ShapeDtypeStruct((own_rows, width), low),
        jax.ShapeDtypeStruct((8, width), f32),
        jax.ShapeDtypeStruct((rows, qkv_wide), low),
        jax.ShapeDtypeStruct((rows, out_wide), low),
        jax.ShapeDtypeStruct((rows, 2 * units), low),
        jax.ShapeDtypeStruct((strip, half), low),
    )
    results = pl.pallas_call(
        functools.partial(layer_kernel, {}),
        out_shape=shapes,
        in_specs=[vmem, vmem, smem] + [vmem] * 8,
        out_specs=[vmem] * 7,
        scratch_shapes=scratch,
        compiler_params=pltpu.CompilerParams(
            collective_id=0, has_side_effects=True, vmem_limit_bytes=64 * 2**20
        ),
        name="layer",
    )(
        tokens.reshape(own_rows, width), cotangent.reshape(own_rows, width), lengths,
        w_qkv, w_out, w_gate_up, w_down.T, gain_one, gain_two,
        cosine, sine,
    )
    output, grad_tokens, final_qkv, final_out, final_gu, final_dt, one, two = pl.pallas_call(
        finish_kernel,
        out_shape=(
            jax.ShapeDtypeStruct((own_rows, width), low),
            jax.ShapeDtypeStruct((own_rows, width), low),
            jax.ShapeDtypeStruct((rows, qkv_cols), f32),
            jax.ShapeDtypeStruct((rows, out_cols), f32),
            jax.ShapeDtypeStruct((rows, 2 * units), f32),
            jax.ShapeDtypeStruct((strip, half), f32),
            jax.ShapeDtypeStruct((block,), f32),
            jax.ShapeDtypeStruct((block,), f32),
        ),
        in_specs=[vmem] * 7,
        out_specs=[vmem] * 8,
        name="finish",
    )(*results)
    return (
        output.reshape(tokens.shape), grad_tokens.reshape(tokens.shape),
        one, final_qkv, final_out, two, final_gu, final_dt.T,
    )


def solution(mesh):
    fits = mesh.shape["dp"] == 8 and mesh.shape["ctx"] == 4
    return jax.shard_map(
        on_device_fast if fits else on_device,
        mesh=mesh,
        in_specs=(
            P("dp", "ctx", None),
            P("dp"),
            P("dp"),
            P("dp", "ctx"),
            P("dp", "ctx"),
            P("dp"),
            P("dp", "ctx"),
            P("dp", "ctx"),
            P("dp", "ctx", None),
        ),
        out_specs=(
            P("dp", "ctx", None),
            P("dp", "ctx", None),
            P("dp"),
            P("dp", "ctx"),
            P("dp", "ctx"),
            P("dp"),
            P("dp", "ctx"),
            P("dp", "ctx"),
        ),
        check_vma=False,
    )
```

```python
import enum
import functools
import math

import jax
import jax.numpy as jnp
import numpy as np
from jax import lax
from jax.experimental import pallas as pl
from jax.experimental.pallas import tpu as pltpu
from jax.sharding import PartitionSpec as P

QH = 18
KVH = 6
HD = 64
FF = 3072


EPS = 1e-05
NEGATIVE = -1e30


def angles(position, head_width):
    frequency = 10000.0 ** (-jnp.arange(head_width // 2, dtype=jnp.float32) * 2.0 / head_width)
    angle_table = position.astype(jnp.float32)[:, None] * frequency[None, :]
    return (jnp.cos(angle_table), jnp.sin(angle_table))


def rotate(values_in, cosine, sine_table):
    half_width = values_in.shape[-1] // 2
    first_half = values_in[..., :half_width]
    second = values_in[..., half_width:]
    return jnp.concatenate(
        [first_half * cosine - second * sine_table, second * cosine + first_half * sine_table],
        axis=-1,
    )


def split_heads(values_in, head_count):
    seq_count, row_count, col_count = values_in.shape
    head_width = col_count // head_count
    moved = values_in.reshape(seq_count, row_count, head_count, head_width).transpose(0, 2, 1, 3)
    return moved.reshape(seq_count * head_count, row_count, head_width)


def join_heads(values_in, seq_count):
    item_count, row_count, head_width = values_in.shape
    head_count = item_count // seq_count
    moved = values_in.reshape(seq_count, head_count, row_count, head_width).transpose(0, 2, 1, 3)
    return moved.reshape(seq_count, row_count, head_count * head_width)


def norm_back(source, inverse, gain, grad_in):
    scaled = grad_in * gain
    mean_term = jnp.mean(scaled * source, axis=-1, keepdims=True)
    back_rows = inverse * scaled - source * (inverse * inverse * inverse) * mean_term
    return (back_rows, jnp.sum(grad_in * source * inverse, axis=(0, 1)))


def block_scores(query_rows, key_rows, position, length, group_count, score_scale):
    raw_scores = (
        jnp.einsum("nd,td->nt", query_rows, key_rows, preferred_element_type=jnp.float32)
        * score_scale
    )
    raw_scores = raw_scores.reshape(group_count, position.shape[0], key_rows.shape[0])
    keyidx = jnp.arange(key_rows.shape[0], dtype=jnp.int32)
    allowed = (keyidx[None, :] <= position[:, None]) & (keyidx[None, :] < length)
    return jnp.where(allowed[None], raw_scores, NEGATIVE)


def on_device(tokens, lengths, gain_one, w_qkv, w_out, gain_two, w_gate_up, w_down, cotangent):
    forward_wide = (
        lax.all_gather(w_qkv, "ctx", axis=1, tiled=True),
        lax.all_gather(w_out, "ctx", axis=1, tiled=True),
        lax.all_gather(w_gate_up, "ctx", axis=1, tiled=True),
        lax.all_gather(w_down, "ctx", axis=1, tiled=True),
    )
    qkv_full, out_full, gate_up_full, down_full, gain_fa, gain_fb = (
        lax.all_gather(forward_wide[0], "dp", axis=0, tiled=True),
        lax.all_gather(forward_wide[1], "dp", axis=0, tiled=True),
        lax.all_gather(forward_wide[2], "dp", axis=0, tiled=True),
        lax.all_gather(forward_wide[3], "dp", axis=0, tiled=True),
        lax.all_gather(gain_one, "dp", axis=0, tiled=True),
        lax.all_gather(gain_two, "dp", axis=0, tiled=True),
    )
    seq_count, row_count, model_width = tokens.shape
    query_cols = QH * HD
    key_cols = KVH * HD
    group_count = QH // KVH
    score_scale = 1.0 / math.sqrt(HD)
    position = lax.axis_index("ctx") * row_count + jnp.arange(row_count, dtype=jnp.int32)
    valid_rows = position[None, :] < lengths[:, None]
    cosine, sine_table = angles(position, HD)
    cosine = cosine[:, None, :]
    sine_table = sine_table[:, None, :]
    source = tokens.astype(jnp.float32)
    inverse_one = lax.rsqrt(jnp.mean(source * source, axis=-1, keepdims=True) + EPS)
    normed_one = (source * inverse_one * gain_fa.astype(jnp.float32)).astype(jnp.bfloat16)
    projected = jnp.einsum("bsd,de->bse", normed_one, qkv_full, preferred_element_type=jnp.float32)
    queries = rotate(
        projected[..., :query_cols].reshape(seq_count, row_count, QH, HD), cosine, sine_table
    )
    queries = queries.astype(jnp.bfloat16).reshape(seq_count, row_count, query_cols)
    key_heads = rotate(
        projected[..., query_cols : query_cols + key_cols].reshape(seq_count, row_count, KVH, HD),
        cosine,
        sine_table,
    )
    key_heads = key_heads.astype(jnp.bfloat16).reshape(seq_count, row_count, key_cols)
    value_heads = projected[..., query_cols + key_cols :].astype(jnp.bfloat16)
    keys_all, values_all = (
        lax.all_gather(key_heads, "ctx", axis=1, tiled=True),
        lax.all_gather(value_heads, "ctx", axis=1, tiled=True),
    )
    query_blocks = split_heads(queries, QH).reshape(seq_count * KVH, group_count * row_count, HD)
    key_blocks = split_heads(keys_all, KVH)
    value_blocks = split_heads(values_all, KVH)
    pair_lengths = jnp.repeat(lengths, KVH)

    def forward_block(block_in):
        query_rows, key_rows, value_rows, length = block_in
        scores = block_scores(query_rows, key_rows, position, length, group_count, score_scale)
        row_max = jnp.max(scores, axis=-1, keepdims=True)
        exp_terms = jnp.exp(scores - row_max)
        row_total = jnp.sum(exp_terms, axis=-1, keepdims=True)
        prob_rows = (exp_terms / row_total).astype(jnp.bfloat16)
        result = jnp.einsum(
            "gst,td->gsd", prob_rows, value_rows, preferred_element_type=jnp.float32
        )
        return (result.reshape(-1, HD), (row_max + jnp.log(row_total))[..., 0])

    context_blocks, log_totals = lax.map(
        forward_block, (query_blocks, key_blocks, value_blocks, pair_lengths)
    )
    context = join_heads(context_blocks.reshape(seq_count * QH, row_count, HD), seq_count).astype(
        jnp.bfloat16
    )
    hidden = source + jnp.einsum(
        "bse,ed->bsd", context, out_full, preferred_element_type=jnp.float32
    )
    inverse_two = lax.rsqrt(jnp.mean(hidden * hidden, axis=-1, keepdims=True) + EPS)
    normed_two = (hidden * inverse_two * gain_fb.astype(jnp.float32)).astype(jnp.bfloat16)
    gate_up = jnp.einsum(
        "bsd,df->bsf", normed_two, gate_up_full, preferred_element_type=jnp.float32
    )
    gate_part = gate_up[..., :FF]
    up_part = gate_up[..., FF:]
    gate_sig = jax.nn.sigmoid(gate_part)
    swish_part = gate_part * gate_sig
    activation = (swish_part * up_part).astype(jnp.bfloat16)
    result_rows = hidden + jnp.einsum(
        "bsf,fd->bsd", activation, down_full, preferred_element_type=jnp.float32
    )
    output = jnp.where(valid_rows[..., None], result_rows, 0.0).astype(jnp.bfloat16)
    back_wide = (
        lax.all_gather(w_qkv, "ctx", axis=1, tiled=True),
        lax.all_gather(w_out, "ctx", axis=1, tiled=True),
        lax.all_gather(w_gate_up, "ctx", axis=1, tiled=True),
        lax.all_gather(w_down, "ctx", axis=1, tiled=True),
    )
    qkv_back, out_back, gate_up_back, down_back, gain_ba, gain_bb = (
        lax.all_gather(back_wide[0], "dp", axis=0, tiled=True),
        lax.all_gather(back_wide[1], "dp", axis=0, tiled=True),
        lax.all_gather(back_wide[2], "dp", axis=0, tiled=True),
        lax.all_gather(back_wide[3], "dp", axis=0, tiled=True),
        lax.all_gather(gain_one, "dp", axis=0, tiled=True),
        lax.all_gather(gain_two, "dp", axis=0, tiled=True),
    )
    grad_rows = jnp.where(valid_rows[..., None], cotangent, jnp.zeros_like(cotangent))
    grad_activation = jnp.einsum(
        "bsd,fd->bsf", grad_rows, down_back, preferred_element_type=jnp.float32
    )
    grad_gate = grad_activation * up_part * gate_sig * (1.0 + gate_part * (1.0 - gate_sig))
    grad_up = grad_activation * swish_part
    grad_mix = jnp.concatenate([grad_gate, grad_up], axis=-1).astype(jnp.bfloat16)
    grad_normed_two = jnp.einsum(
        "bsf,df->bsd", grad_mix, gate_up_back, preferred_element_type=jnp.float32
    )
    back_two, grad_gain_two = norm_back(
        hidden, inverse_two, gain_bb.astype(jnp.float32), grad_normed_two
    )
    grad_hidden = grad_rows.astype(jnp.float32) + back_two
    grad_branch = grad_hidden.astype(jnp.bfloat16)
    grad_context = jnp.einsum(
        "bsd,ed->bse", grad_branch, out_back, preferred_element_type=jnp.float32
    ).astype(jnp.bfloat16)
    grad_blocks = split_heads(grad_context, QH).reshape(
        seq_count * KVH, group_count * row_count, HD
    )

    def backward_block(block_in):
        query_rows, key_rows, value_rows, length, log_total, grad_in = block_in
        scores = block_scores(query_rows, key_rows, position, length, group_count, score_scale)
        prob_rows = jnp.exp(scores - log_total[..., None])
        grad_grouped = grad_in.reshape(group_count, -1, HD)
        grad_probs = jnp.einsum(
            "gsd,td->gst", grad_grouped, value_rows, preferred_element_type=jnp.float32
        )
        grad_value = jnp.einsum(
            "gst,gsd->td",
            prob_rows.astype(jnp.bfloat16),
            grad_grouped,
            preferred_element_type=jnp.float32,
        )
        row_delta = jnp.sum(prob_rows * grad_probs, axis=-1, keepdims=True)
        grad_scores = (prob_rows * (grad_probs - row_delta)).astype(jnp.bfloat16)
        grad_query = (
            jnp.einsum("gst,td->gsd", grad_scores, key_rows, preferred_element_type=jnp.float32)
            * score_scale
        )
        grad_key = (
            jnp.einsum(
                "gst,gsd->td",
                grad_scores,
                query_rows.reshape(group_count, -1, HD),
                preferred_element_type=jnp.float32,
            )
            * score_scale
        )
        return (grad_query.reshape(-1, HD), grad_key, grad_value)

    query_grads, key_grads, value_grads = lax.map(
        backward_block,
        (query_blocks, key_blocks, value_blocks, pair_lengths, log_totals, grad_blocks),
    )
    key_sums, value_sums = (
        lax.psum_scatter(
            join_heads(key_grads, seq_count).astype(jnp.bfloat16),
            "ctx",
            scatter_dimension=1,
            tiled=True,
        ).astype(jnp.float32),
        lax.psum_scatter(
            join_heads(value_grads, seq_count).astype(jnp.bfloat16),
            "ctx",
            scatter_dimension=1,
            tiled=True,
        ).astype(jnp.float32),
    )
    grad_queries = join_heads(query_grads.reshape(seq_count * QH, row_count, HD), seq_count)
    turned_queries = rotate(grad_queries.reshape(seq_count, row_count, QH, HD), cosine, -sine_table)
    turned_keys = rotate(key_sums.reshape(seq_count, row_count, KVH, HD), cosine, -sine_table)
    grad_mixed = jnp.concatenate(
        [
            turned_queries.reshape(seq_count, row_count, query_cols),
            turned_keys.reshape(seq_count, row_count, key_cols),
            value_sums,
        ],
        axis=-1,
    ).astype(jnp.bfloat16)
    grad_normed_one = jnp.einsum(
        "bse,de->bsd", grad_mixed, qkv_back, preferred_element_type=jnp.float32
    )
    back_one, grad_gain_one = norm_back(
        source, inverse_one, gain_ba.astype(jnp.float32), grad_normed_one
    )
    grad_tokens = (grad_hidden + back_one).astype(jnp.bfloat16)
    exchanged = (
        lax.all_to_all(grad_mixed, "ctx", split_axis=2, concat_axis=1, tiled=True),
        lax.all_to_all(grad_branch, "ctx", split_axis=2, concat_axis=1, tiled=True),
        lax.all_to_all(grad_mix, "ctx", split_axis=2, concat_axis=1, tiled=True),
        lax.all_to_all(grad_rows, "ctx", split_axis=2, concat_axis=1, tiled=True),
    )
    initial = (
        jnp.zeros((model_width, exchanged[0].shape[2]), jnp.float32),
        jnp.zeros((context.shape[2], exchanged[1].shape[2]), jnp.float32),
        jnp.zeros((model_width, exchanged[2].shape[2]), jnp.float32),
        jnp.zeros((activation.shape[2], exchanged[3].shape[2]), jnp.float32),
    )
    pieces = (
        lax.all_gather(normed_one, "ctx", axis=1, tiled=True),
        lax.all_gather(context, "ctx", axis=1, tiled=True),
        lax.all_gather(normed_two, "ctx", axis=1, tiled=True),
        lax.all_gather(activation, "ctx", axis=1, tiled=True),
    )
    updated = []
    for total, piece, right in zip(initial, pieces, exchanged):
        updated.append(jnp.einsum("bsr,bsc->rc", piece, right, preferred_element_type=jnp.float32))
    column_grads = tuple(updated)
    gain_whole = lax.psum((grad_gain_one, grad_gain_two), "ctx")
    final_qkv, final_out, final_gate_up, final_down, final_gain_one, final_gain_two = (
        lax.psum_scatter(
            column_grads[0].astype(jnp.bfloat16), "dp", scatter_dimension=0, tiled=True
        ).astype(jnp.float32),
        lax.psum_scatter(
            column_grads[1].astype(jnp.bfloat16), "dp", scatter_dimension=0, tiled=True
        ).astype(jnp.float32),
        lax.psum_scatter(
            column_grads[2].astype(jnp.bfloat16), "dp", scatter_dimension=0, tiled=True
        ).astype(jnp.float32),
        lax.psum_scatter(
            column_grads[3].astype(jnp.bfloat16), "dp", scatter_dimension=0, tiled=True
        ).astype(jnp.float32),
        lax.psum_scatter(
            gain_whole[0].astype(jnp.bfloat16), "dp", scatter_dimension=0, tiled=True
        ).astype(jnp.float32),
        lax.psum_scatter(
            gain_whole[1].astype(jnp.bfloat16), "dp", scatter_dimension=0, tiled=True
        ).astype(jnp.float32),
    )
    return (
        output,
        grad_tokens,
        final_gain_one,
        final_qkv,
        final_out,
        final_gain_two,
        final_gate_up,
        final_down,
    )


MESH = pl.DeviceIdType.MESH


class Place:
    def __init__(self):
        self.dp = lax.axis_index("dp")
        self.ctx = lax.axis_index("ctx")
        self.z = lax.div(self.dp, 2)
        self.y = lax.rem(self.dp, 2)
        self.x = lax.div(self.ctx, 2)
        self.c = lax.rem(self.ctx, 2)
        self.up = (self.dp + 2, self.ctx)
        self.down = (self.dp - 2, self.ctx)
        self.across = (self.dp + 1 - 2 * self.y, self.ctx)
        self.chip = (self.dp, (1 - self.x) * 2 + self.c)
        self.core = (self.dp, self.x * 2 + 1 - self.c)
        self.has_up = self.z < 3
        self.has_down = self.z > 0


def greet(place):
    barrier = pltpu.get_barrier_semaphore()

    def tell(device):
        pl.semaphore_signal(barrier, inc=1, device_id=device, device_id_type=MESH)

    pl.when(place.has_up)(lambda: tell(place.up))
    pl.when(place.has_down)(lambda: tell(place.down))
    tell(place.across)
    for step in (1, 2, 3):
        tell((place.dp, lax.rem(place.ctx + step, 4)))
    ends = place.has_up.astype(jnp.int32) + place.has_down.astype(jnp.int32)
    pl.semaphore_wait(barrier, 4 + ends)


class Way(enum.IntEnum):
    BELOW = 0
    ABOVE = 1


BELOW, ABOVE = Way.BELOW, Way.ABOVE
SENDS = 80


class Wires:
    def __init__(self, send_sems, recv_sems, names):
        self.send_sems = send_sems
        self.recv_sems = recv_sems
        self.index = names
        self.total = sum(names.values()) if names else 0
        self.base = {}
        self.count = 0
        self.live = {}

    def slot(self, name, size=1):
        if name not in self.base:
            self.base[name] = self.total
            self.total += size
        return self.base[name]

    def spot(self, name, plane):
        if name[0] in ("down", "down_y"):
            return self.slot(name[:2])
        if name[0] == "ddown":
            return self.slot(name[:3])
        if name[:2] in GROUPED or name[0] in SWAPS:
            return self.slot(name[:2] if name[:2] in GROUPED else name[:1])
        if len(name) > 2 and isinstance(name[-2], Way):
            way, dist = name[-2:]
            source = plane - dist if way == BELOW else plane + dist
            if name[-3] == "z":
                return self.slot(name[:-2], 5) + source + int(way)
            return self.slot(name[:-2], 4) + source
        return self.slot(name)

    def send(self, src, dst, name, device, cond=None, extra=None):
        number = self.count
        self.count += 1
        self.settle(number - SENDS)
        at = self.spot(name, lax.div(device[0], 2))
        if extra is not None:
            at = at + extra
        copy = pltpu.make_async_remote_copy(
            src_ref=src,
            dst_ref=dst,
            send_sem=self.send_sems.at[number % SENDS],
            recv_sem=self.recv_sems.at[at],
            device_id=device,
            device_id_type=MESH,
        )
        when(cond, copy.start)
        self.live[number] = (copy, cond, name)

    def take(self, dst, name, device, extra=None):
        at = self.spot(name, lax.div(lax.axis_index("dp"), 2))
        if extra is not None:
            at = at + extra
        pltpu.make_async_remote_copy(
            src_ref=dst,
            dst_ref=dst,
            send_sem=self.send_sems.at[0],
            recv_sem=self.recv_sems.at[at],
            device_id=device,
            device_id_type=MESH,
        ).wait_recv()

    def settle(self, number):
        if number in self.live:
            copy, cond, name = self.live.pop(number)
            when(cond, copy.wait_send)

    def drain(self):
        for number in list(self.live):
            self.settle(number)

    def drain_named(self, first):
        for number in list(self.live):
            if self.live[number][2][0] == first:
                self.settle(number)


GROUPED = (("out", "c"), ("out", "d"), ("gain", "y")) + tuple((("gu", n), "y") for n in range(3))
SWAPS = ("pq", "kv", "gb", "gm")


def both(first, second):
    return second if first is None else jnp.logical_and(first, second)


def source_valid(place, way, dist):
    return place.z >= dist if way == BELOW else place.z + dist <= 3


def source_pos(place, way, dist):
    return place.dp - 2 * dist if way == BELOW else place.dp + 2 * dist


def flood_start(wires, place, name, own, block, spread):
    wires.send(own, block(place.dp), (name, BELOW, 1), place.up, place.has_up)
    wires.send(own, block(place.dp), (name, ABOVE, 1), place.down, place.has_down)
    wires.send(own, block(place.dp), (name, "y", 0, 0), place.across)
    spread(own, place.dp, (0, 0, 0), None)


def flood_step(wires, place, name, block, spread, way, dist):
    here = source_valid(place, way, dist)
    pos = source_pos(place, way, dist)
    view = block(pos)
    came_from = place.down if way == BELOW else place.up
    pl.when(here)(lambda: wires.take(view, (name, way, dist), came_from))
    if dist < 3:
        onward = place.up if way == BELOW else place.down
        more = place.has_up if way == BELOW else place.has_down
        wires.send(view, view, (name, way, dist + 1), onward, jnp.logical_and(here, more))
    wires.send(view, view, (name, "y", way, dist), place.across, here)
    spread(view, pos, (0, way, dist), here)


def flood_side(wires, place, name, block, spread, way, dist):
    if dist == 0:
        here, pos = None, place.dp
    else:
        here, pos = source_valid(place, way, dist), source_pos(place, way, dist)
    pos = pos + 1 - 2 * place.y
    view = block(pos)
    if here is None:
        wires.take(view, (name, "y", 0, 0), place.across)
    else:
        pl.when(here)(lambda: wires.take(view, (name, "y", way, dist), place.across))
    spread(view, pos, (1, way, dist), here)


HOPS = [(way, dist) for dist in (1, 2, 3) for way in (BELOW, ABOVE)]


def no_spread(view, pos, key, cond):
    return None


def add_rows(dst, srcs, out=None, cast=None, chunk=48):
    out = dst if out is None else out
    total_rows = dst.shape[0]
    assert total_rows % chunk == 0

    def body(i, carry):
        at = pl.ds(pl.multiple_of(i * chunk, 16), chunk)
        total = dst[at, :].astype(jnp.float32)
        for src in srcs:
            total = total + src[at, :].astype(jnp.float32)
        out[at, :] = total.astype(out.dtype)
        return carry

    lax.fori_loop(0, total_rows // chunk, body, 0)


def when(cond, action):
    if cond is None:
        action()
    else:
        pl.when(cond)(action)


DRAIN = [(way, dist) for dist in (3, 2, 1, 0) for way in (BELOW, ABOVE)]


def nn(a, b):
    return jnp.dot(a, b, preferred_element_type=jnp.float32)


def nt(a, b):
    return lax.dot_general(a, b, (((1,), (1,)), ((), ())), preferred_element_type=jnp.float32)


def tn(a, b):
    return lax.dot_general(a, b, (((0,), (0,)), ((), ())), preferred_element_type=jnp.float32)


def layer_kernel(
    names,
    tokens, cot, lengths, qkv_in, out_in, gu_in, dt_in, gain_one, gain_two, cos_table, sin_table,
    output, grad_tokens, gain_out, qkv_out, out_out, gu_out, dt_out,
    w_qkv, w_out, w_ff, d_qkv, d_out, d_ff, gain_all, gain_row, cos, sin,
    tok_all, n1_all, n2_all, g_all, ctx_all, hidden, grad_hidden, proj, q_st, kv_all, p_st, att, go_st,
    wide, gm, pq, pq_in, gb_all, gm_all, act, d_gu, gp, gp_box, op, op_box, dkv, dkv_box,
    qkv_side, out_side, gu_side, down_side, qkv_inbox, out_inbox, gu_inbox, down_inbox,
    up_inbox, up_side, gu_mix, down_mix, gain_box, gain_acc,
    send_sems, recv_sems, local_sems,
):
    f32, low = jnp.float32, jnp.bfloat16
    place = Place()
    wires = Wires(send_sems, recv_sems, names)
    dp, ctx, z, y, x, c = place.dp, place.ctx, place.z, place.y, place.x, place.c
    rows = qkv_in.shape[0]
    strip, half = dt_in.shape
    width = tokens.shape[1]
    own_rows = tokens.shape[0]
    slots_here = own_rows // 2
    qkv_cols, out_cols = qkv_in.shape[1], out_in.shape[1]
    qkv_wide, out_wide = w_qkv.shape[1], w_out.shape[2]
    group = QH // KVH
    slabs = KVH // 2
    q_slabs = QH // 2
    span = 3 * half
    deep = w_ff.shape[0]
    score_scale = 1.0 / math.sqrt(HD)
    TILES = range(2)

    greet(place)

    def block_rows(pos):
        return pl.ds(pl.multiple_of(pos * rows, 16), rows)

    def lead_rows(lead):
        return pl.ds(pl.multiple_of(lead * own_rows, 16), own_rows)

    here_rows = lead_rows(ctx)
    my_rows = block_rows(dp)

    def share(name, ref):
        mine = ref.at[here_rows]
        wires.send(mine, mine, (name, "x"), place.chip)
        wires.send(mine, mine, (name, "c"), place.core)

    def share_on(name, ref):
        far = ref.at[lead_rows(place.chip[1])]
        wires.take(far, (name, "x"), place.chip)
        wires.send(far, far, (name, "d"), place.core)

    def share_end(name, ref):
        for mark, lead in (("c", place.core[1]), ("d", 3 - ctx)):
            wires.take(ref.at[lead_rows(lead)], (name, mark), place.core)

    def swap_start(name, src, dst):
        for step in (1, 2, 3):
            peer = lax.rem(ctx + step, 4)
            wires.send(src(peer), dst(ctx), (name, step), (dp, peer))

    def swap_end(name, three):
        wires.take(three, (name, 1), place.core)

    locals_ = []

    def local(src, dst, cond=None):
        copy = pltpu.make_async_copy(src, dst, local_sems.at[len(locals_)])
        locals_.append((copy, cond))
        when(cond, copy.start)

    SIDES = [(0, 0)] + HOPS
    WAYS = {0: [(0, 0)], 1: HOPS[:2], 2: HOPS[2:4], 3: HOPS[4:]}

    class Flood:
        def __init__(self, name, block, spread=no_spread):
            self.name, self.block, self.spread = name, block, spread

        def start(self):
            flood_start(wires, place, self.name, self.block(dp), self.block, self.spread)

        def hop(self, dist, way):
            way = Way(way)
            flood_step(wires, place, self.name, self.block, self.spread, way, dist)

        def side(self, dist, way):
            way = Way(way) if dist else way
            flood_side(wires, place, self.name, self.block, self.spread, way, dist)

    class PairFlood:
        def __init__(self, name, ref, cols):
            self.name, self.ref, self.cols = name, ref, cols

        def pair(self, plane):
            return self.ref.at[pl.ds(pl.multiple_of(2 * rows * plane, 16), 2 * rows), self.cols]

        def one(self, pos):
            return self.ref.at[block_rows(pos), self.cols]

        def start(self):
            wires.send(self.one(dp), self.one(dp), (self.name, "y"), place.across)

        def side(self):
            wires.take(self.one(place.across[0]), (self.name, "y"), place.across)
            view = self.pair(z)
            wires.send(view, view, (self.name, BELOW, 1), place.up, place.has_up)
            wires.send(view, view, (self.name, ABOVE, 1), place.down, place.has_down)

        def hop(self, dist, way):
            way = Way(way)
            here = source_valid(place, way, dist)
            view = self.pair(z - dist if way == BELOW else z + dist)
            came_from = place.down if way == BELOW else place.up
            pl.when(here)(lambda: wires.take(view, (self.name, way, dist), came_from))
            if dist < 3:
                onward = place.up if way == BELOW else place.down
                more = place.has_up if way == BELOW else place.has_down
                wires.send(view, view, (self.name, way, dist + 1), onward, jnp.logical_and(here, more))

    def out_block(lead, pos):
        return w_out.at[lead, block_rows(pos)]

    def out_spread(view, pos, key, cond):
        wires.send(view, out_block(ctx, pos), ("out", "x") + key, place.chip, cond)
        wires.send(view, out_block(ctx, pos), ("out", "c") + key, place.core, cond)

    qkv_flood = Flood("qkv", lambda pos: w_qkv.at[block_rows(pos)])
    gain_flood = Flood("gain", lambda pos: gain_all.at[pos])
    out_flood = Flood("out", functools.partial(out_block, ctx), out_spread)

    PARTS = [(tile, part) for tile in TILES for part in range(2)]

    def part_cols(number):
        tile, part = PARTS[number]
        return pl.ds(tile * span + part * half, half)

    def gu_view(ref, number, pos):
        return ref.at[block_rows(pos), part_cols(number)]

    gu_floods = [Flood(("gu", number), functools.partial(gu_view, w_ff, number)) for number in range(3)]
    up_flood = PairFlood("up", w_ff, part_cols(3))

    def spots(column, dist, way=None):
        for way, dist in WAYS[dist] if way is None else [(way, dist)]:
            if dist == 0:
                here, pos = None, dp
            else:
                here, pos = source_valid(place, way, dist), source_pos(place, way, dist)
            if column == 1:
                pos = pos + 1 - 2 * y
            yield (column, way, dist), here, pos

    def out_chip(column, dist, way):
        way = Way(way) if dist else way
        for key, here, pos in spots(column, dist, way):
            view = out_block(place.chip[1], pos)
            when(here, lambda: wires.take(view, ("out", "x") + key, place.chip))
            wires.send(view, view, ("out", "d") + key, place.core, here)

    def out_core():
        for mark, lead in (("c", place.core[1]), ("d", 3 - ctx)):
            wires.take(w_out.at[lead], ("out", mark), place.core)

    def gu_sides(number):
        wires.take(w_ff.at[pl.ds(0, 4 * rows), part_cols(number)], (("gu", number), "y"), place.across)

    def mix_start(tile):
        for part in range(2):
            target = 2 * c + part
            src = gu_in.at[:, pl.ds((2 * part + tile) * half, half)]
            dst = w_ff.at[my_rows, pl.ds(pl.multiple_of(tile * span + x * half, 128), half)]
            wires.slot(("gu_mix", tile), 2)
            wires.send(src, dst, ("gu_mix", tile), (dp, target), target != ctx, extra=x)
            local(src, dst, target == ctx)

    def mix_end(number):
        tile, part = PARTS[number]
        origin = part * 2 + x
        view = gu_view(w_ff, number, dp)
        pl.when(origin != ctx)(lambda: wires.take(view, ("gu_mix", tile), (dp, origin), extra=part))

    lanes = pl.ds(pl.multiple_of(y * span + 2 * half, 128), half)
    other_lanes = pl.ds(pl.multiple_of((1 - y) * span + 2 * half, 128), half)
    at_home = ctx == z

    def strips_of(ref, at):
        return [ref.at[pl.ds(j * strip, strip), at] for j in range(4)]

    strips, other_strips = strips_of(w_ff, lanes), strips_of(w_ff, other_lanes)

    def down_mix_start():
        dst = w_ff.at[pl.ds(pl.multiple_of(ctx * strip, 16), strip), lanes]
        wires.slot(("down_mix",), 4)
        wires.send(dt_in, dst, ("down_mix",), (dp, z), ctx != z, extra=ctx)
        local(dt_in, dst, ctx == z)

    def tables():
        for table, ref in ((cos_table, cos), (sin_table, sin)):
            mine = table[pl.ds(pl.multiple_of(ctx * slots_here, 16), slots_here), :]
            ref[:slots_here, :] = mine
            ref[slots_here:, :] = mine

    def down_start(j):
        pl.when(jnp.logical_and(at_home, ctx != j))(lambda: wires.take(strips[j], ("down_mix",), (dp, j), extra=j))
        wires.send(strips[j], strips[j], ("down", j, BELOW, 1), place.up, jnp.logical_and(at_home, place.has_up))
        wires.send(strips[j], strips[j], ("down", j, ABOVE, 1), place.down, jnp.logical_and(at_home, place.has_down))
        wires.send(strips[j], strips[j], ("down_y", j, 0, 0), place.across, at_home)

    def down_hop(dist, j):
        for way in (BELOW, ABOVE):
            here = (z - ctx if way == BELOW else ctx - z) == dist
            came_from = place.down if way == BELOW else place.up
            onward = place.up if way == BELOW else place.down
            more = place.has_up if way == BELOW else place.has_down
            pl.when(here)(lambda: wires.take(strips[j], ("down", j, way, dist), came_from))
            if dist < 3:
                wires.send(strips[j], strips[j], ("down", j, way, dist + 1), onward, jnp.logical_and(here, more))
            wires.send(strips[j], strips[j], ("down_y", j, way, dist), place.across, here)

    def down_side_end():
        for way, dist in SIDES:
            here = at_home if dist == 0 else (z - ctx if way == BELOW else ctx - z) == dist

            def take():
                for j in range(4):
                    wires.take(other_strips[j], ("down_y", j, way, dist), place.across)

            pl.when(here)(take)

    row_at = lax.broadcasted_iota(jnp.int32, (own_rows, 1), 0)
    first_seq = row_at < slots_here
    position = ctx * slots_here + jnp.where(first_seq, row_at, row_at - slots_here)
    valid = position < jnp.where(first_seq, lengths[0], lengths[1])
    def tokens_start():
        tok_all[here_rows, :] = tokens[...]
        share("tok", tok_all)

    def qkv_start():
        w_qkv[my_rows, :] = jnp.zeros((rows, qkv_wide), low)
        w_qkv[my_rows, :qkv_cols] = qkv_in[...]
        qkv_flood.start()

    def gain_start():
        gain_all[dp] = jnp.zeros(gain_all.shape[1:], f32)
        gain_all[dp, 0:1, :rows] = gain_one[...].reshape(1, rows).astype(f32)
        gain_all[dp, 1:2, :rows] = gain_two[...].reshape(1, rows).astype(f32)
        gain_flood.start()

    def out_start():
        w_out[ctx, my_rows, :] = jnp.zeros((rows, out_wide), low)
        w_out[ctx, my_rows, :out_cols] = out_in[...]
        out_flood.start()

    def cot_start():
        g_all[here_rows, :] = jnp.where(valid, cot[...].astype(f32), 0.0).astype(low)
        share("cot", g_all)

    def gain_sides():
        wires.take(gain_all.at[pl.ds(0, 4)], ("gain", "y"), place.across)

    gain_a = lambda: gain_row[0:1, :width]
    gain_b = lambda: gain_row[1:2, :width]

    def norm(values):
        return lax.rsqrt(jnp.mean(values * values, axis=-1, keepdims=True) + EPS)

    lane = lax.broadcasted_iota(jnp.int32, (own_rows, 128), 1)
    low_half = lax.rem(lane, HD) < HD // 2
    side_of = lax.div(lane, HD)

    def turn(values, sign):
        swapped = jnp.where(low_half, pltpu.roll(values, 128 - HD // 2, 1), pltpu.roll(values, HD // 2, 1))
        return values * cos[...] + swapped * (sin[...] * sign)

    def head_spots():
        for head in range(QH):
            kv = head // group
            yield head // 2, head % 2, kv // 2, kv % 2, (kv % 2 * group + head % group) * slots_here

    def stack_heads(slab_of, dest, scale):
        for slab, side, key_slab, key_side, at in head_spots():
            values = slab_of(slab)
            if side != key_side:
                values = pltpu.roll(values, HD, 1)
            values = (jnp.where(side_of == key_side, values, 0.0) * scale).astype(low)
            for seq in range(2):
                dest[seq * slabs + key_slab, at : at + slots_here, :] = values[
                    seq * slots_here : (seq + 1) * slots_here
                ]

    def unstack_heads(src, slab):
        total = jnp.zeros((own_rows, 128), f32)
        for at_slab, side, key_slab, key_side, at in head_spots():
            if at_slab != slab:
                continue
            values = jnp.concatenate(
                [src[seq * slabs + key_slab, at : at + slots_here, :] for seq in range(2)], axis=0
            )
            values = jnp.where(side_of == key_side, values, 0.0)
            if side != key_side:
                values = pltpu.roll(values, HD, 1)
            total = total + values
        return total

    def project():
        gain_row[...] = jnp.zeros(gain_row.shape, f32)
        for pos in range(8):
            piece = gain_all[pos]
            shift = (pos * rows) % 128
            if shift:
                piece = pltpu.roll(piece, shift, 1)
            at = (pos * rows) // 128 * 128
            gain_row[:, at : at + 256] += piece

        def body(i, carry):
            at = lead_rows(i)
            source = tok_all[at, :].astype(f32)
            n1_all[at, :] = (source * norm(source) * gain_a()).astype(low)
            return carry

        lax.fori_loop(0, 4, body, 0)
        pq[...] = nn(n1_all[...], w_qkv[...]).reshape(pq.shape)
        pq_in[ctx] = pq[ctx]
        swap_start("pq", lambda peer: pq.at[peer], lambda sender: pq_in.at[sender])

    def pq_end():
        swap_end("pq", pq_in.at[pl.ds(0, 3)])
        proj[...] = jnp.zeros(proj.shape, f32)
        for j in range(4):
            part = jnp.concatenate([pq_in[j], jnp.zeros((own_rows, 128), f32)], axis=1)
            at = qkv_cols * j
            if at % 128:
                part = pltpu.roll(part, at % 128, 1)
            proj[:, at // 128 * 128 : at // 128 * 128 + qkv_wide + 128] += part

    turned = {}

    def query_slab(slab):
        if slab not in turned:
            turned[slab] = turn(proj[:, slab * 128 : slab * 128 + 128], 1.0)
        return turned[slab]

    def slot_view(lead):
        return kv_all.at[:, :, pl.ds(pl.multiple_of(lead * slots_here, 16), slots_here)]

    def kv_start():
        my_slots = pl.ds(pl.multiple_of(ctx * slots_here, 16), slots_here)
        for slab in range(2 * slabs):
            at = (q_slabs + slab) * 128
            values = proj[:, at : at + 128]
            if slab < slabs:
                values = turn(values, 1.0)
            values = values.astype(low)
            for seq in range(2):
                kv_all[seq, slab, my_slots, :] = values[seq * slots_here : (seq + 1) * slots_here]

        swap_start("kv", lambda peer: slot_view(ctx), slot_view)

    def queries():
        stack_heads(query_slab, q_st, score_scale)

    def kv_end():
        swap_end("kv", kv_all.at[:, :, pl.ds(0, 3 * slots_here)])

    stack = q_st.shape[1]
    slots = kv_all.shape[2]

    def attend(i, carry):
        seq, slab = lax.div(i, slabs), lax.rem(i, slabs)
        scores = nt(q_st[i], kv_all[seq, slab])
        at = ctx * slots_here + lax.rem(lax.broadcasted_iota(jnp.int32, (stack, slots), 0), slots_here)
        key_at = lax.broadcasted_iota(jnp.int32, (stack, slots), 1)
        length = jnp.where(seq == 0, lengths[0], lengths[1])
        allowed = jnp.logical_and(key_at <= at, key_at < length)
        scores = jnp.where(allowed, scores, NEGATIVE)
        terms = jnp.exp(scores - jnp.max(scores, axis=-1, keepdims=True))
        probs = (terms / jnp.sum(terms, axis=-1, keepdims=True)).astype(low)
        p_st[i] = probs
        att[i] = nn(probs, kv_all[seq, slabs + slab])
        return carry

    def attention():
        lax.fori_loop(0, 2 * slabs, attend, 0)
        for slab in range(q_slabs):
            ctx_all[here_rows, slab * 128 : slab * 128 + 128] = unstack_heads(att, slab).astype(low)
        share("ctx", ctx_all)

    def out_project():
        hidden[...] = tokens[...].astype(f32)
        for j in range(4):
            part = nn(ctx_all[here_rows, :], w_out[j])
            at = out_cols * j
            if at % 128:
                part = pltpu.roll(part, at % 128, 1)
            hidden[:, at // 128 * 128 : at // 128 * 128 + out_wide] += part
        n2_all[here_rows, :] = (hidden[...] * norm(hidden[...]) * gain_b()).astype(low)
        share("n2", n2_all)

    tall = 2 * own_rows

    def feed(tile):
        def body(i, carry):
            at = pl.ds(0, 4 * own_rows)
            gate = nn(n2_all[at, :], w_ff[:, tile * span : tile * span + half])
            up = nn(n2_all[at, :], w_ff[:, tile * span + half : tile * span + 2 * half])
            back = nn(g_all[at, :], w_ff[:, tile * span + 2 * half : (tile + 1) * span])
            sig = jax.nn.sigmoid(gate)
            swish = gate * sig
            act[tile, at, :] = (swish * up).astype(low)
            d_gu[tile, at, :half] = (back * up * sig * (1.0 + gate * (1.0 - sig))).astype(low)
            d_gu[tile, at, half:] = (back * swish).astype(low)
            return carry

        body(0, 0)

    def grad_ff(tile):
        def body(m, carry):
            at = pl.ds(pl.multiple_of(m * width, 128), width)
            d_ff[at, tile * span : tile * span + 2 * half] = tn(n2_all[:, at], d_gu[tile]).astype(low)
            d_ff[at, tile * span + 2 * half : (tile + 1) * span] = tn(g_all[:, at], act[tile]).astype(low)
            return carry

        lax.fori_loop(0, 1, body, 0)

    across_core = (1 - x) * 2 + 1 - c
    across_own = (1 - x) * 2 + c
    beside = x * 2 + 1 - c
    wide_tile = width

    def group_send(name, ref, box, which):
        lead, mark = ((across_core, "cx"), (beside, "cc"))[which]
        wires.send(ref.at[lead], box.at[which], (name, mark), place.core)

    def group_on(name, ref, box):
        wires.take(box.at[0], (name, "cx"), place.core)
        mine = ref.at[across_own]
        mine[...] = (mine[...].astype(f32) + box[0].astype(f32)).astype(low)
        wires.send(mine, box.at[2], (name, "x"), place.chip)

    def group_end(name, ref, box):
        wires.take(box.at[1], (name, "cc"), place.core)
        wires.take(box.at[2], (name, "x"), place.chip)
        return ref[ctx].astype(f32) + box[1].astype(f32) + box[2].astype(f32)

    def pair_rows(half_x):
        return pl.ds(pl.multiple_of(half_x * tall, 16), tall)

    def group_product(ref, terms):
        def compute(half_x):
            def body(n, carry):
                at = pl.ds(pl.multiple_of(n * wide_tile, 128), wide_tile)
                total = None
                for left, right in terms:
                    term = nt(left(pair_rows(half_x)), right(at))
                    total = term if total is None else total + term
                ref[2 * half_x, :, at] = total[:own_rows].astype(low)
                ref[2 * half_x + 1, :, at] = total[own_rows:].astype(low)
                return carry

            lax.fori_loop(0, width // wide_tile, body, 0)

        return compute

    back_terms = [
        (lambda at, tile=tile: d_gu[tile, at, :], lambda at, tile=tile: w_ff[at, tile * span : tile * span + 2 * half])
        for tile in TILES
    ]
    forward_terms = [
        (lambda at, tile=tile: act[tile, at, :], lambda at, tile=tile: w_ff[at, tile * span + 2 * half : (tile + 1) * span])
        for tile in TILES
    ]

    def key_pos(way, dist):
        if dist == 0:
            return None, dp
        return source_valid(place, way, dist), source_pos(place, way, dist)

    KEYS = {3: DRAIN[:2], 2: DRAIN[2:4], 1: DRAIN[4:6], 0: [(BELOW, 0)]}
    flip = 1 - 2 * y

    def z_add(name, view, boxes, inbox, way, dist):
        here, pos = key_pos(way, dist)
        mine = view(pos)
        if dist == 0:
            wires.take(boxes.at[way, dist], (name, "y", way, dist), place.across)
            add_rows(mine, [boxes.at[way, dist]])
            for end, fed, feeder in ((BELOW, place.has_up, place.up), (ABOVE, place.has_down, place.down)):

                def own():
                    wires.take(inbox.at[end, 0], (name, "z", end, 0), feeder)
                    add_rows(mine, [inbox.at[end, 0]])

                pl.when(fed)(own)
            return
        fed = place.has_up if way == BELOW else place.has_down
        feeder = place.up if way == BELOW else place.down
        onward = place.down if way == BELOW else place.up
        side = boxes.at[way, dist]

        def first():
            wires.take(side, (name, "y", way, dist), place.across)
            add_rows(mine, [side])

        if dist == 3:
            pl.when(here)(first)
        else:

            def more():
                wires.take(side, (name, "y", way, dist), place.across)
                wires.take(inbox.at[way, dist], (name, "z", way, dist), feeder)
                add_rows(mine, [side, inbox.at[way, dist]])

            pl.when(jnp.logical_and(here, jnp.logical_not(fed)))(first)
            pl.when(jnp.logical_and(here, fed))(more)
        wires.send(mine, inbox.at[way, dist - 1], (name, "z", way, dist - 1), onward, here)

    class Sink:
        def __init__(self, name, view, side, inbox):
            self.name, self.view, self.side, self.inbox = name, view, side, inbox

        def send(self, dist, way):
            way = Way(way) if dist else way
            here, pos = key_pos(way, dist)
            wires.send(
                self.view(pos + flip), self.side.at[way, dist],
                (self.name, "y", way, dist), place.across, here,
            )

        def add(self, dist, way):
            way = Way(way) if dist else way
            z_add(self.name, self.view, self.side, self.inbox, way, dist)

    gu_sinks = [
        Sink(("dgu", number), functools.partial(gu_view, d_ff, number), gu_side.at[number], gu_inbox.at[number])
        for number in range(3)
    ]
    out_sink = Sink("dout", lambda pos: d_out.at[block_rows(pos)], out_side, out_inbox)
    qkv_sink = Sink("dqkv", lambda pos: d_qkv.at[block_rows(pos)], qkv_side, qkv_inbox)
    d_strips, d_other_strips = strips_of(d_ff, lanes), strips_of(d_ff, other_lanes)

    def down_send(tile, j):
        wires.send(d_other_strips[j], down_side.at[j], ("ddown_y", j), place.across, (1 - y) == tile)

    def down_add(dist, j):
        if dist == 0:

            def finish():
                wires.take(down_side.at[j], ("ddown_y", j), place.across)
                add_rows(d_strips[j], [down_side.at[j]])
                for end, fed, feeder in ((BELOW, place.has_up, place.up), (ABOVE, place.has_down, place.down)):

                    def more():
                        wires.take(down_inbox.at[end, j], ("ddown", j, end, 0), feeder)
                        add_rows(d_strips[j], [down_inbox.at[end, j]])

                    pl.when(fed)(more)

            pl.when(at_home)(finish)
            return
        for way in (BELOW, ABOVE):
            here = (z - ctx if way == BELOW else ctx - z) == dist
            fed = place.has_up if way == BELOW else place.has_down
            feeder = place.up if way == BELOW else place.down
            onward = place.down if way == BELOW else place.up

            def first():
                wires.take(down_side.at[j], ("ddown_y", j), place.across)
                add_rows(d_strips[j], [down_side.at[j]])

            def more():
                wires.take(down_side.at[j], ("ddown_y", j), place.across)
                wires.take(down_inbox.at[way, j], ("ddown", j, way, dist), feeder)
                add_rows(d_strips[j], [down_side.at[j], down_inbox.at[way, j]])

            pl.when(jnp.logical_and(here, jnp.logical_not(fed)))(first)
            pl.when(jnp.logical_and(here, fed))(more)
            wires.send(d_strips[j], down_inbox.at[way, j], ("ddown", j, way, dist - 1), onward, here)

    class PairSink:
        def __init__(self, name, ref, cols, inbox, side):
            self.name, self.ref, self.cols, self.inbox, self.side = name, ref, cols, inbox, side

        def pair(self, plane):
            return self.ref.at[pl.ds(pl.multiple_of(2 * rows * plane, 16), 2 * rows), self.cols]

        def one(self, pos):
            return self.ref.at[block_rows(pos), self.cols]

        def add(self, dist, way):
            if dist == 0:
                mine = self.pair(z)
                for end, fed, feeder in ((BELOW, place.has_up, place.up), (ABOVE, place.has_down, place.down)):

                    def more():
                        wires.take(self.inbox.at[end, 0], (self.name, "z", end, 0), feeder)
                        add_rows(mine, [self.inbox.at[end, 0]])

                    pl.when(fed)(more)
                wires.send(self.one(place.across[0]), self.side, (self.name, "y"), place.across)
                return
            way = Way(way)
            here = source_valid(place, way, dist)
            mine = self.pair(z - dist if way == BELOW else z + dist)
            fed = place.has_up if way == BELOW else place.has_down
            feeder = place.up if way == BELOW else place.down
            onward = place.down if way == BELOW else place.up
            if dist < 3:

                def more():
                    wires.take(self.inbox.at[way, dist], (self.name, "z", way, dist), feeder)
                    add_rows(mine, [self.inbox.at[way, dist]])

                pl.when(jnp.logical_and(here, fed))(more)
            wires.send(mine, self.inbox.at[way, dist - 1], (self.name, "z", way, dist - 1), onward, here)

        def end(self):
            wires.take(self.side, (self.name, "y"), place.across)
            add_rows(self.one(dp), [self.side])

    up_sink = PairSink("dup", d_ff, part_cols(3), up_inbox, up_side)

    def gu_finish(number):
        tile, part = PARTS[number]
        target = part * 2 + x
        block = gu_view(d_ff, number, dp)
        wires.slot(("dgu_mix", tile), 2)
        wires.send(block, gu_mix.at[c, tile], ("dgu_mix", tile), (dp, target), target != ctx, extra=c)
        pl.when(target == ctx)(lambda: add_rows(block, [], out=gu_mix.at[c, tile]))

    def gu_end(number):
        tile, part = PARTS[number]
        origin = 2 * c + part
        box = gu_mix.at[part, tile]
        pl.when(origin != ctx)(lambda: wires.take(box, ("dgu_mix", tile), (dp, origin), extra=part))
        add_rows(box, [], out=gu_out.at[:, pl.ds((2 * part + tile) * half, half)])

    def down_finish():
        for j in range(4):
            wires.send(d_strips[j], down_mix, ("ddown_mix",), (dp, j), jnp.logical_and(at_home, ctx != j))
            pl.when(jnp.logical_and(at_home, ctx == j))(functools.partial(add_rows, d_strips[j], [], down_mix))

    def down_end():
        pl.when(ctx != z)(lambda: wires.take(down_mix, ("ddown_mix",), (dp, z)))
        add_rows(down_mix, [], out=dt_out)

    def norm_back(values, inverse, gain, grad_in):
        scaled = grad_in * gain
        mean_term = jnp.mean(scaled * values, axis=-1, keepdims=True)
        back = inverse * scaled - values * (inverse * inverse * inverse) * mean_term
        return back, jnp.sum(grad_in * values * inverse, axis=0, keepdims=True)

    def gp_block(which):
        half_x = 1 - x if which == 0 else x
        group_product(gp, back_terms)(half_x)
        group_send("gp", gp, gp_box, which)

    def op_block(which):
        half_x = 1 - x if which == 0 else x
        group_product(op, forward_terms)(half_x)
        group_send("op", op, op_box, which)

    def hidden_back():
        gain_acc[0] = jnp.zeros(gain_out.shape, f32)
        back_two, gain_two_grad = norm_back(hidden[...], norm(hidden[...]), gain_b(), group_end("gp", gp, gp_box))
        gain_acc[0, 1:2, :] = gain_two_grad
        grad_hidden[...] = g_all[here_rows, :].astype(f32) + back_two
        out_lane = lax.broadcasted_iota(jnp.int32, (own_rows, out_wide), 1)
        for j in range(4):
            at = out_cols * j
            part = grad_hidden[:, at // 128 * 128 : at // 128 * 128 + out_wide]
            if at % 128:
                part = pltpu.roll(part, out_wide - at % 128, 1)
            wide[j] = jnp.where(out_lane < out_cols, part, 0.0).astype(low)
        gb_all[here_rows, :] = wide[ctx]
        swap_start("gb", lambda peer: wide.at[peer], lambda sender: gb_all.at[lead_rows(sender)])

    def context_back(n, carry):
        at = pl.ds(pl.multiple_of(n * wide_tile, 128), wide_tile)
        total = nt(wide[0], w_out[0, at, :])
        for j in range(1, 4):
            total = total + nt(wide[j], w_out[j, at, :])
        proj[:, at] = total
        return carry

    def grad_context():
        lax.fori_loop(0, width // wide_tile, context_back, 0)
        stack_heads(lambda slab: proj[:, slab * 128 : slab * 128 + 128], go_st, 1.0)

    def attend_back(i, carry):
        seq, slab = lax.div(i, slabs), lax.rem(i, slabs)
        grad_probs = nt(go_st[i], kv_all[seq, slabs + slab])
        probs = p_st[i].astype(f32)
        delta = jnp.sum(probs * grad_probs, axis=-1, keepdims=True)
        grad_scores = (probs * (grad_probs - delta)).astype(low)
        att[i] = nn(grad_scores, kv_all[seq, slab]) * score_scale
        grad_key = tn(grad_scores, q_st[i])
        grad_value = tn(p_st[i], go_st[i])
        for j in range(4):
            part = slice(j * slots_here, (j + 1) * slots_here)
            dkv[j, seq, slab] = grad_key[part].astype(low)
            dkv[j, seq, slabs + slab] = grad_value[part].astype(low)
        return carry

    def attention_back():
        lax.fori_loop(0, 2 * slabs, attend_back, 0)
        group_send("dkv", dkv, dkv_box, 0)
        group_send("dkv", dkv, dkv_box, 1)

    def gb_end():
        swap_end("gb", gb_all.at[pl.ds(0, 3 * own_rows)])

    def grad_out(m, carry):
        at = pl.ds(pl.multiple_of(m * width, 128), width)
        d_out[at, :] = tn(ctx_all[:, at], gb_all[...]).astype(low)
        return carry

    def grad_out_all():
        lax.fori_loop(0, 1, grad_out, 0)

    def grad_mixed():
        sums = group_end("dkv", dkv, dkv_box)
        proj[...] = jnp.zeros(proj.shape, f32)
        for slab in range(q_slabs):
            proj[:, slab * 128 : slab * 128 + 128] = turn(unstack_heads(att, slab), -1.0)
        for slab in range(2 * slabs):
            values = jnp.concatenate([sums[0, slab], sums[1, slab]], axis=0)
            if slab < slabs:
                values = turn(values, -1.0)
            at = (q_slabs + slab) * 128
            proj[:, at : at + 128] = values
        qkv_lane = lax.broadcasted_iota(jnp.int32, (own_rows, qkv_wide), 1)
        for j in range(4):
            at = qkv_cols * j
            part = proj[:, at // 128 * 128 : at // 128 * 128 + qkv_wide + 128]
            if at % 128:
                part = pltpu.roll(part, qkv_wide + 128 - at % 128, 1)
            gm[j] = jnp.where(qkv_lane < qkv_cols, part[:, :qkv_wide], 0.0).astype(low)
        gm_all[here_rows, :] = gm[ctx]
        swap_start("gm", lambda peer: gm.at[peer], lambda sender: gm_all.at[lead_rows(sender)])

    def gm_end():
        swap_end("gm", gm_all.at[pl.ds(0, 3 * own_rows)])

    def grad_qkv(m, carry):
        at = pl.ds(pl.multiple_of(m * width, 128), width)
        d_qkv[at, :] = tn(n1_all[:, at], gm_all[...]).astype(low)
        return carry

    def grad_qkv_all():
        lax.fori_loop(0, 1, grad_qkv, 0)

    tokens_terms = [(lambda at: gm_all[at, :], lambda at: w_qkv[at, :])]

    def gt_block(which):
        if which == 0:
            wires.drain_named("gp")
        half_x = 1 - x if which == 0 else x
        group_product(gp, tokens_terms)(half_x)
        group_send("gt", gp, gp_box, which)

    def output_end():
        result = hidden[...] + group_end("op", op, op_box)
        output[...] = jnp.where(valid, result, 0.0).astype(low)

    def tokens_end():
        source = tokens[...].astype(f32)
        back_one, gain_one_grad = norm_back(source, norm(source), gain_a(), group_end("gt", gp, gp_box))
        gain_acc[0, 0:1, :] = gain_one_grad
        grad_tokens[...] = (grad_hidden[...] + back_one).astype(low)

    low_end, high_end = z == 0, z == 3
    mid_low, mid_high = z == 1, z == 2

    def gain_send(hop):
        def go(device, cond=None):
            wires.send(gain_acc.at[hop], gain_box.at[hop], ("gain_sum", hop), device, cond)

        if hop < 3:
            go((place.core, place.chip, place.across)[hop])
        elif hop == 3:
            go(place.up, low_end)
            go(place.down, high_end)
        elif hop == 4:
            go(place.up, mid_low)
            go(place.down, mid_high)
        else:
            go(place.down, mid_low)
            go(place.up, mid_high)

    def gain_take(hop):
        def add(device):
            wires.take(gain_box.at[hop], ("gain_sum", hop), device)
            gain_acc[hop + 1] = gain_acc[hop] + gain_box[hop]

        def last(device):
            wires.take(gain_box.at[hop], ("gain_sum", hop), device)
            gain_out[...] = gain_box[hop]

        def done():
            gain_out[...] = gain_acc[hop]

        if hop < 3:
            add((place.core, place.chip, place.across)[hop])
        elif hop == 3:
            pl.when(mid_low)(lambda: add(place.down))
            pl.when(mid_high)(lambda: add(place.up))
        elif hop == 4:
            pl.when(mid_low)(lambda: add(place.up))
            pl.when(mid_high)(lambda: add(place.down))
        else:
            pl.when(low_end)(lambda: last(place.up))
            pl.when(high_end)(lambda: last(place.down))
            pl.when(mid_low)(done)
            pl.when(mid_high)(done)

    def out_end():
        out_out[...] = d_out[my_rows, :]

    def qkv_end():
        qkv_out[...] = d_qkv[my_rows, :]

    def locals_end():
        for copy, cond in locals_:
            when(cond, copy.wait)

    mix_start(0)
    qkv_start()
    out_start()
    tokens_start()
    out_chip(0, 0, 0)
    qkv_flood.hop(1, 0)
    qkv_flood.hop(1, 1)
    down_mix_start()
    mix_start(1)
    tables()
    locals_end()
    mix_end(0)
    mix_end(1)
    gu_floods[0].start()
    gu_floods[1].start()
    cot_start()
    gain_start()
    gain_flood.hop(1, 0)
    gain_flood.hop(1, 1)
    out_flood.hop(1, 0)
    out_flood.hop(1, 1)
    gain_flood.hop(2, 0)
    gain_flood.hop(2, 1)
    gain_flood.hop(3, 0)
    gain_flood.hop(3, 1)
    qkv_flood.hop(2, 0)
    qkv_flood.hop(2, 1)
    qkv_flood.side(1, 0)
    qkv_flood.side(1, 1)
    qkv_flood.hop(3, 0)
    qkv_flood.hop(3, 1)
    share_on("tok", tok_all)
    out_flood.side(0, 0)
    down_start(0)
    down_start(1)
    down_start(2)
    down_start(3)
    out_flood.hop(2, 0)
    out_flood.hop(2, 1)
    qkv_flood.side(3, 0)
    qkv_flood.side(3, 1)
    gain_sides()
    mix_end(2)
    mix_end(3)
    up_flood.start()
    gu_floods[2].start()
    qkv_flood.side(0, 0)
    qkv_flood.side(2, 0)
    qkv_flood.side(2, 1)
    share_end("tok", tok_all)
    project()
    out_flood.hop(3, 0)
    out_flood.hop(3, 1)
    down_hop(1, 0)
    down_hop(1, 1)
    down_hop(1, 2)
    down_hop(1, 3)
    share_on("cot", g_all)
    gu_floods[2].hop(1, 0)
    gu_floods[2].hop(1, 1)
    share_end("cot", g_all)
    gu_floods[0].hop(1, 0)
    gu_floods[1].hop(1, 0)
    gu_floods[0].hop(1, 1)
    gu_floods[1].hop(1, 1)
    out_chip(0, 2, 0)
    out_chip(0, 2, 1)
    out_chip(0, 1, 0)
    out_chip(0, 1, 1)
    pq_end()
    kv_start()
    out_flood.side(1, 0)
    out_flood.side(1, 1)
    down_hop(2, 0)
    down_hop(2, 1)
    down_hop(2, 2)
    down_hop(2, 3)
    out_flood.side(3, 0)
    out_flood.side(3, 1)
    queries()
    down_hop(3, 0)
    down_hop(3, 1)
    down_hop(3, 2)
    down_hop(3, 3)
    out_flood.side(2, 0)
    out_flood.side(2, 1)
    kv_end()
    up_flood.side()
    attention()
    out_chip(1, 2, 0)
    out_chip(1, 2, 1)
    gu_floods[0].hop(2, 0)
    gu_floods[1].hop(2, 0)
    gu_floods[0].hop(2, 1)
    gu_floods[1].hop(2, 1)
    out_chip(1, 0, 0)
    out_chip(0, 3, 0)
    out_chip(0, 3, 1)
    out_chip(1, 1, 0)
    out_chip(1, 1, 1)
    out_chip(1, 3, 0)
    out_chip(1, 3, 1)
    out_core()
    out_project()
    up_flood.hop(1, 0)
    up_flood.hop(1, 1)
    gu_floods[0].hop(3, 0)
    gu_floods[1].hop(3, 0)
    gu_floods[0].hop(3, 1)
    gu_floods[1].hop(3, 1)
    down_side_end()
    gu_floods[2].hop(2, 0)
    gu_floods[2].hop(2, 1)
    share_on("n2", n2_all)
    up_flood.hop(2, 0)
    up_flood.hop(2, 1)
    gu_sides(0)
    gu_sides(1)
    share_end("n2", n2_all)
    feed(0)
    gu_floods[2].hop(3, 0)
    gu_floods[2].hop(3, 1)
    grad_ff(0)
    gu_sinks[0].send(3, 0)
    gu_sinks[1].send(3, 0)
    gu_sinks[0].send(3, 1)
    gu_sinks[1].send(3, 1)
    gu_sinks[0].send(2, 0)
    gu_sinks[1].send(2, 0)
    gu_sinks[0].send(2, 1)
    gu_sinks[1].send(2, 1)
    gu_sides(2)
    up_flood.hop(3, 0)
    up_flood.hop(3, 1)
    feed(1)
    grad_ff(1)
    up_sink.add(3, 0)
    up_sink.add(3, 1)
    gu_sinks[2].send(3, 0)
    gu_sinks[2].send(3, 1)
    down_send(1, 0)
    down_send(1, 1)
    down_send(1, 2)
    down_send(1, 3)
    down_send(0, 0)
    down_send(0, 1)
    down_send(0, 2)
    down_send(0, 3)
    gu_sinks[0].send(1, 0)
    gu_sinks[1].send(1, 0)
    gu_sinks[0].send(1, 1)
    gu_sinks[1].send(1, 1)
    gu_sinks[2].send(2, 0)
    gu_sinks[2].send(2, 1)
    gu_sinks[0].add(3, 0)
    gu_sinks[1].add(3, 0)
    gu_sinks[0].add(3, 1)
    gu_sinks[1].add(3, 1)
    gu_sinks[2].send(0, 0)
    gp_block(0)
    share_on("ctx", ctx_all)
    group_on("gp", gp, gp_box)
    gu_sinks[0].send(0, 0)
    gu_sinks[1].send(0, 0)
    op_block(1)
    op_block(0)
    up_sink.add(2, 0)
    up_sink.add(2, 1)
    gp_block(1)
    gu_sinks[2].add(3, 0)
    gu_sinks[2].add(3, 1)
    gu_sinks[0].add(2, 0)
    gu_sinks[1].add(2, 0)
    gu_sinks[0].add(2, 1)
    gu_sinks[1].add(2, 1)
    hidden_back()
    grad_context()
    attention_back()
    up_sink.add(1, 0)
    up_sink.add(1, 1)
    group_on("dkv", dkv, dkv_box)
    gb_end()
    share_end("ctx", ctx_all)
    grad_out_all()
    gu_sinks[2].send(1, 0)
    gu_sinks[2].send(1, 1)
    out_sink.send(3, 0)
    out_sink.send(3, 1)
    down_add(3, 0)
    down_add(3, 1)
    down_add(3, 2)
    down_add(3, 3)
    grad_mixed()
    gu_sinks[0].add(1, 0)
    gu_sinks[1].add(1, 0)
    gu_sinks[0].add(1, 1)
    gu_sinks[1].add(1, 1)
    down_add(2, 0)
    down_add(2, 1)
    down_add(2, 2)
    down_add(2, 3)
    out_sink.send(1, 0)
    out_sink.send(1, 1)
    group_on("op", op, op_box)
    gu_sinks[2].add(2, 0)
    gu_sinks[2].add(2, 1)
    gm_end()
    gt_block(0)
    gt_block(1)
    up_sink.add(0, 0)
    grad_qkv_all()
    qkv_sink.send(3, 0)
    qkv_sink.send(3, 1)
    out_sink.send(2, 0)
    out_sink.send(2, 1)
    group_on("gt", gp, gp_box)
    qkv_sink.send(2, 0)
    qkv_sink.send(2, 1)
    down_add(1, 0)
    down_add(1, 1)
    down_add(1, 2)
    down_add(1, 3)
    gu_sinks[0].add(0, 0)
    gu_sinks[1].add(0, 0)
    gu_finish(0)
    gu_finish(1)
    tokens_end()
    gain_send(0)
    gain_take(0)
    gu_sinks[2].add(1, 0)
    gu_sinks[2].add(1, 1)
    gain_send(1)
    gain_take(1)
    out_sink.add(3, 0)
    out_sink.add(3, 1)
    gain_send(2)
    qkv_sink.send(1, 0)
    qkv_sink.send(1, 1)
    qkv_sink.add(3, 0)
    qkv_sink.add(3, 1)
    out_sink.add(2, 0)
    out_sink.add(2, 1)
    qkv_sink.add(2, 0)
    qkv_sink.add(2, 1)
    down_add(0, 0)
    down_add(0, 1)
    down_add(0, 2)
    down_add(0, 3)
    down_finish()
    gain_take(2)
    gu_sinks[2].add(0, 0)
    out_sink.send(0, 0)
    qkv_sink.send(0, 0)
    output_end()
    up_sink.end()
    gain_send(3)
    out_sink.add(1, 0)
    out_sink.add(1, 1)
    gain_take(3)
    gu_finish(2)
    gu_finish(3)
    gain_send(4)
    qkv_sink.add(1, 0)
    qkv_sink.add(1, 1)
    out_sink.add(0, 0)
    gain_take(4)
    gain_send(5)
    out_end()
    gu_end(0)
    gu_end(1)
    down_end()
    gu_end(2)
    gu_end(3)
    qkv_sink.add(0, 0)
    qkv_end()
    gain_take(5)
    wires.drain()


def finish_kernel(
    output, grad_tokens, gains, qkv, out, gu, down_t,
    output_end, grad_tokens_end, qkv_end, out_end, gu_end, down_end, one_end, two_end,
):
    f32 = jnp.float32
    output_end[...] = output[...]
    grad_tokens_end[...] = grad_tokens[...]
    qkv_end[...] = qkv[:, : qkv_end.shape[1]].astype(f32)
    out_end[...] = out[:, : out_end.shape[1]].astype(f32)
    gu_end[...] = gu[...].astype(f32)
    down_end[...] = down_t[...].astype(f32)
    block = one_end.shape[0]
    width = gains.shape[1]
    start = lax.axis_index("dp") * block
    mine = pltpu.roll(gains[...], lax.rem(width - start, width), 1)
    one_end[...] = mine[0, :block]
    two_end[...] = mine[1, :block]


def on_device_fast(tokens, lengths, gain_one, w_qkv, w_out, gain_two, w_gate_up, w_down, cotangent):
    seq_count, row_count, width = tokens.shape
    own_rows = seq_count * row_count
    f32, low = jnp.float32, jnp.bfloat16
    block = gain_one.shape[0]
    slots = 4 * row_count
    place_of = np.arange(slots, dtype=np.float32)
    frequency = np.float32(10000.0) ** (-np.arange(HD // 2, dtype=np.float32) * np.float32(2.0 / HD))
    angle = place_of[:, None] * frequency[None, :]
    cosine = np.tile(np.cos(angle), (1, 4))
    sine = np.tile(np.concatenate([-np.sin(angle), np.sin(angle)], axis=1), (1, 2))
    rows, qkv_cols = w_qkv.shape
    out_cols = w_out.shape[1]
    units = w_gate_up.shape[1] // 2
    half, strip = w_down.shape
    qkv_wide = -(-qkv_cols // 128) * 128
    out_wide = -(-out_cols // 128) * 128
    deep = 8 * rows
    slabs = KVH // 2
    stack = 2 * QH // KVH * row_count

    def box(*shape, dtype=low):
        return pltpu.VMEM(shape, dtype)

    scratch = [
        box(deep, qkv_wide), box(4, deep, out_wide), box(deep, 3 * units),
        box(deep, qkv_wide), box(deep, out_wide), box(deep, 3 * units),
        box(8, 8, 256, dtype=f32), box(8, deep + 128, dtype=f32),
        box(own_rows, 128, dtype=f32), box(own_rows, 128, dtype=f32),
        box(4 * own_rows, width), box(4 * own_rows, width), box(4 * own_rows, width),
        box(4 * own_rows, width), box(4 * own_rows, QH * HD),
        box(own_rows, width, dtype=f32), box(own_rows, width, dtype=f32),
        box(own_rows, 4 * qkv_wide, dtype=f32),
        box(seq_count * slabs, stack, 128), box(seq_count, 2 * slabs, slots, 128),
        box(seq_count * slabs, stack, slots), box(seq_count * slabs, stack, 128, dtype=f32),
        box(seq_count * slabs, stack, 128),
        box(4, own_rows, out_wide), box(4, own_rows, qkv_wide),
        box(4, own_rows, qkv_wide, dtype=f32), box(4, own_rows, qkv_wide, dtype=f32),
        box(4 * own_rows, out_wide), box(4 * own_rows, qkv_wide),
        box(2, 4 * own_rows, half), box(2, 4 * own_rows, 2 * half),
        box(4, own_rows, width), box(3, own_rows, width),
        box(4, own_rows, width), box(3, own_rows, width),
        box(4, seq_count, 2 * slabs, row_count, 128), box(3, seq_count, 2 * slabs, row_count, 128),
        box(2, 4, rows, qkv_wide), box(2, 4, rows, out_wide),
        box(3, 2, 4, rows, half), box(4, strip, half),
        box(2, 3, rows, qkv_wide), box(2, 3, rows, out_wide),
        box(3, 2, 3, rows, half), box(2, 4, strip, half),
        box(2, 3, 2 * rows, half), box(rows, half),
        box(2, 2, rows, half), box(strip, half),
        box(6, 8, width, dtype=f32), box(6, 8, width, dtype=f32),
        pltpu.SemaphoreType.DMA((SENDS,)),
        pltpu.SemaphoreType.DMA((180,)),
        pltpu.SemaphoreType.DMA((8,)),
    ]
    vmem = pl.BlockSpec(memory_space=pltpu.MemorySpace.VMEM)
    smem = pl.BlockSpec(memory_space=pltpu.MemorySpace.SMEM)
    shapes = (
        jax.ShapeDtypeStruct((own_rows, width), low),
        jax.ShapeDtypeStruct((own_rows, width), low),
        jax.ShapeDtypeStruct((8, width), f32),
        jax.ShapeDtypeStruct((rows, qkv_wide), low),
        jax.ShapeDtypeStruct((rows, out_wide), low),
        jax.ShapeDtypeStruct((rows, 2 * units), low),
        jax.ShapeDtypeStruct((strip, half), low),
    )
    results = pl.pallas_call(
        functools.partial(layer_kernel, {}),
        out_shape=shapes,
        in_specs=[vmem, vmem, smem] + [vmem] * 8,
        out_specs=[vmem] * 7,
        scratch_shapes=scratch,
        compiler_params=pltpu.CompilerParams(
            collective_id=0, has_side_effects=True, vmem_limit_bytes=64 * 2**20
        ),
        name="layer",
    )(
        tokens.reshape(own_rows, width), cotangent.reshape(own_rows, width), lengths,
        w_qkv, w_out, w_gate_up, w_down.T, gain_one, gain_two,
        cosine, sine,
    )
    output, grad_tokens, final_qkv, final_out, final_gu, final_dt, one, two = pl.pallas_call(
        finish_kernel,
        out_shape=(
            jax.ShapeDtypeStruct((own_rows, width), low),
            jax.ShapeDtypeStruct((own_rows, width), low),
            jax.ShapeDtypeStruct((rows, qkv_cols), f32),
            jax.ShapeDtypeStruct((rows, out_cols), f32),
            jax.ShapeDtypeStruct((rows, 2 * units), f32),
            jax.ShapeDtypeStruct((strip, half), f32),
            jax.ShapeDtypeStruct((block,), f32),
            jax.ShapeDtypeStruct((block,), f32),
        ),
        in_specs=[vmem] * 7,
        out_specs=[vmem] * 8,
        name="finish",
    )(*results)
    return (
        output.reshape(tokens.shape), grad_tokens.reshape(tokens.shape),
        one, final_qkv, final_out, two, final_gu, final_dt.T,
    )


def solution(mesh):
    fits = mesh.shape["dp"] == 8 and mesh.shape["ctx"] == 4
    return jax.shard_map(
        on_device_fast if fits else on_device,
        mesh=mesh,
        in_specs=(
            P("dp", "ctx", None),
            P("dp"),
            P("dp"),
            P("dp", "ctx"),
            P("dp", "ctx"),
            P("dp"),
            P("dp", "ctx"),
            P("dp", "ctx"),
            P("dp", "ctx", None),
        ),
        out_specs=(
            P("dp", "ctx", None),
            P("dp", "ctx", None),
            P("dp"),
            P("dp", "ctx"),
            P("dp", "ctx"),
            P("dp"),
            P("dp", "ctx"),
            P("dp", "ctx"),
        ),
        check_vma=False,
    )
```

```python
import enum
import functools
import math

import jax
import jax.numpy as jnp
import numpy as np
from jax import lax
from jax.experimental import pallas as pl
from jax.experimental.pallas import tpu as pltpu
from jax.sharding import PartitionSpec as P

QH = 18
KVH = 6
HD = 64
FF = 3072


EPS = 1e-05
NEGATIVE = -1e30


def angles(position, head_width):
    frequency = 10000.0 ** (-jnp.arange(head_width // 2, dtype=jnp.float32) * 2.0 / head_width)
    angle_table = position.astype(jnp.float32)[:, None] * frequency[None, :]
    return (jnp.cos(angle_table), jnp.sin(angle_table))


def rotate(values_in, cosine, sine_table):
    half_width = values_in.shape[-1] // 2
    first_half = values_in[..., :half_width]
    second = values_in[..., half_width:]
    return jnp.concatenate(
        [first_half * cosine - second * sine_table, second * cosine + first_half * sine_table],
        axis=-1,
    )


def split_heads(values_in, head_count):
    seq_count, row_count, col_count = values_in.shape
    head_width = col_count // head_count
    moved = values_in.reshape(seq_count, row_count, head_count, head_width).transpose(0, 2, 1, 3)
    return moved.reshape(seq_count * head_count, row_count, head_width)


def join_heads(values_in, seq_count):
    item_count, row_count, head_width = values_in.shape
    head_count = item_count // seq_count
    moved = values_in.reshape(seq_count, head_count, row_count, head_width).transpose(0, 2, 1, 3)
    return moved.reshape(seq_count, row_count, head_count * head_width)


def norm_back(source, inverse, gain, grad_in):
    scaled = grad_in * gain
    mean_term = jnp.mean(scaled * source, axis=-1, keepdims=True)
    back_rows = inverse * scaled - source * (inverse * inverse * inverse) * mean_term
    return (back_rows, jnp.sum(grad_in * source * inverse, axis=(0, 1)))


def block_scores(query_rows, key_rows, position, length, group_count, score_scale):
    raw_scores = (
        jnp.einsum("nd,td->nt", query_rows, key_rows, preferred_element_type=jnp.float32)
        * score_scale
    )
    raw_scores = raw_scores.reshape(group_count, position.shape[0], key_rows.shape[0])
    keyidx = jnp.arange(key_rows.shape[0], dtype=jnp.int32)
    allowed = (keyidx[None, :] <= position[:, None]) & (keyidx[None, :] < length)
    return jnp.where(allowed[None], raw_scores, NEGATIVE)


def on_device(tokens, lengths, gain_one, w_qkv, w_out, gain_two, w_gate_up, w_down, cotangent):
    forward_wide = (
        lax.all_gather(w_qkv, "ctx", axis=1, tiled=True),
        lax.all_gather(w_out, "ctx", axis=1, tiled=True),
        lax.all_gather(w_gate_up, "ctx", axis=1, tiled=True),
        lax.all_gather(w_down, "ctx", axis=1, tiled=True),
    )
    qkv_full, out_full, gate_up_full, down_full, gain_fa, gain_fb = (
        lax.all_gather(forward_wide[0], "dp", axis=0, tiled=True),
        lax.all_gather(forward_wide[1], "dp", axis=0, tiled=True),
        lax.all_gather(forward_wide[2], "dp", axis=0, tiled=True),
        lax.all_gather(forward_wide[3], "dp", axis=0, tiled=True),
        lax.all_gather(gain_one, "dp", axis=0, tiled=True),
        lax.all_gather(gain_two, "dp", axis=0, tiled=True),
    )
    seq_count, row_count, model_width = tokens.shape
    query_cols = QH * HD
    key_cols = KVH * HD
    group_count = QH // KVH
    score_scale = 1.0 / math.sqrt(HD)
    position = lax.axis_index("ctx") * row_count + jnp.arange(row_count, dtype=jnp.int32)
    valid_rows = position[None, :] < lengths[:, None]
    cosine, sine_table = angles(position, HD)
    cosine = cosine[:, None, :]
    sine_table = sine_table[:, None, :]
    source = tokens.astype(jnp.float32)
    inverse_one = lax.rsqrt(jnp.mean(source * source, axis=-1, keepdims=True) + EPS)
    normed_one = (source * inverse_one * gain_fa.astype(jnp.float32)).astype(jnp.bfloat16)
    projected = jnp.einsum("bsd,de->bse", normed_one, qkv_full, preferred_element_type=jnp.float32)
    queries = rotate(
        projected[..., :query_cols].reshape(seq_count, row_count, QH, HD), cosine, sine_table
    )
    queries = queries.astype(jnp.bfloat16).reshape(seq_count, row_count, query_cols)
    key_heads = rotate(
        projected[..., query_cols : query_cols + key_cols].reshape(seq_count, row_count, KVH, HD),
        cosine,
        sine_table,
    )
    key_heads = key_heads.astype(jnp.bfloat16).reshape(seq_count, row_count, key_cols)
    value_heads = projected[..., query_cols + key_cols :].astype(jnp.bfloat16)
    keys_all, values_all = (
        lax.all_gather(key_heads, "ctx", axis=1, tiled=True),
        lax.all_gather(value_heads, "ctx", axis=1, tiled=True),
    )
    query_blocks = split_heads(queries, QH).reshape(seq_count * KVH, group_count * row_count, HD)
    key_blocks = split_heads(keys_all, KVH)
    value_blocks = split_heads(values_all, KVH)
    pair_lengths = jnp.repeat(lengths, KVH)

    def forward_block(block_in):
        query_rows, key_rows, value_rows, length = block_in
        scores = block_scores(query_rows, key_rows, position, length, group_count, score_scale)
        row_max = jnp.max(scores, axis=-1, keepdims=True)
        exp_terms = jnp.exp(scores - row_max)
        row_total = jnp.sum(exp_terms, axis=-1, keepdims=True)
        prob_rows = (exp_terms / row_total).astype(jnp.bfloat16)
        result = jnp.einsum(
            "gst,td->gsd", prob_rows, value_rows, preferred_element_type=jnp.float32
        )
        return (result.reshape(-1, HD), (row_max + jnp.log(row_total))[..., 0])

    context_blocks, log_totals = lax.map(
        forward_block, (query_blocks, key_blocks, value_blocks, pair_lengths)
    )
    context = join_heads(context_blocks.reshape(seq_count * QH, row_count, HD), seq_count).astype(
        jnp.bfloat16
    )
    hidden = source + jnp.einsum(
        "bse,ed->bsd", context, out_full, preferred_element_type=jnp.float32
    )
    inverse_two = lax.rsqrt(jnp.mean(hidden * hidden, axis=-1, keepdims=True) + EPS)
    normed_two = (hidden * inverse_two * gain_fb.astype(jnp.float32)).astype(jnp.bfloat16)
    gate_up = jnp.einsum(
        "bsd,df->bsf", normed_two, gate_up_full, preferred_element_type=jnp.float32
    )
    gate_part = gate_up[..., :FF]
    up_part = gate_up[..., FF:]
    gate_sig = jax.nn.sigmoid(gate_part)
    swish_part = gate_part * gate_sig
    activation = (swish_part * up_part).astype(jnp.bfloat16)
    result_rows = hidden + jnp.einsum(
        "bsf,fd->bsd", activation, down_full, preferred_element_type=jnp.float32
    )
    output = jnp.where(valid_rows[..., None], result_rows, 0.0).astype(jnp.bfloat16)
    back_wide = (
        lax.all_gather(w_qkv, "ctx", axis=1, tiled=True),
        lax.all_gather(w_out, "ctx", axis=1, tiled=True),
        lax.all_gather(w_gate_up, "ctx", axis=1, tiled=True),
        lax.all_gather(w_down, "ctx", axis=1, tiled=True),
    )
    qkv_back, out_back, gate_up_back, down_back, gain_ba, gain_bb = (
        lax.all_gather(back_wide[0], "dp", axis=0, tiled=True),
        lax.all_gather(back_wide[1], "dp", axis=0, tiled=True),
        lax.all_gather(back_wide[2], "dp", axis=0, tiled=True),
        lax.all_gather(back_wide[3], "dp", axis=0, tiled=True),
        lax.all_gather(gain_one, "dp", axis=0, tiled=True),
        lax.all_gather(gain_two, "dp", axis=0, tiled=True),
    )
    grad_rows = jnp.where(valid_rows[..., None], cotangent, jnp.zeros_like(cotangent))
    grad_activation = jnp.einsum(
        "bsd,fd->bsf", grad_rows, down_back, preferred_element_type=jnp.float32
    )
    grad_gate = grad_activation * up_part * gate_sig * (1.0 + gate_part * (1.0 - gate_sig))
    grad_up = grad_activation * swish_part
    grad_mix = jnp.concatenate([grad_gate, grad_up], axis=-1).astype(jnp.bfloat16)
    grad_normed_two = jnp.einsum(
        "bsf,df->bsd", grad_mix, gate_up_back, preferred_element_type=jnp.float32
    )
    back_two, grad_gain_two = norm_back(
        hidden, inverse_two, gain_bb.astype(jnp.float32), grad_normed_two
    )
    grad_hidden = grad_rows.astype(jnp.float32) + back_two
    grad_branch = grad_hidden.astype(jnp.bfloat16)
    grad_context = jnp.einsum(
        "bsd,ed->bse", grad_branch, out_back, preferred_element_type=jnp.float32
    ).astype(jnp.bfloat16)
    grad_blocks = split_heads(grad_context, QH).reshape(
        seq_count * KVH, group_count * row_count, HD
    )

    def backward_block(block_in):
        query_rows, key_rows, value_rows, length, log_total, grad_in = block_in
        scores = block_scores(query_rows, key_rows, position, length, group_count, score_scale)
        prob_rows = jnp.exp(scores - log_total[..., None])
        grad_grouped = grad_in.reshape(group_count, -1, HD)
        grad_probs = jnp.einsum(
            "gsd,td->gst", grad_grouped, value_rows, preferred_element_type=jnp.float32
        )
        grad_value = jnp.einsum(
            "gst,gsd->td",
            prob_rows.astype(jnp.bfloat16),
            grad_grouped,
            preferred_element_type=jnp.float32,
        )
        row_delta = jnp.sum(prob_rows * grad_probs, axis=-1, keepdims=True)
        grad_scores = (prob_rows * (grad_probs - row_delta)).astype(jnp.bfloat16)
        grad_query = (
            jnp.einsum("gst,td->gsd", grad_scores, key_rows, preferred_element_type=jnp.float32)
            * score_scale
        )
        grad_key = (
            jnp.einsum(
                "gst,gsd->td",
                grad_scores,
                query_rows.reshape(group_count, -1, HD),
                preferred_element_type=jnp.float32,
            )
            * score_scale
        )
        return (grad_query.reshape(-1, HD), grad_key, grad_value)

    query_grads, key_grads, value_grads = lax.map(
        backward_block,
        (query_blocks, key_blocks, value_blocks, pair_lengths, log_totals, grad_blocks),
    )
    key_sums, value_sums = (
        lax.psum_scatter(
            join_heads(key_grads, seq_count).astype(jnp.bfloat16),
            "ctx",
            scatter_dimension=1,
            tiled=True,
        ).astype(jnp.float32),
        lax.psum_scatter(
            join_heads(value_grads, seq_count).astype(jnp.bfloat16),
            "ctx",
            scatter_dimension=1,
            tiled=True,
        ).astype(jnp.float32),
    )
    grad_queries = join_heads(query_grads.reshape(seq_count * QH, row_count, HD), seq_count)
    turned_queries = rotate(grad_queries.reshape(seq_count, row_count, QH, HD), cosine, -sine_table)
    turned_keys = rotate(key_sums.reshape(seq_count, row_count, KVH, HD), cosine, -sine_table)
    grad_mixed = jnp.concatenate(
        [
            turned_queries.reshape(seq_count, row_count, query_cols),
            turned_keys.reshape(seq_count, row_count, key_cols),
            value_sums,
        ],
        axis=-1,
    ).astype(jnp.bfloat16)
    grad_normed_one = jnp.einsum(
        "bse,de->bsd", grad_mixed, qkv_back, preferred_element_type=jnp.float32
    )
    back_one, grad_gain_one = norm_back(
        source, inverse_one, gain_ba.astype(jnp.float32), grad_normed_one
    )
    grad_tokens = (grad_hidden + back_one).astype(jnp.bfloat16)
    exchanged = (
        lax.all_to_all(grad_mixed, "ctx", split_axis=2, concat_axis=1, tiled=True),
        lax.all_to_all(grad_branch, "ctx", split_axis=2, concat_axis=1, tiled=True),
        lax.all_to_all(grad_mix, "ctx", split_axis=2, concat_axis=1, tiled=True),
        lax.all_to_all(grad_rows, "ctx", split_axis=2, concat_axis=1, tiled=True),
    )
    initial = (
        jnp.zeros((model_width, exchanged[0].shape[2]), jnp.float32),
        jnp.zeros((context.shape[2], exchanged[1].shape[2]), jnp.float32),
        jnp.zeros((model_width, exchanged[2].shape[2]), jnp.float32),
        jnp.zeros((activation.shape[2], exchanged[3].shape[2]), jnp.float32),
    )
    pieces = (
        lax.all_gather(normed_one, "ctx", axis=1, tiled=True),
        lax.all_gather(context, "ctx", axis=1, tiled=True),
        lax.all_gather(normed_two, "ctx", axis=1, tiled=True),
        lax.all_gather(activation, "ctx", axis=1, tiled=True),
    )
    updated = []
    for total, piece, right in zip(initial, pieces, exchanged):
        updated.append(jnp.einsum("bsr,bsc->rc", piece, right, preferred_element_type=jnp.float32))
    column_grads = tuple(updated)
    gain_whole = lax.psum((grad_gain_one, grad_gain_two), "ctx")
    final_qkv, final_out, final_gate_up, final_down, final_gain_one, final_gain_two = (
        lax.psum_scatter(
            column_grads[0].astype(jnp.bfloat16), "dp", scatter_dimension=0, tiled=True
        ).astype(jnp.float32),
        lax.psum_scatter(
            column_grads[1].astype(jnp.bfloat16), "dp", scatter_dimension=0, tiled=True
        ).astype(jnp.float32),
        lax.psum_scatter(
            column_grads[2].astype(jnp.bfloat16), "dp", scatter_dimension=0, tiled=True
        ).astype(jnp.float32),
        lax.psum_scatter(
            column_grads[3].astype(jnp.bfloat16), "dp", scatter_dimension=0, tiled=True
        ).astype(jnp.float32),
        lax.psum_scatter(
            gain_whole[0].astype(jnp.bfloat16), "dp", scatter_dimension=0, tiled=True
        ).astype(jnp.float32),
        lax.psum_scatter(
            gain_whole[1].astype(jnp.bfloat16), "dp", scatter_dimension=0, tiled=True
        ).astype(jnp.float32),
    )
    return (
        output,
        grad_tokens,
        final_gain_one,
        final_qkv,
        final_out,
        final_gain_two,
        final_gate_up,
        final_down,
    )


MESH = pl.DeviceIdType.MESH


class Place:
    def __init__(self):
        self.dp = lax.axis_index("dp")
        self.ctx = lax.axis_index("ctx")
        self.z = lax.div(self.dp, 2)
        self.y = lax.rem(self.dp, 2)
        self.x = lax.div(self.ctx, 2)
        self.c = lax.rem(self.ctx, 2)
        self.up = (self.dp + 2, self.ctx)
        self.down = (self.dp - 2, self.ctx)
        self.across = (self.dp + 1 - 2 * self.y, self.ctx)
        self.chip = (self.dp, (1 - self.x) * 2 + self.c)
        self.core = (self.dp, self.x * 2 + 1 - self.c)
        self.has_up = self.z < 3
        self.has_down = self.z > 0


def greet(place):
    barrier = pltpu.get_barrier_semaphore()

    def tell(device):
        pl.semaphore_signal(barrier, inc=1, device_id=device, device_id_type=MESH)

    pl.when(place.has_up)(lambda: tell(place.up))
    pl.when(place.has_down)(lambda: tell(place.down))
    tell(place.across)
    for step in (1, 2, 3):
        tell((place.dp, lax.rem(place.ctx + step, 4)))
    ends = place.has_up.astype(jnp.int32) + place.has_down.astype(jnp.int32)
    pl.semaphore_wait(barrier, 4 + ends)


class Way(enum.IntEnum):
    BELOW = 0
    ABOVE = 1


BELOW, ABOVE = Way.BELOW, Way.ABOVE
RINGS = (12, 16, 28, 24, 16)
SENDS = sum(RINGS)


class Wires:
    def __init__(self, send_sems, recv_sems, names, place):
        self.kinds = ((place.core,), (place.chip,), (place.across,), (place.up, place.down))
        self.counts = [0] * len(RINGS)
        self.send_sems = send_sems
        self.recv_sems = recv_sems
        self.index = names
        self.total = sum(names.values()) if names else 0
        self.base = {}
        self.live = {}

    def slot(self, name, size=1):
        if name not in self.base:
            self.base[name] = self.total
            self.total += size
        return self.base[name]

    def spot(self, name, plane):
        if name[0] in ("down", "down_y"):
            return self.slot(name[:2])
        if name[0] == "ddown":
            return self.slot(name[:3])
        if name[:2] in GROUPED or name[0] in SWAPS:
            return self.slot(name[:2] if name[:2] in GROUPED else name[:1])
        if len(name) > 2 and isinstance(name[-2], Way):
            way, dist = name[-2:]
            source = plane - dist if way == BELOW else plane + dist
            if name[-3] == "z":
                return self.slot(name[:-2], 5) + source + int(way)
            return self.slot(name[:-2], 4) + source
        return self.slot(name)

    def send(self, src, dst, name, device, cond=None, extra=None):
        kind = 4
        for at, devices in enumerate(self.kinds):
            if any(device is known for known in devices):
                kind = at
        number = (kind, self.counts[kind])
        self.counts[kind] += 1
        self.settle((kind, number[1] - RINGS[kind]))
        at = self.spot(name, lax.div(device[0], 2))
        if extra is not None:
            at = at + extra
        copy = pltpu.make_async_remote_copy(
            src_ref=src,
            dst_ref=dst,
            send_sem=self.send_sems.at[sum(RINGS[:kind]) + number[1] % RINGS[kind]],
            recv_sem=self.recv_sems.at[at],
            device_id=device,
            device_id_type=MESH,
        )
        when(cond, copy.start)
        self.live[number] = (copy, cond, name)

    def take(self, dst, name, device, extra=None):
        at = self.spot(name, lax.div(lax.axis_index("dp"), 2))
        if extra is not None:
            at = at + extra
        pltpu.make_async_remote_copy(
            src_ref=dst,
            dst_ref=dst,
            send_sem=self.send_sems.at[0],
            recv_sem=self.recv_sems.at[at],
            device_id=device,
            device_id_type=MESH,
        ).wait_recv()

    def settle(self, number):
        if number in self.live:
            copy, cond, name = self.live.pop(number)
            when(cond, copy.wait_send)

    def drain(self):
        for number in list(self.live):
            self.settle(number)

    def drain_named(self, first):
        for number in list(self.live):
            if self.live[number][2][0] == first:
                self.settle(number)


GROUPED = (("out", "c"), ("out", "d"), ("gain", "y")) + tuple((("gu", n), "y") for n in range(3))
SWAPS = ("pq", "kv", "gb", "gm")


def both(first, second):
    return second if first is None else jnp.logical_and(first, second)


def source_valid(place, way, dist):
    return place.z >= dist if way == BELOW else place.z + dist <= 3


def source_pos(place, way, dist):
    return place.dp - 2 * dist if way == BELOW else place.dp + 2 * dist


def flood_start(wires, place, name, own, block, spread):
    wires.send(own, block(place.dp), (name, BELOW, 1), place.up, place.has_up)
    wires.send(own, block(place.dp), (name, ABOVE, 1), place.down, place.has_down)
    wires.send(own, block(place.dp), (name, "y", 0, 0), place.across)
    spread(own, place.dp, (0, 0, 0), None)


def flood_step(wires, place, name, block, spread, way, dist):
    here = source_valid(place, way, dist)
    pos = source_pos(place, way, dist)
    view = block(pos)
    came_from = place.down if way == BELOW else place.up
    pl.when(here)(lambda: wires.take(view, (name, way, dist), came_from))
    if dist < 3:
        onward = place.up if way == BELOW else place.down
        more = place.has_up if way == BELOW else place.has_down
        wires.send(view, view, (name, way, dist + 1), onward, jnp.logical_and(here, more))
    wires.send(view, view, (name, "y", way, dist), place.across, here)
    spread(view, pos, (0, way, dist), here)


def flood_side(wires, place, name, block, spread, way, dist):
    if dist == 0:
        here, pos = None, place.dp
    else:
        here, pos = source_valid(place, way, dist), source_pos(place, way, dist)
    pos = pos + 1 - 2 * place.y
    view = block(pos)
    if here is None:
        wires.take(view, (name, "y", 0, 0), place.across)
    else:
        pl.when(here)(lambda: wires.take(view, (name, "y", way, dist), place.across))
    spread(view, pos, (1, way, dist), here)


HOPS = [(way, dist) for dist in (1, 2, 3) for way in (BELOW, ABOVE)]


def no_spread(view, pos, key, cond):
    return None


def add_rows(dst, srcs, out=None, cast=None, chunk=48):
    out = dst if out is None else out
    total_rows = dst.shape[0]
    if total_rows % chunk:
        chunk = total_rows

    def body(i, carry):
        at = pl.ds(pl.multiple_of(i * chunk, 16), chunk)
        total = dst[at, :].astype(jnp.float32)
        for src in srcs:
            total = total + src[at, :].astype(jnp.float32)
        out[at, :] = total.astype(out.dtype)
        return carry

    lax.fori_loop(0, total_rows // chunk, body, 0)


def when(cond, action):
    if cond is None:
        action()
    else:
        pl.when(cond)(action)


DRAIN = [(way, dist) for dist in (3, 2, 1, 0) for way in (BELOW, ABOVE)]


def nn(a, b):
    return jnp.dot(a, b, preferred_element_type=jnp.float32)


def nt(a, b):
    return lax.dot_general(a, b, (((1,), (1,)), ((), ())), preferred_element_type=jnp.float32)


def tn(a, b):
    return lax.dot_general(a, b, (((0,), (0,)), ((), ())), preferred_element_type=jnp.float32)


def layer_kernel(
    names,
    tokens, cot, lengths, qkv_in, out_in, gu_in, dt_in, gain_one, gain_two, cos_table, sin_table,
    output, grad_tokens, gain_out, qkv_out, out_out, gu_out, dt_out,
    w_qkv, w_out, w_rest, out_pad, w_ff, d_qkv, d_out, d_ff, gain_all, gain_row, cos, sin,
    tok_all, n1_all, n2_all, g_all, ctx_all, hidden, grad_hidden, proj, q_st, kv_all, p_st, att, go_st,
    wide, gm, pq, pq_in, gb_all, gm_all, act, d_gu, gp, gp_box, op, op_box, dkv, dkv_box,
    qkv_side, out_side, gu_side, down_side, qkv_inbox, out_inbox, gu_inbox, down_inbox,
    up_inbox, up_side, gu_mix, down_mix, gain_box, gain_acc,
    send_sems, recv_sems, local_sems,
):
    f32, low = jnp.float32, jnp.bfloat16
    place = Place()
    wires = Wires(send_sems, recv_sems, names, place)
    dp, ctx, z, y, x, c = place.dp, place.ctx, place.z, place.y, place.x, place.c
    rows = qkv_in.shape[0]
    strip, half = dt_in.shape
    width = tokens.shape[1]
    own_rows = tokens.shape[0]
    slots_here = own_rows // 2
    qkv_cols, out_cols = qkv_in.shape[1], out_in.shape[1]
    qkv_wide, out_wide = w_qkv.shape[1], out_pad.shape[1]
    main = w_out.shape[2]
    packed = w_out.shape[1] // 8
    spare = packed - rows
    rest = out_cols - main
    pieces = -(-rows // spare)
    group = QH // KVH
    slabs = KVH // 2
    q_slabs = QH // 2
    span = 3 * half
    deep = w_ff.shape[0]
    score_scale = 1.0 / math.sqrt(HD)
    TILES = range(2)

    greet(place)

    def block_rows(pos):
        return pl.ds(pl.multiple_of(pos * rows, 16), rows)

    def lead_rows(lead):
        return pl.ds(pl.multiple_of(lead * own_rows, 16), own_rows)

    here_rows = lead_rows(ctx)
    my_rows = block_rows(dp)

    def share(name, ref):
        mine = ref.at[here_rows]
        wires.send(mine, mine, (name, "x"), place.chip)
        wires.send(mine, mine, (name, "c"), place.core)

    def share_on(name, ref):
        far = ref.at[lead_rows(place.chip[1])]
        wires.take(far, (name, "x"), place.chip)
        wires.send(far, far, (name, "d"), place.core)

    def share_end(name, ref):
        for mark, lead in (("c", place.core[1]), ("d", 3 - ctx)):
            wires.take(ref.at[lead_rows(lead)], (name, mark), place.core)

    def swap_start(name, src, dst):
        for step in (1, 2, 3):
            peer = lax.rem(ctx + step, 4)
            wires.send(src(peer), dst(ctx), (name, step), (dp, peer))

    def swap_end(name, three):
        wires.take(three, (name, 1), place.core)

    locals_ = []

    def local(src, dst, cond=None):
        copy = pltpu.make_async_copy(src, dst, local_sems.at[len(locals_)])
        locals_.append((copy, cond))
        when(cond, copy.start)

    SIDES = [(0, 0)] + HOPS
    WAYS = {0: [(0, 0)], 1: HOPS[:2], 2: HOPS[2:4], 3: HOPS[4:]}

    class Flood:
        def __init__(self, name, block, spread=no_spread):
            self.name, self.block, self.spread = name, block, spread

        def start(self):
            flood_start(wires, place, self.name, self.block(dp), self.block, self.spread)

        def hop(self, dist, way):
            way = Way(way)
            flood_step(wires, place, self.name, self.block, self.spread, way, dist)

        def side(self, dist, way):
            way = Way(way) if dist else way
            flood_side(wires, place, self.name, self.block, self.spread, way, dist)

    class PairFlood:
        def __init__(self, name, ref, cols):
            self.name, self.ref, self.cols = name, ref, cols

        def pair(self, plane):
            return self.ref.at[pl.ds(pl.multiple_of(2 * rows * plane, 16), 2 * rows), self.cols]

        def one(self, pos):
            return self.ref.at[block_rows(pos), self.cols]

        def start(self):
            wires.send(self.one(dp), self.one(dp), (self.name, "y"), place.across)

        def side(self):
            wires.take(self.one(place.across[0]), (self.name, "y"), place.across)
            view = self.pair(z)
            wires.send(view, view, (self.name, BELOW, 1), place.up, place.has_up)
            wires.send(view, view, (self.name, ABOVE, 1), place.down, place.has_down)

        def hop(self, dist, way):
            way = Way(way)
            here = source_valid(place, way, dist)
            view = self.pair(z - dist if way == BELOW else z + dist)
            came_from = place.down if way == BELOW else place.up
            pl.when(here)(lambda: wires.take(view, (self.name, way, dist), came_from))
            if dist < 3:
                onward = place.up if way == BELOW else place.down
                more = place.has_up if way == BELOW else place.has_down
                wires.send(view, view, (self.name, way, dist + 1), onward, jnp.logical_and(here, more))

    def packed_rows(pos):
        return pl.ds(pl.multiple_of(pos * packed, 16), packed)

    def pack(values, dest):
        dest[:rows, :] = values[:, :main].astype(low)
        for slab in range(0, main, 128):
            total = jnp.zeros((spare, 128), f32)
            for number in range(slab // rest, min(pieces, (slab + 128) // rest)):
                height = min(spare, rows - number * spare)
                piece = values[number * spare : number * spare + height, main : main + 128]
                if height < spare:
                    piece = jnp.concatenate([piece, jnp.zeros((spare - height, 128), f32)], axis=0)
                shift = number * rest - slab
                total = total + (pltpu.roll(piece, shift, 1) if shift else piece)
            dest[rows:, slab : slab + 128] = total.astype(low)

    def unpack(view, dest):
        keep = lax.broadcasted_iota(jnp.int32, (spare, 128), 1) < rest
        for number in range(pieces):
            slab = number * rest // 128 * 128
            shift = number * rest - slab
            piece = view[rows:, slab : slab + 128].astype(f32)
            piece = pltpu.roll(piece, 128 - shift, 1) if shift else piece
            height = min(spare, rows - number * spare)
            piece = jnp.where(keep, piece, 0.0).astype(low)
            dest[number * spare : number * spare + height, :] = piece[:height]

    def out_weights(j):
        first = jnp.concatenate([w_out[j, pos * packed : pos * packed + rows, :] for pos in range(8)], axis=0)
        return jnp.concatenate([first, w_rest[j]], axis=1)

    def out_block(lead, pos):
        return w_out.at[lead, packed_rows(pos)]

    def out_spread(view, pos, key, cond):
        wires.send(view, out_block(ctx, pos), ("out", "x") + key, place.chip, cond)
        wires.send(view, out_block(ctx, pos), ("out", "c") + key, place.core, cond)

    qkv_flood = Flood("qkv", lambda pos: w_qkv.at[block_rows(pos)])
    gain_flood = Flood("gain", lambda pos: gain_all.at[pos])
    out_flood = Flood("out", functools.partial(out_block, ctx), out_spread)

    PARTS = [(tile, part) for tile in TILES for part in range(2)]

    def part_cols(number):
        tile, part = PARTS[number]
        return pl.ds(tile * span + part * half, half)

    def gu_view(ref, number, pos):
        return ref.at[block_rows(pos), part_cols(number)]

    gu_floods = [Flood(("gu", number), functools.partial(gu_view, w_ff, number)) for number in range(3)]
    up_flood = PairFlood("up", w_ff, part_cols(3))

    def spots(column, dist, way=None):
        for way, dist in WAYS[dist] if way is None else [(way, dist)]:
            if dist == 0:
                here, pos = None, dp
            else:
                here, pos = source_valid(place, way, dist), source_pos(place, way, dist)
            if column == 1:
                pos = pos + 1 - 2 * y
            yield (column, way, dist), here, pos

    def out_chip(column, dist, way):
        way = Way(way) if dist else way
        for key, here, pos in spots(column, dist, way):
            view = out_block(place.chip[1], pos)
            when(here, lambda: wires.take(view, ("out", "x") + key, place.chip))
            wires.send(view, view, ("out", "d") + key, place.core, here)

    def out_core():
        for mark, lead in (("c", place.core[1]), ("d", 3 - ctx)):
            wires.take(w_out.at[lead], ("out", mark), place.core)

    def gu_sides(number):
        wires.take(w_ff.at[pl.ds(0, 4 * rows), part_cols(number)], (("gu", number), "y"), place.across)

    def mix_start(tile):
        for part in range(2):
            target = 2 * c + part
            src = gu_in.at[:, pl.ds((2 * part + tile) * half, half)]
            dst = w_ff.at[my_rows, pl.ds(pl.multiple_of(tile * span + x * half, 128), half)]
            wires.slot(("gu_mix", tile), 2)
            wires.send(src, dst, ("gu_mix", tile), (dp, target), target != ctx, extra=x)
            local(src, dst, target == ctx)

    def mix_end(number):
        tile, part = PARTS[number]
        origin = part * 2 + x
        view = gu_view(w_ff, number, dp)
        pl.when(origin != ctx)(lambda: wires.take(view, ("gu_mix", tile), (dp, origin), extra=part))

    lanes = pl.ds(pl.multiple_of(y * span + 2 * half, 128), half)
    other_lanes = pl.ds(pl.multiple_of((1 - y) * span + 2 * half, 128), half)
    at_home = ctx == z

    def strips_of(ref, at):
        return [ref.at[pl.ds(j * strip, strip), at] for j in range(4)]

    strips, other_strips = strips_of(w_ff, lanes), strips_of(w_ff, other_lanes)

    def down_mix_start():
        dst = w_ff.at[pl.ds(pl.multiple_of(ctx * strip, 16), strip), lanes]
        wires.slot(("down_mix",), 4)
        wires.send(dt_in, dst, ("down_mix",), (dp, z), ctx != z, extra=ctx)
        local(dt_in, dst, ctx == z)

    def tables():
        for table, ref in ((cos_table, cos), (sin_table, sin)):
            mine = table[pl.ds(pl.multiple_of(ctx * slots_here, 16), slots_here), :]
            ref[:slots_here, :] = mine
            ref[slots_here:, :] = mine

    def down_start(j):
        pl.when(jnp.logical_and(at_home, ctx != j))(lambda: wires.take(strips[j], ("down_mix",), (dp, j), extra=j))
        wires.send(strips[j], strips[j], ("down", j, BELOW, 1), place.up, jnp.logical_and(at_home, place.has_up))
        wires.send(strips[j], strips[j], ("down", j, ABOVE, 1), place.down, jnp.logical_and(at_home, place.has_down))
        wires.send(strips[j], strips[j], ("down_y", j, 0, 0), place.across, at_home)

    def down_hop(dist, j):
        for way in (BELOW, ABOVE):
            here = (z - ctx if way == BELOW else ctx - z) == dist
            came_from = place.down if way == BELOW else place.up
            onward = place.up if way == BELOW else place.down
            more = place.has_up if way == BELOW else place.has_down
            pl.when(here)(lambda: wires.take(strips[j], ("down", j, way, dist), came_from))
            if dist < 3:
                wires.send(strips[j], strips[j], ("down", j, way, dist + 1), onward, jnp.logical_and(here, more))
            wires.send(strips[j], strips[j], ("down_y", j, way, dist), place.across, here)

    def down_side_end():
        for way, dist in SIDES:
            here = at_home if dist == 0 else (z - ctx if way == BELOW else ctx - z) == dist

            def take():
                for j in range(4):
                    wires.take(other_strips[j], ("down_y", j, way, dist), place.across)

            pl.when(here)(take)

    row_at = lax.broadcasted_iota(jnp.int32, (own_rows, 1), 0)
    first_seq = row_at < slots_here
    position = ctx * slots_here + jnp.where(first_seq, row_at, row_at - slots_here)
    valid = position < jnp.where(first_seq, lengths[0], lengths[1])
    def tokens_start():
        tok_all[here_rows, :] = tokens[...]
        share("tok", tok_all)

    def qkv_start():
        w_qkv[my_rows, :] = jnp.zeros((rows, qkv_wide), low)
        w_qkv[my_rows, :qkv_cols] = qkv_in[...]
        qkv_flood.start()

    def gain_start():
        gain_all[dp] = jnp.zeros(gain_all.shape[1:], f32)
        gain_all[dp, 0:1, :rows] = gain_one[...].reshape(1, rows).astype(f32)
        gain_all[dp, 1:2, :rows] = gain_two[...].reshape(1, rows).astype(f32)
        gain_flood.start()

    def out_start():
        out_pad[...] = jnp.zeros(out_pad.shape, low)
        out_pad[:, :out_cols] = out_in[...]
        pack(out_pad[...].astype(f32), out_block(ctx, dp))
        out_flood.start()

    def cot_start():
        g_all[here_rows, :] = jnp.where(valid, cot[...].astype(f32), 0.0).astype(low)
        share("cot", g_all)

    def gain_sides():
        wires.take(gain_all.at[pl.ds(0, 4)], ("gain", "y"), place.across)

    gain_a = lambda: gain_row[0:1, :width]
    gain_b = lambda: gain_row[1:2, :width]

    def norm(values):
        return lax.rsqrt(jnp.mean(values * values, axis=-1, keepdims=True) + EPS)

    lane = lax.broadcasted_iota(jnp.int32, (own_rows, 128), 1)
    low_half = lax.rem(lane, HD) < HD // 2
    side_of = lax.div(lane, HD)

    def turn(values, sign):
        swapped = jnp.where(low_half, pltpu.roll(values, 128 - HD // 2, 1), pltpu.roll(values, HD // 2, 1))
        return values * cos[...] + swapped * (sin[...] * sign)

    def head_spots():
        for head in range(QH):
            kv = head // group
            yield head // 2, head % 2, kv // 2, kv % 2, (kv % 2 * group + head % group) * slots_here

    def stack_heads(slab_of, dest, scale):
        for slab, side, key_slab, key_side, at in head_spots():
            values = slab_of(slab)
            if side != key_side:
                values = pltpu.roll(values, HD, 1)
            values = (jnp.where(side_of == key_side, values, 0.0) * scale).astype(low)
            for seq in range(2):
                dest[seq * slabs + key_slab, at : at + slots_here, :] = values[
                    seq * slots_here : (seq + 1) * slots_here
                ]

    def unstack_heads(src, slab):
        total = jnp.zeros((own_rows, 128), f32)
        for at_slab, side, key_slab, key_side, at in head_spots():
            if at_slab != slab:
                continue
            values = jnp.concatenate(
                [src[seq * slabs + key_slab, at : at + slots_here, :] for seq in range(2)], axis=0
            )
            values = jnp.where(side_of == key_side, values, 0.0)
            if side != key_side:
                values = pltpu.roll(values, HD, 1)
            total = total + values
        return total

    def project():
        gain_row[...] = jnp.zeros(gain_row.shape, f32)
        for pos in range(8):
            piece = gain_all[pos]
            shift = (pos * rows) % 128
            if shift:
                piece = pltpu.roll(piece, shift, 1)
            at = (pos * rows) // 128 * 128
            gain_row[:, at : at + 256] += piece

        def body(i, carry):
            at = lead_rows(i)
            source = tok_all[at, :].astype(f32)
            n1_all[at, :] = (source * norm(source) * gain_a()).astype(low)
            return carry

        lax.fori_loop(0, 4, body, 0)
        pq[...] = nn(n1_all[...], w_qkv[...]).reshape(pq.shape)
        pq_in[ctx] = pq[ctx]
        swap_start("pq", lambda peer: pq.at[peer], lambda sender: pq_in.at[sender])

    def pq_end():
        swap_end("pq", pq_in.at[pl.ds(0, 3)])
        proj[...] = jnp.zeros(proj.shape, f32)
        for j in range(4):
            part = jnp.concatenate([pq_in[j], jnp.zeros((own_rows, 128), f32)], axis=1)
            at = qkv_cols * j
            if at % 128:
                part = pltpu.roll(part, at % 128, 1)
            proj[:, at // 128 * 128 : at // 128 * 128 + qkv_wide + 128] += part

    turned = {}

    def query_slab(slab):
        if slab not in turned:
            turned[slab] = turn(proj[:, slab * 128 : slab * 128 + 128], 1.0)
        return turned[slab]

    def slot_view(lead):
        return kv_all.at[:, :, pl.ds(pl.multiple_of(lead * slots_here, 16), slots_here)]

    def kv_start():
        my_slots = pl.ds(pl.multiple_of(ctx * slots_here, 16), slots_here)
        for slab in range(2 * slabs):
            at = (q_slabs + slab) * 128
            values = proj[:, at : at + 128]
            if slab < slabs:
                values = turn(values, 1.0)
            values = values.astype(low)
            for seq in range(2):
                kv_all[seq, slab, my_slots, :] = values[seq * slots_here : (seq + 1) * slots_here]

        swap_start("kv", lambda peer: slot_view(ctx), slot_view)

    def queries():
        stack_heads(query_slab, q_st, score_scale)

    def kv_end():
        swap_end("kv", kv_all.at[:, :, pl.ds(0, 3 * slots_here)])

    stack = q_st.shape[1]
    slots = kv_all.shape[2]

    def attend(i, carry):
        seq, slab = lax.div(i, slabs), lax.rem(i, slabs)
        scores = nt(q_st[i], kv_all[seq, slab])
        at = ctx * slots_here + lax.rem(lax.broadcasted_iota(jnp.int32, (stack, slots), 0), slots_here)
        key_at = lax.broadcasted_iota(jnp.int32, (stack, slots), 1)
        length = jnp.where(seq == 0, lengths[0], lengths[1])
        allowed = jnp.logical_and(key_at <= at, key_at < length)
        scores = jnp.where(allowed, scores, NEGATIVE)
        terms = jnp.exp(scores - jnp.max(scores, axis=-1, keepdims=True))
        probs = (terms / jnp.sum(terms, axis=-1, keepdims=True)).astype(low)
        p_st[i] = probs
        att[i] = nn(probs, kv_all[seq, slabs + slab])
        return carry

    def attention():
        lax.fori_loop(0, 2 * slabs, attend, 0)
        for slab in range(q_slabs):
            ctx_all[here_rows, slab * 128 : slab * 128 + 128] = unstack_heads(att, slab).astype(low)
        share("ctx", ctx_all)

    def out_project():
        for j in range(4):
            for pos in range(8):
                unpack(w_out.at[j, packed_rows(pos)], w_rest.at[j, block_rows(pos)])
        hidden[...] = tokens[...].astype(f32)
        for j in range(4):
            part = nn(ctx_all[here_rows, :], out_weights(j))
            at = out_cols * j
            if at % 128:
                part = pltpu.roll(part, at % 128, 1)
            hidden[:, at // 128 * 128 : at // 128 * 128 + out_wide] += part
        n2_all[here_rows, :] = (hidden[...] * norm(hidden[...]) * gain_b()).astype(low)
        share("n2", n2_all)

    tall = 2 * own_rows

    def feed(tile):
        def body(i, carry):
            at = pl.ds(0, 4 * own_rows)
            gate = nn(n2_all[at, :], w_ff[:, tile * span : tile * span + half])
            up = nn(n2_all[at, :], w_ff[:, tile * span + half : tile * span + 2 * half])
            back = nn(g_all[at, :], w_ff[:, tile * span + 2 * half : (tile + 1) * span])
            sig = jax.nn.sigmoid(gate)
            swish = gate * sig
            act[tile, at, :] = (swish * up).astype(low)
            d_gu[tile, at, :half] = (back * up * sig * (1.0 + gate * (1.0 - sig))).astype(low)
            d_gu[tile, at, half:] = (back * swish).astype(low)
            return carry

        body(0, 0)

    def grad_ff(tile):
        def body(m, carry):
            at = pl.ds(pl.multiple_of(m * width, 128), width)
            d_ff[at, tile * span : tile * span + 2 * half] = tn(n2_all[:, at], d_gu[tile]).astype(low)
            d_ff[at, tile * span + 2 * half : (tile + 1) * span] = tn(g_all[:, at], act[tile]).astype(low)
            return carry

        lax.fori_loop(0, 1, body, 0)

    across_core = (1 - x) * 2 + 1 - c
    across_own = (1 - x) * 2 + c
    beside = x * 2 + 1 - c
    wide_tile = width

    def group_send(name, ref, box, which):
        lead, mark = ((across_core, "cx"), (beside, "cc"))[which]
        wires.send(ref.at[lead], box.at[which], (name, mark), place.core)

    def group_on(name, ref, box):
        wires.take(box.at[0], (name, "cx"), place.core)
        mine = ref.at[across_own]
        mine[...] = (mine[...].astype(f32) + box[0].astype(f32)).astype(low)
        wires.send(mine, box.at[2], (name, "x"), place.chip)

    def group_end(name, ref, box):
        wires.take(box.at[1], (name, "cc"), place.core)
        wires.take(box.at[2], (name, "x"), place.chip)
        return ref[ctx].astype(f32) + box[1].astype(f32) + box[2].astype(f32)

    def pair_rows(half_x):
        return pl.ds(pl.multiple_of(half_x * tall, 16), tall)

    def group_product(ref, terms):
        def compute(half_x):
            def body(n, carry):
                at = pl.ds(pl.multiple_of(n * wide_tile, 128), wide_tile)
                total = None
                for left, right in terms:
                    term = nt(left(pair_rows(half_x)), right(at))
                    total = term if total is None else total + term
                ref[2 * half_x, :, at] = total[:own_rows].astype(low)
                ref[2 * half_x + 1, :, at] = total[own_rows:].astype(low)
                return carry

            lax.fori_loop(0, width // wide_tile, body, 0)

        return compute

    back_terms = [
        (lambda at, tile=tile: d_gu[tile, at, :], lambda at, tile=tile: w_ff[at, tile * span : tile * span + 2 * half])
        for tile in TILES
    ]
    forward_terms = [
        (lambda at, tile=tile: act[tile, at, :], lambda at, tile=tile: w_ff[at, tile * span + 2 * half : (tile + 1) * span])
        for tile in TILES
    ]

    def key_pos(way, dist):
        if dist == 0:
            return None, dp
        return source_valid(place, way, dist), source_pos(place, way, dist)

    KEYS = {3: DRAIN[:2], 2: DRAIN[2:4], 1: DRAIN[4:6], 0: [(BELOW, 0)]}
    flip = 1 - 2 * y

    def z_add(name, view, boxes, inbox, way, dist):
        here, pos = key_pos(way, dist)
        mine = view(pos)
        if dist == 0:
            wires.take(boxes.at[way, dist], (name, "y", way, dist), place.across)
            add_rows(mine, [boxes.at[way, dist]])
            for end, fed, feeder in ((BELOW, place.has_up, place.up), (ABOVE, place.has_down, place.down)):

                def own():
                    wires.take(inbox.at[end, 0], (name, "z", end, 0), feeder)
                    add_rows(mine, [inbox.at[end, 0]])

                pl.when(fed)(own)
            return
        fed = place.has_up if way == BELOW else place.has_down
        feeder = place.up if way == BELOW else place.down
        onward = place.down if way == BELOW else place.up
        side = boxes.at[way, dist]

        def first():
            wires.take(side, (name, "y", way, dist), place.across)
            add_rows(mine, [side])

        if dist == 3:
            pl.when(here)(first)
        else:

            def more():
                wires.take(side, (name, "y", way, dist), place.across)
                wires.take(inbox.at[way, dist], (name, "z", way, dist), feeder)
                add_rows(mine, [side, inbox.at[way, dist]])

            pl.when(jnp.logical_and(here, jnp.logical_not(fed)))(first)
            pl.when(jnp.logical_and(here, fed))(more)
        wires.send(mine, inbox.at[way, dist - 1], (name, "z", way, dist - 1), onward, here)

    class Sink:
        def __init__(self, name, view, side, inbox):
            self.name, self.view, self.side, self.inbox = name, view, side, inbox

        def send(self, dist, way):
            way = Way(way) if dist else way
            here, pos = key_pos(way, dist)
            wires.send(
                self.view(pos + flip), self.side.at[way, dist],
                (self.name, "y", way, dist), place.across, here,
            )

        def add(self, dist, way):
            way = Way(way) if dist else way
            z_add(self.name, self.view, self.side, self.inbox, way, dist)

    gu_sinks = [
        Sink(("dgu", number), functools.partial(gu_view, d_ff, number), gu_side.at[number], gu_inbox.at[number])
        for number in range(3)
    ]
    out_sink = Sink("dout", lambda pos: d_out.at[packed_rows(pos)], out_side, out_inbox)
    qkv_sink = Sink("dqkv", lambda pos: d_qkv.at[block_rows(pos)], qkv_side, qkv_inbox)
    d_strips, d_other_strips = strips_of(d_ff, lanes), strips_of(d_ff, other_lanes)

    def down_send(tile, j):
        wires.send(d_other_strips[j], down_side.at[j], ("ddown_y", j), place.across, (1 - y) == tile)

    def down_add(dist, j):
        if dist == 0:

            def finish():
                wires.take(down_side.at[j], ("ddown_y", j), place.across)
                add_rows(d_strips[j], [down_side.at[j]])
                for end, fed, feeder in ((BELOW, place.has_up, place.up), (ABOVE, place.has_down, place.down)):

                    def more():
                        wires.take(down_inbox.at[end, j], ("ddown", j, end, 0), feeder)
                        add_rows(d_strips[j], [down_inbox.at[end, j]])

                    pl.when(fed)(more)

            pl.when(at_home)(finish)
            return
        for way in (BELOW, ABOVE):
            here = (z - ctx if way == BELOW else ctx - z) == dist
            fed = place.has_up if way == BELOW else place.has_down
            feeder = place.up if way == BELOW else place.down
            onward = place.down if way == BELOW else place.up

            def first():
                wires.take(down_side.at[j], ("ddown_y", j), place.across)
                add_rows(d_strips[j], [down_side.at[j]])

            def more():
                wires.take(down_side.at[j], ("ddown_y", j), place.across)
                wires.take(down_inbox.at[way, j], ("ddown", j, way, dist), feeder)
                add_rows(d_strips[j], [down_side.at[j], down_inbox.at[way, j]])

            pl.when(jnp.logical_and(here, jnp.logical_not(fed)))(first)
            pl.when(jnp.logical_and(here, fed))(more)
            wires.send(d_strips[j], down_inbox.at[way, j], ("ddown", j, way, dist - 1), onward, here)

    class PairSink:
        def __init__(self, name, ref, cols, inbox, side):
            self.name, self.ref, self.cols, self.inbox, self.side = name, ref, cols, inbox, side

        def pair(self, plane):
            return self.ref.at[pl.ds(pl.multiple_of(2 * rows * plane, 16), 2 * rows), self.cols]

        def one(self, pos):
            return self.ref.at[block_rows(pos), self.cols]

        def add(self, dist, way):
            if dist == 0:
                mine = self.pair(z)
                for end, fed, feeder in ((BELOW, place.has_up, place.up), (ABOVE, place.has_down, place.down)):

                    def more():
                        wires.take(self.inbox.at[end, 0], (self.name, "z", end, 0), feeder)
                        add_rows(mine, [self.inbox.at[end, 0]])

                    pl.when(fed)(more)
                wires.send(self.one(place.across[0]), self.side, (self.name, "y"), place.across)
                return
            way = Way(way)
            here = source_valid(place, way, dist)
            mine = self.pair(z - dist if way == BELOW else z + dist)
            fed = place.has_up if way == BELOW else place.has_down
            feeder = place.up if way == BELOW else place.down
            onward = place.down if way == BELOW else place.up
            if dist < 3:

                def more():
                    wires.take(self.inbox.at[way, dist], (self.name, "z", way, dist), feeder)
                    add_rows(mine, [self.inbox.at[way, dist]])

                pl.when(jnp.logical_and(here, fed))(more)
            wires.send(mine, self.inbox.at[way, dist - 1], (self.name, "z", way, dist - 1), onward, here)

        def end(self):
            wires.take(self.side, (self.name, "y"), place.across)
            add_rows(self.one(dp), [self.side])

    up_sink = PairSink("dup", d_ff, part_cols(3), up_inbox, up_side)

    def gu_finish(number):
        tile, part = PARTS[number]
        target = part * 2 + x
        block = gu_view(d_ff, number, dp)
        wires.slot(("dgu_mix", tile), 2)
        wires.send(block, gu_mix.at[c, tile], ("dgu_mix", tile), (dp, target), target != ctx, extra=c)
        pl.when(target == ctx)(lambda: add_rows(block, [], out=gu_mix.at[c, tile]))

    def gu_end(number):
        tile, part = PARTS[number]
        origin = 2 * c + part
        box = gu_mix.at[part, tile]
        pl.when(origin != ctx)(lambda: wires.take(box, ("dgu_mix", tile), (dp, origin), extra=part))
        add_rows(box, [], out=gu_out.at[:, pl.ds((2 * part + tile) * half, half)])

    def down_finish():
        for j in range(4):
            wires.send(d_strips[j], down_mix, ("ddown_mix",), (dp, j), jnp.logical_and(at_home, ctx != j))
            pl.when(jnp.logical_and(at_home, ctx == j))(functools.partial(add_rows, d_strips[j], [], down_mix))

    def down_end():
        pl.when(ctx != z)(lambda: wires.take(down_mix, ("ddown_mix",), (dp, z)))
        add_rows(down_mix, [], out=dt_out)

    def norm_back(values, inverse, gain, grad_in):
        scaled = grad_in * gain
        mean_term = jnp.mean(scaled * values, axis=-1, keepdims=True)
        back = inverse * scaled - values * (inverse * inverse * inverse) * mean_term
        return back, jnp.sum(grad_in * values * inverse, axis=0, keepdims=True)

    def gp_block(which):
        half_x = 1 - x if which == 0 else x
        group_product(gp, back_terms)(half_x)
        group_send("gp", gp, gp_box, which)

    def op_block(which):
        half_x = 1 - x if which == 0 else x
        group_product(op, forward_terms)(half_x)
        group_send("op", op, op_box, which)

    def hidden_back():
        gain_acc[0] = jnp.zeros(gain_out.shape, f32)
        back_two, gain_two_grad = norm_back(hidden[...], norm(hidden[...]), gain_b(), group_end("gp", gp, gp_box))
        gain_acc[0, 1:2, :] = gain_two_grad
        grad_hidden[...] = g_all[here_rows, :].astype(f32) + back_two
        out_lane = lax.broadcasted_iota(jnp.int32, (own_rows, out_wide), 1)
        for j in range(4):
            at = out_cols * j
            part = grad_hidden[:, at // 128 * 128 : at // 128 * 128 + out_wide]
            if at % 128:
                part = pltpu.roll(part, out_wide - at % 128, 1)
            wide[j] = jnp.where(out_lane < out_cols, part, 0.0).astype(low)
        gb_all[here_rows, :] = wide[ctx]
        swap_start("gb", lambda peer: wide.at[peer], lambda sender: gb_all.at[lead_rows(sender)])

    def context_back(n, carry):
        at = pl.ds(0, width)
        total = nt(wide[0], out_weights(0))
        for j in range(1, 4):
            total = total + nt(wide[j], out_weights(j))
        proj[:, at] = total
        return carry

    def grad_context():
        lax.fori_loop(0, width // wide_tile, context_back, 0)
        stack_heads(lambda slab: proj[:, slab * 128 : slab * 128 + 128], go_st, 1.0)

    def attend_back(i, carry):
        seq, slab = lax.div(i, slabs), lax.rem(i, slabs)
        grad_probs = nt(go_st[i], kv_all[seq, slabs + slab])
        probs = p_st[i].astype(f32)
        delta = jnp.sum(probs * grad_probs, axis=-1, keepdims=True)
        grad_scores = (probs * (grad_probs - delta)).astype(low)
        att[i] = nn(grad_scores, kv_all[seq, slab]) * score_scale
        grad_key = tn(grad_scores, q_st[i])
        grad_value = tn(p_st[i], go_st[i])
        for j in range(4):
            part = slice(j * slots_here, (j + 1) * slots_here)
            dkv[j, seq, slab] = grad_key[part].astype(low)
            dkv[j, seq, slabs + slab] = grad_value[part].astype(low)
        return carry

    def attention_back():
        lax.fori_loop(0, 2 * slabs, attend_back, 0)
        group_send("dkv", dkv, dkv_box, 0)
        group_send("dkv", dkv, dkv_box, 1)

    def gb_end():
        swap_end("gb", gb_all.at[pl.ds(0, 3 * own_rows)])

    def grad_out_all():
        result = tn(ctx_all[...], gb_all[...])
        for pos in range(8):
            pack(result[pos * rows : (pos + 1) * rows], d_out.at[packed_rows(pos)])

    def grad_mixed():
        sums = group_end("dkv", dkv, dkv_box)
        proj[...] = jnp.zeros(proj.shape, f32)
        for slab in range(q_slabs):
            proj[:, slab * 128 : slab * 128 + 128] = turn(unstack_heads(att, slab), -1.0)
        for slab in range(2 * slabs):
            values = jnp.concatenate([sums[0, slab], sums[1, slab]], axis=0)
            if slab < slabs:
                values = turn(values, -1.0)
            at = (q_slabs + slab) * 128
            proj[:, at : at + 128] = values
        qkv_lane = lax.broadcasted_iota(jnp.int32, (own_rows, qkv_wide), 1)
        for j in range(4):
            at = qkv_cols * j
            part = proj[:, at // 128 * 128 : at // 128 * 128 + qkv_wide + 128]
            if at % 128:
                part = pltpu.roll(part, qkv_wide + 128 - at % 128, 1)
            gm[j] = jnp.where(qkv_lane < qkv_cols, part[:, :qkv_wide], 0.0).astype(low)
        gm_all[here_rows, :] = gm[ctx]
        swap_start("gm", lambda peer: gm.at[peer], lambda sender: gm_all.at[lead_rows(sender)])

    def gm_end():
        swap_end("gm", gm_all.at[pl.ds(0, 3 * own_rows)])

    def grad_qkv(m, carry):
        at = pl.ds(pl.multiple_of(m * width, 128), width)
        d_qkv[at, :] = tn(n1_all[:, at], gm_all[...]).astype(low)
        return carry

    def grad_qkv_all():
        lax.fori_loop(0, 1, grad_qkv, 0)

    tokens_terms = [(lambda at: gm_all[at, :], lambda at: w_qkv[at, :])]

    def gt_block(which):
        if which == 0:
            wires.drain_named("gp")
        half_x = 1 - x if which == 0 else x
        group_product(gp, tokens_terms)(half_x)
        group_send("gt", gp, gp_box, which)

    def output_end():
        result = hidden[...] + group_end("op", op, op_box)
        output[...] = jnp.where(valid, result, 0.0).astype(low)

    def tokens_end():
        source = tokens[...].astype(f32)
        back_one, gain_one_grad = norm_back(source, norm(source), gain_a(), group_end("gt", gp, gp_box))
        gain_acc[0, 0:1, :] = gain_one_grad
        grad_tokens[...] = (grad_hidden[...] + back_one).astype(low)

    low_end, high_end = z == 0, z == 3
    mid_low, mid_high = z == 1, z == 2

    def gain_send(hop):
        def go(device, cond=None):
            wires.send(gain_acc.at[hop], gain_box.at[hop], ("gain_sum", hop), device, cond)

        if hop < 3:
            go((place.core, place.chip, place.across)[hop])
        elif hop == 3:
            go(place.up, low_end)
            go(place.down, high_end)
        elif hop == 4:
            go(place.up, mid_low)
            go(place.down, mid_high)
        else:
            go(place.down, mid_low)
            go(place.up, mid_high)

    def gain_take(hop):
        def add(device):
            wires.take(gain_box.at[hop], ("gain_sum", hop), device)
            gain_acc[hop + 1] = gain_acc[hop] + gain_box[hop]

        def last(device):
            wires.take(gain_box.at[hop], ("gain_sum", hop), device)
            gain_out[...] = gain_box[hop]

        def done():
            gain_out[...] = gain_acc[hop]

        if hop < 3:
            add((place.core, place.chip, place.across)[hop])
        elif hop == 3:
            pl.when(mid_low)(lambda: add(place.down))
            pl.when(mid_high)(lambda: add(place.up))
        elif hop == 4:
            pl.when(mid_low)(lambda: add(place.up))
            pl.when(mid_high)(lambda: add(place.down))
        else:
            pl.when(low_end)(lambda: last(place.up))
            pl.when(high_end)(lambda: last(place.down))
            pl.when(mid_low)(done)
            pl.when(mid_high)(done)

    def out_end():
        mine = d_out.at[packed_rows(dp)]
        out_out[:, :main] = mine[:rows, :]
        unpack(mine, out_out.at[:, pl.ds(main, 128)])

    def qkv_end():
        qkv_out[...] = d_qkv[my_rows, :]

    def locals_end():
        for copy, cond in locals_:
            when(cond, copy.wait)

    mix_start(0)
    qkv_start()
    out_start()
    down_mix_start()
    tables()
    tokens_start()
    mix_start(1)
    cot_start()
    out_chip(0, 0, 0)
    mix_end(0)
    locals_end()
    gu_floods[0].start()
    qkv_flood.hop(1, 1)
    mix_end(1)
    out_flood.hop(1, 1)
    out_flood.side(0, 0)
    qkv_flood.hop(1, 0)
    qkv_flood.hop(2, 0)
    gain_start()
    gain_flood.hop(1, 0)
    gain_flood.hop(2, 0)
    gain_flood.hop(3, 0)
    out_flood.hop(1, 0)
    gu_floods[1].start()
    gain_flood.hop(1, 1)
    gain_flood.hop(2, 1)
    gain_flood.hop(3, 1)
    qkv_flood.hop(2, 1)
    qkv_flood.hop(3, 1)
    out_flood.hop(2, 0)
    qkv_flood.side(1, 0)
    qkv_flood.hop(3, 0)
    down_start(1)
    share_on("tok", tok_all)
    out_flood.hop(2, 1)
    out_flood.hop(3, 1)
    mix_end(2)
    gu_floods[2].start()
    down_start(0)
    gain_sides()
    qkv_flood.side(3, 0)
    qkv_flood.side(2, 0)
    qkv_flood.side(2, 1)
    down_start(3)
    share_end("tok", tok_all)
    gu_floods[0].hop(1, 0)
    qkv_flood.side(3, 1)
    qkv_flood.side(0, 0)
    qkv_flood.side(1, 1)
    project()
    down_hop(1, 1)
    down_hop(2, 1)
    down_hop(1, 0)
    down_hop(2, 0)
    out_flood.hop(3, 0)
    mix_end(3)
    out_chip(0, 1, 0)
    up_flood.start()
    down_start(2)
    down_hop(1, 3)
    down_hop(1, 2)
    down_hop(2, 2)
    gu_floods[0].hop(2, 0)
    gu_floods[2].hop(1, 0)
    pq_end()
    kv_start()
    gu_floods[0].hop(1, 1)
    out_flood.side(3, 0)
    down_hop(3, 2)
    out_chip(0, 3, 0)
    gu_floods[0].hop(3, 0)
    share_on("cot", g_all)
    gu_floods[1].hop(1, 1)
    queries()
    out_flood.side(1, 1)
    down_hop(2, 3)
    gu_floods[2].hop(1, 1)
    out_flood.side(1, 0)
    out_chip(0, 1, 1)
    down_hop(3, 1)
    out_flood.side(2, 0)
    out_flood.side(3, 1)
    down_hop(3, 3)
    out_flood.side(2, 1)
    out_chip(0, 2, 0)
    down_hop(3, 0)
    up_flood.side()
    gu_floods[1].hop(1, 0)
    gu_floods[1].hop(2, 1)
    kv_end()
    attention()
    gu_floods[0].hop(2, 1)
    out_chip(1, 0, 0)
    out_chip(1, 3, 0)
    out_chip(1, 1, 1)
    out_chip(0, 2, 1)
    out_chip(1, 1, 0)
    up_flood.hop(1, 0)
    out_chip(0, 3, 1)
    out_chip(1, 2, 1)
    out_chip(1, 3, 1)
    share_end("cot", g_all)
    out_chip(1, 2, 0)
    gu_floods[1].hop(3, 1)
    out_core()
    up_flood.hop(1, 1)
    gu_floods[1].hop(2, 0)
    out_project()
    gu_floods[0].hop(3, 1)
    gu_floods[2].hop(2, 0)
    down_side_end()
    up_flood.hop(2, 0)
    gu_floods[2].hop(2, 1)
    up_flood.hop(2, 1)
    gu_floods[1].hop(3, 0)
    gu_floods[2].hop(3, 1)
    share_on("n2", n2_all)
    gu_sides(0)
    gu_sides(1)
    share_end("n2", n2_all)
    gu_floods[2].hop(3, 0)
    feed(0)
    grad_ff(0)
    gu_sinks[1].send(3, 0)
    gu_sinks[0].send(3, 1)
    gu_sinks[0].send(2, 1)
    up_flood.hop(3, 1)
    gu_sides(2)
    gu_sinks[1].send(3, 1)
    gu_sinks[0].send(2, 0)
    up_flood.hop(3, 0)
    feed(1)
    grad_ff(1)
    gu_sinks[1].send(2, 0)
    gu_sinks[1].send(2, 1)
    up_sink.add(3, 1)
    up_sink.add(3, 0)
    gu_sinks[0].send(3, 0)
    gu_sinks[2].send(3, 1)
    gp_block(0)
    down_send(0, 0)
    gu_sinks[2].send(3, 0)
    gu_sinks[1].send(1, 0)
    down_send(1, 0)
    op_block(0)
    down_send(0, 1)
    down_send(0, 3)
    group_on("gp", gp, gp_box)
    group_on("op", op, op_box)
    gp_block(1)
    down_send(0, 2)
    gu_sinks[1].add(3, 0)
    gu_sinks[1].add(2, 0)
    down_send(1, 1)
    down_send(1, 3)
    gu_sinks[0].send(0, 0)
    gu_sinks[0].send(1, 1)
    gu_sinks[2].send(2, 0)
    up_sink.add(2, 1)
    gu_sinks[0].add(3, 0)
    up_sink.add(1, 1)
    gu_sinks[0].add(2, 0)
    gu_sinks[1].add(3, 1)
    share_on("ctx", ctx_all)
    hidden_back()
    grad_context()
    up_sink.add(2, 0)
    gu_sinks[0].add(3, 1)
    attention_back()
    group_on("dkv", dkv, dkv_box)
    share_end("ctx", ctx_all)
    down_send(1, 2)
    down_add(3, 0)
    gu_sinks[2].add(3, 0)
    gb_end()
    gu_sinks[2].send(1, 0)
    down_add(3, 1)
    gu_sinks[2].send(2, 1)
    gu_sinks[0].add(2, 1)
    grad_out_all()
    out_sink.send(3, 0)
    down_add(3, 3)
    gu_sinks[2].add(3, 1)
    gu_sinks[0].send(1, 0)
    gu_sinks[1].send(1, 1)
    gu_sinks[1].add(2, 1)
    gu_sinks[1].add(1, 0)
    grad_mixed()
    out_sink.send(3, 1)
    down_add(3, 2)
    up_sink.add(1, 0)
    down_add(2, 1)
    down_add(2, 3)
    gm_end()
    grad_qkv_all()
    out_sink.send(1, 1)
    gu_sinks[2].send(1, 1)
    out_sink.send(1, 0)
    gu_sinks[0].add(1, 1)
    gu_sinks[2].send(0, 0)
    qkv_sink.send(3, 1)
    down_add(1, 1)
    gu_sinks[2].add(2, 0)
    gt_block(0)
    down_add(1, 3)
    gu_sinks[1].send(0, 0)
    down_add(0, 1)
    down_add(2, 0)
    gt_block(1)
    down_add(2, 2)
    gu_sinks[2].add(2, 1)
    gu_sinks[1].add(1, 1)
    out_sink.send(2, 0)
    group_on("gt", gp, gp_box)
    out_sink.add(3, 1)
    qkv_sink.send(3, 0)
    gu_sinks[0].add(1, 0)
    up_sink.add(0, 0)
    qkv_sink.send(2, 0)
    out_sink.send(2, 1)
    down_add(1, 0)
    qkv_sink.send(2, 1)
    tokens_end()
    gain_send(0)
    gain_take(0)
    out_sink.add(3, 0)
    gu_sinks[2].add(1, 1)
    gain_send(1)
    down_add(1, 2)
    gu_sinks[2].add(1, 0)
    gu_sinks[0].add(0, 0)
    gu_finish(0)
    gain_take(1)
    qkv_sink.add(3, 1)
    out_sink.add(2, 1)
    gain_send(2)
    down_add(0, 0)
    op_block(1)
    qkv_sink.send(1, 0)
    qkv_sink.add(3, 0)
    gu_sinks[1].add(0, 0)
    gu_finish(1)
    down_add(0, 3)
    qkv_sink.send(1, 1)
    qkv_sink.send(0, 0)
    up_sink.end()
    gu_sinks[2].add(0, 0)
    gu_finish(3)
    out_sink.add(2, 0)
    output_end()
    gu_finish(2)
    gain_take(2)
    gain_send(3)
    qkv_sink.add(2, 1)
    qkv_sink.add(2, 0)
    gain_take(3)
    gain_send(4)
    out_sink.send(0, 0)
    down_add(0, 2)
    down_finish()
    out_sink.add(1, 1)
    out_sink.add(1, 0)
    gu_end(0)
    qkv_sink.add(1, 0)
    qkv_sink.add(1, 1)
    gain_take(4)
    gain_send(5)
    out_sink.add(0, 0)
    out_end()
    gu_end(3)
    gu_end(1)
    down_end()
    gu_end(2)
    qkv_sink.add(0, 0)
    qkv_end()
    gain_take(5)
    wires.drain()


def finish_kernel(
    output, grad_tokens, gains, qkv, out, gu, down_t,
    output_end, grad_tokens_end, qkv_end, out_end, gu_end, down_end, one_end, two_end,
):
    f32 = jnp.float32
    output_end[...] = output[...]
    grad_tokens_end[...] = grad_tokens[...]
    qkv_end[...] = qkv[:, : qkv_end.shape[1]].astype(f32)
    out_end[...] = out[:, : out_end.shape[1]].astype(f32)
    gu_end[...] = gu[...].astype(f32)
    down_end[...] = down_t[...].astype(f32)
    block = one_end.shape[0]
    width = gains.shape[1]
    start = lax.axis_index("dp") * block
    mine = pltpu.roll(gains[...], lax.rem(width - start, width), 1)
    one_end[...] = mine[0, :block]
    two_end[...] = mine[1, :block]


def on_device_fast(tokens, lengths, gain_one, w_qkv, w_out, gain_two, w_gate_up, w_down, cotangent):
    seq_count, row_count, width = tokens.shape
    own_rows = seq_count * row_count
    f32, low = jnp.float32, jnp.bfloat16
    block = gain_one.shape[0]
    slots = 4 * row_count
    place_of = np.arange(slots, dtype=np.float32)
    frequency = np.float32(10000.0) ** (-np.arange(HD // 2, dtype=np.float32) * np.float32(2.0 / HD))
    angle = place_of[:, None] * frequency[None, :]
    cosine = np.tile(np.cos(angle), (1, 4))
    sine = np.tile(np.concatenate([-np.sin(angle), np.sin(angle)], axis=1), (1, 2))
    rows, qkv_cols = w_qkv.shape
    out_cols = w_out.shape[1]
    units = w_gate_up.shape[1] // 2
    half, strip = w_down.shape
    qkv_wide = -(-qkv_cols // 128) * 128
    out_wide = -(-out_cols // 128) * 128
    deep = 8 * rows
    main = out_cols // 128 * 128
    packed = rows + 32
    slabs = KVH // 2
    stack = 2 * QH // KVH * row_count

    def box(*shape, dtype=low):
        return pltpu.VMEM(shape, dtype)

    scratch = [
        box(deep, qkv_wide), box(4, 8 * packed, main), box(4, deep, 128), box(rows, out_wide), box(deep, 3 * units),
        box(deep, qkv_wide), box(8 * packed, main), box(deep, 3 * units),
        box(8, 8, 256, dtype=f32), box(8, deep + 128, dtype=f32),
        box(own_rows, 128, dtype=f32), box(own_rows, 128, dtype=f32),
        box(4 * own_rows, width), box(4 * own_rows, width), box(4 * own_rows, width),
        box(4 * own_rows, width), box(4 * own_rows, QH * HD),
        box(own_rows, width, dtype=f32), box(own_rows, width, dtype=f32),
        box(own_rows, 4 * qkv_wide, dtype=f32),
        box(seq_count * slabs, stack, 128), box(seq_count, 2 * slabs, slots, 128),
        box(seq_count * slabs, stack, slots), box(seq_count * slabs, stack, 128, dtype=f32),
        box(seq_count * slabs, stack, 128),
        box(4, own_rows, out_wide), box(4, own_rows, qkv_wide),
        box(4, own_rows, qkv_wide, dtype=f32), box(4, own_rows, qkv_wide, dtype=f32),
        box(4 * own_rows, out_wide), box(4 * own_rows, qkv_wide),
        box(2, 4 * own_rows, half), box(2, 4 * own_rows, 2 * half),
        box(4, own_rows, width), box(3, own_rows, width),
        box(4, own_rows, width), box(3, own_rows, width),
        box(4, seq_count, 2 * slabs, row_count, 128), box(3, seq_count, 2 * slabs, row_count, 128),
        box(2, 4, rows, qkv_wide), box(2, 4, packed, main),
        box(3, 2, 4, rows, half), box(4, strip, half),
        box(2, 3, rows, qkv_wide), box(2, 3, packed, main),
        box(3, 2, 3, rows, half), box(2, 4, strip, half),
        box(2, 3, 2 * rows, half), box(rows, half),
        box(2, 2, rows, half), box(strip, half),
        box(6, 8, width, dtype=f32), box(6, 8, width, dtype=f32),
        pltpu.SemaphoreType.DMA((SENDS,)),
        pltpu.SemaphoreType.DMA((180,)),
        pltpu.SemaphoreType.DMA((8,)),
    ]
    vmem = pl.BlockSpec(memory_space=pltpu.MemorySpace.VMEM)
    hbm = pl.BlockSpec(memory_space=pltpu.MemorySpace.HBM)
    smem = pl.BlockSpec(memory_space=pltpu.MemorySpace.SMEM)
    shapes = (
        jax.ShapeDtypeStruct((own_rows, width), low),
        jax.ShapeDtypeStruct((own_rows, width), low),
        jax.ShapeDtypeStruct((8, width), f32),
        jax.ShapeDtypeStruct((rows, qkv_wide), low),
        jax.ShapeDtypeStruct((rows, out_wide), low),
        jax.ShapeDtypeStruct((rows, 2 * units), low),
        jax.ShapeDtypeStruct((strip, half), low),
    )
    results = pl.pallas_call(
        functools.partial(layer_kernel, {}),
        out_shape=shapes,
        in_specs=[vmem, vmem, smem, vmem, vmem, hbm, hbm] + [vmem] * 4,
        out_specs=[vmem] * 7,
        scratch_shapes=scratch,
        compiler_params=pltpu.CompilerParams(
            collective_id=0, has_side_effects=True, vmem_limit_bytes=64 * 2**20
        ),
        name="layer",
    )(
        tokens.reshape(own_rows, width), cotangent.reshape(own_rows, width), lengths,
        w_qkv, w_out, w_gate_up, w_down.T, gain_one, gain_two,
        cosine, sine,
    )
    output, grad_tokens, final_qkv, final_out, final_gu, final_dt, one, two = pl.pallas_call(
        finish_kernel,
        out_shape=(
            jax.ShapeDtypeStruct((own_rows, width), low),
            jax.ShapeDtypeStruct((own_rows, width), low),
            jax.ShapeDtypeStruct((rows, qkv_cols), f32),
            jax.ShapeDtypeStruct((rows, out_cols), f32),
            jax.ShapeDtypeStruct((rows, 2 * units), f32),
            jax.ShapeDtypeStruct((strip, half), f32),
            jax.ShapeDtypeStruct((block,), f32),
            jax.ShapeDtypeStruct((block,), f32),
        ),
        in_specs=[vmem] * 7,
        out_specs=[vmem] * 8,
        name="finish",
    )(*results)
    return (
        output.reshape(tokens.shape), grad_tokens.reshape(tokens.shape),
        one, final_qkv, final_out, two, final_gu, final_dt.T,
    )


def solution(mesh):
    fits = mesh.shape["dp"] == 8 and mesh.shape["ctx"] == 4
    return jax.shard_map(
        on_device_fast if fits else on_device,
        mesh=mesh,
        in_specs=(
            P("dp", "ctx", None),
            P("dp"),
            P("dp"),
            P("dp", "ctx"),
            P("dp", "ctx"),
            P("dp"),
            P("dp", "ctx"),
            P("dp", "ctx"),
            P("dp", "ctx", None),
        ),
        out_specs=(
            P("dp", "ctx", None),
            P("dp", "ctx", None),
            P("dp"),
            P("dp", "ctx"),
            P("dp", "ctx"),
            P("dp"),
            P("dp", "ctx"),
            P("dp", "ctx"),
        ),
        check_vma=False,
    )
```

```python
import enum
import functools
import math

import jax
import jax.numpy as jnp
import numpy as np
from jax import lax
from jax.experimental import pallas as pl
from jax.experimental.pallas import tpu as pltpu
from jax.sharding import PartitionSpec as P

QH = 18
KVH = 6
HD = 64
FF = 3072


EPS = 1e-05
NEGATIVE = -1e30


def angles(position, head_width):
    frequency = 10000.0 ** (-jnp.arange(head_width // 2, dtype=jnp.float32) * 2.0 / head_width)
    angle_table = position.astype(jnp.float32)[:, None] * frequency[None, :]
    return (jnp.cos(angle_table), jnp.sin(angle_table))


def rotate(values_in, cosine, sine_table):
    half_width = values_in.shape[-1] // 2
    first_half = values_in[..., :half_width]
    second = values_in[..., half_width:]
    return jnp.concatenate(
        [first_half * cosine - second * sine_table, second * cosine + first_half * sine_table],
        axis=-1,
    )


def split_heads(values_in, head_count):
    seq_count, row_count, col_count = values_in.shape
    head_width = col_count // head_count
    moved = values_in.reshape(seq_count, row_count, head_count, head_width).transpose(0, 2, 1, 3)
    return moved.reshape(seq_count * head_count, row_count, head_width)


def join_heads(values_in, seq_count):
    item_count, row_count, head_width = values_in.shape
    head_count = item_count // seq_count
    moved = values_in.reshape(seq_count, head_count, row_count, head_width).transpose(0, 2, 1, 3)
    return moved.reshape(seq_count, row_count, head_count * head_width)


def norm_back(source, inverse, gain, grad_in):
    scaled = grad_in * gain
    mean_term = jnp.mean(scaled * source, axis=-1, keepdims=True)
    back_rows = inverse * scaled - source * (inverse * inverse * inverse) * mean_term
    return (back_rows, jnp.sum(grad_in * source * inverse, axis=(0, 1)))


def block_scores(query_rows, key_rows, position, length, group_count, score_scale):
    raw_scores = (
        jnp.einsum("nd,td->nt", query_rows, key_rows, preferred_element_type=jnp.float32)
        * score_scale
    )
    raw_scores = raw_scores.reshape(group_count, position.shape[0], key_rows.shape[0])
    keyidx = jnp.arange(key_rows.shape[0], dtype=jnp.int32)
    allowed = (keyidx[None, :] <= position[:, None]) & (keyidx[None, :] < length)
    return jnp.where(allowed[None], raw_scores, NEGATIVE)


def on_device(tokens, lengths, gain_one, w_qkv, w_out, gain_two, w_gate_up, w_down, cotangent):
    forward_wide = (
        lax.all_gather(w_qkv, "ctx", axis=1, tiled=True),
        lax.all_gather(w_out, "ctx", axis=1, tiled=True),
        lax.all_gather(w_gate_up, "ctx", axis=1, tiled=True),
        lax.all_gather(w_down, "ctx", axis=1, tiled=True),
    )
    qkv_full, out_full, gate_up_full, down_full, gain_fa, gain_fb = (
        lax.all_gather(forward_wide[0], "dp", axis=0, tiled=True),
        lax.all_gather(forward_wide[1], "dp", axis=0, tiled=True),
        lax.all_gather(forward_wide[2], "dp", axis=0, tiled=True),
        lax.all_gather(forward_wide[3], "dp", axis=0, tiled=True),
        lax.all_gather(gain_one, "dp", axis=0, tiled=True),
        lax.all_gather(gain_two, "dp", axis=0, tiled=True),
    )
    seq_count, row_count, model_width = tokens.shape
    query_cols = QH * HD
    key_cols = KVH * HD
    group_count = QH // KVH
    score_scale = 1.0 / math.sqrt(HD)
    position = lax.axis_index("ctx") * row_count + jnp.arange(row_count, dtype=jnp.int32)
    valid_rows = position[None, :] < lengths[:, None]
    cosine, sine_table = angles(position, HD)
    cosine = cosine[:, None, :]
    sine_table = sine_table[:, None, :]
    source = tokens.astype(jnp.float32)
    inverse_one = lax.rsqrt(jnp.mean(source * source, axis=-1, keepdims=True) + EPS)
    normed_one = (source * inverse_one * gain_fa.astype(jnp.float32)).astype(jnp.bfloat16)
    projected = jnp.einsum("bsd,de->bse", normed_one, qkv_full, preferred_element_type=jnp.float32)
    queries = rotate(
        projected[..., :query_cols].reshape(seq_count, row_count, QH, HD), cosine, sine_table
    )
    queries = queries.astype(jnp.bfloat16).reshape(seq_count, row_count, query_cols)
    key_heads = rotate(
        projected[..., query_cols : query_cols + key_cols].reshape(seq_count, row_count, KVH, HD),
        cosine,
        sine_table,
    )
    key_heads = key_heads.astype(jnp.bfloat16).reshape(seq_count, row_count, key_cols)
    value_heads = projected[..., query_cols + key_cols :].astype(jnp.bfloat16)
    keys_all, values_all = (
        lax.all_gather(key_heads, "ctx", axis=1, tiled=True),
        lax.all_gather(value_heads, "ctx", axis=1, tiled=True),
    )
    query_blocks = split_heads(queries, QH).reshape(seq_count * KVH, group_count * row_count, HD)
    key_blocks = split_heads(keys_all, KVH)
    value_blocks = split_heads(values_all, KVH)
    pair_lengths = jnp.repeat(lengths, KVH)

    def forward_block(block_in):
        query_rows, key_rows, value_rows, length = block_in
        scores = block_scores(query_rows, key_rows, position, length, group_count, score_scale)
        row_max = jnp.max(scores, axis=-1, keepdims=True)
        exp_terms = jnp.exp(scores - row_max)
        row_total = jnp.sum(exp_terms, axis=-1, keepdims=True)
        prob_rows = (exp_terms / row_total).astype(jnp.bfloat16)
        result = jnp.einsum(
            "gst,td->gsd", prob_rows, value_rows, preferred_element_type=jnp.float32
        )
        return (result.reshape(-1, HD), (row_max + jnp.log(row_total))[..., 0])

    context_blocks, log_totals = lax.map(
        forward_block, (query_blocks, key_blocks, value_blocks, pair_lengths)
    )
    context = join_heads(context_blocks.reshape(seq_count * QH, row_count, HD), seq_count).astype(
        jnp.bfloat16
    )
    hidden = source + jnp.einsum(
        "bse,ed->bsd", context, out_full, preferred_element_type=jnp.float32
    )
    inverse_two = lax.rsqrt(jnp.mean(hidden * hidden, axis=-1, keepdims=True) + EPS)
    normed_two = (hidden * inverse_two * gain_fb.astype(jnp.float32)).astype(jnp.bfloat16)
    gate_up = jnp.einsum(
        "bsd,df->bsf", normed_two, gate_up_full, preferred_element_type=jnp.float32
    )
    gate_part = gate_up[..., :FF]
    up_part = gate_up[..., FF:]
    gate_sig = jax.nn.sigmoid(gate_part)
    swish_part = gate_part * gate_sig
    activation = (swish_part * up_part).astype(jnp.bfloat16)
    result_rows = hidden + jnp.einsum(
        "bsf,fd->bsd", activation, down_full, preferred_element_type=jnp.float32
    )
    output = jnp.where(valid_rows[..., None], result_rows, 0.0).astype(jnp.bfloat16)
    back_wide = (
        lax.all_gather(w_qkv, "ctx", axis=1, tiled=True),
        lax.all_gather(w_out, "ctx", axis=1, tiled=True),
        lax.all_gather(w_gate_up, "ctx", axis=1, tiled=True),
        lax.all_gather(w_down, "ctx", axis=1, tiled=True),
    )
    qkv_back, out_back, gate_up_back, down_back, gain_ba, gain_bb = (
        lax.all_gather(back_wide[0], "dp", axis=0, tiled=True),
        lax.all_gather(back_wide[1], "dp", axis=0, tiled=True),
        lax.all_gather(back_wide[2], "dp", axis=0, tiled=True),
        lax.all_gather(back_wide[3], "dp", axis=0, tiled=True),
        lax.all_gather(gain_one, "dp", axis=0, tiled=True),
        lax.all_gather(gain_two, "dp", axis=0, tiled=True),
    )
    grad_rows = jnp.where(valid_rows[..., None], cotangent, jnp.zeros_like(cotangent))
    grad_activation = jnp.einsum(
        "bsd,fd->bsf", grad_rows, down_back, preferred_element_type=jnp.float32
    )
    grad_gate = grad_activation * up_part * gate_sig * (1.0 + gate_part * (1.0 - gate_sig))
    grad_up = grad_activation * swish_part
    grad_mix = jnp.concatenate([grad_gate, grad_up], axis=-1).astype(jnp.bfloat16)
    grad_normed_two = jnp.einsum(
        "bsf,df->bsd", grad_mix, gate_up_back, preferred_element_type=jnp.float32
    )
    back_two, grad_gain_two = norm_back(
        hidden, inverse_two, gain_bb.astype(jnp.float32), grad_normed_two
    )
    grad_hidden = grad_rows.astype(jnp.float32) + back_two
    grad_branch = grad_hidden.astype(jnp.bfloat16)
    grad_context = jnp.einsum(
        "bsd,ed->bse", grad_branch, out_back, preferred_element_type=jnp.float32
    ).astype(jnp.bfloat16)
    grad_blocks = split_heads(grad_context, QH).reshape(
        seq_count * KVH, group_count * row_count, HD
    )

    def backward_block(block_in):
        query_rows, key_rows, value_rows, length, log_total, grad_in = block_in
        scores = block_scores(query_rows, key_rows, position, length, group_count, score_scale)
        prob_rows = jnp.exp(scores - log_total[..., None])
        grad_grouped = grad_in.reshape(group_count, -1, HD)
        grad_probs = jnp.einsum(
            "gsd,td->gst", grad_grouped, value_rows, preferred_element_type=jnp.float32
        )
        grad_value = jnp.einsum(
            "gst,gsd->td",
            prob_rows.astype(jnp.bfloat16),
            grad_grouped,
            preferred_element_type=jnp.float32,
        )
        row_delta = jnp.sum(prob_rows * grad_probs, axis=-1, keepdims=True)
        grad_scores = (prob_rows * (grad_probs - row_delta)).astype(jnp.bfloat16)
        grad_query = (
            jnp.einsum("gst,td->gsd", grad_scores, key_rows, preferred_element_type=jnp.float32)
            * score_scale
        )
        grad_key = (
            jnp.einsum(
                "gst,gsd->td",
                grad_scores,
                query_rows.reshape(group_count, -1, HD),
                preferred_element_type=jnp.float32,
            )
            * score_scale
        )
        return (grad_query.reshape(-1, HD), grad_key, grad_value)

    query_grads, key_grads, value_grads = lax.map(
        backward_block,
        (query_blocks, key_blocks, value_blocks, pair_lengths, log_totals, grad_blocks),
    )
    key_sums, value_sums = (
        lax.psum_scatter(
            join_heads(key_grads, seq_count).astype(jnp.bfloat16),
            "ctx",
            scatter_dimension=1,
            tiled=True,
        ).astype(jnp.float32),
        lax.psum_scatter(
            join_heads(value_grads, seq_count).astype(jnp.bfloat16),
            "ctx",
            scatter_dimension=1,
            tiled=True,
        ).astype(jnp.float32),
    )
    grad_queries = join_heads(query_grads.reshape(seq_count * QH, row_count, HD), seq_count)
    turned_queries = rotate(grad_queries.reshape(seq_count, row_count, QH, HD), cosine, -sine_table)
    turned_keys = rotate(key_sums.reshape(seq_count, row_count, KVH, HD), cosine, -sine_table)
    grad_mixed = jnp.concatenate(
        [
            turned_queries.reshape(seq_count, row_count, query_cols),
            turned_keys.reshape(seq_count, row_count, key_cols),
            value_sums,
        ],
        axis=-1,
    ).astype(jnp.bfloat16)
    grad_normed_one = jnp.einsum(
        "bse,de->bsd", grad_mixed, qkv_back, preferred_element_type=jnp.float32
    )
    back_one, grad_gain_one = norm_back(
        source, inverse_one, gain_ba.astype(jnp.float32), grad_normed_one
    )
    grad_tokens = (grad_hidden + back_one).astype(jnp.bfloat16)
    exchanged = (
        lax.all_to_all(grad_mixed, "ctx", split_axis=2, concat_axis=1, tiled=True),
        lax.all_to_all(grad_branch, "ctx", split_axis=2, concat_axis=1, tiled=True),
        lax.all_to_all(grad_mix, "ctx", split_axis=2, concat_axis=1, tiled=True),
        lax.all_to_all(grad_rows, "ctx", split_axis=2, concat_axis=1, tiled=True),
    )
    initial = (
        jnp.zeros((model_width, exchanged[0].shape[2]), jnp.float32),
        jnp.zeros((context.shape[2], exchanged[1].shape[2]), jnp.float32),
        jnp.zeros((model_width, exchanged[2].shape[2]), jnp.float32),
        jnp.zeros((activation.shape[2], exchanged[3].shape[2]), jnp.float32),
    )
    pieces = (
        lax.all_gather(normed_one, "ctx", axis=1, tiled=True),
        lax.all_gather(context, "ctx", axis=1, tiled=True),
        lax.all_gather(normed_two, "ctx", axis=1, tiled=True),
        lax.all_gather(activation, "ctx", axis=1, tiled=True),
    )
    updated = []
    for total, piece, right in zip(initial, pieces, exchanged):
        updated.append(jnp.einsum("bsr,bsc->rc", piece, right, preferred_element_type=jnp.float32))
    column_grads = tuple(updated)
    gain_whole = lax.psum((grad_gain_one, grad_gain_two), "ctx")
    final_qkv, final_out, final_gate_up, final_down, final_gain_one, final_gain_two = (
        lax.psum_scatter(
            column_grads[0].astype(jnp.bfloat16), "dp", scatter_dimension=0, tiled=True
        ).astype(jnp.float32),
        lax.psum_scatter(
            column_grads[1].astype(jnp.bfloat16), "dp", scatter_dimension=0, tiled=True
        ).astype(jnp.float32),
        lax.psum_scatter(
            column_grads[2].astype(jnp.bfloat16), "dp", scatter_dimension=0, tiled=True
        ).astype(jnp.float32),
        lax.psum_scatter(
            column_grads[3].astype(jnp.bfloat16), "dp", scatter_dimension=0, tiled=True
        ).astype(jnp.float32),
        lax.psum_scatter(
            gain_whole[0].astype(jnp.bfloat16), "dp", scatter_dimension=0, tiled=True
        ).astype(jnp.float32),
        lax.psum_scatter(
            gain_whole[1].astype(jnp.bfloat16), "dp", scatter_dimension=0, tiled=True
        ).astype(jnp.float32),
    )
    return (
        output,
        grad_tokens,
        final_gain_one,
        final_qkv,
        final_out,
        final_gain_two,
        final_gate_up,
        final_down,
    )


MESH = pl.DeviceIdType.MESH


class Place:
    def __init__(self):
        self.dp = lax.axis_index("dp")
        self.ctx = lax.axis_index("ctx")
        self.z = lax.div(self.dp, 2)
        self.y = lax.rem(self.dp, 2)
        self.x = lax.div(self.ctx, 2)
        self.c = lax.rem(self.ctx, 2)
        self.up = (self.dp + 2, self.ctx)
        self.down = (self.dp - 2, self.ctx)
        self.across = (self.dp + 1 - 2 * self.y, self.ctx)
        self.chip = (self.dp, (1 - self.x) * 2 + self.c)
        self.core = (self.dp, self.x * 2 + 1 - self.c)
        self.has_up = self.z < 3
        self.has_down = self.z > 0


def greet(place):
    barrier = pltpu.get_barrier_semaphore()

    def tell(device):
        pl.semaphore_signal(barrier, inc=1, device_id=device, device_id_type=MESH)

    pl.when(place.has_up)(lambda: tell(place.up))
    pl.when(place.has_down)(lambda: tell(place.down))
    tell(place.across)
    for step in (1, 2, 3):
        tell((place.dp, lax.rem(place.ctx + step, 4)))
    ends = place.has_up.astype(jnp.int32) + place.has_down.astype(jnp.int32)
    pl.semaphore_wait(barrier, 4 + ends)


class Way(enum.IntEnum):
    BELOW = 0
    ABOVE = 1


BELOW, ABOVE = Way.BELOW, Way.ABOVE
RINGS = (12, 16, 28, 24, 16)
SENDS = sum(RINGS)


class Wires:
    def __init__(self, send_sems, recv_sems, names, place):
        self.kinds = ((place.core,), (place.chip,), (place.across,), (place.up, place.down))
        self.counts = [0] * len(RINGS)
        self.send_sems = send_sems
        self.recv_sems = recv_sems
        self.index = names
        self.total = sum(names.values()) if names else 0
        self.base = {}
        self.live = {}

    def slot(self, name, size=1):
        if name not in self.base:
            self.base[name] = self.total
            self.total += size
        return self.base[name]

    def spot(self, name, plane):
        if name[0] in ("down", "down_y"):
            return self.slot(name[:2])
        if name[0] == "ddown":
            return self.slot(name[:3])
        if name[:2] in GROUPED or name[0] in SWAPS:
            return self.slot(name[:2] if name[:2] in GROUPED else name[:1])
        if len(name) > 2 and isinstance(name[-2], Way):
            way, dist = name[-2:]
            source = plane - dist if way == BELOW else plane + dist
            if name[-3] == "z":
                return self.slot(name[:-2], 5) + source + int(way)
            return self.slot(name[:-2], 4) + source
        return self.slot(name)

    def send(self, src, dst, name, device, cond=None, extra=None):
        kind = 4
        for at, devices in enumerate(self.kinds):
            if any(device is known for known in devices):
                kind = at
        number = (kind, self.counts[kind])
        self.counts[kind] += 1
        self.settle((kind, number[1] - RINGS[kind]))
        at = self.spot(name, lax.div(device[0], 2))
        if extra is not None:
            at = at + extra
        copy = pltpu.make_async_remote_copy(
            src_ref=src,
            dst_ref=dst,
            send_sem=self.send_sems.at[sum(RINGS[:kind]) + number[1] % RINGS[kind]],
            recv_sem=self.recv_sems.at[at],
            device_id=device,
            device_id_type=MESH,
        )
        when(cond, copy.start)
        self.live[number] = (copy, cond, name)

    def take(self, dst, name, device, extra=None):
        at = self.spot(name, lax.div(lax.axis_index("dp"), 2))
        if extra is not None:
            at = at + extra
        pltpu.make_async_remote_copy(
            src_ref=dst,
            dst_ref=dst,
            send_sem=self.send_sems.at[0],
            recv_sem=self.recv_sems.at[at],
            device_id=device,
            device_id_type=MESH,
        ).wait_recv()

    def settle(self, number):
        if number in self.live:
            copy, cond, name = self.live.pop(number)
            when(cond, copy.wait_send)

    def drain(self):
        for number in list(self.live):
            self.settle(number)

    def drain_named(self, first):
        for number in list(self.live):
            if self.live[number][2][0] == first:
                self.settle(number)


GROUPED = (("out", "c"), ("out", "d"), ("gain", "y")) + tuple((("gu", n), "y") for n in range(3))
SWAPS = ("pq", "kv", "gb", "gm")


def both(first, second):
    return second if first is None else jnp.logical_and(first, second)


def source_valid(place, way, dist):
    return place.z >= dist if way == BELOW else place.z + dist <= 3


def source_pos(place, way, dist):
    return place.dp - 2 * dist if way == BELOW else place.dp + 2 * dist


def flood_start(wires, place, name, own, block, spread):
    wires.send(own, block(place.dp), (name, BELOW, 1), place.up, place.has_up)
    wires.send(own, block(place.dp), (name, ABOVE, 1), place.down, place.has_down)
    wires.send(own, block(place.dp), (name, "y", 0, 0), place.across)
    spread(own, place.dp, (0, 0, 0), None)


def flood_step(wires, place, name, block, spread, way, dist):
    here = source_valid(place, way, dist)
    pos = source_pos(place, way, dist)
    view = block(pos)
    came_from = place.down if way == BELOW else place.up
    pl.when(here)(lambda: wires.take(view, (name, way, dist), came_from))
    if dist < 3:
        onward = place.up if way == BELOW else place.down
        more = place.has_up if way == BELOW else place.has_down
        wires.send(view, view, (name, way, dist + 1), onward, jnp.logical_and(here, more))
    wires.send(view, view, (name, "y", way, dist), place.across, here)
    spread(view, pos, (0, way, dist), here)


def flood_side(wires, place, name, block, spread, way, dist):
    if dist == 0:
        here, pos = None, place.dp
    else:
        here, pos = source_valid(place, way, dist), source_pos(place, way, dist)
    pos = pos + 1 - 2 * place.y
    view = block(pos)
    if here is None:
        wires.take(view, (name, "y", 0, 0), place.across)
    else:
        pl.when(here)(lambda: wires.take(view, (name, "y", way, dist), place.across))
    spread(view, pos, (1, way, dist), here)


HOPS = [(way, dist) for dist in (1, 2, 3) for way in (BELOW, ABOVE)]


def no_spread(view, pos, key, cond):
    return None


def add_rows(dst, srcs, out=None, cast=None, chunk=48):
    out = dst if out is None else out
    total_rows = dst.shape[0]
    if total_rows % chunk:
        chunk = total_rows

    def body(i, carry):
        at = pl.ds(pl.multiple_of(i * chunk, 16), chunk)
        total = dst[at, :].astype(jnp.float32)
        for src in srcs:
            total = total + src[at, :].astype(jnp.float32)
        out[at, :] = total.astype(out.dtype)
        return carry

    lax.fori_loop(0, total_rows // chunk, body, 0)


def when(cond, action):
    if cond is None:
        action()
    else:
        pl.when(cond)(action)


DRAIN = [(way, dist) for dist in (3, 2, 1, 0) for way in (BELOW, ABOVE)]


def nn(a, b):
    return jnp.dot(a, b, preferred_element_type=jnp.float32)


def nt(a, b):
    return lax.dot_general(a, b, (((1,), (1,)), ((), ())), preferred_element_type=jnp.float32)


def tn(a, b):
    return lax.dot_general(a, b, (((0,), (0,)), ((), ())), preferred_element_type=jnp.float32)


def layer_kernel(
    names,
    tokens, cot, lengths, qkv_in, out_in, gu_in, dt_in, gain_one, gain_two, cos_table, sin_table,
    output, grad_tokens, gain_out, qkv_out, out_out, gu_out, dt_out,
    w_qkv, w_out, w_rest, out_pad, w_ff, d_qkv, d_out, d_ff, gain_all, gain_row, cos, sin,
    tok_all, n1_all, n2_all, g_all, ctx_all, hidden, grad_hidden, proj, q_st, kv_all, p_st, att, go_st,
    wide, gm, pq, pq_in, gb_all, gm_all, act, d_gu, gp, gp_box, op, op_box, dkv, dkv_box,
    qkv_side, out_side, gu_side, down_side, qkv_inbox, out_inbox, gu_inbox, down_inbox,
    up_inbox, up_side, gu_mix, down_mix, gain_box, gain_acc,
    send_sems, recv_sems, local_sems,
):
    f32, low = jnp.float32, jnp.bfloat16
    place = Place()
    wires = Wires(send_sems, recv_sems, names, place)
    dp, ctx, z, y, x, c = place.dp, place.ctx, place.z, place.y, place.x, place.c
    rows = qkv_in.shape[0]
    strip, half = dt_in.shape
    width = tokens.shape[1]
    own_rows = tokens.shape[0]
    slots_here = own_rows // 2
    qkv_cols, out_cols = qkv_in.shape[1], out_in.shape[1]
    qkv_wide, out_wide = w_qkv.shape[1], out_pad.shape[1]
    main = w_out.shape[2]
    packed = w_out.shape[1] // 8
    spare = packed - rows
    rest = out_cols - main
    pieces = -(-rows // spare)
    group = QH // KVH
    slabs = KVH // 2
    q_slabs = QH // 2
    span = 3 * half
    deep = w_ff.shape[0]
    score_scale = 1.0 / math.sqrt(HD)
    TILES = range(2)

    greet(place)

    def block_rows(pos):
        return pl.ds(pl.multiple_of(pos * rows, 16), rows)

    def lead_rows(lead):
        return pl.ds(pl.multiple_of(lead * own_rows, 16), own_rows)

    here_rows = lead_rows(ctx)
    my_rows = block_rows(dp)

    def share(name, ref):
        mine = ref.at[here_rows]
        wires.send(mine, mine, (name, "x"), place.chip)
        wires.send(mine, mine, (name, "c"), place.core)

    def share_on(name, ref):
        far = ref.at[lead_rows(place.chip[1])]
        wires.take(far, (name, "x"), place.chip)
        wires.send(far, far, (name, "d"), place.core)

    def share_end(name, ref):
        for mark, lead in (("c", place.core[1]), ("d", 3 - ctx)):
            wires.take(ref.at[lead_rows(lead)], (name, mark), place.core)

    def swap_start(name, src, dst):
        for step in (1, 2, 3):
            peer = lax.rem(ctx + step, 4)
            wires.send(src(peer), dst(ctx), (name, step), (dp, peer))

    def swap_end(name, three):
        wires.take(three, (name, 1), place.core)

    locals_ = []

    def local(src, dst, cond=None):
        copy = pltpu.make_async_copy(src, dst, local_sems.at[len(locals_)])
        locals_.append((copy, cond))
        when(cond, copy.start)

    SIDES = [(0, 0)] + HOPS
    WAYS = {0: [(0, 0)], 1: HOPS[:2], 2: HOPS[2:4], 3: HOPS[4:]}

    class Flood:
        def __init__(self, name, block, spread=no_spread):
            self.name, self.block, self.spread = name, block, spread

        def start(self):
            flood_start(wires, place, self.name, self.block(dp), self.block, self.spread)

        def hop(self, dist, way):
            way = Way(way)
            flood_step(wires, place, self.name, self.block, self.spread, way, dist)

        def side(self, dist, way):
            way = Way(way) if dist else way
            flood_side(wires, place, self.name, self.block, self.spread, way, dist)

    class PairFlood:
        def __init__(self, name, ref, cols):
            self.name, self.ref, self.cols = name, ref, cols

        def pair(self, plane):
            return self.ref.at[pl.ds(pl.multiple_of(2 * rows * plane, 16), 2 * rows), self.cols]

        def one(self, pos):
            return self.ref.at[block_rows(pos), self.cols]

        def start(self):
            wires.send(self.one(dp), self.one(dp), (self.name, "y"), place.across)

        def side(self):
            wires.take(self.one(place.across[0]), (self.name, "y"), place.across)
            view = self.pair(z)
            wires.send(view, view, (self.name, BELOW, 1), place.up, place.has_up)
            wires.send(view, view, (self.name, ABOVE, 1), place.down, place.has_down)

        def hop(self, dist, way):
            way = Way(way)
            here = source_valid(place, way, dist)
            view = self.pair(z - dist if way == BELOW else z + dist)
            came_from = place.down if way == BELOW else place.up
            pl.when(here)(lambda: wires.take(view, (self.name, way, dist), came_from))
            if dist < 3:
                onward = place.up if way == BELOW else place.down
                more = place.has_up if way == BELOW else place.has_down
                wires.send(view, view, (self.name, way, dist + 1), onward, jnp.logical_and(here, more))

    def packed_rows(pos):
        return pl.ds(pl.multiple_of(pos * packed, 16), packed)

    def pack(values, dest):
        dest[:rows, :] = values[:, :main].astype(low)
        for slab in range(0, main, 128):
            total = jnp.zeros((spare, 128), f32)
            for number in range(slab // rest, min(pieces, (slab + 128) // rest)):
                height = min(spare, rows - number * spare)
                piece = values[number * spare : number * spare + height, main : main + 128]
                if height < spare:
                    piece = jnp.concatenate([piece, jnp.zeros((spare - height, 128), f32)], axis=0)
                shift = number * rest - slab
                total = total + (pltpu.roll(piece, shift, 1) if shift else piece)
            dest[rows:, slab : slab + 128] = total.astype(low)

    def unpack(view, dest):
        keep = lax.broadcasted_iota(jnp.int32, (spare, 128), 1) < rest
        for number in range(pieces):
            slab = number * rest // 128 * 128
            shift = number * rest - slab
            piece = view[rows:, slab : slab + 128].astype(f32)
            piece = pltpu.roll(piece, 128 - shift, 1) if shift else piece
            height = min(spare, rows - number * spare)
            piece = jnp.where(keep, piece, 0.0).astype(low)
            dest[number * spare : number * spare + height, :] = piece[:height]

    def out_weights(j):
        first = jnp.concatenate([w_out[j, pos * packed : pos * packed + rows, :] for pos in range(8)], axis=0)
        return jnp.concatenate([first, w_rest[j]], axis=1)

    def out_block(lead, pos):
        return w_out.at[lead, packed_rows(pos)]

    def out_spread(view, pos, key, cond):
        wires.send(view, out_block(ctx, pos), ("out", "x") + key, place.chip, cond)
        wires.send(view, out_block(ctx, pos), ("out", "c") + key, place.core, cond)

    qkv_flood = Flood("qkv", lambda pos: w_qkv.at[block_rows(pos)])
    gain_flood = Flood("gain", lambda pos: gain_all.at[pos])
    out_flood = Flood("out", functools.partial(out_block, ctx), out_spread)

    PARTS = [(tile, part) for tile in TILES for part in range(2)]

    def part_cols(number):
        tile, part = PARTS[number]
        return pl.ds(tile * span + part * half, half)

    def gu_view(ref, number, pos):
        return ref.at[block_rows(pos), part_cols(number)]

    gu_floods = [Flood(("gu", number), functools.partial(gu_view, w_ff, number)) for number in range(3)]
    up_flood = PairFlood("up", w_ff, part_cols(3))

    def spots(column, dist, way=None):
        for way, dist in WAYS[dist] if way is None else [(way, dist)]:
            if dist == 0:
                here, pos = None, dp
            else:
                here, pos = source_valid(place, way, dist), source_pos(place, way, dist)
            if column == 1:
                pos = pos + 1 - 2 * y
            yield (column, way, dist), here, pos

    def out_chip(column, dist, way):
        way = Way(way) if dist else way
        for key, here, pos in spots(column, dist, way):
            view = out_block(place.chip[1], pos)
            when(here, lambda: wires.take(view, ("out", "x") + key, place.chip))
            wires.send(view, view, ("out", "d") + key, place.core, here)

    def out_core():
        for mark, lead in (("c", place.core[1]), ("d", 3 - ctx)):
            wires.take(w_out.at[lead], ("out", mark), place.core)

    def gu_sides(number):
        wires.take(w_ff.at[pl.ds(0, 4 * rows), part_cols(number)], (("gu", number), "y"), place.across)

    def mix_start(tile):
        for part in range(2):
            target = 2 * c + part
            src = gu_in.at[:, pl.ds((2 * part + tile) * half, half)]
            dst = w_ff.at[my_rows, pl.ds(pl.multiple_of(tile * span + x * half, 128), half)]
            wires.slot(("gu_mix", tile), 2)
            wires.send(src, dst, ("gu_mix", tile), (dp, target), target != ctx, extra=x)
            local(src, dst, target == ctx)

    def mix_end(number):
        tile, part = PARTS[number]
        origin = part * 2 + x
        view = gu_view(w_ff, number, dp)
        pl.when(origin != ctx)(lambda: wires.take(view, ("gu_mix", tile), (dp, origin), extra=part))

    lanes = pl.ds(pl.multiple_of(y * span + 2 * half, 128), half)
    other_lanes = pl.ds(pl.multiple_of((1 - y) * span + 2 * half, 128), half)
    at_home = ctx == z

    def strips_of(ref, at):
        return [ref.at[pl.ds(j * strip, strip), at] for j in range(4)]

    strips, other_strips = strips_of(w_ff, lanes), strips_of(w_ff, other_lanes)

    def down_mix_start():
        dst = w_ff.at[pl.ds(pl.multiple_of(ctx * strip, 16), strip), lanes]
        wires.slot(("down_mix",), 4)
        wires.send(dt_in, dst, ("down_mix",), (dp, z), ctx != z, extra=ctx)
        local(dt_in, dst, ctx == z)

    def tables():
        for table, ref in ((cos_table, cos), (sin_table, sin)):
            mine = table[pl.ds(pl.multiple_of(ctx * slots_here, 16), slots_here), :]
            ref[:slots_here, :] = mine
            ref[slots_here:, :] = mine

    def down_start(j):
        pl.when(jnp.logical_and(at_home, ctx != j))(lambda: wires.take(strips[j], ("down_mix",), (dp, j), extra=j))
        wires.send(strips[j], strips[j], ("down", j, BELOW, 1), place.up, jnp.logical_and(at_home, place.has_up))
        wires.send(strips[j], strips[j], ("down", j, ABOVE, 1), place.down, jnp.logical_and(at_home, place.has_down))
        wires.send(strips[j], strips[j], ("down_y", j, 0, 0), place.across, at_home)

    def down_hop(dist, j):
        for way in (BELOW, ABOVE):
            here = (z - ctx if way == BELOW else ctx - z) == dist
            came_from = place.down if way == BELOW else place.up
            onward = place.up if way == BELOW else place.down
            more = place.has_up if way == BELOW else place.has_down
            pl.when(here)(lambda: wires.take(strips[j], ("down", j, way, dist), came_from))
            if dist < 3:
                wires.send(strips[j], strips[j], ("down", j, way, dist + 1), onward, jnp.logical_and(here, more))
            wires.send(strips[j], strips[j], ("down_y", j, way, dist), place.across, here)

    def down_side_end():
        for way, dist in SIDES:
            here = at_home if dist == 0 else (z - ctx if way == BELOW else ctx - z) == dist

            def take():
                for j in range(4):
                    wires.take(other_strips[j], ("down_y", j, way, dist), place.across)

            pl.when(here)(take)

    row_at = lax.broadcasted_iota(jnp.int32, (own_rows, 1), 0)
    first_seq = row_at < slots_here
    position = ctx * slots_here + jnp.where(first_seq, row_at, row_at - slots_here)
    valid = position < jnp.where(first_seq, lengths[0], lengths[1])
    def tokens_start():
        tok_all[here_rows, :] = tokens[...]
        share("tok", tok_all)

    def qkv_start():
        w_qkv[my_rows, :] = jnp.zeros((rows, qkv_wide), low)
        w_qkv[my_rows, :qkv_cols] = qkv_in[...]
        qkv_flood.start()

    def gain_start():
        gain_all[dp] = jnp.zeros(gain_all.shape[1:], f32)
        gain_all[dp, 0:1, :rows] = gain_one[...].reshape(1, rows).astype(f32)
        gain_all[dp, 1:2, :rows] = gain_two[...].reshape(1, rows).astype(f32)
        gain_flood.start()

    def out_start():
        out_pad[...] = jnp.zeros(out_pad.shape, low)
        out_pad[:, :out_cols] = out_in[...]
        pack(out_pad[...].astype(f32), out_block(ctx, dp))
        out_flood.start()

    def cot_start():
        g_all[here_rows, :] = jnp.where(valid, cot[...].astype(f32), 0.0).astype(low)
        share("cot", g_all)

    def gain_sides():
        wires.take(gain_all.at[pl.ds(0, 4)], ("gain", "y"), place.across)

    gain_a = lambda: gain_row[0:1, :width]
    gain_b = lambda: gain_row[1:2, :width]

    def norm(values):
        return lax.rsqrt(jnp.mean(values * values, axis=-1, keepdims=True) + EPS)

    lane = lax.broadcasted_iota(jnp.int32, (own_rows, 128), 1)
    low_half = lax.rem(lane, HD) < HD // 2
    side_of = lax.div(lane, HD)

    def turn(values, sign):
        swapped = jnp.where(low_half, pltpu.roll(values, 128 - HD // 2, 1), pltpu.roll(values, HD // 2, 1))
        return values * cos[...] + swapped * (sin[...] * sign)

    def head_spots():
        for head in range(QH):
            kv = head // group
            yield head // 2, head % 2, kv // 2, kv % 2, (kv % 2 * group + head % group) * slots_here

    def stack_heads(slab_of, dest, scale):
        for slab, side, key_slab, key_side, at in head_spots():
            values = slab_of(slab)
            if side != key_side:
                values = pltpu.roll(values, HD, 1)
            values = (jnp.where(side_of == key_side, values, 0.0) * scale).astype(low)
            for seq in range(2):
                dest[seq * slabs + key_slab, at : at + slots_here, :] = values[
                    seq * slots_here : (seq + 1) * slots_here
                ]

    def unstack_heads(src, slab):
        total = jnp.zeros((own_rows, 128), f32)
        for at_slab, side, key_slab, key_side, at in head_spots():
            if at_slab != slab:
                continue
            values = jnp.concatenate(
                [src[seq * slabs + key_slab, at : at + slots_here, :] for seq in range(2)], axis=0
            )
            values = jnp.where(side_of == key_side, values, 0.0)
            if side != key_side:
                values = pltpu.roll(values, HD, 1)
            total = total + values
        return total

    def project():
        gain_row[...] = jnp.zeros(gain_row.shape, f32)
        for pos in range(8):
            piece = gain_all[pos]
            shift = (pos * rows) % 128
            if shift:
                piece = pltpu.roll(piece, shift, 1)
            at = (pos * rows) // 128 * 128
            gain_row[:, at : at + 256] += piece

        def body(i, carry):
            at = lead_rows(i)
            source = tok_all[at, :].astype(f32)
            n1_all[at, :] = (source * norm(source) * gain_a()).astype(low)
            return carry

        lax.fori_loop(0, 4, body, 0)
        pq[...] = nn(n1_all[...], w_qkv[...]).reshape(pq.shape)
        pq_in[ctx] = pq[ctx]
        swap_start("pq", lambda peer: pq.at[peer], lambda sender: pq_in.at[sender])

    def pq_end():
        swap_end("pq", pq_in.at[pl.ds(0, 3)])
        proj[...] = jnp.zeros(proj.shape, f32)
        for j in range(4):
            part = jnp.concatenate([pq_in[j], jnp.zeros((own_rows, 128), f32)], axis=1)
            at = qkv_cols * j
            if at % 128:
                part = pltpu.roll(part, at % 128, 1)
            proj[:, at // 128 * 128 : at // 128 * 128 + qkv_wide + 128] += part

    turned = {}

    def query_slab(slab):
        if slab not in turned:
            turned[slab] = turn(proj[:, slab * 128 : slab * 128 + 128], 1.0)
        return turned[slab]

    def slot_view(lead):
        return kv_all.at[:, :, pl.ds(pl.multiple_of(lead * slots_here, 16), slots_here)]

    def kv_start():
        my_slots = pl.ds(pl.multiple_of(ctx * slots_here, 16), slots_here)
        for slab in range(2 * slabs):
            at = (q_slabs + slab) * 128
            values = proj[:, at : at + 128]
            if slab < slabs:
                values = turn(values, 1.0)
            values = values.astype(low)
            for seq in range(2):
                kv_all[seq, slab, my_slots, :] = values[seq * slots_here : (seq + 1) * slots_here]

        swap_start("kv", lambda peer: slot_view(ctx), slot_view)

    def queries():
        stack_heads(query_slab, q_st, score_scale)

    def kv_end():
        swap_end("kv", kv_all.at[:, :, pl.ds(0, 3 * slots_here)])

    stack = q_st.shape[1]
    slots = kv_all.shape[2]

    def attend(i, carry):
        seq, slab = lax.div(i, slabs), lax.rem(i, slabs)
        scores = nt(q_st[i], kv_all[seq, slab])
        at = ctx * slots_here + lax.rem(lax.broadcasted_iota(jnp.int32, (stack, slots), 0), slots_here)
        key_at = lax.broadcasted_iota(jnp.int32, (stack, slots), 1)
        length = jnp.where(seq == 0, lengths[0], lengths[1])
        allowed = jnp.logical_and(key_at <= at, key_at < length)
        scores = jnp.where(allowed, scores, NEGATIVE)
        terms = jnp.exp(scores - jnp.max(scores, axis=-1, keepdims=True))
        probs = (terms / jnp.sum(terms, axis=-1, keepdims=True)).astype(low)
        p_st[i] = probs
        att[i] = nn(probs, kv_all[seq, slabs + slab])
        return carry

    def attention():
        lax.fori_loop(0, 2 * slabs, attend, 0)
        for slab in range(q_slabs):
            ctx_all[here_rows, slab * 128 : slab * 128 + 128] = unstack_heads(att, slab).astype(low)
        share("ctx", ctx_all)

    def out_project():
        for j in range(4):
            for pos in range(8):
                unpack(w_out.at[j, packed_rows(pos)], w_rest.at[j, block_rows(pos)])
        hidden[...] = tokens[...].astype(f32)
        for j in range(4):
            part = nn(ctx_all[here_rows, :], out_weights(j))
            at = out_cols * j
            if at % 128:
                part = pltpu.roll(part, at % 128, 1)
            hidden[:, at // 128 * 128 : at // 128 * 128 + out_wide] += part
        n2_all[here_rows, :] = (hidden[...] * norm(hidden[...]) * gain_b()).astype(low)
        share("n2", n2_all)

    tall = 2 * own_rows

    def feed(tile):
        def body(i, carry):
            at = pl.ds(0, 4 * own_rows)
            gate = nn(n2_all[at, :], w_ff[:, tile * span : tile * span + half])
            up = nn(n2_all[at, :], w_ff[:, tile * span + half : tile * span + 2 * half])
            back = nn(g_all[at, :], w_ff[:, tile * span + 2 * half : (tile + 1) * span])
            sig = jax.nn.sigmoid(gate)
            swish = gate * sig
            act[tile, at, :] = (swish * up).astype(low)
            d_gu[tile, at, :half] = (back * up * sig * (1.0 + gate * (1.0 - sig))).astype(low)
            d_gu[tile, at, half:] = (back * swish).astype(low)
            return carry

        body(0, 0)

    def grad_ff(tile):
        def body(m, carry):
            at = pl.ds(pl.multiple_of(m * width, 128), width)
            d_ff[at, tile * span : tile * span + 2 * half] = tn(n2_all[:, at], d_gu[tile]).astype(low)
            d_ff[at, tile * span + 2 * half : (tile + 1) * span] = tn(g_all[:, at], act[tile]).astype(low)
            return carry

        lax.fori_loop(0, 1, body, 0)

    across_core = (1 - x) * 2 + 1 - c
    across_own = (1 - x) * 2 + c
    beside = x * 2 + 1 - c
    wide_tile = width

    def group_send(name, ref, box, which):
        lead, mark = ((across_core, "cx"), (beside, "cc"))[which]
        wires.send(ref.at[lead], box.at[which], (name, mark), place.core)

    def group_on(name, ref, box):
        wires.take(box.at[0], (name, "cx"), place.core)
        mine = ref.at[across_own]
        mine[...] = (mine[...].astype(f32) + box[0].astype(f32)).astype(low)
        wires.send(mine, box.at[2], (name, "x"), place.chip)

    def group_end(name, ref, box):
        wires.take(box.at[1], (name, "cc"), place.core)
        wires.take(box.at[2], (name, "x"), place.chip)
        return ref[ctx].astype(f32) + box[1].astype(f32) + box[2].astype(f32)

    def pair_rows(half_x):
        return pl.ds(pl.multiple_of(half_x * tall, 16), tall)

    def group_product(ref, terms):
        def compute(half_x):
            def body(n, carry):
                at = pl.ds(pl.multiple_of(n * wide_tile, 128), wide_tile)
                total = None
                for left, right in terms:
                    term = nt(left(pair_rows(half_x)), right(at))
                    total = term if total is None else total + term
                ref[2 * half_x, :, at] = total[:own_rows].astype(low)
                ref[2 * half_x + 1, :, at] = total[own_rows:].astype(low)
                return carry

            lax.fori_loop(0, width // wide_tile, body, 0)

        return compute

    back_terms = [
        (lambda at, tile=tile: d_gu[tile, at, :], lambda at, tile=tile: w_ff[at, tile * span : tile * span + 2 * half])
        for tile in TILES
    ]
    forward_terms = [
        (lambda at, tile=tile: act[tile, at, :], lambda at, tile=tile: w_ff[at, tile * span + 2 * half : (tile + 1) * span])
        for tile in TILES
    ]

    def key_pos(way, dist):
        if dist == 0:
            return None, dp
        return source_valid(place, way, dist), source_pos(place, way, dist)

    KEYS = {3: DRAIN[:2], 2: DRAIN[2:4], 1: DRAIN[4:6], 0: [(BELOW, 0)]}
    flip = 1 - 2 * y

    def z_add(name, view, boxes, inbox, way, dist):
        here, pos = key_pos(way, dist)
        mine = view(pos)
        if dist == 0:
            wires.take(boxes.at[way, dist], (name, "y", way, dist), place.across)
            add_rows(mine, [boxes.at[way, dist]])
            for end, fed, feeder in ((BELOW, place.has_up, place.up), (ABOVE, place.has_down, place.down)):

                def own():
                    wires.take(inbox.at[end, 0], (name, "z", end, 0), feeder)
                    add_rows(mine, [inbox.at[end, 0]])

                pl.when(fed)(own)
            return
        fed = place.has_up if way == BELOW else place.has_down
        feeder = place.up if way == BELOW else place.down
        onward = place.down if way == BELOW else place.up
        side = boxes.at[way, dist]

        def first():
            wires.take(side, (name, "y", way, dist), place.across)
            add_rows(mine, [side])

        if dist == 3:
            pl.when(here)(first)
        else:

            def more():
                wires.take(side, (name, "y", way, dist), place.across)
                wires.take(inbox.at[way, dist], (name, "z", way, dist), feeder)
                add_rows(mine, [side, inbox.at[way, dist]])

            pl.when(jnp.logical_and(here, jnp.logical_not(fed)))(first)
            pl.when(jnp.logical_and(here, fed))(more)
        wires.send(mine, inbox.at[way, dist - 1], (name, "z", way, dist - 1), onward, here)

    class Sink:
        def __init__(self, name, view, side, inbox):
            self.name, self.view, self.side, self.inbox = name, view, side, inbox

        def send(self, dist, way):
            way = Way(way) if dist else way
            here, pos = key_pos(way, dist)
            wires.send(
                self.view(pos + flip), self.side.at[way, dist],
                (self.name, "y", way, dist), place.across, here,
            )

        def add(self, dist, way):
            way = Way(way) if dist else way
            z_add(self.name, self.view, self.side, self.inbox, way, dist)

    gu_sinks = [
        Sink(("dgu", number), functools.partial(gu_view, d_ff, number), gu_side.at[number], gu_inbox.at[number])
        for number in range(3)
    ]
    out_sink = Sink("dout", lambda pos: d_out.at[packed_rows(pos)], out_side, out_inbox)
    qkv_sink = Sink("dqkv", lambda pos: d_qkv.at[block_rows(pos)], qkv_side, qkv_inbox)
    d_strips, d_other_strips = strips_of(d_ff, lanes), strips_of(d_ff, other_lanes)

    def down_send(tile, j):
        wires.send(d_other_strips[j], down_side.at[j], ("ddown_y", j), place.across, (1 - y) == tile)

    def down_add(dist, j):
        if dist == 0:

            def finish():
                wires.take(down_side.at[j], ("ddown_y", j), place.across)
                add_rows(d_strips[j], [down_side.at[j]])
                for end, fed, feeder in ((BELOW, place.has_up, place.up), (ABOVE, place.has_down, place.down)):

                    def more():
                        wires.take(down_inbox.at[end, j], ("ddown", j, end, 0), feeder)
                        add_rows(d_strips[j], [down_inbox.at[end, j]])

                    pl.when(fed)(more)

            pl.when(at_home)(finish)
            return
        for way in (BELOW, ABOVE):
            here = (z - ctx if way == BELOW else ctx - z) == dist
            fed = place.has_up if way == BELOW else place.has_down
            feeder = place.up if way == BELOW else place.down
            onward = place.down if way == BELOW else place.up

            def first():
                wires.take(down_side.at[j], ("ddown_y", j), place.across)
                add_rows(d_strips[j], [down_side.at[j]])

            def more():
                wires.take(down_side.at[j], ("ddown_y", j), place.across)
                wires.take(down_inbox.at[way, j], ("ddown", j, way, dist), feeder)
                add_rows(d_strips[j], [down_side.at[j], down_inbox.at[way, j]])

            pl.when(jnp.logical_and(here, jnp.logical_not(fed)))(first)
            pl.when(jnp.logical_and(here, fed))(more)
            wires.send(d_strips[j], down_inbox.at[way, j], ("ddown", j, way, dist - 1), onward, here)

    class PairSink:
        def __init__(self, name, ref, cols, inbox, side):
            self.name, self.ref, self.cols, self.inbox, self.side = name, ref, cols, inbox, side

        def pair(self, plane):
            return self.ref.at[pl.ds(pl.multiple_of(2 * rows * plane, 16), 2 * rows), self.cols]

        def one(self, pos):
            return self.ref.at[block_rows(pos), self.cols]

        def add(self, dist, way):
            if dist == 0:
                mine = self.pair(z)
                for end, fed, feeder in ((BELOW, place.has_up, place.up), (ABOVE, place.has_down, place.down)):

                    def more():
                        wires.take(self.inbox.at[end, 0], (self.name, "z", end, 0), feeder)
                        add_rows(mine, [self.inbox.at[end, 0]])

                    pl.when(fed)(more)
                wires.send(self.one(place.across[0]), self.side, (self.name, "y"), place.across)
                return
            way = Way(way)
            here = source_valid(place, way, dist)
            mine = self.pair(z - dist if way == BELOW else z + dist)
            fed = place.has_up if way == BELOW else place.has_down
            feeder = place.up if way == BELOW else place.down
            onward = place.down if way == BELOW else place.up
            if dist < 3:

                def more():
                    wires.take(self.inbox.at[way, dist], (self.name, "z", way, dist), feeder)
                    add_rows(mine, [self.inbox.at[way, dist]])

                pl.when(jnp.logical_and(here, fed))(more)
            wires.send(mine, self.inbox.at[way, dist - 1], (self.name, "z", way, dist - 1), onward, here)

        def end(self):
            wires.take(self.side, (self.name, "y"), place.across)
            add_rows(self.one(dp), [self.side])

    up_sink = PairSink("dup", d_ff, part_cols(3), up_inbox, up_side)

    def gu_finish(number):
        tile, part = PARTS[number]
        target = part * 2 + x
        block = gu_view(d_ff, number, dp)
        wires.slot(("dgu_mix", tile), 2)
        wires.send(block, gu_mix.at[c, tile], ("dgu_mix", tile), (dp, target), target != ctx, extra=c)
        pl.when(target == ctx)(lambda: add_rows(block, [], out=gu_mix.at[c, tile]))

    def gu_end(number):
        tile, part = PARTS[number]
        origin = 2 * c + part
        box = gu_mix.at[part, tile]
        pl.when(origin != ctx)(lambda: wires.take(box, ("dgu_mix", tile), (dp, origin), extra=part))
        add_rows(box, [], out=gu_out.at[:, pl.ds((2 * part + tile) * half, half)])

    def down_finish():
        for j in range(4):
            wires.send(d_strips[j], down_mix, ("ddown_mix",), (dp, j), jnp.logical_and(at_home, ctx != j))
            pl.when(jnp.logical_and(at_home, ctx == j))(functools.partial(add_rows, d_strips[j], [], down_mix))

    def down_end():
        pl.when(ctx != z)(lambda: wires.take(down_mix, ("ddown_mix",), (dp, z)))
        add_rows(down_mix, [], out=dt_out)

    def norm_back(values, inverse, gain, grad_in):
        scaled = grad_in * gain
        mean_term = jnp.mean(scaled * values, axis=-1, keepdims=True)
        back = inverse * scaled - values * (inverse * inverse * inverse) * mean_term
        return back, jnp.sum(grad_in * values * inverse, axis=0, keepdims=True)

    def gp_block(which):
        half_x = 1 - x if which == 0 else x
        group_product(gp, back_terms)(half_x)
        group_send("gp", gp, gp_box, which)

    def op_block(which):
        half_x = 1 - x if which == 0 else x
        group_product(op, forward_terms)(half_x)
        group_send("op", op, op_box, which)

    def hidden_back():
        gain_acc[0] = jnp.zeros(gain_out.shape, f32)
        back_two, gain_two_grad = norm_back(hidden[...], norm(hidden[...]), gain_b(), group_end("gp", gp, gp_box))
        gain_acc[0, 1:2, :] = gain_two_grad
        grad_hidden[...] = g_all[here_rows, :].astype(f32) + back_two
        out_lane = lax.broadcasted_iota(jnp.int32, (own_rows, out_wide), 1)
        for j in range(4):
            at = out_cols * j
            part = grad_hidden[:, at // 128 * 128 : at // 128 * 128 + out_wide]
            if at % 128:
                part = pltpu.roll(part, out_wide - at % 128, 1)
            wide[j] = jnp.where(out_lane < out_cols, part, 0.0).astype(low)
        gb_all[here_rows, :] = wide[ctx]
        swap_start("gb", lambda peer: wide.at[peer], lambda sender: gb_all.at[lead_rows(sender)])

    def context_back(n, carry):
        at = pl.ds(0, width)
        total = nt(wide[0], out_weights(0))
        for j in range(1, 4):
            total = total + nt(wide[j], out_weights(j))
        proj[:, at] = total
        return carry

    def grad_context():
        lax.fori_loop(0, width // wide_tile, context_back, 0)
        stack_heads(lambda slab: proj[:, slab * 128 : slab * 128 + 128], go_st, 1.0)

    def attend_back(i, carry):
        seq, slab = lax.div(i, slabs), lax.rem(i, slabs)
        grad_probs = nt(go_st[i], kv_all[seq, slabs + slab])
        probs = p_st[i].astype(f32)
        delta = jnp.sum(probs * grad_probs, axis=-1, keepdims=True)
        grad_scores = (probs * (grad_probs - delta)).astype(low)
        att[i] = nn(grad_scores, kv_all[seq, slab]) * score_scale
        grad_key = tn(grad_scores, q_st[i])
        grad_value = tn(p_st[i], go_st[i])
        for j in range(4):
            part = slice(j * slots_here, (j + 1) * slots_here)
            dkv[j, seq, slab] = grad_key[part].astype(low)
            dkv[j, seq, slabs + slab] = grad_value[part].astype(low)
        return carry

    def attention_back():
        lax.fori_loop(0, 2 * slabs, attend_back, 0)
        group_send("dkv", dkv, dkv_box, 0)
        group_send("dkv", dkv, dkv_box, 1)

    def gb_end():
        swap_end("gb", gb_all.at[pl.ds(0, 3 * own_rows)])

    def grad_out_all():
        result = tn(ctx_all[...], gb_all[...])
        for pos in range(8):
            pack(result[pos * rows : (pos + 1) * rows], d_out.at[packed_rows(pos)])

    def grad_mixed():
        sums = group_end("dkv", dkv, dkv_box)
        proj[...] = jnp.zeros(proj.shape, f32)
        for slab in range(q_slabs):
            proj[:, slab * 128 : slab * 128 + 128] = turn(unstack_heads(att, slab), -1.0)
        for slab in range(2 * slabs):
            values = jnp.concatenate([sums[0, slab], sums[1, slab]], axis=0)
            if slab < slabs:
                values = turn(values, -1.0)
            at = (q_slabs + slab) * 128
            proj[:, at : at + 128] = values
        qkv_lane = lax.broadcasted_iota(jnp.int32, (own_rows, qkv_wide), 1)
        for j in range(4):
            at = qkv_cols * j
            part = proj[:, at // 128 * 128 : at // 128 * 128 + qkv_wide + 128]
            if at % 128:
                part = pltpu.roll(part, qkv_wide + 128 - at % 128, 1)
            gm[j] = jnp.where(qkv_lane < qkv_cols, part[:, :qkv_wide], 0.0).astype(low)
        gm_all[here_rows, :] = gm[ctx]
        swap_start("gm", lambda peer: gm.at[peer], lambda sender: gm_all.at[lead_rows(sender)])

    def gm_end():
        swap_end("gm", gm_all.at[pl.ds(0, 3 * own_rows)])

    def grad_qkv(m, carry):
        at = pl.ds(pl.multiple_of(m * width, 128), width)
        d_qkv[at, :] = tn(n1_all[:, at], gm_all[...]).astype(low)
        return carry

    def grad_qkv_all():
        lax.fori_loop(0, 1, grad_qkv, 0)

    tokens_terms = [(lambda at: gm_all[at, :], lambda at: w_qkv[at, :])]

    def gt_block(which):
        if which == 0:
            wires.drain_named("gp")
        half_x = 1 - x if which == 0 else x
        group_product(gp, tokens_terms)(half_x)
        group_send("gt", gp, gp_box, which)

    def output_end():
        result = hidden[...] + group_end("op", op, op_box)
        output[...] = jnp.where(valid, result, 0.0).astype(low)

    def tokens_end():
        source = tokens[...].astype(f32)
        back_one, gain_one_grad = norm_back(source, norm(source), gain_a(), group_end("gt", gp, gp_box))
        gain_acc[0, 0:1, :] = gain_one_grad
        grad_tokens[...] = (grad_hidden[...] + back_one).astype(low)

    low_end, high_end = z == 0, z == 3
    mid_low, mid_high = z == 1, z == 2

    def gain_send(hop):
        def go(device, cond=None):
            wires.send(gain_acc.at[hop], gain_box.at[hop], ("gain_sum", hop), device, cond)

        if hop < 3:
            go((place.core, place.chip, place.across)[hop])
        elif hop == 3:
            go(place.up, low_end)
            go(place.down, high_end)
        elif hop == 4:
            go(place.up, mid_low)
            go(place.down, mid_high)
        else:
            go(place.down, mid_low)
            go(place.up, mid_high)

    def gain_take(hop):
        def add(device):
            wires.take(gain_box.at[hop], ("gain_sum", hop), device)
            gain_acc[hop + 1] = gain_acc[hop] + gain_box[hop]

        def last(device):
            wires.take(gain_box.at[hop], ("gain_sum", hop), device)
            gain_out[...] = gain_box[hop]

        def done():
            gain_out[...] = gain_acc[hop]

        if hop < 3:
            add((place.core, place.chip, place.across)[hop])
        elif hop == 3:
            pl.when(mid_low)(lambda: add(place.down))
            pl.when(mid_high)(lambda: add(place.up))
        elif hop == 4:
            pl.when(mid_low)(lambda: add(place.up))
            pl.when(mid_high)(lambda: add(place.down))
        else:
            pl.when(low_end)(lambda: last(place.up))
            pl.when(high_end)(lambda: last(place.down))
            pl.when(mid_low)(done)
            pl.when(mid_high)(done)

    def out_end():
        mine = d_out.at[packed_rows(dp)]
        out_out[:, :main] = mine[:rows, :]
        unpack(mine, out_out.at[:, pl.ds(main, 128)])

    def qkv_end():
        qkv_out[...] = d_qkv[my_rows, :]

    def locals_end():
        for copy, cond in locals_:
            when(cond, copy.wait)

    mix_start(0)
    tables()
    qkv_start()
    out_start()
    mix_start(1)
    tokens_start()
    out_chip(0, 0, 0)
    down_mix_start()
    locals_end()
    mix_end(0)
    gu_floods[0].start()
    mix_end(1)
    gu_floods[1].start()
    qkv_flood.hop(1, 0)
    qkv_flood.hop(1, 1)
    gain_start()
    gain_flood.hop(1, 0)
    qkv_flood.hop(2, 0)
    out_flood.hop(1, 1)
    out_flood.hop(1, 0)
    gain_flood.hop(2, 0)
    gain_flood.hop(1, 1)
    gain_flood.hop(2, 1)
    qkv_flood.hop(2, 1)
    gu_floods[0].hop(1, 0)
    out_flood.side(0, 0)
    gain_flood.hop(3, 0)
    gain_flood.hop(3, 1)
    qkv_flood.hop(3, 0)
    qkv_flood.side(1, 0)
    mix_end(3)
    out_flood.hop(2, 1)
    qkv_flood.hop(3, 1)
    down_start(1)
    out_flood.hop(2, 0)
    cot_start()
    share_on("tok", tok_all)
    mix_end(2)
    gu_floods[2].start()
    qkv_flood.side(2, 0)
    out_flood.hop(3, 1)
    down_start(0)
    out_chip(0, 1, 0)
    qkv_flood.side(0, 0)
    qkv_flood.side(3, 1)
    qkv_flood.side(3, 0)
    qkv_flood.side(2, 1)
    down_start(3)
    qkv_flood.side(1, 1)
    share_end("tok", tok_all)
    gain_sides()
    project()
    out_flood.hop(3, 0)
    down_hop(1, 1)
    down_hop(2, 1)
    down_hop(1, 0)
    down_hop(2, 0)
    out_flood.side(1, 0)
    up_flood.start()
    down_hop(1, 3)
    down_start(2)
    down_hop(1, 2)
    gu_floods[2].hop(1, 0)
    gu_floods[0].hop(1, 1)
    pq_end()
    kv_start()
    out_chip(0, 3, 1)
    out_chip(0, 2, 1)
    gu_floods[0].hop(2, 0)
    gu_floods[0].hop(2, 1)
    out_chip(1, 0, 0)
    gu_floods[2].hop(1, 1)
    down_hop(3, 1)
    gu_floods[1].hop(1, 1)
    down_hop(2, 3)
    share_on("cot", g_all)
    out_chip(0, 3, 0)
    out_flood.side(3, 0)
    gu_floods[1].hop(1, 0)
    out_flood.side(3, 1)
    out_chip(1, 1, 0)
    queries()
    out_flood.side(2, 0)
    out_flood.side(1, 1)
    down_hop(2, 2)
    out_chip(0, 2, 0)
    up_flood.side()
    down_hop(3, 0)
    out_flood.side(2, 1)
    gu_floods[0].hop(3, 0)
    kv_end()
    attention()
    down_hop(3, 3)
    down_hop(3, 2)
    out_chip(1, 3, 0)
    out_chip(1, 1, 1)
    gu_floods[0].hop(3, 1)
    out_chip(1, 2, 0)
    gu_floods[1].hop(2, 0)
    up_flood.hop(1, 0)
    out_chip(1, 2, 1)
    out_chip(1, 3, 1)
    gu_floods[1].hop(2, 1)
    out_chip(0, 1, 1)
    share_end("cot", g_all)
    out_core()
    out_project()
    gu_floods[1].hop(3, 1)
    up_flood.hop(1, 1)
    gu_floods[1].hop(3, 0)
    gu_floods[2].hop(2, 1)
    gu_floods[2].hop(2, 0)
    gu_floods[2].hop(3, 0)
    gu_floods[2].hop(3, 1)
    up_flood.hop(2, 0)
    up_flood.hop(2, 1)
    share_on("n2", n2_all)
    share_end("n2", n2_all)
    gu_sides(0)
    gu_sides(1)
    down_side_end()
    feed(0)
    grad_ff(0)
    gu_sinks[0].send(3, 1)
    gu_sinks[1].send(2, 1)
    gu_sinks[0].send(3, 0)
    gu_sinks[1].send(3, 0)
    gu_sinks[1].send(2, 0)
    down_send(0, 0)
    up_flood.hop(3, 1)
    up_flood.hop(3, 0)
    gu_sides(2)
    feed(1)
    grad_ff(1)
    up_sink.add(3, 1)
    down_send(1, 0)
    up_sink.add(3, 0)
    gu_sinks[0].send(2, 0)
    gu_sinks[1].send(3, 1)
    gp_block(0)
    op_block(0)
    group_on("gp", gp, gp_box)
    gp_block(1)
    gu_sinks[0].send(2, 1)
    down_send(1, 1)
    down_send(0, 1)
    up_sink.add(2, 1)
    gu_sinks[2].send(2, 1)
    gu_sinks[0].add(3, 0)
    gu_sinks[1].add(3, 0)
    gu_sinks[1].add(2, 0)
    up_sink.add(2, 0)
    gu_sinks[2].send(3, 1)
    group_on("op", op, op_box)
    gu_sinks[2].send(3, 0)
    gu_sinks[1].send(1, 0)
    gu_sinks[0].add(2, 0)
    down_send(0, 3)
    down_send(1, 3)
    down_add(3, 0)
    gu_sinks[2].send(2, 0)
    gu_sinks[0].send(1, 1)
    up_sink.add(1, 1)
    hidden_back()
    down_send(0, 2)
    gu_sinks[0].add(3, 1)
    share_on("ctx", ctx_all)
    grad_context()
    attention_back()
    down_add(3, 1)
    down_send(1, 2)
    gu_sinks[1].add(3, 1)
    group_on("dkv", dkv, dkv_box)
    gu_sinks[0].add(2, 1)
    share_end("ctx", ctx_all)
    gb_end()
    grad_out_all()
    down_add(3, 3)
    gu_sinks[2].send(1, 1)
    out_sink.send(3, 0)
    gu_sinks[1].send(1, 1)
    gu_sinks[1].add(1, 0)
    gu_sinks[1].add(2, 1)
    down_add(2, 1)
    grad_mixed()
    gu_sinks[2].add(3, 1)
    gu_sinks[2].send(0, 0)
    gu_sinks[2].add(3, 0)
    gu_sinks[2].send(1, 0)
    down_add(2, 3)
    down_add(1, 1)
    up_sink.add(1, 0)
    gu_sinks[0].add(1, 1)
    out_sink.send(3, 1)
    out_sink.send(1, 1)
    gu_sinks[0].send(1, 0)
    gm_end()
    down_add(2, 0)
    gu_sinks[0].send(0, 0)
    gt_block(0)
    group_on("gt", gp, gp_box)
    grad_qkv_all()
    qkv_sink.send(2, 1)
    qkv_sink.send(3, 0)
    down_add(3, 2)
    qkv_sink.send(3, 1)
    gu_sinks[2].add(2, 0)
    gu_sinks[2].add(2, 1)
    down_add(1, 3)
    gu_sinks[1].send(0, 0)
    gt_block(1)
    gu_sinks[1].add(1, 1)
    down_add(2, 2)
    down_add(1, 0)
    qkv_sink.send(2, 0)
    gu_sinks[0].add(1, 0)
    out_sink.send(1, 0)
    gu_sinks[2].add(1, 1)
    up_sink.add(0, 0)
    out_sink.add(3, 1)
    out_sink.send(2, 1)
    gu_sinks[2].add(1, 0)
    tokens_end()
    out_sink.send(2, 0)
    gain_send(0)
    gain_take(0)
    gain_send(1)
    gain_take(1)
    gain_send(2)
    out_sink.add(3, 0)
    op_block(1)
    down_add(1, 2)
    qkv_sink.add(3, 1)
    gu_sinks[0].add(0, 0)
    gu_finish(0)
    qkv_sink.add(3, 0)
    qkv_sink.send(1, 1)
    out_sink.add(2, 0)
    out_sink.add(2, 1)
    gu_sinks[1].add(0, 0)
    down_add(0, 1)
    gu_sinks[2].add(0, 0)
    gu_finish(1)
    up_sink.end()
    qkv_sink.send(1, 0)
    gain_take(2)
    gain_send(3)
    qkv_sink.add(2, 1)
    qkv_sink.add(2, 0)
    down_add(0, 0)
    down_add(0, 2)
    down_add(0, 3)
    down_finish()
    out_sink.add(1, 0)
    gu_finish(3)
    out_sink.add(1, 1)
    gu_finish(2)
    output_end()
    gain_take(3)
    gu_end(0)
    gu_end(1)
    gain_send(4)
    qkv_sink.send(0, 0)
    qkv_sink.add(1, 1)
    qkv_sink.add(1, 0)
    out_sink.send(0, 0)
    gain_take(4)
    gain_send(5)
    gu_end(3)
    out_sink.add(0, 0)
    out_end()
    qkv_sink.add(0, 0)
    qkv_end()
    gu_end(2)
    gain_take(5)
    down_end()
    wires.drain()


def finish_kernel(
    output, grad_tokens, gains, qkv, out, gu, down_t,
    output_end, grad_tokens_end, qkv_end, out_end, gu_end, down_end, one_end, two_end,
):
    f32 = jnp.float32
    output_end[...] = output[...]
    grad_tokens_end[...] = grad_tokens[...]
    qkv_end[...] = qkv[:, : qkv_end.shape[1]].astype(f32)
    out_end[...] = out[:, : out_end.shape[1]].astype(f32)
    gu_end[...] = gu[...].astype(f32)
    down_end[...] = down_t[...].astype(f32)
    block = one_end.shape[0]
    width = gains.shape[1]
    start = lax.axis_index("dp") * block
    mine = pltpu.roll(gains[...], lax.rem(width - start, width), 1)
    one_end[...] = mine[0, :block]
    two_end[...] = mine[1, :block]


def on_device_fast(tokens, lengths, gain_one, w_qkv, w_out, gain_two, w_gate_up, w_down, cotangent):
    seq_count, row_count, width = tokens.shape
    own_rows = seq_count * row_count
    f32, low = jnp.float32, jnp.bfloat16
    block = gain_one.shape[0]
    slots = 4 * row_count
    place_of = np.arange(slots, dtype=np.float32)
    frequency = np.float32(10000.0) ** (-np.arange(HD // 2, dtype=np.float32) * np.float32(2.0 / HD))
    angle = place_of[:, None] * frequency[None, :]
    cosine = np.tile(np.cos(angle), (1, 4))
    sine = np.tile(np.concatenate([-np.sin(angle), np.sin(angle)], axis=1), (1, 2))
    rows, qkv_cols = w_qkv.shape
    out_cols = w_out.shape[1]
    units = w_gate_up.shape[1] // 2
    half, strip = w_down.shape
    qkv_wide = -(-qkv_cols // 128) * 128
    out_wide = -(-out_cols // 128) * 128
    deep = 8 * rows
    main = out_cols // 128 * 128
    packed = rows + 32
    slabs = KVH // 2
    stack = 2 * QH // KVH * row_count

    def box(*shape, dtype=low):
        return pltpu.VMEM(shape, dtype)

    scratch = [
        box(deep, qkv_wide), box(4, 8 * packed, main), box(4, deep, 128), box(rows, out_wide), box(deep, 3 * units),
        box(deep, qkv_wide), box(8 * packed, main), box(deep, 3 * units),
        box(8, 8, 256, dtype=f32), box(8, deep + 128, dtype=f32),
        box(own_rows, 128, dtype=f32), box(own_rows, 128, dtype=f32),
        box(4 * own_rows, width), box(4 * own_rows, width), box(4 * own_rows, width),
        box(4 * own_rows, width), box(4 * own_rows, QH * HD),
        box(own_rows, width, dtype=f32), box(own_rows, width, dtype=f32),
        box(own_rows, 4 * qkv_wide, dtype=f32),
        box(seq_count * slabs, stack, 128), box(seq_count, 2 * slabs, slots, 128),
        box(seq_count * slabs, stack, slots), box(seq_count * slabs, stack, 128, dtype=f32),
        box(seq_count * slabs, stack, 128),
        box(4, own_rows, out_wide), box(4, own_rows, qkv_wide),
        box(4, own_rows, qkv_wide, dtype=f32), box(4, own_rows, qkv_wide, dtype=f32),
        box(4 * own_rows, out_wide), box(4 * own_rows, qkv_wide),
        box(2, 4 * own_rows, half), box(2, 4 * own_rows, 2 * half),
        box(4, own_rows, width), box(3, own_rows, width),
        box(4, own_rows, width), box(3, own_rows, width),
        box(4, seq_count, 2 * slabs, row_count, 128), box(3, seq_count, 2 * slabs, row_count, 128),
        box(2, 4, rows, qkv_wide), box(2, 4, packed, main),
        box(3, 2, 4, rows, half), box(4, strip, half),
        box(2, 3, rows, qkv_wide), box(2, 3, packed, main),
        box(3, 2, 3, rows, half), box(2, 4, strip, half),
        box(2, 3, 2 * rows, half), box(rows, half),
        box(2, 2, rows, half), box(strip, half),
        box(6, 8, width, dtype=f32), box(6, 8, width, dtype=f32),
        pltpu.SemaphoreType.DMA((SENDS,)),
        pltpu.SemaphoreType.DMA((180,)),
        pltpu.SemaphoreType.DMA((8,)),
    ]
    vmem = pl.BlockSpec(memory_space=pltpu.MemorySpace.VMEM)
    hbm = pl.BlockSpec(memory_space=pltpu.MemorySpace.HBM)
    smem = pl.BlockSpec(memory_space=pltpu.MemorySpace.SMEM)
    shapes = (
        jax.ShapeDtypeStruct((own_rows, width), low),
        jax.ShapeDtypeStruct((own_rows, width), low),
        jax.ShapeDtypeStruct((8, width), f32),
        jax.ShapeDtypeStruct((rows, qkv_wide), low),
        jax.ShapeDtypeStruct((rows, out_wide), low),
        jax.ShapeDtypeStruct((rows, 2 * units), low),
        jax.ShapeDtypeStruct((strip, half), low),
    )
    results = pl.pallas_call(
        functools.partial(layer_kernel, {}),
        out_shape=shapes,
        in_specs=[vmem, vmem, smem, vmem, vmem, hbm, hbm] + [vmem] * 4,
        out_specs=[vmem] * 7,
        scratch_shapes=scratch,
        compiler_params=pltpu.CompilerParams(
            collective_id=0, has_side_effects=True, vmem_limit_bytes=64 * 2**20
        ),
        name="layer",
    )(
        tokens.reshape(own_rows, width), cotangent.reshape(own_rows, width), lengths,
        w_qkv, w_out, w_gate_up, w_down.T, gain_one, gain_two,
        cosine, sine,
    )
    output, grad_tokens, final_qkv, final_out, final_gu, final_dt, one, two = pl.pallas_call(
        finish_kernel,
        out_shape=(
            jax.ShapeDtypeStruct((own_rows, width), low),
            jax.ShapeDtypeStruct((own_rows, width), low),
            jax.ShapeDtypeStruct((rows, qkv_cols), f32),
            jax.ShapeDtypeStruct((rows, out_cols), f32),
            jax.ShapeDtypeStruct((rows, 2 * units), f32),
            jax.ShapeDtypeStruct((strip, half), f32),
            jax.ShapeDtypeStruct((block,), f32),
            jax.ShapeDtypeStruct((block,), f32),
        ),
        in_specs=[vmem] * 7,
        out_specs=[vmem] * 8,
        name="finish",
    )(*results)
    return (
        output.reshape(tokens.shape), grad_tokens.reshape(tokens.shape),
        one, final_qkv, final_out, two, final_gu, final_dt.T,
    )


def solution(mesh):
    fits = mesh.shape["dp"] == 8 and mesh.shape["ctx"] == 4
    return jax.shard_map(
        on_device_fast if fits else on_device,
        mesh=mesh,
        in_specs=(
            P("dp", "ctx", None),
            P("dp"),
            P("dp"),
            P("dp", "ctx"),
            P("dp", "ctx"),
            P("dp"),
            P("dp", "ctx"),
            P("dp", "ctx"),
            P("dp", "ctx", None),
        ),
        out_specs=(
            P("dp", "ctx", None),
            P("dp", "ctx", None),
            P("dp"),
            P("dp", "ctx"),
            P("dp", "ctx"),
            P("dp"),
            P("dp", "ctx"),
            P("dp", "ctx"),
        ),
        check_vma=False,
    )
```

```python
import enum
import functools
import math

import jax
import jax.numpy as jnp
import numpy as np
from jax import lax
from jax.experimental import pallas as pl
from jax.experimental.pallas import tpu as pltpu
from jax.sharding import PartitionSpec as P

QH = 18
KVH = 6
HD = 64
FF = 3072


EPS = 1e-05
NEGATIVE = -1e30


def angles(position, head_width):
    frequency = 10000.0 ** (-jnp.arange(head_width // 2, dtype=jnp.float32) * 2.0 / head_width)
    angle_table = position.astype(jnp.float32)[:, None] * frequency[None, :]
    return (jnp.cos(angle_table), jnp.sin(angle_table))


def rotate(values_in, cosine, sine_table):
    half_width = values_in.shape[-1] // 2
    first_half = values_in[..., :half_width]
    second = values_in[..., half_width:]
    return jnp.concatenate(
        [first_half * cosine - second * sine_table, second * cosine + first_half * sine_table],
        axis=-1,
    )


def split_heads(values_in, head_count):
    seq_count, row_count, col_count = values_in.shape
    head_width = col_count // head_count
    moved = values_in.reshape(seq_count, row_count, head_count, head_width).transpose(0, 2, 1, 3)
    return moved.reshape(seq_count * head_count, row_count, head_width)


def join_heads(values_in, seq_count):
    item_count, row_count, head_width = values_in.shape
    head_count = item_count // seq_count
    moved = values_in.reshape(seq_count, head_count, row_count, head_width).transpose(0, 2, 1, 3)
    return moved.reshape(seq_count, row_count, head_count * head_width)


def norm_back(source, inverse, gain, grad_in):
    scaled = grad_in * gain
    mean_term = jnp.mean(scaled * source, axis=-1, keepdims=True)
    back_rows = inverse * scaled - source * (inverse * inverse * inverse) * mean_term
    return (back_rows, jnp.sum(grad_in * source * inverse, axis=(0, 1)))


def block_scores(query_rows, key_rows, position, length, group_count, score_scale):
    raw_scores = (
        jnp.einsum("nd,td->nt", query_rows, key_rows, preferred_element_type=jnp.float32)
        * score_scale
    )
    raw_scores = raw_scores.reshape(group_count, position.shape[0], key_rows.shape[0])
    keyidx = jnp.arange(key_rows.shape[0], dtype=jnp.int32)
    allowed = (keyidx[None, :] <= position[:, None]) & (keyidx[None, :] < length)
    return jnp.where(allowed[None], raw_scores, NEGATIVE)


def on_device(tokens, lengths, gain_one, w_qkv, w_out, gain_two, w_gate_up, w_down, cotangent):
    forward_wide = (
        lax.all_gather(w_qkv, "ctx", axis=1, tiled=True),
        lax.all_gather(w_out, "ctx", axis=1, tiled=True),
        lax.all_gather(w_gate_up, "ctx", axis=1, tiled=True),
        lax.all_gather(w_down, "ctx", axis=1, tiled=True),
    )
    qkv_full, out_full, gate_up_full, down_full, gain_fa, gain_fb = (
        lax.all_gather(forward_wide[0], "dp", axis=0, tiled=True),
        lax.all_gather(forward_wide[1], "dp", axis=0, tiled=True),
        lax.all_gather(forward_wide[2], "dp", axis=0, tiled=True),
        lax.all_gather(forward_wide[3], "dp", axis=0, tiled=True),
        lax.all_gather(gain_one, "dp", axis=0, tiled=True),
        lax.all_gather(gain_two, "dp", axis=0, tiled=True),
    )
    seq_count, row_count, model_width = tokens.shape
    query_cols = QH * HD
    key_cols = KVH * HD
    group_count = QH // KVH
    score_scale = 1.0 / math.sqrt(HD)
    position = lax.axis_index("ctx") * row_count + jnp.arange(row_count, dtype=jnp.int32)
    valid_rows = position[None, :] < lengths[:, None]
    cosine, sine_table = angles(position, HD)
    cosine = cosine[:, None, :]
    sine_table = sine_table[:, None, :]
    source = tokens.astype(jnp.float32)
    inverse_one = lax.rsqrt(jnp.mean(source * source, axis=-1, keepdims=True) + EPS)
    normed_one = (source * inverse_one * gain_fa.astype(jnp.float32)).astype(jnp.bfloat16)
    projected = jnp.einsum("bsd,de->bse", normed_one, qkv_full, preferred_element_type=jnp.float32)
    queries = rotate(
        projected[..., :query_cols].reshape(seq_count, row_count, QH, HD), cosine, sine_table
    )
    queries = queries.astype(jnp.bfloat16).reshape(seq_count, row_count, query_cols)
    key_heads = rotate(
        projected[..., query_cols : query_cols + key_cols].reshape(seq_count, row_count, KVH, HD),
        cosine,
        sine_table,
    )
    key_heads = key_heads.astype(jnp.bfloat16).reshape(seq_count, row_count, key_cols)
    value_heads = projected[..., query_cols + key_cols :].astype(jnp.bfloat16)
    keys_all, values_all = (
        lax.all_gather(key_heads, "ctx", axis=1, tiled=True),
        lax.all_gather(value_heads, "ctx", axis=1, tiled=True),
    )
    query_blocks = split_heads(queries, QH).reshape(seq_count * KVH, group_count * row_count, HD)
    key_blocks = split_heads(keys_all, KVH)
    value_blocks = split_heads(values_all, KVH)
    pair_lengths = jnp.repeat(lengths, KVH)

    def forward_block(block_in):
        query_rows, key_rows, value_rows, length = block_in
        scores = block_scores(query_rows, key_rows, position, length, group_count, score_scale)
        row_max = jnp.max(scores, axis=-1, keepdims=True)
        exp_terms = jnp.exp(scores - row_max)
        row_total = jnp.sum(exp_terms, axis=-1, keepdims=True)
        prob_rows = (exp_terms / row_total).astype(jnp.bfloat16)
        result = jnp.einsum(
            "gst,td->gsd", prob_rows, value_rows, preferred_element_type=jnp.float32
        )
        return (result.reshape(-1, HD), (row_max + jnp.log(row_total))[..., 0])

    context_blocks, log_totals = lax.map(
        forward_block, (query_blocks, key_blocks, value_blocks, pair_lengths)
    )
    context = join_heads(context_blocks.reshape(seq_count * QH, row_count, HD), seq_count).astype(
        jnp.bfloat16
    )
    hidden = source + jnp.einsum(
        "bse,ed->bsd", context, out_full, preferred_element_type=jnp.float32
    )
    inverse_two = lax.rsqrt(jnp.mean(hidden * hidden, axis=-1, keepdims=True) + EPS)
    normed_two = (hidden * inverse_two * gain_fb.astype(jnp.float32)).astype(jnp.bfloat16)
    gate_up = jnp.einsum(
        "bsd,df->bsf", normed_two, gate_up_full, preferred_element_type=jnp.float32
    )
    gate_part = gate_up[..., :FF]
    up_part = gate_up[..., FF:]
    gate_sig = jax.nn.sigmoid(gate_part)
    swish_part = gate_part * gate_sig
    activation = (swish_part * up_part).astype(jnp.bfloat16)
    result_rows = hidden + jnp.einsum(
        "bsf,fd->bsd", activation, down_full, preferred_element_type=jnp.float32
    )
    output = jnp.where(valid_rows[..., None], result_rows, 0.0).astype(jnp.bfloat16)
    back_wide = (
        lax.all_gather(w_qkv, "ctx", axis=1, tiled=True),
        lax.all_gather(w_out, "ctx", axis=1, tiled=True),
        lax.all_gather(w_gate_up, "ctx", axis=1, tiled=True),
        lax.all_gather(w_down, "ctx", axis=1, tiled=True),
    )
    qkv_back, out_back, gate_up_back, down_back, gain_ba, gain_bb = (
        lax.all_gather(back_wide[0], "dp", axis=0, tiled=True),
        lax.all_gather(back_wide[1], "dp", axis=0, tiled=True),
        lax.all_gather(back_wide[2], "dp", axis=0, tiled=True),
        lax.all_gather(back_wide[3], "dp", axis=0, tiled=True),
        lax.all_gather(gain_one, "dp", axis=0, tiled=True),
        lax.all_gather(gain_two, "dp", axis=0, tiled=True),
    )
    grad_rows = jnp.where(valid_rows[..., None], cotangent, jnp.zeros_like(cotangent))
    grad_activation = jnp.einsum(
        "bsd,fd->bsf", grad_rows, down_back, preferred_element_type=jnp.float32
    )
    grad_gate = grad_activation * up_part * gate_sig * (1.0 + gate_part * (1.0 - gate_sig))
    grad_up = grad_activation * swish_part
    grad_mix = jnp.concatenate([grad_gate, grad_up], axis=-1).astype(jnp.bfloat16)
    grad_normed_two = jnp.einsum(
        "bsf,df->bsd", grad_mix, gate_up_back, preferred_element_type=jnp.float32
    )
    back_two, grad_gain_two = norm_back(
        hidden, inverse_two, gain_bb.astype(jnp.float32), grad_normed_two
    )
    grad_hidden = grad_rows.astype(jnp.float32) + back_two
    grad_branch = grad_hidden.astype(jnp.bfloat16)
    grad_context = jnp.einsum(
        "bsd,ed->bse", grad_branch, out_back, preferred_element_type=jnp.float32
    ).astype(jnp.bfloat16)
    grad_blocks = split_heads(grad_context, QH).reshape(
        seq_count * KVH, group_count * row_count, HD
    )

    def backward_block(block_in):
        query_rows, key_rows, value_rows, length, log_total, grad_in = block_in
        scores = block_scores(query_rows, key_rows, position, length, group_count, score_scale)
        prob_rows = jnp.exp(scores - log_total[..., None])
        grad_grouped = grad_in.reshape(group_count, -1, HD)
        grad_probs = jnp.einsum(
            "gsd,td->gst", grad_grouped, value_rows, preferred_element_type=jnp.float32
        )
        grad_value = jnp.einsum(
            "gst,gsd->td",
            prob_rows.astype(jnp.bfloat16),
            grad_grouped,
            preferred_element_type=jnp.float32,
        )
        row_delta = jnp.sum(prob_rows * grad_probs, axis=-1, keepdims=True)
        grad_scores = (prob_rows * (grad_probs - row_delta)).astype(jnp.bfloat16)
        grad_query = (
            jnp.einsum("gst,td->gsd", grad_scores, key_rows, preferred_element_type=jnp.float32)
            * score_scale
        )
        grad_key = (
            jnp.einsum(
                "gst,gsd->td",
                grad_scores,
                query_rows.reshape(group_count, -1, HD),
                preferred_element_type=jnp.float32,
            )
            * score_scale
        )
        return (grad_query.reshape(-1, HD), grad_key, grad_value)

    query_grads, key_grads, value_grads = lax.map(
        backward_block,
        (query_blocks, key_blocks, value_blocks, pair_lengths, log_totals, grad_blocks),
    )
    key_sums, value_sums = (
        lax.psum_scatter(
            join_heads(key_grads, seq_count).astype(jnp.bfloat16),
            "ctx",
            scatter_dimension=1,
            tiled=True,
        ).astype(jnp.float32),
        lax.psum_scatter(
            join_heads(value_grads, seq_count).astype(jnp.bfloat16),
            "ctx",
            scatter_dimension=1,
            tiled=True,
        ).astype(jnp.float32),
    )
    grad_queries = join_heads(query_grads.reshape(seq_count * QH, row_count, HD), seq_count)
    turned_queries = rotate(grad_queries.reshape(seq_count, row_count, QH, HD), cosine, -sine_table)
    turned_keys = rotate(key_sums.reshape(seq_count, row_count, KVH, HD), cosine, -sine_table)
    grad_mixed = jnp.concatenate(
        [
            turned_queries.reshape(seq_count, row_count, query_cols),
            turned_keys.reshape(seq_count, row_count, key_cols),
            value_sums,
        ],
        axis=-1,
    ).astype(jnp.bfloat16)
    grad_normed_one = jnp.einsum(
        "bse,de->bsd", grad_mixed, qkv_back, preferred_element_type=jnp.float32
    )
    back_one, grad_gain_one = norm_back(
        source, inverse_one, gain_ba.astype(jnp.float32), grad_normed_one
    )
    grad_tokens = (grad_hidden + back_one).astype(jnp.bfloat16)
    exchanged = (
        lax.all_to_all(grad_mixed, "ctx", split_axis=2, concat_axis=1, tiled=True),
        lax.all_to_all(grad_branch, "ctx", split_axis=2, concat_axis=1, tiled=True),
        lax.all_to_all(grad_mix, "ctx", split_axis=2, concat_axis=1, tiled=True),
        lax.all_to_all(grad_rows, "ctx", split_axis=2, concat_axis=1, tiled=True),
    )
    initial = (
        jnp.zeros((model_width, exchanged[0].shape[2]), jnp.float32),
        jnp.zeros((context.shape[2], exchanged[1].shape[2]), jnp.float32),
        jnp.zeros((model_width, exchanged[2].shape[2]), jnp.float32),
        jnp.zeros((activation.shape[2], exchanged[3].shape[2]), jnp.float32),
    )
    pieces = (
        lax.all_gather(normed_one, "ctx", axis=1, tiled=True),
        lax.all_gather(context, "ctx", axis=1, tiled=True),
        lax.all_gather(normed_two, "ctx", axis=1, tiled=True),
        lax.all_gather(activation, "ctx", axis=1, tiled=True),
    )
    updated = []
    for total, piece, right in zip(initial, pieces, exchanged):
        updated.append(jnp.einsum("bsr,bsc->rc", piece, right, preferred_element_type=jnp.float32))
    column_grads = tuple(updated)
    gain_whole = lax.psum((grad_gain_one, grad_gain_two), "ctx")
    final_qkv, final_out, final_gate_up, final_down, final_gain_one, final_gain_two = (
        lax.psum_scatter(
            column_grads[0].astype(jnp.bfloat16), "dp", scatter_dimension=0, tiled=True
        ).astype(jnp.float32),
        lax.psum_scatter(
            column_grads[1].astype(jnp.bfloat16), "dp", scatter_dimension=0, tiled=True
        ).astype(jnp.float32),
        lax.psum_scatter(
            column_grads[2].astype(jnp.bfloat16), "dp", scatter_dimension=0, tiled=True
        ).astype(jnp.float32),
        lax.psum_scatter(
            column_grads[3].astype(jnp.bfloat16), "dp", scatter_dimension=0, tiled=True
        ).astype(jnp.float32),
        lax.psum_scatter(
            gain_whole[0].astype(jnp.bfloat16), "dp", scatter_dimension=0, tiled=True
        ).astype(jnp.float32),
        lax.psum_scatter(
            gain_whole[1].astype(jnp.bfloat16), "dp", scatter_dimension=0, tiled=True
        ).astype(jnp.float32),
    )
    return (
        output,
        grad_tokens,
        final_gain_one,
        final_qkv,
        final_out,
        final_gain_two,
        final_gate_up,
        final_down,
    )


MESH = pl.DeviceIdType.MESH


class Place:
    def __init__(self):
        self.dp = lax.axis_index("dp")
        self.ctx = lax.axis_index("ctx")
        self.z = lax.div(self.dp, 2)
        self.y = lax.rem(self.dp, 2)
        self.x = lax.div(self.ctx, 2)
        self.c = lax.rem(self.ctx, 2)
        self.up = (self.dp + 2, self.ctx)
        self.down = (self.dp - 2, self.ctx)
        self.across = (self.dp + 1 - 2 * self.y, self.ctx)
        self.chip = (self.dp, (1 - self.x) * 2 + self.c)
        self.core = (self.dp, self.x * 2 + 1 - self.c)
        self.has_up = self.z < 3
        self.has_down = self.z > 0


def greet(place):
    barrier = pltpu.get_barrier_semaphore()

    def tell(device):
        pl.semaphore_signal(barrier, inc=1, device_id=device, device_id_type=MESH)

    pl.when(place.has_up)(lambda: tell(place.up))
    pl.when(place.has_down)(lambda: tell(place.down))
    tell(place.across)
    for step in (1, 2, 3):
        tell((place.dp, lax.rem(place.ctx + step, 4)))
    ends = place.has_up.astype(jnp.int32) + place.has_down.astype(jnp.int32)
    pl.semaphore_wait(barrier, 4 + ends)


class Way(enum.IntEnum):
    BELOW = 0
    ABOVE = 1


BELOW, ABOVE = Way.BELOW, Way.ABOVE
RINGS = (8, 14, 24, 20, 12)
SENDS = sum(RINGS)


class Wires:
    def __init__(self, send_sems, recv_sems, names, place):
        self.kinds = ((place.core,), (place.chip,), (place.across,), (place.up, place.down))
        self.counts = [0] * len(RINGS)
        self.send_sems = send_sems
        self.recv_sems = recv_sems
        self.index = names
        self.total = sum(names.values()) if names else 0
        self.base = {}
        self.live = {}

    def slot(self, name, size=1):
        if name not in self.base:
            self.base[name] = self.total
            self.total += size
        return self.base[name]

    def spot(self, name, plane):
        if name[0] in ("down", "down_y"):
            return self.slot(name[:2])
        if name[0] == "ddown":
            return self.slot(name[:3])
        if name[:2] in GROUPED or name[0] in SWAPS:
            return self.slot(name[:2] if name[:2] in GROUPED else name[:1])
        if len(name) > 2 and isinstance(name[-2], Way):
            way, dist = name[-2:]
            source = plane - dist if way == BELOW else plane + dist
            if name[-3] == "z":
                return self.slot(name[:-2], 5) + source + int(way)
            return self.slot(name[:-2], 4) + source
        return self.slot(name)

    def send(self, src, dst, name, device, cond=None, extra=None):
        kind = 4
        for at, devices in enumerate(self.kinds):
            if any(device is known for known in devices):
                kind = at
        number = (kind, self.counts[kind])
        self.counts[kind] += 1
        self.settle((kind, number[1] - RINGS[kind]))
        at = self.spot(name, lax.div(device[0], 2))
        if extra is not None:
            at = at + extra
        copy = pltpu.make_async_remote_copy(
            src_ref=src,
            dst_ref=dst,
            send_sem=self.send_sems.at[sum(RINGS[:kind]) + number[1] % RINGS[kind]],
            recv_sem=self.recv_sems.at[at],
            device_id=device,
            device_id_type=MESH,
        )
        when(cond, copy.start)
        self.live[number] = (copy, cond, name)

    def take(self, dst, name, device, extra=None):
        at = self.spot(name, lax.div(lax.axis_index("dp"), 2))
        if extra is not None:
            at = at + extra
        pltpu.make_async_remote_copy(
            src_ref=dst,
            dst_ref=dst,
            send_sem=self.send_sems.at[0],
            recv_sem=self.recv_sems.at[at],
            device_id=device,
            device_id_type=MESH,
        ).wait_recv()

    def settle(self, number):
        if number in self.live:
            copy, cond, name = self.live.pop(number)
            when(cond, copy.wait_send)

    def drain(self):
        for number in list(self.live):
            self.settle(number)

    def drain_named(self, first):
        for number in list(self.live):
            if self.live[number][2][0] == first:
                self.settle(number)


GROUPED = (("out", "c"), ("out", "d"), ("gain", "y")) + tuple((("gu", n), "y") for n in range(3))
SWAPS = ("pq", "kv", "gb", "gm")


def both(first, second):
    return second if first is None else jnp.logical_and(first, second)


def source_valid(place, way, dist):
    return place.z >= dist if way == BELOW else place.z + dist <= 3


def source_pos(place, way, dist):
    return place.dp - 2 * dist if way == BELOW else place.dp + 2 * dist


def flood_start(wires, place, name, own, block, spread):
    wires.send(own, block(place.dp), (name, BELOW, 1), place.up, place.has_up)
    wires.send(own, block(place.dp), (name, ABOVE, 1), place.down, place.has_down)
    wires.send(own, block(place.dp), (name, "y", 0, 0), place.across)
    spread(own, place.dp, (0, 0, 0), None)


def flood_step(wires, place, name, block, spread, way, dist):
    here = source_valid(place, way, dist)
    pos = source_pos(place, way, dist)
    view = block(pos)
    came_from = place.down if way == BELOW else place.up
    pl.when(here)(lambda: wires.take(view, (name, way, dist), came_from))
    if dist < 3:
        onward = place.up if way == BELOW else place.down
        more = place.has_up if way == BELOW else place.has_down
        wires.send(view, view, (name, way, dist + 1), onward, jnp.logical_and(here, more))
    wires.send(view, view, (name, "y", way, dist), place.across, here)
    spread(view, pos, (0, way, dist), here)


def flood_side(wires, place, name, block, spread, way, dist):
    if dist == 0:
        here, pos = None, place.dp
    else:
        here, pos = source_valid(place, way, dist), source_pos(place, way, dist)
    pos = pos + 1 - 2 * place.y
    view = block(pos)
    if here is None:
        wires.take(view, (name, "y", 0, 0), place.across)
    else:
        pl.when(here)(lambda: wires.take(view, (name, "y", way, dist), place.across))
    spread(view, pos, (1, way, dist), here)


HOPS = [(way, dist) for dist in (1, 2, 3) for way in (BELOW, ABOVE)]


def no_spread(view, pos, key, cond):
    return None


def add_rows(dst, srcs, out=None, cast=None, chunk=48):
    out = dst if out is None else out
    total_rows = dst.shape[0]
    if total_rows % chunk:
        chunk = total_rows

    def body(i, carry):
        at = pl.ds(pl.multiple_of(i * chunk, 16), chunk)
        total = dst[at, :].astype(jnp.float32)
        for src in srcs:
            total = total + src[at, :].astype(jnp.float32)
        out[at, :] = total.astype(out.dtype)
        return carry

    lax.fori_loop(0, total_rows // chunk, body, 0)


def when(cond, action):
    if cond is None:
        action()
    else:
        pl.when(cond)(action)


DRAIN = [(way, dist) for dist in (3, 2, 1, 0) for way in (BELOW, ABOVE)]


def nn(a, b):
    return jnp.dot(a, b, preferred_element_type=jnp.float32)


def nt(a, b):
    return lax.dot_general(a, b, (((1,), (1,)), ((), ())), preferred_element_type=jnp.float32)


def tn(a, b):
    return lax.dot_general(a, b, (((0,), (0,)), ((), ())), preferred_element_type=jnp.float32)


def layer_kernel(
    names,
    tokens, cot, lengths, qkv_in, out_in, gu_in, dt_in, gain_one, gain_two, cos_table, sin_table,
    output, grad_tokens, gain_out, qkv_out, out_out, gu_out, dt_out,
    w_qkv, w_out, w_rest, out_pad, w_ff, d_qkv, d_out, d_ff, gain_all, gain_row, cos, sin,
    tok_all, n1_all, n2_all, g_all, ctx_all, hidden, grad_hidden, proj, q_st, kv_all, p_st, att, go_st,
    wide, gm, pq, pq_in, gb_all, gm_all, act, d_gu, gp, gp_box, op, op_box, dkv, dkv_box,
    qkv_side, out_side, gu_side, down_side, qkv_inbox, out_inbox, gu_inbox, down_inbox,
    up_inbox, up_side, gu_mix, down_mix, gain_box, gain_acc,
    send_sems, recv_sems, local_sems,
):
    f32, low = jnp.float32, jnp.bfloat16
    place = Place()
    wires = Wires(send_sems, recv_sems, names, place)
    dp, ctx, z, y, x, c = place.dp, place.ctx, place.z, place.y, place.x, place.c
    rows = qkv_in.shape[0]
    strip, half = dt_in.shape
    width = tokens.shape[1]
    own_rows = tokens.shape[0]
    slots_here = own_rows // 2
    qkv_cols, out_cols = qkv_in.shape[1], out_in.shape[1]
    qkv_wide, out_wide = w_qkv.shape[1], out_pad.shape[1]
    main = w_out.shape[2]
    packed = w_out.shape[1] // 8
    spare = packed - rows
    rest = out_cols - main
    pieces = -(-rows // spare)
    group = QH // KVH
    slabs = KVH // 2
    q_slabs = QH // 2
    span = 3 * half
    deep = w_ff.shape[0]
    score_scale = 1.0 / math.sqrt(HD)
    TILES = range(2)

    greet(place)

    def block_rows(pos):
        return pl.ds(pl.multiple_of(pos * rows, 16), rows)

    def lead_rows(lead):
        return pl.ds(pl.multiple_of(lead * own_rows, 16), own_rows)

    here_rows = lead_rows(ctx)
    my_rows = block_rows(dp)

    def share(name, ref):
        mine = ref.at[here_rows]
        wires.send(mine, mine, (name, "x"), place.chip)
        wires.send(mine, mine, (name, "c"), place.core)

    def share_on(name, ref):
        far = ref.at[lead_rows(place.chip[1])]
        wires.take(far, (name, "x"), place.chip)
        wires.send(far, far, (name, "d"), place.core)

    def share_end(name, ref):
        for mark, lead in (("c", place.core[1]), ("d", 3 - ctx)):
            wires.take(ref.at[lead_rows(lead)], (name, mark), place.core)

    def swap_start(name, src, dst):
        for step in (1, 2, 3):
            peer = lax.rem(ctx + step, 4)
            wires.send(src(peer), dst(ctx), (name, step), (dp, peer))

    def swap_end(name, three):
        wires.take(three, (name, 1), place.core)

    locals_ = []

    def local(src, dst, cond=None):
        copy = pltpu.make_async_copy(src, dst, local_sems.at[len(locals_)])
        locals_.append((copy, cond))
        when(cond, copy.start)

    SIDES = [(0, 0)] + HOPS
    WAYS = {0: [(0, 0)], 1: HOPS[:2], 2: HOPS[2:4], 3: HOPS[4:]}

    class Flood:
        def __init__(self, name, block, spread=no_spread):
            self.name, self.block, self.spread = name, block, spread

        def start(self):
            flood_start(wires, place, self.name, self.block(dp), self.block, self.spread)

        def hop(self, dist, way):
            way = Way(way)
            flood_step(wires, place, self.name, self.block, self.spread, way, dist)

        def side(self, dist, way):
            way = Way(way) if dist else way
            flood_side(wires, place, self.name, self.block, self.spread, way, dist)

    class PairFlood:
        def __init__(self, name, ref, cols):
            self.name, self.ref, self.cols = name, ref, cols

        def pair(self, plane):
            return self.ref.at[pl.ds(pl.multiple_of(2 * rows * plane, 16), 2 * rows), self.cols]

        def one(self, pos):
            return self.ref.at[block_rows(pos), self.cols]

        def start(self):
            wires.send(self.one(dp), self.one(dp), (self.name, "y"), place.across)

        def side(self):
            wires.take(self.one(place.across[0]), (self.name, "y"), place.across)
            view = self.pair(z)
            wires.send(view, view, (self.name, BELOW, 1), place.up, place.has_up)
            wires.send(view, view, (self.name, ABOVE, 1), place.down, place.has_down)

        def hop(self, dist, way):
            way = Way(way)
            here = source_valid(place, way, dist)
            view = self.pair(z - dist if way == BELOW else z + dist)
            came_from = place.down if way == BELOW else place.up
            pl.when(here)(lambda: wires.take(view, (self.name, way, dist), came_from))
            if dist < 3:
                onward = place.up if way == BELOW else place.down
                more = place.has_up if way == BELOW else place.has_down
                wires.send(view, view, (self.name, way, dist + 1), onward, jnp.logical_and(here, more))

    def packed_rows(pos):
        return pl.ds(pl.multiple_of(pos * packed, 16), packed)

    def pack(values, dest):
        dest[:rows, :] = values[:, :main].astype(low)
        for slab in range(0, main, 128):
            total = jnp.zeros((spare, 128), f32)
            for number in range(slab // rest, min(pieces, (slab + 128) // rest)):
                height = min(spare, rows - number * spare)
                piece = values[number * spare : number * spare + height, main : main + 128]
                if height < spare:
                    piece = jnp.concatenate([piece, jnp.zeros((spare - height, 128), f32)], axis=0)
                shift = number * rest - slab
                total = total + (pltpu.roll(piece, shift, 1) if shift else piece)
            dest[rows:, slab : slab + 128] = total.astype(low)

    def unpack(view, dest):
        keep = lax.broadcasted_iota(jnp.int32, (spare, 128), 1) < rest
        for number in range(pieces):
            slab = number * rest // 128 * 128
            shift = number * rest - slab
            piece = view[rows:, slab : slab + 128].astype(f32)
            piece = pltpu.roll(piece, 128 - shift, 1) if shift else piece
            height = min(spare, rows - number * spare)
            piece = jnp.where(keep, piece, 0.0).astype(low)
            dest[number * spare : number * spare + height, :] = piece[:height]

    def out_weights(j):
        first = jnp.concatenate([w_out[j, pos * packed : pos * packed + rows, :] for pos in range(8)], axis=0)
        return jnp.concatenate([first, w_rest[j]], axis=1)

    def out_block(lead, pos):
        return w_out.at[lead, packed_rows(pos)]

    def out_spread(view, pos, key, cond):
        wires.send(view, out_block(ctx, pos), ("out", "x") + key, place.chip, cond)
        wires.send(view, out_block(ctx, pos), ("out", "c") + key, place.core, cond)

    qkv_flood = Flood("qkv", lambda pos: w_qkv.at[block_rows(pos)])
    gain_flood = Flood("gain", lambda pos: gain_all.at[pos])
    out_flood = Flood("out", functools.partial(out_block, ctx), out_spread)

    PARTS = [(tile, part) for tile in TILES for part in range(2)]

    def part_cols(number):
        tile, part = PARTS[number]
        return pl.ds(tile * span + part * half, half)

    def gu_view(ref, number, pos):
        return ref.at[block_rows(pos), part_cols(number)]

    gu_floods = [Flood(("gu", number), functools.partial(gu_view, w_ff, number)) for number in range(3)]
    up_flood = PairFlood("up", w_ff, part_cols(3))

    def spots(column, dist, way=None):
        for way, dist in WAYS[dist] if way is None else [(way, dist)]:
            if dist == 0:
                here, pos = None, dp
            else:
                here, pos = source_valid(place, way, dist), source_pos(place, way, dist)
            if column == 1:
                pos = pos + 1 - 2 * y
            yield (column, way, dist), here, pos

    def out_chip(column, dist, way):
        way = Way(way) if dist else way
        for key, here, pos in spots(column, dist, way):
            view = out_block(place.chip[1], pos)
            when(here, lambda: wires.take(view, ("out", "x") + key, place.chip))
            wires.send(view, view, ("out", "d") + key, place.core, here)

    def out_core():
        for mark, lead in (("c", place.core[1]), ("d", 3 - ctx)):
            wires.take(w_out.at[lead], ("out", mark), place.core)

    def gu_sides(number):
        wires.take(w_ff.at[pl.ds(0, 4 * rows), part_cols(number)], (("gu", number), "y"), place.across)

    def mix_start(tile):
        for part in range(2):
            target = 2 * c + part
            src = gu_in.at[:, pl.ds((2 * part + tile) * half, half)]
            dst = w_ff.at[my_rows, pl.ds(pl.multiple_of(tile * span + x * half, 128), half)]
            wires.slot(("gu_mix", tile), 2)
            wires.send(src, dst, ("gu_mix", tile), (dp, target), target != ctx, extra=x)
            local(src, dst, target == ctx)

    def mix_end(number):
        tile, part = PARTS[number]
        origin = part * 2 + x
        view = gu_view(w_ff, number, dp)
        pl.when(origin != ctx)(lambda: wires.take(view, ("gu_mix", tile), (dp, origin), extra=part))

    lanes = pl.ds(pl.multiple_of(y * span + 2 * half, 128), half)
    other_lanes = pl.ds(pl.multiple_of((1 - y) * span + 2 * half, 128), half)
    at_home = ctx == z

    def strips_of(ref, at):
        return [ref.at[pl.ds(j * strip, strip), at] for j in range(4)]

    strips, other_strips = strips_of(w_ff, lanes), strips_of(w_ff, other_lanes)

    def down_mix_start():
        dst = w_ff.at[pl.ds(pl.multiple_of(ctx * strip, 16), strip), lanes]
        wires.slot(("down_mix",), 4)
        wires.send(dt_in, dst, ("down_mix",), (dp, z), ctx != z, extra=ctx)
        local(dt_in, dst, ctx == z)

    def tables():
        for table, ref in ((cos_table, cos), (sin_table, sin)):
            mine = table[pl.ds(pl.multiple_of(ctx * slots_here, 16), slots_here), :]
            ref[:slots_here, :] = mine
            ref[slots_here:, :] = mine

    def down_start(j):
        pl.when(jnp.logical_and(at_home, ctx != j))(lambda: wires.take(strips[j], ("down_mix",), (dp, j), extra=j))
        wires.send(strips[j], strips[j], ("down", j, BELOW, 1), place.up, jnp.logical_and(at_home, place.has_up))
        wires.send(strips[j], strips[j], ("down", j, ABOVE, 1), place.down, jnp.logical_and(at_home, place.has_down))
        wires.send(strips[j], strips[j], ("down_y", j, 0, 0), place.across, at_home)

    def down_hop(dist, j):
        for way in (BELOW, ABOVE):
            here = (z - ctx if way == BELOW else ctx - z) == dist
            came_from = place.down if way == BELOW else place.up
            onward = place.up if way == BELOW else place.down
            more = place.has_up if way == BELOW else place.has_down
            pl.when(here)(lambda: wires.take(strips[j], ("down", j, way, dist), came_from))
            if dist < 3:
                wires.send(strips[j], strips[j], ("down", j, way, dist + 1), onward, jnp.logical_and(here, more))
            wires.send(strips[j], strips[j], ("down_y", j, way, dist), place.across, here)

    def down_side_end():
        for way, dist in SIDES:
            here = at_home if dist == 0 else (z - ctx if way == BELOW else ctx - z) == dist

            def take():
                for j in range(4):
                    wires.take(other_strips[j], ("down_y", j, way, dist), place.across)

            pl.when(here)(take)

    row_at = lax.broadcasted_iota(jnp.int32, (own_rows, 1), 0)
    first_seq = row_at < slots_here
    position = ctx * slots_here + jnp.where(first_seq, row_at, row_at - slots_here)
    valid = position < jnp.where(first_seq, lengths[0], lengths[1])
    def tokens_start():
        tok_all[here_rows, :] = tokens[...]
        share("tok", tok_all)

    def qkv_start():
        w_qkv[my_rows, :] = jnp.zeros((rows, qkv_wide), low)
        w_qkv[my_rows, :qkv_cols] = qkv_in[...]
        qkv_flood.start()

    def gain_start():
        gain_all[dp] = jnp.zeros(gain_all.shape[1:], f32)
        gain_all[dp, 0:1, :rows] = gain_one[...].reshape(1, rows).astype(f32)
        gain_all[dp, 1:2, :rows] = gain_two[...].reshape(1, rows).astype(f32)
        gain_flood.start()

    def out_start():
        out_pad[...] = jnp.zeros(out_pad.shape, low)
        out_pad[:, :out_cols] = out_in[...]
        pack(out_pad[...].astype(f32), out_block(ctx, dp))
        out_flood.start()

    def cot_start():
        g_all[here_rows, :] = jnp.where(valid, cot[...].astype(f32), 0.0).astype(low)
        share("cot", g_all)

    def gain_sides():
        wires.take(gain_all.at[pl.ds(0, 4)], ("gain", "y"), place.across)

    gain_a = lambda: gain_row[0:1, :width]
    gain_b = lambda: gain_row[1:2, :width]

    def norm(values):
        return lax.rsqrt(jnp.mean(values * values, axis=-1, keepdims=True) + EPS)

    lane = lax.broadcasted_iota(jnp.int32, (own_rows, 128), 1)
    low_half = lax.rem(lane, HD) < HD // 2
    side_of = lax.div(lane, HD)

    def turn(values, sign):
        swapped = jnp.where(low_half, pltpu.roll(values, 128 - HD // 2, 1), pltpu.roll(values, HD // 2, 1))
        return values * cos[...] + swapped * (sin[...] * sign)

    def head_spots():
        for head in range(QH):
            kv = head // group
            yield head // 2, head % 2, kv // 2, kv % 2, (kv % 2 * group + head % group) * slots_here

    def stack_heads(slab_of, dest, scale):
        for slab, side, key_slab, key_side, at in head_spots():
            values = slab_of(slab)
            if side != key_side:
                values = pltpu.roll(values, HD, 1)
            values = (jnp.where(side_of == key_side, values, 0.0) * scale).astype(low)
            for seq in range(2):
                dest[seq * slabs + key_slab, at : at + slots_here, :] = values[
                    seq * slots_here : (seq + 1) * slots_here
                ]

    def unstack_heads(src, slab):
        total = jnp.zeros((own_rows, 128), f32)
        for at_slab, side, key_slab, key_side, at in head_spots():
            if at_slab != slab:
                continue
            values = jnp.concatenate(
                [src[seq * slabs + key_slab, at : at + slots_here, :] for seq in range(2)], axis=0
            )
            values = jnp.where(side_of == key_side, values, 0.0)
            if side != key_side:
                values = pltpu.roll(values, HD, 1)
            total = total + values
        return total

    def project():
        gain_row[...] = jnp.zeros(gain_row.shape, f32)
        for pos in range(8):
            piece = gain_all[pos]
            shift = (pos * rows) % 128
            if shift:
                piece = pltpu.roll(piece, shift, 1)
            at = (pos * rows) // 128 * 128
            gain_row[:, at : at + 256] += piece

        def body(i, carry):
            at = lead_rows(i)
            source = tok_all[at, :].astype(f32)
            n1_all[at, :] = (source * norm(source) * gain_a()).astype(low)
            return carry

        lax.fori_loop(0, 4, body, 0)
        pq[...] = nn(n1_all[...], w_qkv[...]).reshape(pq.shape)
        pq_in[ctx] = pq[ctx]
        swap_start("pq", lambda peer: pq.at[peer], lambda sender: pq_in.at[sender])

    def pq_end():
        swap_end("pq", pq_in.at[pl.ds(0, 3)])
        proj[...] = jnp.zeros(proj.shape, f32)
        for j in range(4):
            part = jnp.concatenate([pq_in[j], jnp.zeros((own_rows, 128), f32)], axis=1)
            at = qkv_cols * j
            if at % 128:
                part = pltpu.roll(part, at % 128, 1)
            proj[:, at // 128 * 128 : at // 128 * 128 + qkv_wide + 128] += part

    turned = {}

    def query_slab(slab):
        if slab not in turned:
            turned[slab] = turn(proj[:, slab * 128 : slab * 128 + 128], 1.0)
        return turned[slab]

    def slot_view(lead):
        return kv_all.at[:, :, pl.ds(pl.multiple_of(lead * slots_here, 16), slots_here)]

    def kv_start():
        my_slots = pl.ds(pl.multiple_of(ctx * slots_here, 16), slots_here)
        for slab in range(2 * slabs):
            at = (q_slabs + slab) * 128
            values = proj[:, at : at + 128]
            if slab < slabs:
                values = turn(values, 1.0)
            values = values.astype(low)
            for seq in range(2):
                kv_all[seq, slab, my_slots, :] = values[seq * slots_here : (seq + 1) * slots_here]

        swap_start("kv", lambda peer: slot_view(ctx), slot_view)

    def queries():
        stack_heads(query_slab, q_st, score_scale)

    def kv_end():
        swap_end("kv", kv_all.at[:, :, pl.ds(0, 3 * slots_here)])

    stack = q_st.shape[1]
    slots = kv_all.shape[2]

    def attend(i, carry):
        seq, slab = lax.div(i, slabs), lax.rem(i, slabs)
        scores = nt(q_st[i], kv_all[seq, slab])
        at = ctx * slots_here + lax.rem(lax.broadcasted_iota(jnp.int32, (stack, slots), 0), slots_here)
        key_at = lax.broadcasted_iota(jnp.int32, (stack, slots), 1)
        length = jnp.where(seq == 0, lengths[0], lengths[1])
        allowed = jnp.logical_and(key_at <= at, key_at < length)
        scores = jnp.where(allowed, scores, NEGATIVE)
        terms = jnp.exp(scores - jnp.max(scores, axis=-1, keepdims=True))
        probs = (terms / jnp.sum(terms, axis=-1, keepdims=True)).astype(low)
        p_st[i] = probs
        att[i] = nn(probs, kv_all[seq, slabs + slab])
        return carry

    def attention():
        lax.fori_loop(0, 2 * slabs, attend, 0)
        for slab in range(q_slabs):
            ctx_all[here_rows, slab * 128 : slab * 128 + 128] = unstack_heads(att, slab).astype(low)
        share("ctx", ctx_all)

    def out_project():
        for j in range(4):
            for pos in range(8):
                unpack(w_out.at[j, packed_rows(pos)], w_rest.at[j, block_rows(pos)])
        hidden[...] = tokens[...].astype(f32)
        for j in range(4):
            part = nn(ctx_all[here_rows, :], out_weights(j))
            at = out_cols * j
            if at % 128:
                part = pltpu.roll(part, at % 128, 1)
            hidden[:, at // 128 * 128 : at // 128 * 128 + out_wide] += part
        n2_all[here_rows, :] = (hidden[...] * norm(hidden[...]) * gain_b()).astype(low)
        share("n2", n2_all)

    tall = 2 * own_rows

    def feed(tile):
        def body(i, carry):
            at = pl.ds(0, 4 * own_rows)
            gate = nn(n2_all[at, :], w_ff[:, tile * span : tile * span + half])
            up = nn(n2_all[at, :], w_ff[:, tile * span + half : tile * span + 2 * half])
            back = nn(g_all[at, :], w_ff[:, tile * span + 2 * half : (tile + 1) * span])
            sig = jax.nn.sigmoid(gate)
            swish = gate * sig
            act[tile, at, :] = (swish * up).astype(low)
            d_gu[tile, at, :half] = (back * up * sig * (1.0 + gate * (1.0 - sig))).astype(low)
            d_gu[tile, at, half:] = (back * swish).astype(low)
            return carry

        body(0, 0)

    def grad_ff(tile):
        def body(m, carry):
            at = pl.ds(pl.multiple_of(m * width, 128), width)
            d_ff[at, tile * span : tile * span + 2 * half] = tn(n2_all[:, at], d_gu[tile]).astype(low)
            d_ff[at, tile * span + 2 * half : (tile + 1) * span] = tn(g_all[:, at], act[tile]).astype(low)
            return carry

        lax.fori_loop(0, 1, body, 0)

    across_core = (1 - x) * 2 + 1 - c
    across_own = (1 - x) * 2 + c
    beside = x * 2 + 1 - c
    wide_tile = width

    def group_send(name, ref, box, which):
        lead, mark = ((across_core, "cx"), (beside, "cc"))[which]
        wires.send(ref.at[lead], box.at[which], (name, mark), place.core)

    def group_on(name, ref, box):
        wires.take(box.at[0], (name, "cx"), place.core)
        mine = ref.at[across_own]
        mine[...] = (mine[...].astype(f32) + box[0].astype(f32)).astype(low)
        wires.send(mine, box.at[2], (name, "x"), place.chip)

    def group_end(name, ref, box):
        wires.take(box.at[1], (name, "cc"), place.core)
        wires.take(box.at[2], (name, "x"), place.chip)
        return ref[ctx].astype(f32) + box[1].astype(f32) + box[2].astype(f32)

    def pair_rows(half_x):
        return pl.ds(pl.multiple_of(half_x * tall, 16), tall)

    def group_product(ref, terms):
        def compute(half_x):
            def body(n, carry):
                at = pl.ds(pl.multiple_of(n * wide_tile, 128), wide_tile)
                total = None
                for left, right in terms:
                    term = nt(left(pair_rows(half_x)), right(at))
                    total = term if total is None else total + term
                ref[2 * half_x, :, at] = total[:own_rows].astype(low)
                ref[2 * half_x + 1, :, at] = total[own_rows:].astype(low)
                return carry

            lax.fori_loop(0, width // wide_tile, body, 0)

        return compute

    back_terms = [
        (lambda at, tile=tile: d_gu[tile, at, :], lambda at, tile=tile: w_ff[at, tile * span : tile * span + 2 * half])
        for tile in TILES
    ]
    forward_terms = [
        (lambda at, tile=tile: act[tile, at, :], lambda at, tile=tile: w_ff[at, tile * span + 2 * half : (tile + 1) * span])
        for tile in TILES
    ]

    def key_pos(way, dist):
        if dist == 0:
            return None, dp
        return source_valid(place, way, dist), source_pos(place, way, dist)

    KEYS = {3: DRAIN[:2], 2: DRAIN[2:4], 1: DRAIN[4:6], 0: [(BELOW, 0)]}
    flip = 1 - 2 * y

    def z_add(name, view, boxes, inbox, way, dist):
        here, pos = key_pos(way, dist)
        mine = view(pos)
        if dist == 0:
            wires.take(boxes.at[way, dist], (name, "y", way, dist), place.across)
            add_rows(mine, [boxes.at[way, dist]])
            for end, fed, feeder in ((BELOW, place.has_up, place.up), (ABOVE, place.has_down, place.down)):

                def own():
                    wires.take(inbox.at[end, 0], (name, "z", end, 0), feeder)
                    add_rows(mine, [inbox.at[end, 0]])

                pl.when(fed)(own)
            return
        fed = place.has_up if way == BELOW else place.has_down
        feeder = place.up if way == BELOW else place.down
        onward = place.down if way == BELOW else place.up
        side = boxes.at[way, dist]

        def first():
            wires.take(side, (name, "y", way, dist), place.across)
            add_rows(mine, [side])

        if dist == 3:
            pl.when(here)(first)
        else:

            def more():
                wires.take(side, (name, "y", way, dist), place.across)
                wires.take(inbox.at[way, dist], (name, "z", way, dist), feeder)
                add_rows(mine, [side, inbox.at[way, dist]])

            pl.when(jnp.logical_and(here, jnp.logical_not(fed)))(first)
            pl.when(jnp.logical_and(here, fed))(more)
        wires.send(mine, inbox.at[way, dist - 1], (name, "z", way, dist - 1), onward, here)

    class Sink:
        def __init__(self, name, view, side, inbox):
            self.name, self.view, self.side, self.inbox = name, view, side, inbox

        def send(self, dist, way):
            way = Way(way) if dist else way
            here, pos = key_pos(way, dist)
            wires.send(
                self.view(pos + flip), self.side.at[way, dist],
                (self.name, "y", way, dist), place.across, here,
            )

        def add(self, dist, way):
            way = Way(way) if dist else way
            z_add(self.name, self.view, self.side, self.inbox, way, dist)

    gu_sinks = [
        Sink(("dgu", number), functools.partial(gu_view, d_ff, number), gu_side.at[number], gu_inbox.at[number])
        for number in range(3)
    ]
    out_sink = Sink("dout", lambda pos: d_out.at[packed_rows(pos)], out_side, out_inbox)
    qkv_sink = Sink("dqkv", lambda pos: d_qkv.at[block_rows(pos)], qkv_side, qkv_inbox)
    d_strips, d_other_strips = strips_of(d_ff, lanes), strips_of(d_ff, other_lanes)

    def down_send(tile, j):
        wires.send(d_other_strips[j], down_side.at[j], ("ddown_y", j), place.across, (1 - y) == tile)

    def down_add(dist, j):
        if dist == 0:

            def finish():
                wires.take(down_side.at[j], ("ddown_y", j), place.across)
                add_rows(d_strips[j], [down_side.at[j]])
                for end, fed, feeder in ((BELOW, place.has_up, place.up), (ABOVE, place.has_down, place.down)):

                    def more():
                        wires.take(down_inbox.at[end, j], ("ddown", j, end, 0), feeder)
                        add_rows(d_strips[j], [down_inbox.at[end, j]])

                    pl.when(fed)(more)

            pl.when(at_home)(finish)
            return
        for way in (BELOW, ABOVE):
            here = (z - ctx if way == BELOW else ctx - z) == dist
            fed = place.has_up if way == BELOW else place.has_down
            feeder = place.up if way == BELOW else place.down
            onward = place.down if way == BELOW else place.up

            def first():
                wires.take(down_side.at[j], ("ddown_y", j), place.across)
                add_rows(d_strips[j], [down_side.at[j]])

            def more():
                wires.take(down_side.at[j], ("ddown_y", j), place.across)
                wires.take(down_inbox.at[way, j], ("ddown", j, way, dist), feeder)
                add_rows(d_strips[j], [down_side.at[j], down_inbox.at[way, j]])

            pl.when(jnp.logical_and(here, jnp.logical_not(fed)))(first)
            pl.when(jnp.logical_and(here, fed))(more)
            wires.send(d_strips[j], down_inbox.at[way, j], ("ddown", j, way, dist - 1), onward, here)

    class PairSink:
        def __init__(self, name, ref, cols, inbox, side):
            self.name, self.ref, self.cols, self.inbox, self.side = name, ref, cols, inbox, side

        def pair(self, plane):
            return self.ref.at[pl.ds(pl.multiple_of(2 * rows * plane, 16), 2 * rows), self.cols]

        def one(self, pos):
            return self.ref.at[block_rows(pos), self.cols]

        def add(self, dist, way):
            if dist == 0:
                mine = self.pair(z)
                for end, fed, feeder in ((BELOW, place.has_up, place.up), (ABOVE, place.has_down, place.down)):

                    def more():
                        wires.take(self.inbox.at[end, 0], (self.name, "z", end, 0), feeder)
                        add_rows(mine, [self.inbox.at[end, 0]])

                    pl.when(fed)(more)
                wires.send(self.one(place.across[0]), self.side, (self.name, "y"), place.across)
                return
            way = Way(way)
            here = source_valid(place, way, dist)
            mine = self.pair(z - dist if way == BELOW else z + dist)
            fed = place.has_up if way == BELOW else place.has_down
            feeder = place.up if way == BELOW else place.down
            onward = place.down if way == BELOW else place.up
            if dist < 3:

                def more():
                    wires.take(self.inbox.at[way, dist], (self.name, "z", way, dist), feeder)
                    add_rows(mine, [self.inbox.at[way, dist]])

                pl.when(jnp.logical_and(here, fed))(more)
            wires.send(mine, self.inbox.at[way, dist - 1], (self.name, "z", way, dist - 1), onward, here)

        def end(self):
            wires.take(self.side, (self.name, "y"), place.across)
            add_rows(self.one(dp), [self.side])

    up_sink = PairSink("dup", d_ff, part_cols(3), up_inbox, up_side)

    def gu_finish(number):
        tile, part = PARTS[number]
        target = part * 2 + x
        block = gu_view(d_ff, number, dp)
        wires.slot(("dgu_mix", tile), 2)
        wires.send(block, gu_mix.at[c, tile], ("dgu_mix", tile), (dp, target), target != ctx, extra=c)
        pl.when(target == ctx)(lambda: add_rows(block, [], out=gu_mix.at[c, tile]))

    def gu_end(number):
        tile, part = PARTS[number]
        origin = 2 * c + part
        box = gu_mix.at[part, tile]
        pl.when(origin != ctx)(lambda: wires.take(box, ("dgu_mix", tile), (dp, origin), extra=part))
        add_rows(box, [], out=gu_out.at[:, pl.ds((2 * part + tile) * half, half)])

    def down_finish():
        for j in range(4):
            wires.send(d_strips[j], down_mix, ("ddown_mix",), (dp, j), jnp.logical_and(at_home, ctx != j))
            pl.when(jnp.logical_and(at_home, ctx == j))(functools.partial(add_rows, d_strips[j], [], down_mix))

    def down_end():
        pl.when(ctx != z)(lambda: wires.take(down_mix, ("ddown_mix",), (dp, z)))
        add_rows(down_mix, [], out=dt_out)

    def norm_back(values, inverse, gain, grad_in):
        scaled = grad_in * gain
        mean_term = jnp.mean(scaled * values, axis=-1, keepdims=True)
        back = inverse * scaled - values * (inverse * inverse * inverse) * mean_term
        return back, jnp.sum(grad_in * values * inverse, axis=0, keepdims=True)

    def gp_block(which):
        half_x = 1 - x if which == 0 else x
        group_product(gp, back_terms)(half_x)
        group_send("gp", gp, gp_box, which)

    def op_block(which):
        half_x = 1 - x if which == 0 else x
        group_product(op, forward_terms)(half_x)
        group_send("op", op, op_box, which)

    def hidden_back():
        gain_acc[0] = jnp.zeros(gain_out.shape, f32)
        back_two, gain_two_grad = norm_back(hidden[...], norm(hidden[...]), gain_b(), group_end("gp", gp, gp_box))
        gain_acc[0, 1:2, :] = gain_two_grad
        grad_hidden[...] = g_all[here_rows, :].astype(f32) + back_two
        out_lane = lax.broadcasted_iota(jnp.int32, (own_rows, out_wide), 1)
        for j in range(4):
            at = out_cols * j
            part = grad_hidden[:, at // 128 * 128 : at // 128 * 128 + out_wide]
            if at % 128:
                part = pltpu.roll(part, out_wide - at % 128, 1)
            wide[j] = jnp.where(out_lane < out_cols, part, 0.0).astype(low)
        gb_all[here_rows, :] = wide[ctx]
        swap_start("gb", lambda peer: wide.at[peer], lambda sender: gb_all.at[lead_rows(sender)])

    def context_back(n, carry):
        at = pl.ds(0, width)
        total = nt(wide[0], out_weights(0))
        for j in range(1, 4):
            total = total + nt(wide[j], out_weights(j))
        proj[:, at] = total
        return carry

    def grad_context():
        lax.fori_loop(0, width // wide_tile, context_back, 0)
        stack_heads(lambda slab: proj[:, slab * 128 : slab * 128 + 128], go_st, 1.0)

    def attend_back(i, carry):
        seq, slab = lax.div(i, slabs), lax.rem(i, slabs)
        grad_probs = nt(go_st[i], kv_all[seq, slabs + slab])
        probs = p_st[i].astype(f32)
        delta = jnp.sum(probs * grad_probs, axis=-1, keepdims=True)
        grad_scores = (probs * (grad_probs - delta)).astype(low)
        att[i] = nn(grad_scores, kv_all[seq, slab]) * score_scale
        grad_key = tn(grad_scores, q_st[i])
        grad_value = tn(p_st[i], go_st[i])
        for j in range(4):
            part = slice(j * slots_here, (j + 1) * slots_here)
            dkv[j, seq, slab] = grad_key[part].astype(low)
            dkv[j, seq, slabs + slab] = grad_value[part].astype(low)
        return carry

    def attention_back():
        lax.fori_loop(0, 2 * slabs, attend_back, 0)
        group_send("dkv", dkv, dkv_box, 0)
        group_send("dkv", dkv, dkv_box, 1)

    def gb_end():
        swap_end("gb", gb_all.at[pl.ds(0, 3 * own_rows)])

    def grad_out_all():
        result = tn(ctx_all[...], gb_all[...])
        for pos in range(8):
            pack(result[pos * rows : (pos + 1) * rows], d_out.at[packed_rows(pos)])

    def grad_mixed():
        sums = group_end("dkv", dkv, dkv_box)
        proj[...] = jnp.zeros(proj.shape, f32)
        for slab in range(q_slabs):
            proj[:, slab * 128 : slab * 128 + 128] = turn(unstack_heads(att, slab), -1.0)
        for slab in range(2 * slabs):
            values = jnp.concatenate([sums[0, slab], sums[1, slab]], axis=0)
            if slab < slabs:
                values = turn(values, -1.0)
            at = (q_slabs + slab) * 128
            proj[:, at : at + 128] = values
        qkv_lane = lax.broadcasted_iota(jnp.int32, (own_rows, qkv_wide), 1)
        for j in range(4):
            at = qkv_cols * j
            part = proj[:, at // 128 * 128 : at // 128 * 128 + qkv_wide + 128]
            if at % 128:
                part = pltpu.roll(part, qkv_wide + 128 - at % 128, 1)
            gm[j] = jnp.where(qkv_lane < qkv_cols, part[:, :qkv_wide], 0.0).astype(low)
        gm_all[here_rows, :] = gm[ctx]
        swap_start("gm", lambda peer: gm.at[peer], lambda sender: gm_all.at[lead_rows(sender)])

    def gm_end():
        swap_end("gm", gm_all.at[pl.ds(0, 3 * own_rows)])

    def grad_qkv(m, carry):
        at = pl.ds(pl.multiple_of(m * width, 128), width)
        d_qkv[at, :] = tn(n1_all[:, at], gm_all[...]).astype(low)
        return carry

    def grad_qkv_all():
        lax.fori_loop(0, 1, grad_qkv, 0)

    tokens_terms = [(lambda at: gm_all[at, :], lambda at: w_qkv[at, :])]

    def gt_block(which):
        if which == 0:
            wires.drain_named("gp")
        half_x = 1 - x if which == 0 else x
        group_product(gp, tokens_terms)(half_x)
        group_send("gt", gp, gp_box, which)

    def output_end():
        result = hidden[...] + group_end("op", op, op_box)
        output[...] = jnp.where(valid, result, 0.0).astype(low)

    def tokens_end():
        source = tokens[...].astype(f32)
        back_one, gain_one_grad = norm_back(source, norm(source), gain_a(), group_end("gt", gp, gp_box))
        gain_acc[0, 0:1, :] = gain_one_grad
        grad_tokens[...] = (grad_hidden[...] + back_one).astype(low)

    low_end, high_end = z == 0, z == 3
    mid_low, mid_high = z == 1, z == 2

    def gain_send(hop):
        def go(device, cond=None):
            wires.send(gain_acc.at[hop], gain_box.at[hop], ("gain_sum", hop), device, cond)

        if hop < 3:
            go((place.core, place.chip, place.across)[hop])
        elif hop == 3:
            go(place.up, low_end)
            go(place.down, high_end)
        elif hop == 4:
            go(place.up, mid_low)
            go(place.down, mid_high)
        else:
            go(place.down, mid_low)
            go(place.up, mid_high)

    def gain_take(hop):
        def add(device):
            wires.take(gain_box.at[hop], ("gain_sum", hop), device)
            gain_acc[hop + 1] = gain_acc[hop] + gain_box[hop]

        def last(device):
            wires.take(gain_box.at[hop], ("gain_sum", hop), device)
            gain_out[...] = gain_box[hop]

        def done():
            gain_out[...] = gain_acc[hop]

        if hop < 3:
            add((place.core, place.chip, place.across)[hop])
        elif hop == 3:
            pl.when(mid_low)(lambda: add(place.down))
            pl.when(mid_high)(lambda: add(place.up))
        elif hop == 4:
            pl.when(mid_low)(lambda: add(place.up))
            pl.when(mid_high)(lambda: add(place.down))
        else:
            pl.when(low_end)(lambda: last(place.up))
            pl.when(high_end)(lambda: last(place.down))
            pl.when(mid_low)(done)
            pl.when(mid_high)(done)

    def out_end():
        mine = d_out.at[packed_rows(dp)]
        out_out[:, :main] = mine[:rows, :]
        unpack(mine, out_out.at[:, pl.ds(main, 128)])

    def qkv_end():
        qkv_out[...] = d_qkv[my_rows, :]

    def locals_end():
        for copy, cond in locals_:
            when(cond, copy.wait)

    mix_start(0)
    tables()
    qkv_start()
    out_start()
    mix_start(1)
    tokens_start()
    out_chip(0, 0, 0)
    down_mix_start()
    locals_end()
    mix_end(0)
    gu_floods[0].start()
    mix_end(1)
    gu_floods[1].start()
    qkv_flood.hop(1, 0)
    qkv_flood.hop(1, 1)
    gain_start()
    gain_flood.hop(1, 0)
    qkv_flood.hop(2, 0)
    out_flood.hop(1, 1)
    out_flood.hop(1, 0)
    gain_flood.hop(2, 0)
    gain_flood.hop(1, 1)
    gain_flood.hop(2, 1)
    qkv_flood.hop(2, 1)
    gu_floods[0].hop(1, 0)
    out_flood.side(0, 0)
    gain_flood.hop(3, 0)
    gain_flood.hop(3, 1)
    qkv_flood.hop(3, 0)
    qkv_flood.side(1, 0)
    mix_end(3)
    out_flood.hop(2, 1)
    qkv_flood.hop(3, 1)
    down_start(1)
    out_flood.hop(2, 0)
    cot_start()
    share_on("tok", tok_all)
    mix_end(2)
    gu_floods[2].start()
    qkv_flood.side(2, 0)
    out_flood.hop(3, 1)
    down_start(0)
    out_chip(0, 1, 0)
    qkv_flood.side(0, 0)
    qkv_flood.side(3, 1)
    qkv_flood.side(3, 0)
    qkv_flood.side(2, 1)
    down_start(3)
    qkv_flood.side(1, 1)
    share_end("tok", tok_all)
    gain_sides()
    project()
    out_flood.hop(3, 0)
    down_hop(1, 1)
    down_hop(2, 1)
    down_hop(1, 0)
    down_hop(2, 0)
    out_flood.side(1, 0)
    up_flood.start()
    down_hop(1, 3)
    down_start(2)
    down_hop(1, 2)
    gu_floods[2].hop(1, 0)
    gu_floods[0].hop(1, 1)
    pq_end()
    kv_start()
    out_chip(0, 3, 1)
    out_chip(0, 2, 1)
    gu_floods[0].hop(2, 0)
    gu_floods[0].hop(2, 1)
    out_chip(1, 0, 0)
    gu_floods[2].hop(1, 1)
    down_hop(3, 1)
    gu_floods[1].hop(1, 1)
    down_hop(2, 3)
    share_on("cot", g_all)
    out_chip(0, 3, 0)
    out_flood.side(3, 0)
    gu_floods[1].hop(1, 0)
    out_flood.side(3, 1)
    out_chip(1, 1, 0)
    queries()
    out_flood.side(2, 0)
    out_flood.side(1, 1)
    down_hop(2, 2)
    out_chip(0, 2, 0)
    up_flood.side()
    down_hop(3, 0)
    out_flood.side(2, 1)
    gu_floods[0].hop(3, 0)
    kv_end()
    attention()
    down_hop(3, 3)
    down_hop(3, 2)
    out_chip(1, 3, 0)
    out_chip(1, 1, 1)
    gu_floods[0].hop(3, 1)
    out_chip(1, 2, 0)
    gu_floods[1].hop(2, 0)
    up_flood.hop(1, 0)
    out_chip(1, 2, 1)
    out_chip(1, 3, 1)
    gu_floods[1].hop(2, 1)
    out_chip(0, 1, 1)
    share_end("cot", g_all)
    out_core()
    out_project()
    gu_floods[1].hop(3, 1)
    up_flood.hop(1, 1)
    gu_floods[1].hop(3, 0)
    gu_floods[2].hop(2, 1)
    gu_floods[2].hop(2, 0)
    gu_floods[2].hop(3, 0)
    gu_floods[2].hop(3, 1)
    up_flood.hop(2, 0)
    up_flood.hop(2, 1)
    share_on("n2", n2_all)
    share_end("n2", n2_all)
    gu_sides(0)
    gu_sides(1)
    down_side_end()
    feed(0)
    grad_ff(0)
    gu_sinks[0].send(3, 1)
    gu_sinks[1].send(2, 1)
    gu_sinks[0].send(3, 0)
    gu_sinks[1].send(3, 0)
    gu_sinks[1].send(2, 0)
    down_send(0, 0)
    up_flood.hop(3, 1)
    up_flood.hop(3, 0)
    gu_sides(2)
    feed(1)
    grad_ff(1)
    up_sink.add(3, 1)
    down_send(1, 0)
    up_sink.add(3, 0)
    gu_sinks[0].send(2, 0)
    gu_sinks[1].send(3, 1)
    gp_block(0)
    op_block(0)
    group_on("gp", gp, gp_box)
    gp_block(1)
    gu_sinks[0].send(2, 1)
    down_send(1, 1)
    down_send(0, 1)
    up_sink.add(2, 1)
    gu_sinks[2].send(2, 1)
    gu_sinks[0].add(3, 0)
    gu_sinks[1].add(3, 0)
    gu_sinks[1].add(2, 0)
    up_sink.add(2, 0)
    gu_sinks[2].send(3, 1)
    group_on("op", op, op_box)
    gu_sinks[2].send(3, 0)
    gu_sinks[1].send(1, 0)
    gu_sinks[0].add(2, 0)
    down_send(0, 3)
    down_send(1, 3)
    down_add(3, 0)
    gu_sinks[2].send(2, 0)
    gu_sinks[0].send(1, 1)
    up_sink.add(1, 1)
    hidden_back()
    down_send(0, 2)
    gu_sinks[0].add(3, 1)
    share_on("ctx", ctx_all)
    grad_context()
    attention_back()
    down_add(3, 1)
    down_send(1, 2)
    gu_sinks[1].add(3, 1)
    group_on("dkv", dkv, dkv_box)
    gu_sinks[0].add(2, 1)
    share_end("ctx", ctx_all)
    gb_end()
    grad_out_all()
    down_add(3, 3)
    gu_sinks[2].send(1, 1)
    out_sink.send(3, 0)
    gu_sinks[1].send(1, 1)
    gu_sinks[1].add(1, 0)
    gu_sinks[1].add(2, 1)
    down_add(2, 1)
    grad_mixed()
    gu_sinks[2].add(3, 1)
    gu_sinks[2].send(0, 0)
    gu_sinks[2].add(3, 0)
    gu_sinks[2].send(1, 0)
    down_add(2, 3)
    down_add(1, 1)
    up_sink.add(1, 0)
    gu_sinks[0].add(1, 1)
    out_sink.send(3, 1)
    out_sink.send(1, 1)
    gu_sinks[0].send(1, 0)
    gm_end()
    down_add(2, 0)
    gu_sinks[0].send(0, 0)
    gt_block(0)
    group_on("gt", gp, gp_box)
    grad_qkv_all()
    qkv_sink.send(2, 1)
    qkv_sink.send(3, 0)
    down_add(3, 2)
    qkv_sink.send(3, 1)
    gu_sinks[2].add(2, 0)
    gu_sinks[2].add(2, 1)
    down_add(1, 3)
    gu_sinks[1].send(0, 0)
    gt_block(1)
    gu_sinks[1].add(1, 1)
    down_add(2, 2)
    down_add(1, 0)
    qkv_sink.send(2, 0)
    gu_sinks[0].add(1, 0)
    out_sink.send(1, 0)
    gu_sinks[2].add(1, 1)
    up_sink.add(0, 0)
    out_sink.add(3, 1)
    out_sink.send(2, 1)
    gu_sinks[2].add(1, 0)
    tokens_end()
    out_sink.send(2, 0)
    gain_send(0)
    gain_take(0)
    gain_send(1)
    gain_take(1)
    gain_send(2)
    out_sink.add(3, 0)
    op_block(1)
    down_add(1, 2)
    qkv_sink.add(3, 1)
    gu_sinks[0].add(0, 0)
    gu_finish(0)
    qkv_sink.add(3, 0)
    qkv_sink.send(1, 1)
    out_sink.add(2, 0)
    out_sink.add(2, 1)
    gu_sinks[1].add(0, 0)
    down_add(0, 1)
    gu_sinks[2].add(0, 0)
    gu_finish(1)
    up_sink.end()
    qkv_sink.send(1, 0)
    gain_take(2)
    gain_send(3)
    qkv_sink.add(2, 1)
    qkv_sink.add(2, 0)
    down_add(0, 0)
    down_add(0, 2)
    down_add(0, 3)
    down_finish()
    out_sink.add(1, 0)
    gu_finish(3)
    out_sink.add(1, 1)
    gu_finish(2)
    output_end()
    gain_take(3)
    gu_end(0)
    gu_end(1)
    gain_send(4)
    qkv_sink.send(0, 0)
    qkv_sink.add(1, 1)
    qkv_sink.add(1, 0)
    out_sink.send(0, 0)
    gain_take(4)
    gain_send(5)
    gu_end(3)
    out_sink.add(0, 0)
    out_end()
    qkv_sink.add(0, 0)
    qkv_end()
    gu_end(2)
    gain_take(5)
    down_end()
    wires.drain()


def finish_kernel(
    output, grad_tokens, gains, qkv, out, gu, down_t,
    output_end, grad_tokens_end, qkv_end, out_end, gu_end, down_end, one_end, two_end,
):
    f32 = jnp.float32
    output_end[...] = output[...]
    grad_tokens_end[...] = grad_tokens[...]
    qkv_end[...] = qkv[:, : qkv_end.shape[1]].astype(f32)
    out_end[...] = out[:, : out_end.shape[1]].astype(f32)
    gu_end[...] = gu[...].astype(f32)
    down_end[...] = down_t[...].astype(f32)
    block = one_end.shape[0]
    width = gains.shape[1]
    start = lax.axis_index("dp") * block
    mine = pltpu.roll(gains[...], lax.rem(width - start, width), 1)
    one_end[...] = mine[0, :block]
    two_end[...] = mine[1, :block]


def on_device_fast(tokens, lengths, gain_one, w_qkv, w_out, gain_two, w_gate_up, w_down, cotangent):
    seq_count, row_count, width = tokens.shape
    own_rows = seq_count * row_count
    f32, low = jnp.float32, jnp.bfloat16
    block = gain_one.shape[0]
    slots = 4 * row_count
    place_of = np.arange(slots, dtype=np.float32)
    frequency = np.float32(10000.0) ** (-np.arange(HD // 2, dtype=np.float32) * np.float32(2.0 / HD))
    angle = place_of[:, None] * frequency[None, :]
    cosine = np.tile(np.cos(angle), (1, 4))
    sine = np.tile(np.concatenate([-np.sin(angle), np.sin(angle)], axis=1), (1, 2))
    rows, qkv_cols = w_qkv.shape
    out_cols = w_out.shape[1]
    units = w_gate_up.shape[1] // 2
    half, strip = w_down.shape
    qkv_wide = -(-qkv_cols // 128) * 128
    out_wide = -(-out_cols // 128) * 128
    deep = 8 * rows
    main = out_cols // 128 * 128
    packed = rows + 32
    slabs = KVH // 2
    stack = 2 * QH // KVH * row_count

    def box(*shape, dtype=low):
        return pltpu.VMEM(shape, dtype)

    scratch = [
        box(deep, qkv_wide), box(4, 8 * packed, main), box(4, deep, 128), box(rows, out_wide), box(deep, 3 * units),
        box(deep, qkv_wide), box(8 * packed, main), box(deep, 3 * units),
        box(8, 8, 256, dtype=f32), box(8, deep + 128, dtype=f32),
        box(own_rows, 128, dtype=f32), box(own_rows, 128, dtype=f32),
        box(4 * own_rows, width), box(4 * own_rows, width), box(4 * own_rows, width),
        box(4 * own_rows, width), box(4 * own_rows, QH * HD),
        box(own_rows, width, dtype=f32), box(own_rows, width, dtype=f32),
        box(own_rows, 4 * qkv_wide, dtype=f32),
        box(seq_count * slabs, stack, 128), box(seq_count, 2 * slabs, slots, 128),
        box(seq_count * slabs, stack, slots), box(seq_count * slabs, stack, 128, dtype=f32),
        box(seq_count * slabs, stack, 128),
        box(4, own_rows, out_wide), box(4, own_rows, qkv_wide),
        box(4, own_rows, qkv_wide, dtype=f32), box(4, own_rows, qkv_wide, dtype=f32),
        box(4 * own_rows, out_wide), box(4 * own_rows, qkv_wide),
        box(2, 4 * own_rows, half), box(2, 4 * own_rows, 2 * half),
        box(4, own_rows, width), box(3, own_rows, width),
        box(4, own_rows, width), box(3, own_rows, width),
        box(4, seq_count, 2 * slabs, row_count, 128), box(3, seq_count, 2 * slabs, row_count, 128),
        box(2, 4, rows, qkv_wide), box(2, 4, packed, main),
        box(3, 2, 4, rows, half), box(4, strip, half),
        box(2, 3, rows, qkv_wide), box(2, 3, packed, main),
        box(3, 2, 3, rows, half), box(2, 4, strip, half),
        box(2, 3, 2 * rows, half), box(rows, half),
        box(2, 2, rows, half), box(strip, half),
        box(6, 8, width, dtype=f32), box(6, 8, width, dtype=f32),
        pltpu.SemaphoreType.DMA((SENDS,)),
        pltpu.SemaphoreType.DMA((178,)),
        pltpu.SemaphoreType.DMA((8,)),
    ]
    vmem = pl.BlockSpec(memory_space=pltpu.MemorySpace.VMEM)
    hbm = pl.BlockSpec(memory_space=pltpu.MemorySpace.HBM)
    smem = pl.BlockSpec(memory_space=pltpu.MemorySpace.SMEM)
    shapes = (
        jax.ShapeDtypeStruct((own_rows, width), low),
        jax.ShapeDtypeStruct((own_rows, width), low),
        jax.ShapeDtypeStruct((8, width), f32),
        jax.ShapeDtypeStruct((rows, qkv_wide), low),
        jax.ShapeDtypeStruct((rows, out_wide), low),
        jax.ShapeDtypeStruct((rows, 2 * units), low),
        jax.ShapeDtypeStruct((strip, half), low),
    )
    results = pl.pallas_call(
        functools.partial(layer_kernel, {}),
        out_shape=shapes,
        in_specs=[vmem, vmem, smem, vmem, vmem, hbm, hbm] + [vmem] * 4,
        out_specs=[vmem] * 7,
        scratch_shapes=scratch,
        compiler_params=pltpu.CompilerParams(
            collective_id=0, has_side_effects=True, vmem_limit_bytes=64 * 2**20
        ),
        name="layer",
    )(
        tokens.reshape(own_rows, width), cotangent.reshape(own_rows, width), lengths,
        w_qkv, w_out, w_gate_up, w_down.T, gain_one, gain_two,
        cosine, sine,
    )
    output, grad_tokens, final_qkv, final_out, final_gu, final_dt, one, two = pl.pallas_call(
        finish_kernel,
        out_shape=(
            jax.ShapeDtypeStruct((own_rows, width), low),
            jax.ShapeDtypeStruct((own_rows, width), low),
            jax.ShapeDtypeStruct((rows, qkv_cols), f32),
            jax.ShapeDtypeStruct((rows, out_cols), f32),
            jax.ShapeDtypeStruct((rows, 2 * units), f32),
            jax.ShapeDtypeStruct((strip, half), f32),
            jax.ShapeDtypeStruct((block,), f32),
            jax.ShapeDtypeStruct((block,), f32),
        ),
        in_specs=[vmem] * 7,
        out_specs=[vmem] * 8,
        name="finish",
    )(*results)
    return (
        output.reshape(tokens.shape), grad_tokens.reshape(tokens.shape),
        one, final_qkv, final_out, two, final_gu, final_dt.T,
    )


def solution(mesh):
    fits = mesh.shape["dp"] == 8 and mesh.shape["ctx"] == 4
    return jax.shard_map(
        on_device_fast if fits else on_device,
        mesh=mesh,
        in_specs=(
            P("dp", "ctx", None),
            P("dp"),
            P("dp"),
            P("dp", "ctx"),
            P("dp", "ctx"),
            P("dp"),
            P("dp", "ctx"),
            P("dp", "ctx"),
            P("dp", "ctx", None),
        ),
        out_specs=(
            P("dp", "ctx", None),
            P("dp", "ctx", None),
            P("dp"),
            P("dp", "ctx"),
            P("dp", "ctx"),
            P("dp"),
            P("dp", "ctx"),
            P("dp", "ctx"),
        ),
        check_vma=False,
    )
```
